32 devices in a mesh: rep: 4 (over y, x), fsdp: 8 (over z, core).
Axes of the slice: x: 2, y: 2, z: 4, core: 2. Of those that a mesh axis runs over, the one named last changes fastest.
Arguments:
- tokens: bfloat16 [16384, 768], P(('rep', 'fsdp')), may hold values from -6 to 6
- cotangent: bfloat16 [16384, 768], P(('rep', 'fsdp')), may hold values from -6 to 6
- place: int32 [16384], P(('rep', 'fsdp')), may hold values from 0 to 4095, as said below
- seq_lengths: int32 [32, 4], P(('rep', 'fsdp')), may hold values from 0 to 512, as said below
- random_blocks: int32 [256, 12, 3], P(('rep', 'fsdp')), may hold values from 0 to 7
- owner_slot: int32 [12], replicated, may hold values from 0 to 15, as said below
- flat_weights: float32 [768, 9216], P('fsdp')
- vectors: float32 [768, 12], P('fsdp')
- moment_first: float32 [768, 12], P('fsdp')
- moment_second: float32 [768, 12], P('fsdp')
- stat_left: float32 [16, 768, 768], P('fsdp')
- stat_right: float32 [16, 768, 768], P('fsdp')
- root_left: float32 [16, 768, 768], P('fsdp')
- root_right: float32 [16, 768, 768], P('fsdp')
Outputs:
- layer_out: bfloat16 [16384, 768], P(('rep', 'fsdp'))
- input_grad: bfloat16 [16384, 768], P(('rep', 'fsdp'))
- weight_grads: float32 [768, 9216], P('fsdp')
- new_weights: float32 [768, 9216], P('fsdp')
- new_left: float32 [16, 768, 768], P('fsdp')
- new_right: float32 [16, 768, 768], P('fsdp')
- new_first: float32 [768, 12], P('fsdp')
- new_second: float32 [768, 12], P('fsdp')
- new_vectors: float32 [768, 12], P('fsdp')
The draws below stay inside these ranges and needn't reach their ends.
Inputs may be any that keep to these rules, and one draw needn't show every extreme that they name: Within each group place is a permutation of the group's slots; slots d * 512 to (d + 1) * 512 - 1 are those of device d. Each device sends exactly 64 of its tokens to each device of its group, and those from device s take that device's slots s * 64 onward in increasing arrival order. `seq_lengths`: A pack's sequences take together at most 8 blocks; length 0 marks an unused entry; in every group some pack holds a sequence of exactly 512 tokens. `owner_slot`: Distinct; slot o lies on device o // 2 of each group.
All inputs are finite; a program needn't handle non-finite values.
Results may differ from the reference program's by a relative error of at most 0.014.
The reference program's roundings to bfloat16 on the way count: a program that leaves them out, or rounds other values in their place, can miss the bound.
Values may be sent and summed in bfloat16 or wider, within the bound.
A program may use at most 192 MiB of HBM per device.

```python
import math
import jax
import jax.numpy as jnp
from jax import lax

D = 768
H = 12
HD = 64
FF = 3072
BLK = 64
NGLOB = 2
NRAND = 3
STEP = 10
SEQ_DEV = 4
TOK_DEV = 512
LMAX = 512
NBLK = 12
NVEC = 12
OWNER_SLOTS = 16
GROUP_TOK = 4096
PACKS = 32
TOKENS = 16384


def owner_table(key):
    shuffled = jax.random.permutation(jax.random.fold_in(key, 11), OWNER_SLOTS).astype(jnp.int32)
    target = jax.random.randint(jax.random.fold_in(key, 12), (), 0, NBLK).astype(jnp.int32)
    places = jnp.arange(OWNER_SLOTS, dtype=jnp.int32)
    where_top = jnp.sum(jnp.where(shuffled == OWNER_SLOTS - 1, places, 0)).astype(jnp.int32)
    swapped = shuffled.at[where_top].set(shuffled[target]).at[target].set(OWNER_SLOTS - 1)
    return swapped[:NBLK].astype(jnp.int32)


def draw_owner_slot(key, part):
    return owner_table(key)


def draw_place(key, part):
    group_peers = GROUP_TOK // TOK_DEV
    share_rows = TOK_DEV // group_peers
    sender_keys = jax.random.split(jax.random.fold_in(key, 31), PACKS)

    def one_sender(sender_key):
        shuffled = jax.random.permutation(sender_key, TOK_DEV).astype(jnp.int32)
        target = (shuffled % group_peers).astype(jnp.int32)
        table = (target[:, None] == jnp.arange(group_peers, dtype=jnp.int32)[None, :]).astype(jnp.int32)
        before = jnp.cumsum(table, axis=0) - table
        rank = jnp.sum(before * table, axis=1).astype(jnp.int32)
        return (target, rank)
    target, rank = jax.vmap(one_sender)(sender_keys)
    sender_pos = (jnp.arange(PACKS, dtype=jnp.int32) % group_peers)[:, None]
    result = target * TOK_DEV + sender_pos * share_rows + rank
    return result.reshape(TOKENS).astype(jnp.int32)


def draw_seq_lengths(key, part):
    group_peers = GROUP_TOK // TOK_DEV
    block_total = TOK_DEV // BLK
    most_blocks = LMAX // BLK
    cuts = jnp.sort(jax.random.randint(jax.random.fold_in(key, 21), (PACKS, SEQ_DEV - 1), 0, block_total + 1), axis=1)
    edges = jnp.concatenate([jnp.zeros((PACKS, 1), jnp.int32), cuts.astype(jnp.int32), jnp.full((PACKS, 1), block_total, jnp.int32)], axis=1)
    pieces = jnp.minimum(edges[:, 1:] - edges[:, :-1], most_blocks)
    pads = jax.random.randint(jax.random.fold_in(key, 22), (PACKS, SEQ_DEV), 0, BLK)
    lengths = jnp.where(pieces > 0, pieces * BLK - pads, 0)
    chosen = jax.random.randint(jax.random.fold_in(key, 23), (PACKS // group_peers,), 0, group_peers)
    chosen_row = jnp.arange(PACKS, dtype=jnp.int32) % group_peers == jnp.repeat(chosen, group_peers)
    whole = jnp.where(jnp.arange(SEQ_DEV, dtype=jnp.int32) == 0, LMAX, 0)
    return jnp.where(chosen_row[:, None], whole[None, :], lengths).astype(jnp.int32)


def column_scales():
    blocks = jnp.arange(NBLK * D) // D
    narrow = (D / 2.0) ** (-0.5)
    drawn = D ** (-0.5)
    wide_out = (D // 8) ** (-0.5)
    down_scale = FF ** (-0.5)
    return jnp.where(blocks < 2, narrow, jnp.where(blocks == 2, drawn, jnp.where(blocks == 3, wide_out, jnp.where(blocks < 4 + FF // D, drawn, down_scale))))


def draw_flat_weights(key, part):
    base = jax.random.normal(key, (D, NBLK * D))
    return (base * column_scales()[None, :]).astype(jnp.float32)


def draw_vectors(key, part):
    noise = jax.random.normal(jax.random.fold_in(key, 41), (D, NVEC)) * 0.3
    gains = jax.random.uniform(jax.random.fold_in(key, 42), (D, NVEC), minval=0.7, maxval=1.3)
    columns = jnp.arange(NVEC)
    is_gain = (columns == 4) | (columns == 6)
    return jnp.where(is_gain[None, :], gains, noise).astype(jnp.float32)


def vector_scales():
    columns = jnp.arange(NVEC)
    table = jnp.array([0.15, 0.5, 0.55, 0.7, 0.8, 0.8, 1.0, 1.0], jnp.float32)
    factor = jnp.where(columns < 8, table[jnp.minimum(columns, 7)], 0.2)
    return factor * math.sqrt(TOKENS)


def draw_moment_first(key, part):
    noise = jax.random.normal(jax.random.fold_in(key, 51), (D, NVEC))
    return (noise * (0.1 / 0.9) * vector_scales()[None, :]).astype(jnp.float32)


def draw_moment_second(key, part):
    factor = jnp.exp(jax.random.uniform(jax.random.fold_in(key, 52), (D, NVEC), minval=0.0, maxval=math.log(4.0)))
    grad_size = vector_scales()[None, :]
    return (factor * (0.001 / 0.999) * grad_size * grad_size).astype(jnp.float32)


def slot_scales(key):
    owners = owner_table(key)
    block_ids = jnp.arange(NBLK)
    per_block = jnp.where(block_ids < 2, 0.15, jnp.where(block_ids == 2, 0.5, jnp.where(block_ids == 3, 0.2, jnp.where(block_ids < 4 + FF // D, 0.2, 0.45))))
    hits = owners[None, :] == jnp.arange(OWNER_SLOTS, dtype=jnp.int32)[:, None]
    factor = jnp.where(jnp.any(hits, axis=1), jnp.sum(jnp.where(hits, per_block[None, :], 0.0), axis=1), 0.3)
    return D * TOKENS * factor * factor


def stat_draw(key, fold_value):
    scale = slot_scales(key)[:, None, None]
    diag_part = jax.random.uniform(jax.random.fold_in(key, fold_value), (OWNER_SLOTS, D), minval=1.0, maxval=4.0)
    noise = jax.random.normal(jax.random.fold_in(key, fold_value + 1), (OWNER_SLOTS, D, D))
    sym = 0.5 * (noise + jnp.swapaxes(noise, 1, 2))
    eye = jnp.eye(D, dtype=jnp.float32)
    return (scale * (eye[None] * diag_part[:, :, None] + 0.5 / math.sqrt(D) * sym)).astype(jnp.float32)


def draw_stat_left(key, part):
    return stat_draw(key, 61)


def draw_stat_right(key, part):
    return stat_draw(key, 63)


def root_draw(key, fold_value):
    diag_part = jax.random.uniform(jax.random.fold_in(key, fold_value), (OWNER_SLOTS, D), minval=0.5, maxval=1.5)
    noise = jax.random.normal(jax.random.fold_in(key, fold_value + 1), (OWNER_SLOTS, D, D))
    sym = 0.5 * (noise + jnp.swapaxes(noise, 1, 2))
    eye = jnp.eye(D, dtype=jnp.float32)
    return (eye[None] * diag_part[:, :, None] + 0.6 / math.sqrt(D) * sym).astype(jnp.float32)


def draw_root_left(key, part):
    return root_draw(key, 71)


def draw_root_right(key, part):
    return root_draw(key, 73)


def with_ends(values, stream_key, low, high):
    spot = [jax.random.randint(jax.random.fold_in(stream_key, axis), (), 0, length) for axis, length in enumerate(values.shape)]
    main_axis = values.shape.index(max(values.shape))
    next_to = spot[:main_axis] + [(spot[main_axis] + 1) % values.shape[main_axis]] + spot[main_axis + 1:]
    return values.at[tuple(spot)].set(low).at[tuple(next_to)].set(high)


def block_scale(key, dims, cuts, low, top_value):
    level = 1.0
    for dim, parts in cuts:
        steps = jax.random.uniform(jax.random.fold_in(jax.random.fold_in(key, 6), dim), (parts,), jnp.float32, low / len(cuts), top_value / len(cuts))
        level = level * jnp.repeat(jnp.exp(steps), dims[dim] // parts).reshape((-1,) + (1,) * (len(dims) - 1 - dim))
    return level


def gaussian(key, extent, deviation, bound, cuts=(), held_as=jnp.bfloat16):
    drawn = jax.random.normal(key, extent, jnp.float32) * deviation
    if len(cuts) > 0:
        drawn = block_scale(key, extent, cuts, -0.22, 0.18) * drawn
    return jnp.clip(drawn, min=-bound, max=bound).astype(held_as)


def setup_inputs(seed: int = 0) -> dict:
    key_of = jax.random.split(jax.random.key(seed), 15)
    return {
        "tokens": gaussian(key_of[0], (TOKENS, D), 1.0, 6.0, ((0, 32),)),
        "cotangent": gaussian(key_of[1], (TOKENS, D), 1.0, 6.0, ((0, 32),)),
        "place": draw_place(jax.random.fold_in(key_of[14], 71), 0),
        "seq_lengths": draw_seq_lengths(jax.random.fold_in(key_of[14], 71), 0),
        "random_blocks": with_ends(jax.random.randint(key_of[4], (TOKENS // BLK, H, NRAND), 0, LMAX // BLK), jax.random.fold_in(key_of[4], 1), 0, (LMAX // BLK) - 1).astype(jnp.int32),
        "owner_slot": draw_owner_slot(jax.random.fold_in(key_of[14], 71), 0),
        "flat_weights": draw_flat_weights(jax.random.fold_in(key_of[14], 71), 0),
        "vectors": draw_vectors(jax.random.fold_in(key_of[14], 71), 0),
        "moment_first": draw_moment_first(jax.random.fold_in(key_of[14], 71), 0),
        "moment_second": draw_moment_second(jax.random.fold_in(key_of[14], 71), 0),
        "stat_left": draw_stat_left(jax.random.fold_in(key_of[14], 71), 0),
        "stat_right": draw_stat_right(jax.random.fold_in(key_of[14], 71), 0),
        "root_left": draw_root_left(jax.random.fold_in(key_of[14], 71), 0),
        "root_right": draw_root_right(jax.random.fold_in(key_of[14], 71), 0),
    }


NORM_EPS = 1e-12
MASKED_SCORE = -1e+30
STAT_DECAY = 0.5
LR_MATRIX = 0.02
LR_VECTOR = 0.1
BETA_ONE = 0.9
BETA_TWO = 0.999
ADAM_EPS = 1e-08
RMS_EPS = 1e-12
PRECISE = lax.Precision.HIGHEST

@jax.custom_vjp
def low(v):
    return lax.optimization_barrier(v.astype(jnp.bfloat16)).astype(jnp.float32)

@jax.custom_vjp
def low_back(v):
    return v

def low_keep(v):
    return (low(v), None)

def low_pass(kept, grad):
    return (grad,)

def back_keep(v):
    return (v, None)

def back_low(kept, grad):
    return (low(grad),)
low.defvjp(low_keep, low_pass)
low_back.defvjp(back_keep, back_low)

def round_both(value):
    return low(low_back(value))

def product(left, right):
    return jnp.dot(left, right, precision=PRECISE, preferred_element_type=jnp.float32)

def layout(lengths):
    blocks = ((lengths + (BLK - 1)) // BLK).astype(jnp.int32)
    block_ends = jnp.cumsum(blocks).astype(jnp.int32)
    starts = ((block_ends - blocks) * BLK).astype(jnp.int32)
    slot_ids = jnp.arange(TOK_DEV, dtype=jnp.int32)
    seq_id = lax.optimization_barrier(jnp.sum((slot_ids // BLK)[:, None] >= block_ends[None, :], axis=1)).astype(jnp.int32)
    member = seq_id[:, None] == jnp.arange(SEQ_DEV, dtype=jnp.int32)[None, :]
    seq_start = lax.optimization_barrier(jnp.sum(jnp.where(member, starts[None, :], 0), axis=1)).astype(jnp.int32)
    length = lax.optimization_barrier(jnp.sum(jnp.where(member, lengths[None, :], 0), axis=1)).astype(jnp.int32)
    seq_blocks = lax.optimization_barrier(jnp.sum(jnp.where(member, blocks[None, :], 0), axis=1)).astype(jnp.int32)
    position = (slot_ids - seq_start).astype(jnp.int32)
    in_use = position < length
    return (seq_id, position, in_use, seq_blocks)

def random_keys(raw_picks, seq_blocks):
    per_block = seq_blocks.reshape(TOK_DEV // BLK, BLK)[:, 0]
    picked = (raw_picks % jnp.maximum(per_block, 1)[:, None, None]).astype(jnp.int32)
    return jnp.repeat(picked, BLK, axis=0)

def allowed(q_seq, q_pos, q_use, q_pick, q_slot, k_seq, k_pos, k_use, k_slot):
    q_block = q_pos // BLK
    k_block = k_pos // BLK
    same_seq = (q_seq[:, None] == k_seq[None, :]) & q_use[:, None] & k_use[None, :]
    nearby = (q_block[:, None] < NGLOB) | (k_block[None, :] < NGLOB) | (jnp.abs(q_block[:, None] - k_block[None, :]) <= 1)
    chosen = jnp.zeros((H, q_seq.shape[0], k_seq.shape[0]), dtype=jnp.bool_)
    for number in range(NRAND):
        chosen = chosen | (k_block[None, None, :] == jnp.transpose(q_pick[:, :, number])[:, :, None])
    alone = jnp.logical_not(q_use)[:, None] & (q_slot[:, None] == k_slot[None, :])
    return (same_seq & nearby)[None] | same_seq[None] & chosen | alone[None]

def layer_norm(hidden, gain, shift):
    center = hidden - lax.optimization_barrier(jnp.mean(hidden, axis=-1, keepdims=True))
    spread = lax.optimization_barrier(jnp.mean(center * center, axis=-1, keepdims=True))
    return center * lax.rsqrt(spread + NORM_EPS) * gain + shift

def pack_forward(inputs, weights_low, vectors_low, lengths, raw_picks):
    seq_id, position, in_use, seq_blocks = layout(lengths)
    picks = random_keys(raw_picks, seq_blocks)
    slot_ids = jnp.arange(TOK_DEV, dtype=jnp.int32)
    b_up = jnp.transpose(vectors_low[:, 8:]).reshape(FF)
    query = round_both(product(inputs, weights_low[:, :D]) + vectors_low[:, 0])
    key_all = round_both(product(inputs, weights_low[:, D:2 * D]))
    value_all = round_both(product(inputs, weights_low[:, 2 * D:3 * D]) + vectors_low[:, 1])
    key_heads = key_all.reshape(TOK_DEV, H, HD)
    value_heads = value_all.reshape(TOK_DEV, H, HD)
    block_rows = min(512, TOK_DEV)
    block_count = TOK_DEV // block_rows
    score_scale = HD ** (-0.5)

    def split_blocks(array):
        return array.reshape((block_count, block_rows) + array.shape[1:])

    def attend(pieces):
        query_block, q_seq, q_pos, q_use, q_pick, q_slot = pieces
        raw_scores = jnp.einsum('qhd,khd->hqk', query_block, key_heads, precision=PRECISE) * score_scale
        scores = low_back(raw_scores)
        keep_mask = allowed(q_seq, q_pos, q_use, q_pick, q_slot, seq_id, position, in_use, slot_ids)
        scores = jnp.where(keep_mask, scores, MASKED_SCORE)
        probs = jax.nn.softmax(scores, axis=-1)
        mixed_block = jnp.einsum('hqk,khd->qhd', low(probs), value_heads, precision=PRECISE)
        return mixed_block.reshape(block_rows, D)
    attended = lax.map(jax.checkpoint(attend), (split_blocks(query.reshape(TOK_DEV, H, HD)), split_blocks(seq_id), split_blocks(position), split_blocks(in_use), split_blocks(picks), split_blocks(slot_ids)))
    mixed = round_both(attended.reshape(TOK_DEV, D))
    branch = low_back(product(mixed, weights_low[:, 3 * D:4 * D]) + vectors_low[:, 2])
    x_one = layer_norm(inputs + branch, vectors_low[:, 4], vectors_low[:, 5])
    pre = low_back(product(low(x_one), weights_low[:, 4 * D:4 * D + FF]) + b_up)
    act = low(jax.nn.gelu(pre, approximate=True))
    down = lax.dot_general(act, weights_low[:, 4 * D + FF:], (((1,), (1,)), ((), ())), precision=PRECISE, preferred_element_type=jnp.float32)
    ffn = low_back(down + vectors_low[:, 3])
    result = layer_norm(x_one + ffn, vectors_low[:, 6], vectors_low[:, 7])
    return result * in_use.astype(jnp.float32)[:, None]

def reference(tokens, cotangent, place, seq_lengths, random_blocks, owner_slot, flat_weights, vectors, moment_first, moment_second, stat_left, stat_right, root_left, root_right):
    arrival = jnp.arange(TOKENS, dtype=jnp.int32)
    target = (arrival // GROUP_TOK * GROUP_TOK + place).astype(jnp.int32)
    x_slots = jnp.zeros((TOKENS, D), jnp.float32).at[target].set(tokens.astype(jnp.float32)).reshape(PACKS, TOK_DEV, D)
    cot_slots = jnp.zeros((TOKENS, D), jnp.float32).at[target].set(cotangent.astype(jnp.float32)).reshape(PACKS, TOK_DEV, D)
    raw_all = random_blocks.reshape(PACKS, TOK_DEV // BLK, H, NRAND)

    def forward(inputs_all, weights_all, vectors_all):
        weights_low = low(weights_all)
        vectors_low = low(vectors_all)

        def one_pack(pieces):
            return pack_forward(pieces[0], weights_low, vectors_low, pieces[1], pieces[2])
        return lax.map(jax.checkpoint(one_pack), (inputs_all, seq_lengths, raw_all))
    outputs, pullback = jax.vjp(forward, x_slots, flat_weights, vectors)
    input_slots, weight_grads, grad_vec = pullback(cot_slots)
    layer_out = outputs.reshape(TOKENS, D)[target].astype(jnp.bfloat16)
    input_grad = input_slots.reshape(TOKENS, D)[target].astype(jnp.bfloat16)
    blocks = jnp.transpose(weight_grads.reshape(D, NBLK, D), (1, 0, 2))
    grad_slots = jnp.zeros((OWNER_SLOTS, D, D), jnp.float32).at[owner_slot].set(blocks)

    def precondition(pieces):
        grad_block, left, right, left_root, right_root = pieces
        fresh_left = STAT_DECAY * left + (1.0 - STAT_DECAY) * jnp.dot(grad_block, jnp.transpose(grad_block), precision=PRECISE)
        fresh_right = STAT_DECAY * right + (1.0 - STAT_DECAY) * jnp.dot(jnp.transpose(grad_block), grad_block, precision=PRECISE)
        direction = jnp.dot(jnp.dot(left_root, grad_block, precision=PRECISE), right_root, precision=PRECISE)
        update = direction * lax.rsqrt(jnp.mean(direction * direction) + RMS_EPS)
        return (fresh_left, fresh_right, update)
    new_left, new_right, updates = lax.map(precondition, (grad_slots, stat_left, stat_right, root_left, root_right))
    step_matrix = jnp.transpose(updates[owner_slot], (1, 0, 2)).reshape(D, NBLK * D)
    new_weights = flat_weights - LR_MATRIX * step_matrix
    first_bias = 1.0 - BETA_ONE ** STEP
    second_bias = 1.0 - BETA_TWO ** STEP
    new_first = BETA_ONE * moment_first + (1.0 - BETA_ONE) * grad_vec
    new_second = BETA_TWO * moment_second + (1.0 - BETA_TWO) * grad_vec * grad_vec
    first_fixed = new_first / first_bias
    second_fixed = new_second / second_bias
    new_vectors = vectors - LR_VECTOR * first_fixed / (jnp.sqrt(second_fixed) + ADAM_EPS)
    return (layer_out, input_grad, weight_grads, new_weights, new_left, new_right, new_first, new_second, new_vectors)
```

```python
import functools

import jax
import jax.numpy as jnp
from jax import lax
from jax.experimental import pallas as pl
from jax.experimental.pallas import tpu as pltpu
from jax.sharding import PartitionSpec as P

D = 768
H = 12
HD = 64
FF = 3072
BLK = 64
NGLOB = 2
NRAND = 3
STEP = 10
SEQ_DEV = 4
TOK_DEV = 512
NBLK = 12


NORM_EPS = 1e-12
MASKED_SCORE = -1e30
STAT_DECAY = 0.5
LR_MATRIX = 0.02
LR_VECTOR = 0.1
BETA_ONE = 0.9
BETA_TWO = 0.999
ADAM_EPS = 1e-08
RMS_EPS = 1e-12
PRECISE = lax.Precision.HIGHEST


def layout(lengths):
    blocks = (lengths + (BLK - 1)) // BLK
    block_ends = jnp.cumsum(blocks)
    starts = (block_ends - blocks) * BLK
    slot_ids = jnp.arange(TOK_DEV, dtype=jnp.int32)
    seq_id = jnp.sum((slot_ids // BLK)[:, None] >= block_ends[None, :], axis=1)
    member = seq_id[:, None] == jnp.arange(SEQ_DEV, dtype=jnp.int32)[None, :]
    seq_start = jnp.sum(jnp.where(member, starts[None, :], 0), axis=1)
    length = jnp.sum(jnp.where(member, lengths[None, :], 0), axis=1)
    seq_blocks = jnp.sum(jnp.where(member, blocks[None, :], 0), axis=1)
    position = slot_ids - seq_start
    in_use = position < length
    return (seq_id, position, in_use, seq_blocks)


def random_keys(raw_picks, seq_blocks):
    per_block = seq_blocks.reshape(TOK_DEV // BLK, BLK)[:, 0]
    picked = raw_picks % jnp.maximum(per_block, 1)[:, None, None]
    return jnp.repeat(picked, BLK, axis=0)


def allowed(q_seq, q_pos, q_use, q_pick, q_slot, k_seq, k_pos, k_use, k_slot):
    q_block = q_pos // BLK
    k_block = k_pos // BLK
    same_seq = (q_seq[:, None] == k_seq[None, :]) & q_use[:, None] & k_use[None, :]
    nearby = (
        (q_block[:, None] < NGLOB)
        | (k_block[None, :] < NGLOB)
        | (jnp.abs(q_block[:, None] - k_block[None, :]) <= 1)
    )
    chosen = jnp.zeros((H, q_seq.shape[0], k_seq.shape[0]), dtype=jnp.bool_)
    for number in range(NRAND):
        chosen = chosen | (
            k_block[None, None, :] == jnp.transpose(q_pick[:, :, number])[:, :, None]
        )
    alone = jnp.logical_not(q_use)[:, None] & (q_slot[:, None] == k_slot[None, :])
    return (same_seq & nearby)[None] | same_seq[None] & chosen | alone[None]


def layer_norm(hidden, gain, shift):
    center = hidden - jnp.mean(hidden, axis=-1, keepdims=True)
    spread = jnp.mean(center * center, axis=-1, keepdims=True)
    return center * lax.rsqrt(spread + NORM_EPS) * gain + shift


def gelu_tanh(pre_act):
    return jax.nn.gelu(pre_act, approximate=True)


def contract_rows(left, right):
    return lax.dot_general(
        left, right, (((0,), (0,)), ((), ())), preferred_element_type=jnp.float32
    )


def contract_cols(left, right):
    return lax.dot_general(
        left, right, (((1,), (1,)), ((), ())), preferred_element_type=jnp.float32
    )


MESH = pl.DeviceIdType.MESH
HALF = 48
GCOLS = 3072
JCOLS = 384
MIB = 2**20


class Here:
    def __init__(self):
        r, f = lax.axis_index("rep"), lax.axis_index("fsdp")
        self.r, self.f = r, f
        self.x, self.y = lax.rem(r, 2), lax.div(r, 2)
        self.z, self.c = lax.div(f, 2), lax.rem(f, 2)
        self.to_x = (r + 1 - 2 * self.x, f)
        self.to_y = (r + 2 - 4 * self.y, f)
        self.to_core = (r, f + 1 - 2 * self.c)

    def z_plus(self, step):
        return lax.rem(self.z + step, 4)

    def along(self, step):
        return (self.r, 2 * self.z_plus(step) + self.c)

    def peer(self, step):
        return lax.rem(self.f + step, 8)

    def greet(self):
        barrier = pltpu.get_barrier_semaphore()
        friends = [self.to_x, self.to_y] + [(self.r, self.peer(s)) for s in range(1, 8)]
        for friend in friends:
            pl.semaphore_signal(barrier, inc=1, device_id=friend, device_id_type=MESH)
        return lambda: pl.semaphore_wait(barrier, len(friends))


def send(src, dst, send_sem, recv_sem, device):
    copy = pltpu.make_async_remote_copy(
        src_ref=src,
        dst_ref=dst,
        send_sem=send_sem,
        recv_sem=recv_sem,
        device_id=device,
        device_id_type=MESH,
    )
    copy.start()
    return copy


def local(src, dst, sem):
    copy = pltpu.make_async_copy(src, dst, sem)
    copy.start()
    return copy


def cols(start, width):
    return pl.ds(pl.multiple_of(start, 128), width)


def gather_kernel(
    tok, cot, wf, vec,
    w0, w1, w2, tok_in, cot_in, vec_in,
    wl, zs, zr, xs, xr, ys, yr, ds, dr, cs, cr, ls, ts, tr,
):
    here = Here()
    wait_all = here.greet()
    for g in range(3):
        for h in range(2):
            span = slice(g * GCOLS, (g + 1) * GCOLS)
            wl[h, :, span] = wf[h, :, span].astype(jnp.bfloat16)
    x, y, z, c, f = here.x, here.y, here.z, here.c, here.f
    whole = [w0, w1, w2]
    stays = [
        local(wl.at[:, :, g * GCOLS : (g + 1) * GCOLS], whole[g].at[z, c], ls.at[g]) for g in range(3)
    ]
    stays.append(local(tok.at[f], tok_in.at[f], ls.at[3]))
    stays.append(local(cot.at[f], cot_in.at[f], ls.at[4]))
    stays.append(local(vec, vec_in.at[f], ls.at[5]))
    wait_all()
    wide = GCOLS // 2
    sent = []

    def z_send(g):
        out = []
        for step in (1, 2, 3):
            out.append(
                send(
                    wl.at[x, :, cols(g * GCOLS + y * wide, wide)],
                    whole[g].at[z, c, x, :, cols(y * wide, wide)],
                    zs.at[g, step - 1],
                    zr.at[g, step - 1],
                    here.along(step),
                )
            )
        sent.extend(out)
        return out

    def rows_out(table, landing, number):
        out = []
        for step in range(1, 8):
            to = here.peer(step)
            src = table if number == 2 else table.at[to]
            out.append(
                send(src, landing.at[f], ts.at[number, step - 1], tr.at[number, step - 1], (here.r, to))
            )
        sent.extend(out)
        return out

    def plane(g, copies):
        out = []
        for step in (1, 2, 3):
            copies[step - 1].wait_recv()
            src = lax.rem(z + 4 - step, 4)
            part = whole[g].at[src, c, x, :, cols(y * wide, wide)]
            xc = send(part, part, xs.at[g, step - 1], xr.at[g, step - 1], here.to_x)
            yc = send(part, part, ys.at[g, step - 1], yr.at[g, step - 1], here.to_y)
            out.append((xc, yc))
            sent.extend([xc, yc])
        return out

    def core(g, number, h, j):
        part = whole[g].at[:, c, h, :, cols(j * wide, wide)]
        copy = send(part, part, cs.at[g, number], cr.at[g, number], here.to_core)
        sent.append(copy)
        return copy

    def diagonal(g, copies):
        out = []
        core_copies = [core(g, 0, x, y)]
        for step in (1, 2, 3):
            src = lax.rem(z + 4 - step, 4)
            xc, yc = copies[step - 1]
            xc.wait_recv()
            part = whole[g].at[src, c, 1 - x, :, cols(y * wide, wide // 2)]
            out.append(send(part, part, ds.at[g, 0, step - 1], dr.at[g, 0, step - 1], here.to_y))
            yc.wait_recv()
            part = whole[g].at[src, c, x, :, cols((1 - y) * wide + wide // 2, wide // 2)]
            out.append(send(part, part, ds.at[g, 1, step - 1], dr.at[g, 1, step - 1], here.to_x))
        sent.extend(out)
        core_copies.append(core(g, 1, 1 - x, y))
        core_copies.append(core(g, 2, x, 1 - y))
        for copy in out:
            copy.wait_recv()
        core_copies.append(core(g, 3, 1 - x, 1 - y))
        return core_copies

    z0 = z_send(0)
    small = rows_out(vec, vec_in, 2)
    z1 = z_send(1)
    for g in range(3):
        stays[g].wait()
    p0 = plane(0, z0)
    t0 = rows_out(tok, tok_in, 0)
    p1 = plane(1, z1)
    z2 = z_send(2)
    last = diagonal(0, p0)
    t1 = rows_out(cot, cot_in, 1)
    last += diagonal(1, p1)
    p2 = plane(2, z2)
    last += diagonal(2, p2)
    for copy in last + small + t0 + t1:
        copy.wait_recv()
    for copy in sent:
        copy.wait_send()
    for copy in stays[3:]:
        copy.wait()


def gather_all(tok, cot, flat_weights, vec):
    any_spec = pl.BlockSpec(memory_space=pl.ANY)
    vmem = pl.BlockSpec(memory_space=pltpu.VMEM)
    dma = pltpu.SemaphoreType.DMA
    shape = jax.ShapeDtypeStruct
    low = jnp.bfloat16
    return pl.pallas_call(
        gather_kernel,
        out_shape=[shape((4, 2, 2, HALF, GCOLS), low)] * 3
        + [shape((8, 64, D), low)] * 2
        + [shape((8, 96, 128), low)],
        in_specs=[any_spec, any_spec, vmem, any_spec],
        out_specs=[any_spec] * 6,
        scratch_shapes=[
            pltpu.VMEM((2, HALF, 3 * GCOLS), low),
            dma((3, 3)), dma((3, 3)), dma((3, 3)), dma((3, 3)), dma((3, 3)), dma((3, 3)),
            dma((3, 2, 3)), dma((3, 2, 3)), dma((3, 4)), dma((3, 4)),
            dma((6,)), dma((3, 7)), dma((3, 7)),
        ],
        compiler_params=pltpu.CompilerParams(
            collective_id=0, has_side_effects=True, vmem_limit_bytes=32 * MIB
        ),
        name="gather_all",
    )(tok, cot, flat_weights.reshape(2, HALF, 3 * GCOLS), vec)


def update_kernel(
    block_of, owner,
    gq, go, gu, gd, vec, rows_a, rows_b, outrow, root_l, root_r, stat_l, stat_r, wf, vecs, mom1, mom2,
    layer_out, input_grad, wg, nw, new_l, new_r, out1, out2, outv,
    G, Rc, A1, A2, B1, B2, ZR, F, FX, FY, FD, SO, Gs, Lb, Rb, stg, Pf, UL, UN,
    ta, tb, vb, vr, vt,
    gl, cs, cr, a1s, a1r, b1s, b1r, a2s, a2r, b2s, b2r, zs, zr,
    fs, fr, ts, tr, ss, sr, ps, pr, us, ur, qs, qr, vs, vrs, ls, ks,
):
    low, f32 = jnp.bfloat16, jnp.float32
    here = Here()
    wait_all = here.greet()
    x, y, z, c, f, r = here.x, here.y, here.z, here.c, here.f, here.r
    W = GCOLS // 2
    loads = []
    sources = [(gq, 0)] * 3 + [(go, 3)] + [(gu, 4)] * 4 + [(gd, 8)] * 4
    order = [8, 9, 10, 11, 4, 5, 6, 7, 0, 1, 2, 3]
    by_block = {}
    for b in order:
        ref, first = sources[b]
        by_block[b] = [
            local(
                ref.at[:, :, :, :, pl.ds((b - first) * D + j * JCOLS, JCOLS)],
                G.at[j, :, :, :, :, pl.ds(b * JCOLS, JCOLS)],
                gl.at[b, j],
            )
            for j in range(2)
        ]
    stage = [local(root_l.at[t], stg.at[t], ks.at[t]) for t in range(2)]
    vb[0] = vec[...]
    wait_all()
    sent = []
    got = []
    vec_copy = send(vb.at[0], vr.at[0], vs.at[0], vrs.at[0], here.to_core)
    sent.append(vec_copy)

    def span(g):
        return pl.ds(g * W, W)

    def c_send(g):
        for b in range(4 * g, 4 * g + 4):
            for copy in by_block[b]:
                copy.wait()
        copy = send(
            G.at[:, :, 1 - c, :, :, span(g)], Rc.at[:, :, :, :, span(g)],
            cs.at[g], cr.at[g], here.to_core,
        )
        sent.append(copy)
        return copy

    def first(g, copy):
        copy.wait_recv()

        def add(i, _):
            j, zz, h = lax.div(i, 8), lax.rem(lax.div(i, 2), 4), lax.rem(i, 2)
            G[j, zz, c, h, :, span(g)] = (
                G[j, zz, c, h, :, span(g)].astype(f32) + Rc[j, zz, h, :, span(g)].astype(f32)
            ).astype(low)
            return 0

        lax.fori_loop(0, 16, add, 0)
        a = send(
            G.at[:, 0:2, c, 1 - x, :, span(g)], A1.at[:, :, :, span(g)], a1s.at[g], a1r.at[g], here.to_x
        )
        b = send(
            G.at[1 - y, 2:4, c, :, :, span(g)], B1.at[:, :, :, span(g)], b1s.at[g], b1r.at[g], here.to_y
        )
        sent.extend([a, b])
        return a, b

    def second(g, copies):
        copies[0].wait_recv()

        def add_a(i, _):
            j, zz = lax.div(i, 2), lax.rem(i, 2)
            G[j, zz, c, x, :, span(g)] = (
                G[j, zz, c, x, :, span(g)].astype(f32) + A1[j, zz, :, span(g)].astype(f32)
            ).astype(low)
            return 0

        lax.fori_loop(0, 4, add_a, 0)
        a = send(
            G.at[1 - y, 0:2, c, x, :, span(g)], A2.at[:, :, span(g)], a2s.at[g], a2r.at[g], here.to_y
        )
        copies[1].wait_recv()

        def add_b(i, _):
            zz, h = lax.div(i, 2), lax.rem(i, 2)
            G[y, zz + 2, c, h, :, span(g)] = (
                G[y, zz + 2, c, h, :, span(g)].astype(f32) + B1[zz, h, :, span(g)].astype(f32)
            ).astype(low)
            return 0

        lax.fori_loop(0, 4, add_b, 0)
        b = send(
            G.at[y, 2:4, c, 1 - x, :, span(g)], B2.at[:, :, span(g)], b2s.at[g], b2r.at[g], here.to_x
        )
        sent.extend([a, b])
        return a, b

    def third(g, copies):
        for number, (copy, part) in enumerate(zip(copies, (A2, B2))):
            copy.wait_recv()

            def add(i, _, number=number, part=part):
                zz = 2 * number + i
                G[y, zz, c, x, :, span(g)] = (
                    G[y, zz, c, x, :, span(g)].astype(f32) + part[i, :, span(g)].astype(f32)
                ).astype(low)
                return 0

            lax.fori_loop(0, 2, add, 0)
        out = []
        for step in (1, 2, 3):
            out.append(
                send(
                    G.at[y, here.z_plus(step), c, x, :, span(g)], ZR.at[step - 1, :, span(g)],
                    zs.at[g, step - 1], zr.at[g, step - 1], here.along(step),
                )
            )
        sent.extend(out)
        return out

    def final(g, copies):
        for copy in copies:
            copy.wait_recv()
        for b in range(4 * g, 4 * g + 4):
            at = pl.ds(b * JCOLS, JCOLS)
            total = G[y, z, c, x, :, at].astype(f32)
            for step in range(3):
                total = total + ZR[step, :, at].astype(f32)
            F[b] = total.astype(low)

    def spread(g):
        at = pl.ds(4 * g, 4)
        a = send(F.at[at], FX.at[at], fs.at[g, 0], fr.at[g, 0], here.to_x)
        b = send(F.at[at], FY.at[at], fs.at[g, 1], fr.at[g, 1], here.to_y)
        sent.extend([a, b])
        return a, b

    def put(g, table, h, j):
        for b in range(4 * g, 4 * g + 4):
            wg[h, :, cols(b * D + j * JCOLS, JCOLS)] = table[b].astype(f32)

    def spread_on(g, copies):
        a, b = copies
        a.wait_recv()
        at = pl.ds(4 * g, 2)
        da = send(FX.at[at], FD.at[at], fs.at[g, 2], fr.at[g, 2], here.to_y)
        b.wait_recv()
        at = pl.ds(4 * g + 2, 2)
        db = send(FY.at[at], FD.at[at], fs.at[g, 3], fr.at[g, 3], here.to_x)
        sent.extend([da, db])
        put(g, F, x, y)
        put(g, FX, 1 - x, y)
        put(g, FY, x, 1 - y)
        return da, db

    def spread_end(g, copies):
        for copy in copies:
            copy.wait_recv()
        put(g, FD, 1 - x, 1 - y)

    def token_send(table, landing, number):
        out = []
        for step in range(1, 8):
            to = here.peer(step)
            out.append(
                send(table.at[to], landing.at[f], ts.at[number, step - 1], tr.at[number, step - 1], (r, to))
            )
        own = local(table.at[f], landing.at[f], ls.at[number])
        sent.extend(out)
        return out, own

    def token_end(pair, landing, target):
        for copy in pair[0]:
            copy.wait_recv()
        pair[1].wait()
        hot = (outrow[...] == lax.broadcasted_iota(jnp.int32, (TOK_DEV, TOK_DEV), 1)).astype(f32).astype(low)
        target[...] = jnp.dot(
            hot, landing[...].reshape(TOK_DEV, D), preferred_element_type=f32
        ).astype(low)

    def narrow(target):
        def one(i, _):
            t, at = lax.div(i, 8), pl.ds(pl.multiple_of(lax.rem(i, 8) * 96, 96), 96)
            target[t, at, :] = stg[t, at, :].astype(low)
            return 0

        lax.fori_loop(0, 16, one, 0)

    c2 = c_send(2)
    c1 = c_send(1)
    c0 = c_send(0)
    f2 = first(2, c2)
    f1 = first(1, c1)
    s2 = second(2, f2)
    f0 = first(0, c0)
    vec_copy.wait_recv()
    vb[1] = vb[0] + vr[0]
    vec_copy = send(vb.at[1], vr.at[1], vs.at[1], vrs.at[1], here.to_x)
    sent.append(vec_copy)
    ta_copies = token_send(rows_a, ta, 0)
    s1 = second(1, f1)
    t2 = third(2, s2)
    for copy in stage:
        copy.wait()
    narrow(Lb)
    stage = [local(root_r.at[t], stg.at[t], ks.at[2 + t]) for t in range(2)]
    vec_copy.wait_recv()
    vb[2] = vb[1] + vr[1]
    vec_copy = send(vb.at[2], vr.at[2], vs.at[2], vrs.at[2], here.to_y)
    sent.append(vec_copy)
    s0 = second(0, f0)
    t1 = third(1, s1)
    final(2, t2)
    e2 = spread(2)
    for copy in stage:
        copy.wait()
    narrow(Rb)
    vec_copy.wait_recv()
    vb[3] = vb[2] + vr[2]
    vec_copies = []
    for step in (1, 2, 3):
        vec_copies.append(
            send(vb.at[3], vr.at[2 + step], vs.at[2 + step], vrs.at[2 + step], here.along(step))
        )
    sent.extend(vec_copies)
    t0 = third(0, s0)
    final(1, t1)
    e1 = spread(1)
    d2 = spread_on(2, e2)
    final(0, t0)
    jc = cols(y * JCOLS, JCOLS)
    other = cols((1 - y) * JCOLS, JCOLS)
    slot_copies = []
    for step in range(1, 9):
        to = here.peer(step)
        for t in range(2):
            b = block_of[2 * to + t]
            flag = (b >= 0).astype(f32)
            SO[step - 1, t] = (F[jnp.maximum(b, 0)].astype(f32) * flag).astype(low)
        if step < 8:
            slot_copies.append(
                send(SO.at[step - 1], Gs.at[:, f, x, :, jc], ss.at[step - 1], sr.at[step - 1], (r, to))
            )
    sent.extend(slot_copies)
    own = local(SO.at[7], Gs.at[:, f, x, :, jc], ls.at[2])
    hops = []
    for step in range(8):
        src = lax.rem(f + 8 - step, 8)
        if step == 0:
            own.wait()
        else:
            slot_copies[step - 1].wait_recv()
        part = Gs.at[:, src, x, :, jc]
        hops.append(
            (
                send(part, part, ps.at[0, step], pr.at[0, step], here.to_x),
                send(part, part, ps.at[1, step], pr.at[1, step], here.to_y),
            )
        )
    ends = []
    for step in range(8):
        src = lax.rem(f + 8 - step, 8)
        hops[step][0].wait_recv()
        part = Gs.at[0, src, 1 - x, :, jc]
        ends.append(send(part, part, ps.at[2, step], pr.at[2, step], here.to_y))
        hops[step][1].wait_recv()
        part = Gs.at[1, src, x, :, other]
        ends.append(send(part, part, ps.at[3, step], pr.at[3, step], here.to_x))
        sent.extend(hops[step])
    sent.extend(ends)
    e0 = spread(0)
    d1 = spread_on(1, e1)
    spread_end(2, d2)
    token_end(ta_copies, ta, layer_out)
    tb_copies = token_send(rows_b, tb, 1)
    stage = [local(stat_l.at[0], stg.at[0], ks.at[4]), local(stat_r.at[0], stg.at[1], ks.at[5])]
    for copy in ends:
        copy.wait_recv()

    def block(t):
        return Gs[t].reshape(D, D)

    for t in range(2):
        whole = block(t)

        def left(i, _, t=t, whole=whole):
            at = pl.ds(pl.multiple_of(i * 192, 192), 192)
            Rc[lax.div(i, 2), pl.ds(2 * lax.rem(i, 2), 2), :, :, :D] = (
                jnp.dot(Lb[t, at, :], whole, preferred_element_type=f32)
                .astype(low)
                .reshape(2, 2, HALF, D)
            )
            return 0

        lax.fori_loop(0, 4, left, 0)

        def right(i, total, t=t):
            at = pl.ds(pl.multiple_of(i * 192, 192), 192)
            rows = Rc[lax.div(i, 2), pl.ds(2 * lax.rem(i, 2), 2), :, :, :D].reshape(192, D)
            part = jnp.dot(rows, Rb[t], preferred_element_type=f32)
            Pf[at, :] = part
            return total + jnp.sum(part * part)

        total = lax.fori_loop(0, 4, right, jnp.zeros((), f32))
        scale = lax.rsqrt(jnp.full((1, 1), total * (1.0 / (D * D)) + RMS_EPS, f32))

        def norm(i, _, t=t, scale=scale):
            at = pl.ds(pl.multiple_of(i * 96, 96), 96)
            Rc[t, lax.div(i, 2), :, :, cols(D + lax.rem(i, 2) * D, D)] = (
                (Pf[at, :] * scale).astype(low).reshape(2, HALF, D)
            )
            return 0

        lax.fori_loop(0, 8, norm, 0)

    def update_part(to):
        at = cols(D + lax.rem(to, 2) * D + y * JCOLS, JCOLS)
        return Rc.at[:, lax.div(to, 2), x, :, at]

    ucopies = []
    for step in range(1, 8):
        to = here.peer(step)
        ucopies.append(
            send(update_part(to), UL.at[pl.ds(2 * f, 2)], us.at[step - 1], ur.at[step - 1], (r, to))
        )
    sent.extend(ucopies)
    own = local(update_part(f), UL.at[pl.ds(2 * f, 2)], ls.at[3])
    outs = []
    for t in range(2):
        for copy in stage:
            copy.wait()

        def stat_left(i, _, t=t):
            at = pl.ds(pl.multiple_of(i * 192, 192), 192)
            rows = Gs[t, pl.ds(2 * i, 2)].reshape(192, D)
            part = lax.dot_general(rows, block(t), (((1,), (1,)), ((), ())), preferred_element_type=f32)
            stg[0, at, :] = STAT_DECAY * stg[0, at, :] + (1.0 - STAT_DECAY) * part
            return 0

        lax.fori_loop(0, 4, stat_left, 0)
        outs = [local(stg.at[0], new_l.at[t], ks.at[8 + 2 * t])]
        for i in range(3):
            at = pl.ds(i * 256, 256)
            strip = Gs[t, :, :, :, at].reshape(D, 256)
            part = lax.dot_general(strip, block(t), (((0,), (0,)), ((), ())), preferred_element_type=f32)
            stg[1, at, :] = STAT_DECAY * stg[1, at, :] + (1.0 - STAT_DECAY) * part
        outs.append(local(stg.at[1], new_r.at[t], ks.at[9 + 2 * t]))
        if t == 0:
            for copy in outs:
                copy.wait()
            stage = [local(stat_l.at[1], stg.at[0], ks.at[6]), local(stat_r.at[1], stg.at[1], ks.at[7])]
    d0 = spread_on(0, e0)
    spread_end(1, d1)
    for copy in ucopies:
        copy.wait_recv()
    own.wait()
    for b in range(NBLK):
        UN[b, x, :, jc] = UL[owner[b]]
    part = UN.at[:, x, :, jc]
    qa = send(part, part, qs.at[0], qr.at[0], here.to_x)
    qb = send(part, part, qs.at[1], qr.at[1], here.to_y)
    qa.wait_recv()
    part = UN.at[0:6, 1 - x, :, jc]
    qc = send(part, part, qs.at[2], qr.at[2], here.to_y)
    qb.wait_recv()
    part = UN.at[6:12, x, :, other]
    qd = send(part, part, qs.at[3], qr.at[3], here.to_x)
    sent.extend([qa, qb, qc, qd])
    spread_end(0, d0)
    total = vb[3]
    for copy in vec_copies:
        copy.wait_recv()
    for step in range(3):
        total = total + vr[3 + step]
    tall = jnp.concatenate([total, jnp.zeros((112, D), f32)], axis=0)
    vt[...] = jnp.transpose(tall)
    grad = vt[pl.ds(pl.multiple_of(f * 96, 96), 96), :][:, :NBLK]
    fresh1 = BETA_ONE * mom1[...] + (1.0 - BETA_ONE) * grad
    fresh2 = BETA_TWO * mom2[...] + (1.0 - BETA_TWO) * grad * grad
    out1[...] = fresh1
    out2[...] = fresh2
    outv[...] = vecs[...] - LR_VECTOR * (fresh1 / (1.0 - BETA_ONE**STEP)) / (
        jnp.sqrt(fresh2 / (1.0 - BETA_TWO**STEP)) + ADAM_EPS
    )
    token_end(tb_copies, tb, input_grad)
    qc.wait_recv()
    qd.wait_recv()
    for b in range(NBLK):
        for h in range(2):
            at = slice(b * D, (b + 1) * D)
            nw[h, :, at] = wf[h, :, at] - LR_MATRIX * UN[b, h].astype(f32)
    for copy in outs:
        copy.wait()
    for copy in sent:
        copy.wait_send()


def update_all(
    block_of, owner, gq, go, gu, gd, vec, rows_a, rows_b, outrow, root_l, root_r, stat_l, stat_r, wf,
    vecs, mom1, mom2,
):
    any_spec = pl.BlockSpec(memory_space=pl.ANY)
    vmem = pl.BlockSpec(memory_space=pltpu.VMEM)
    smem = pl.BlockSpec(memory_space=pltpu.SMEM)
    dma = pltpu.SemaphoreType.DMA
    shape = jax.ShapeDtypeStruct
    low, f32 = jnp.bfloat16, jnp.float32
    JW = 12 * JCOLS
    split = lambda a: a.reshape(4, 2, 2, HALF, a.shape[1])
    outs = pl.pallas_call(
        update_kernel,
        out_shape=[
            shape((TOK_DEV, D), low), shape((TOK_DEV, D), low),
            shape((2, HALF, 3 * GCOLS), f32), shape((2, HALF, 3 * GCOLS), f32),
            shape((2, D, D), f32), shape((2, D, D), f32),
            shape((96, NBLK), f32), shape((96, NBLK), f32), shape((96, NBLK), f32),
        ],
        in_specs=[smem, smem] + [any_spec] * 4 + [vmem] + [any_spec] * 2 + [vmem] + [any_spec] * 4 + [vmem] * 4,
        out_specs=[vmem] * 4 + [any_spec] * 2 + [vmem] * 3,
        scratch_shapes=[
            pltpu.VMEM((2, 4, 2, 2, HALF, JW), low),
            pltpu.VMEM((2, 4, 2, HALF, JW), low),
            pltpu.VMEM((2, 2, HALF, JW), low),
            pltpu.VMEM((2, HALF, JW), low),
            pltpu.VMEM((2, 2, HALF, JW), low),
            pltpu.VMEM((2, HALF, JW), low),
            pltpu.VMEM((3, HALF, JW), low),
            pltpu.VMEM((12, HALF, JCOLS), low),
            pltpu.VMEM((12, HALF, JCOLS), low),
            pltpu.VMEM((12, HALF, JCOLS), low),
            pltpu.VMEM((12, HALF, JCOLS), low),
            pltpu.VMEM((8, 2, HALF, JCOLS), low),
            pltpu.VMEM((2, 8, 2, HALF, D), low),
            pltpu.VMEM((2, D, D), low),
            pltpu.VMEM((2, D, D), low),
            pltpu.VMEM((2, D, D), f32),
            pltpu.VMEM((D, D), f32),
            pltpu.VMEM((16, HALF, JCOLS), low),
            pltpu.VMEM((12, 2, HALF, D), low),
            pltpu.VMEM((8, 64, D), low),
            pltpu.VMEM((8, 64, D), low),
            pltpu.VMEM((4, 16, D), f32),
            pltpu.VMEM((6, 16, D), f32),
            pltpu.VMEM((D, 128), f32),
            dma((12, 2)), dma((3,)), dma((3,)),
            dma((3,)), dma((3,)), dma((3,)), dma((3,)), dma((3,)), dma((3,)), dma((3,)), dma((3,)),
            dma((3, 3)), dma((3, 3)), dma((3, 4)), dma((3, 4)),
            dma((2, 7)), dma((2, 7)), dma((7,)), dma((7,)), dma((4, 8)), dma((4, 8)),
            dma((7,)), dma((7,)), dma((4,)), dma((4,)), dma((6,)), dma((6,)), dma((4,)), dma((12,)),
        ],
        compiler_params=pltpu.CompilerParams(
            collective_id=1, has_side_effects=True, vmem_limit_bytes=60 * MIB
        ),
        name="update_all",
    )(
        block_of, owner, split(gq), split(go), split(gu), split(gd), vec, rows_a, rows_b, outrow,
        root_l, root_r, stat_l, stat_r, wf.reshape(2, HALF, 3 * GCOLS), vecs, mom1, mom2,
    )
    return outs


def fast_body(
    tokens,
    cotangent,
    place,
    seq_lengths,
    random_blocks,
    owner_slot,
    flat_weights,
    vectors,
    moment_first,
    moment_second,
    stat_left,
    stat_right,
    root_left,
    root_right,
):
    peers = lax.axis_size("fsdp")
    share_rows = TOK_DEV // peers
    me = lax.axis_index("fsdp")
    low = jnp.bfloat16
    outrow = (place // TOK_DEV) * share_rows + place % TOK_DEV - me * share_rows
    slot_ids = jnp.arange(TOK_DEV, dtype=jnp.int32)
    hot = (slot_ids[:, None] == outrow[None, :]).astype(low)
    tok_out = jnp.dot(hot, tokens, preferred_element_type=jnp.float32).astype(low)
    cot_out = jnp.dot(hot, cotangent, preferred_element_type=jnp.float32).astype(low)
    vec_pad = jnp.pad(vectors.astype(low), ((0, 0), (0, 128 - NBLK)))
    w_attn, w_up, w_down, tok_in, cot_in, vec_in = gather_all(
        tok_out.reshape(peers, share_rows, D),
        cot_out.reshape(peers, share_rows, D),
        flat_weights,
        vec_pad,
    )
    w_attn = w_attn.reshape(D, 4 * D)
    w_up = w_up.reshape(D, FF)
    w_down = w_down.reshape(D, FF)
    inputs = tok_in.reshape(TOK_DEV, D)
    upstream = cot_in.reshape(TOK_DEV, D).astype(jnp.float32)
    vecs_full = vec_in.reshape(D, 128)[:, :NBLK].astype(jnp.float32)
    b_up = jnp.transpose(vecs_full[:, 8:]).reshape(FF)
    seq_id, position, in_use, seq_blocks = layout(seq_lengths[0])
    picks = random_keys(random_blocks, seq_blocks)
    real_rows = in_use.astype(jnp.float32)[:, None]
    bias_qkv = jnp.concatenate([vecs_full[:, 0], jnp.zeros((D,), jnp.float32), vecs_full[:, 1]])
    qkv_low = (
        jnp.dot(inputs, w_attn[:, : 3 * D], preferred_element_type=jnp.float32) + bias_qkv
    ).astype(low)
    qkv_heads = qkv_low.reshape(TOK_DEV, 3, H, HD)
    queries = qkv_heads[:, 0]
    key_heads = qkv_heads[:, 1]
    value_heads = qkv_heads[:, 2]
    score_scale = HD ** (-0.5)
    keep_mask = allowed(
        seq_id, position, in_use, picks, slot_ids, seq_id, position, in_use, slot_ids
    )
    scores = (
        jnp.einsum("qhd,khd->hqk", queries, key_heads, preferred_element_type=jnp.float32)
        * score_scale
    )
    scores = jnp.where(keep_mask, scores, MASKED_SCORE)
    expo = jnp.exp(scores - jnp.max(scores, axis=-1, keepdims=True))
    probs = expo / jnp.sum(expo, axis=-1, keepdims=True)
    probs_low = probs.astype(low)
    mixed = (
        jnp.einsum("hqk,khd->qhd", probs_low, value_heads, preferred_element_type=jnp.float32)
        .reshape(TOK_DEV, D)
        .astype(low)
    )
    branch = (
        jnp.dot(mixed, w_attn[:, 3 * D : 4 * D], preferred_element_type=jnp.float32)
        + vecs_full[:, 2]
    )
    hidden_one = inputs.astype(jnp.float32) + branch
    x_one, norm_one_back = jax.vjp(layer_norm, hidden_one, vecs_full[:, 4], vecs_full[:, 5])
    x_one_low = x_one.astype(low)
    pre_act = jnp.dot(x_one_low, w_up, preferred_element_type=jnp.float32) + b_up
    act, gelu_back = jax.vjp(gelu_tanh, pre_act)
    act_low = act.astype(low)
    ffn = contract_cols(act_low, w_down) + vecs_full[:, 3]
    hidden_two = x_one + ffn
    result, norm_two_back = jax.vjp(layer_norm, hidden_two, vecs_full[:, 6], vecs_full[:, 7])
    layer_rows = (result * real_rows).astype(low)
    d_result = upstream * real_rows
    d_two, d_gain_two, d_shift_two = norm_two_back(d_result)
    d_ffn = d_two.astype(low)
    d_act = jnp.dot(d_ffn, w_down, preferred_element_type=jnp.float32)
    (d_pre,) = gelu_back(d_act)
    d_pre_low = d_pre.astype(low)
    grad_down = contract_rows(d_ffn, act_low).astype(low)
    grad_up = contract_rows(x_one_low, d_pre_low).astype(low)
    d_x_one = d_two + contract_cols(d_pre_low, w_up)
    d_one, d_gain_one, d_shift_one = norm_one_back(d_x_one)
    d_branch = d_one.astype(low)
    grad_out = contract_rows(mixed, d_branch).astype(low)
    d_mixed = contract_cols(d_branch, w_attn[:, 3 * D : 4 * D]).astype(low).reshape(TOK_DEV, H, HD)
    prob_grad = jnp.einsum("qhd,khd->hqk", d_mixed, value_heads, preferred_element_type=jnp.float32)
    score_grad = (
        probs * (prob_grad - jnp.sum(probs * prob_grad, axis=-1, keepdims=True))
    ).astype(low)
    value_grad = jnp.einsum("hqk,qhd->khd", probs_low, d_mixed, preferred_element_type=jnp.float32)
    query_grad = (
        jnp.einsum("hqk,khd->qhd", score_grad, key_heads, preferred_element_type=jnp.float32)
        * score_scale
    )
    key_grad = (
        jnp.einsum("hqk,qhd->khd", score_grad, queries, preferred_element_type=jnp.float32)
        * score_scale
    )
    d_qkv = jnp.concatenate(
        [
            query_grad.reshape(TOK_DEV, D),
            key_grad.reshape(TOK_DEV, D),
            value_grad.reshape(TOK_DEV, D),
        ],
        axis=1,
    ).astype(low)
    grad_qkv = contract_rows(inputs, d_qkv).astype(low)
    d_inputs = d_one + contract_cols(d_qkv, w_attn[:, : 3 * D])
    grad_rows = d_inputs.astype(low)
    qkv_sums = jnp.sum(d_qkv.astype(jnp.float32), axis=0)
    up_sums = jnp.sum(d_pre_low.astype(jnp.float32), axis=0).reshape(FF // D, D)
    vec_grad = jnp.concatenate(
        [
            qkv_sums[None, :D],
            qkv_sums[None, 2 * D :],
            jnp.sum(d_branch.astype(jnp.float32), axis=0)[None],
            jnp.sum(d_ffn.astype(jnp.float32), axis=0)[None],
            d_gain_one[None],
            d_shift_one[None],
            d_gain_two[None],
            d_shift_two[None],
            up_sums,
            jnp.zeros((4, D), jnp.float32),
        ],
        axis=0,
    )
    slots = jnp.arange(16, dtype=jnp.int32)
    hits = slots[:, None] == owner_slot[None, :]
    block_of = jnp.sum(jnp.where(hits, jnp.arange(NBLK, dtype=jnp.int32)[None, :] + 1, 0), axis=1) - 1
    outs = update_all(
        block_of.astype(jnp.int32),
        owner_slot,
        grad_qkv,
        grad_out,
        grad_up,
        grad_down,
        vec_grad,
        layer_rows.reshape(peers, share_rows, D),
        grad_rows.reshape(peers, share_rows, D),
        outrow[:, None],
        root_left,
        root_right,
        stat_left,
        stat_right,
        flat_weights,
        vectors,
        moment_first,
        moment_second,
    )
    layer_out, input_grad, weight_grads, new_weights, *others = outs
    return (
        layer_out,
        input_grad,
        weight_grads.reshape(96, NBLK * D),
        new_weights.reshape(96, NBLK * D),
        *others,
    )


def plain_body(
    tokens,
    cotangent,
    place,
    seq_lengths,
    random_blocks,
    owner_slot,
    flat_weights,
    vectors,
    moment_first,
    moment_second,
    stat_left,
    stat_right,
    root_left,
    root_right,
):
    peers = lax.axis_size("fsdp")
    share_rows = TOK_DEV // peers
    order_ids = jnp.argsort(place)
    outgoing = (
        tokens[order_ids].reshape(peers, share_rows, D),
        cotangent[order_ids].reshape(peers, share_rows, D),
    )
    arrived = (
        lax.all_to_all(outgoing[0], "fsdp", split_axis=0, concat_axis=0, tiled=True),
        lax.all_to_all(outgoing[1], "fsdp", split_axis=0, concat_axis=0, tiled=True),
    )
    inputs = arrived[0].reshape(TOK_DEV, D)
    upstream = arrived[1].reshape(TOK_DEV, D).astype(jnp.float32)
    weight_copy, vector_copy = (
        lax.all_gather(flat_weights.astype(jnp.bfloat16), "fsdp", axis=0, tiled=True),
        lax.all_gather(vectors.astype(jnp.bfloat16), "fsdp", axis=0, tiled=True),
    )
    vecs_full = vector_copy.astype(jnp.float32)
    b_up = jnp.transpose(vecs_full[:, 8:]).reshape(FF)
    seq_id, position, in_use, seq_blocks = layout(seq_lengths[0])
    picks = random_keys(random_blocks, seq_blocks)
    slot_ids = jnp.arange(TOK_DEV, dtype=jnp.int32)
    real_rows = in_use.astype(jnp.float32)[:, None]
    bias_qkv = jnp.concatenate([vecs_full[:, 0], jnp.zeros((D,), jnp.float32), vecs_full[:, 1]])
    qkv_low = (
        jnp.dot(inputs, weight_copy[:, : 3 * D], preferred_element_type=jnp.float32) + bias_qkv
    ).astype(jnp.bfloat16)
    qkv_heads = qkv_low.reshape(TOK_DEV, 3, H, HD)
    queries = qkv_heads[:, 0]
    key_heads = qkv_heads[:, 1]
    value_heads = qkv_heads[:, 2]
    block_rows = min(512, TOK_DEV)
    block_count = TOK_DEV // block_rows
    score_scale = HD ** (-0.5)

    def split_blocks(array):
        return array.reshape((block_count, block_rows) + array.shape[1:])

    block_inputs = (
        split_blocks(queries),
        split_blocks(seq_id),
        split_blocks(position),
        split_blocks(in_use),
        split_blocks(picks),
        split_blocks(slot_ids),
    )

    def scores_of(query_block, q_seq, q_pos, q_use, q_pick, q_slot):
        raw_scores = (
            jnp.einsum("qhd,khd->hqk", query_block, key_heads, preferred_element_type=jnp.float32)
            * score_scale
        )
        keep_mask = allowed(q_seq, q_pos, q_use, q_pick, q_slot, seq_id, position, in_use, slot_ids)
        return jnp.where(keep_mask, raw_scores, MASKED_SCORE)

    def forward_block(pieces):
        scores = scores_of(pieces[0], pieces[1], pieces[2], pieces[3], pieces[4], pieces[5])
        row_max = jnp.max(scores, axis=-1, keepdims=True)
        expo = jnp.exp(scores - row_max)
        row_total = jnp.sum(expo, axis=-1, keepdims=True)
        probs_low = (expo / row_total).astype(jnp.bfloat16)
        mixed_block = jnp.einsum(
            "hqk,khd->qhd", probs_low, value_heads, preferred_element_type=jnp.float32
        )
        return (mixed_block.reshape(block_rows, D), (row_max + jnp.log(row_total))[:, :, 0])

    attended, log_totals = lax.map(forward_block, block_inputs)
    mixed = attended.reshape(TOK_DEV, D).astype(jnp.bfloat16)
    branch = (
        jnp.dot(mixed, weight_copy[:, 3 * D : 4 * D], preferred_element_type=jnp.float32)
        + vecs_full[:, 2]
    )
    hidden_one = inputs.astype(jnp.float32) + branch
    x_one, norm_one_back = jax.vjp(layer_norm, hidden_one, vecs_full[:, 4], vecs_full[:, 5])
    x_one_low = x_one.astype(jnp.bfloat16)
    pre_act = (
        jnp.dot(x_one_low, weight_copy[:, 4 * D : 4 * D + FF], preferred_element_type=jnp.float32)
        + b_up
    )
    act, gelu_back = jax.vjp(gelu_tanh, pre_act)
    act_low = act.astype(jnp.bfloat16)
    ffn = contract_cols(act_low, weight_copy[:, 4 * D + FF :]) + vecs_full[:, 3]
    hidden_two = x_one + ffn
    result, norm_two_back = jax.vjp(layer_norm, hidden_two, vecs_full[:, 6], vecs_full[:, 7])
    layer_rows = (result * real_rows).astype(jnp.bfloat16)
    weight_copy = lax.all_gather(flat_weights.astype(jnp.bfloat16), "fsdp", axis=0, tiled=True)
    d_result = upstream * real_rows
    d_two, d_gain_two, d_shift_two = norm_two_back(d_result)
    d_ffn = d_two.astype(jnp.bfloat16)
    d_act = jnp.dot(d_ffn, weight_copy[:, 4 * D + FF :], preferred_element_type=jnp.float32)
    (d_pre,) = gelu_back(d_act)
    d_pre_low = d_pre.astype(jnp.bfloat16)
    grad_down = contract_rows(d_ffn, act_low)
    grad_up = contract_rows(x_one_low, d_pre_low)
    d_x_one = d_two + contract_cols(d_pre_low, weight_copy[:, 4 * D : 4 * D + FF])
    d_one, d_gain_one, d_shift_one = norm_one_back(d_x_one)
    up_sums = jnp.transpose(jnp.sum(d_pre_low.astype(jnp.float32), axis=0).reshape(FF // D, D))
    ffn_vec = jnp.concatenate(
        [
            jnp.sum(d_ffn.astype(jnp.float32), axis=0)[:, None],
            d_gain_one[:, None],
            d_shift_one[:, None],
            d_gain_two[:, None],
            d_shift_two[:, None],
            up_sums,
        ],
        axis=1,
    )
    ffn_mats = jnp.concatenate([grad_up, grad_down], axis=1)
    d_branch = d_one.astype(jnp.bfloat16)
    grad_out = contract_rows(mixed, d_branch)
    d_mixed = (
        contract_cols(d_branch, weight_copy[:, 3 * D : 4 * D])
        .astype(jnp.bfloat16)
        .reshape(TOK_DEV, H, HD)
    )

    def backward_block(carry, pieces):
        key_grad, value_grad = carry
        query_block = pieces[0]
        log_total = pieces[6]
        out_grad = pieces[7]
        scores = scores_of(pieces[0], pieces[1], pieces[2], pieces[3], pieces[4], pieces[5])
        probs = jnp.exp(scores - log_total[:, :, None])
        probs_low = probs.astype(jnp.bfloat16)
        value_grad = value_grad + jnp.einsum(
            "hqk,qhd->khd", probs_low, out_grad, preferred_element_type=jnp.float32
        )
        prob_grad = jnp.einsum(
            "qhd,khd->hqk", out_grad, value_heads, preferred_element_type=jnp.float32
        )
        score_grad = (
            probs * (prob_grad - jnp.sum(probs * prob_grad, axis=-1, keepdims=True))
        ).astype(jnp.bfloat16)
        query_grad = (
            jnp.einsum("hqk,khd->qhd", score_grad, key_heads, preferred_element_type=jnp.float32)
            * score_scale
        )
        key_grad = (
            key_grad
            + jnp.einsum(
                "hqk,qhd->khd", score_grad, query_block, preferred_element_type=jnp.float32
            )
            * score_scale
        )
        return ((key_grad, value_grad), query_grad)

    zero_heads = jnp.zeros((TOK_DEV, H, HD), jnp.float32)
    (key_grad, value_grad), query_grad = lax.scan(
        backward_block, (zero_heads, zero_heads), block_inputs + (log_totals, split_blocks(d_mixed))
    )
    d_qkv = jnp.concatenate(
        [
            query_grad.reshape(TOK_DEV, D),
            key_grad.reshape(TOK_DEV, D),
            value_grad.reshape(TOK_DEV, D),
        ],
        axis=1,
    ).astype(jnp.bfloat16)
    grad_qkv = contract_rows(inputs, d_qkv)
    d_inputs = d_one + contract_cols(d_qkv, weight_copy[:, : 3 * D])
    qkv_sums = jnp.sum(d_qkv.astype(jnp.float32), axis=0)
    attn_vec = jnp.stack(
        [qkv_sums[:D], qkv_sums[2 * D :], jnp.sum(d_branch.astype(jnp.float32), axis=0)], axis=1
    )
    attn_mats = jnp.concatenate([grad_qkv, grad_out], axis=1)
    mat_shard, vec_shard = (
        lax.psum_scatter(
            jnp.concatenate([attn_mats, ffn_mats], axis=1), "fsdp", scatter_dimension=0, tiled=True
        ),
        lax.psum_scatter(
            jnp.concatenate([attn_vec, ffn_vec], axis=1), "fsdp", scatter_dimension=0, tiled=True
        ),
    )
    mat_part = lax.psum_scatter(
        mat_shard.astype(jnp.bfloat16), "rep", scatter_dimension=1, tiled=True
    ).astype(jnp.float32)
    vec_shard = lax.psum(vec_shard, "rep")
    mat_shard = lax.all_gather(mat_part.astype(jnp.bfloat16), "rep", axis=1, tiled=True).astype(
        mat_part.dtype
    )
    grad_rows = d_inputs.astype(jnp.bfloat16)
    back_pair = (
        lax.all_to_all(
            layer_rows.reshape(peers, share_rows, D),
            "fsdp",
            split_axis=0,
            concat_axis=0,
            tiled=True,
        ),
        lax.all_to_all(
            grad_rows.reshape(peers, share_rows, D), "fsdp", split_axis=0, concat_axis=0, tiled=True
        ),
    )
    layer_out = (
        jnp.zeros((TOK_DEV, D), jnp.bfloat16).at[order_ids].set(back_pair[0].reshape(TOK_DEV, D))
    )
    input_grad = (
        jnp.zeros((TOK_DEV, D), jnp.bfloat16).at[order_ids].set(back_pair[1].reshape(TOK_DEV, D))
    )
    slot_count = stat_left.shape[0]
    rows_dev = flat_weights.shape[0]
    targets = (
        jnp.arange(slot_count, dtype=jnp.int32)[:, None, None]
        + slot_count * jnp.arange(peers, dtype=jnp.int32)[None, :, None]
    )
    select = (owner_slot[None, None, :] == targets).astype(jnp.float32)
    grad_pieces = mat_shard.reshape(rows_dev, NBLK, D)
    outbound = jnp.einsum("snb,rbc->snrc", select, grad_pieces, precision=PRECISE)
    inbound = lax.all_to_all(
        outbound.astype(jnp.bfloat16), "fsdp", split_axis=1, concat_axis=1, tiled=True
    ).astype(outbound.dtype)
    grad_blocks = inbound.reshape(slot_count, D, D)
    new_left = STAT_DECAY * stat_left + (1.0 - STAT_DECAY) * jnp.einsum(
        "sij,skj->sik", grad_blocks, grad_blocks, precision=PRECISE
    )
    new_right = STAT_DECAY * stat_right + (1.0 - STAT_DECAY) * jnp.einsum(
        "sji,sjk->sik", grad_blocks, grad_blocks, precision=PRECISE
    )
    left_applied = jnp.einsum("sij,sjk->sik", root_left, grad_blocks, precision=PRECISE)
    direction = jnp.einsum("sij,sjk->sik", left_applied, root_right, precision=PRECISE)
    update = direction * lax.rsqrt(
        jnp.mean(direction * direction, axis=(1, 2), keepdims=True) + RMS_EPS
    )
    returned = lax.all_to_all(
        update.reshape(slot_count, peers, rows_dev, D).astype(jnp.bfloat16),
        "fsdp",
        split_axis=1,
        concat_axis=1,
        tiled=True,
    ).astype(jnp.float32)
    step_matrix = jnp.einsum("snb,snrc->rbc", select, returned, precision=PRECISE).reshape(
        rows_dev, NBLK * D
    )
    new_weights = flat_weights - LR_MATRIX * step_matrix
    first_bias = 1.0 - BETA_ONE**STEP
    second_bias = 1.0 - BETA_TWO**STEP
    new_first = BETA_ONE * moment_first + (1.0 - BETA_ONE) * vec_shard
    new_second = BETA_TWO * moment_second + (1.0 - BETA_TWO) * vec_shard * vec_shard
    first_fixed = new_first / first_bias
    second_fixed = new_second / second_bias
    new_vectors = vectors - LR_VECTOR * first_fixed / (jnp.sqrt(second_fixed) + ADAM_EPS)
    return (
        layer_out,
        input_grad,
        mat_shard,
        new_weights,
        new_left,
        new_right,
        new_first,
        new_second,
        new_vectors,
    )


def solution(mesh):
    in_specs = (
        P(("rep", "fsdp"), None),
        P(("rep", "fsdp"), None),
        P(("rep", "fsdp")),
        P(("rep", "fsdp"), None),
        P(("rep", "fsdp"), None, None),
        P(),
        P("fsdp", None),
        P("fsdp", None),
        P("fsdp", None),
        P("fsdp", None),
        P("fsdp", None, None),
        P("fsdp", None, None),
        P("fsdp", None, None),
        P("fsdp", None, None),
    )
    out_specs = (
        P(("rep", "fsdp"), None),
        P(("rep", "fsdp"), None),
        P("fsdp", None),
        P("fsdp", None),
        P("fsdp", None, None),
        P("fsdp", None, None),
        P("fsdp", None),
        P("fsdp", None),
        P("fsdp", None),
    )
    shaped = mesh.shape["fsdp"] == 8 and mesh.shape["rep"] == 4
    body = fast_body if shaped else plain_body
    return jax.shard_map(body, mesh=mesh, in_specs=in_specs, out_specs=out_specs, check_vma=False)
```

```python
import functools

import jax
import jax.numpy as jnp
from jax import lax
from jax.experimental import pallas as pl
from jax.experimental.pallas import tpu as pltpu
from jax.sharding import PartitionSpec as P

D = 768
H = 12
HD = 64
FF = 3072
BLK = 64
NGLOB = 2
NRAND = 3
STEP = 10
SEQ_DEV = 4
TOK_DEV = 512
NBLK = 12


NORM_EPS = 1e-12
MASKED_SCORE = -1e30
STAT_DECAY = 0.5
LR_MATRIX = 0.02
LR_VECTOR = 0.1
BETA_ONE = 0.9
BETA_TWO = 0.999
ADAM_EPS = 1e-08
RMS_EPS = 1e-12
PRECISE = lax.Precision.HIGHEST


def layout(lengths):
    blocks = (lengths + (BLK - 1)) // BLK
    block_ends = jnp.cumsum(blocks)
    starts = (block_ends - blocks) * BLK
    slot_ids = jnp.arange(TOK_DEV, dtype=jnp.int32)
    seq_id = jnp.sum((slot_ids // BLK)[:, None] >= block_ends[None, :], axis=1)
    member = seq_id[:, None] == jnp.arange(SEQ_DEV, dtype=jnp.int32)[None, :]
    seq_start = jnp.sum(jnp.where(member, starts[None, :], 0), axis=1)
    length = jnp.sum(jnp.where(member, lengths[None, :], 0), axis=1)
    seq_blocks = jnp.sum(jnp.where(member, blocks[None, :], 0), axis=1)
    position = slot_ids - seq_start
    in_use = position < length
    return (seq_id, position, in_use, seq_blocks)


def random_keys(raw_picks, seq_blocks):
    per_block = seq_blocks.reshape(TOK_DEV // BLK, BLK)[:, 0]
    picked = raw_picks % jnp.maximum(per_block, 1)[:, None, None]
    return jnp.repeat(picked, BLK, axis=0)


def allowed(q_seq, q_pos, q_use, q_pick, q_slot, k_seq, k_pos, k_use, k_slot):
    q_block = q_pos // BLK
    k_block = k_pos // BLK
    same_seq = (q_seq[:, None] == k_seq[None, :]) & q_use[:, None] & k_use[None, :]
    nearby = (
        (q_block[:, None] < NGLOB)
        | (k_block[None, :] < NGLOB)
        | (jnp.abs(q_block[:, None] - k_block[None, :]) <= 1)
    )
    chosen = jnp.zeros((H, q_seq.shape[0], k_seq.shape[0]), dtype=jnp.bool_)
    for number in range(NRAND):
        chosen = chosen | (
            k_block[None, None, :] == jnp.transpose(q_pick[:, :, number])[:, :, None]
        )
    alone = jnp.logical_not(q_use)[:, None] & (q_slot[:, None] == k_slot[None, :])
    return (same_seq & nearby)[None] | same_seq[None] & chosen | alone[None]


def layer_norm(hidden, gain, shift):
    center = hidden - jnp.mean(hidden, axis=-1, keepdims=True)
    spread = jnp.mean(center * center, axis=-1, keepdims=True)
    return center * lax.rsqrt(spread + NORM_EPS) * gain + shift


def gelu_tanh(pre_act):
    return jax.nn.gelu(pre_act, approximate=True)


def contract_rows(left, right):
    return lax.dot_general(
        left, right, (((0,), (0,)), ((), ())), preferred_element_type=jnp.float32
    )


def contract_cols(left, right):
    return lax.dot_general(
        left, right, (((1,), (1,)), ((), ())), preferred_element_type=jnp.float32
    )


MESH = pl.DeviceIdType.MESH
HALF = 48
GCOLS = 3072
JCOLS = 384
MIB = 2**20


class Here:
    def __init__(self, corner=False):
        r, f = lax.axis_index("rep"), lax.axis_index("fsdp")
        self.r, self.f = r, f
        self.x, self.y = lax.rem(r, 2), lax.div(r, 2)
        self.z, self.c = lax.div(f, 2), lax.rem(f, 2)
        self.to_x = (r + 1 - 2 * self.x, f)
        self.to_y = (r + 2 - 4 * self.y, f)
        self.to_d = (3 - r, f)
        self.corner = corner
        self.to_core = (r, f + 1 - 2 * self.c)

    def z_plus(self, step):
        return lax.rem(self.z + step, 4)

    def along(self, step):
        return (self.r, 2 * self.z_plus(step) + self.c)

    def peer(self, step):
        return lax.rem(self.f + step, 8)

    def greet(self):
        barrier = pltpu.get_barrier_semaphore()
        friends = [self.to_x, self.to_y] + [self.to_d] * self.corner
        friends += [(self.r, self.peer(s)) for s in range(1, 8)]
        for friend in friends:
            pl.semaphore_signal(barrier, inc=1, device_id=friend, device_id_type=MESH)
        return lambda: pl.semaphore_wait(barrier, len(friends))


def send(src, dst, send_sem, recv_sem, device):
    copy = pltpu.make_async_remote_copy(
        src_ref=src,
        dst_ref=dst,
        send_sem=send_sem,
        recv_sem=recv_sem,
        device_id=device,
        device_id_type=MESH,
    )
    copy.start()
    return copy


def local(src, dst, sem):
    copy = pltpu.make_async_copy(src, dst, sem)
    copy.start()
    return copy


def cols(start, width):
    return pl.ds(pl.multiple_of(start, 128), width)


def forward_kernel(
    outrow, tok, cot, wf, vec, bias, use, use_row, root_l, root_r,
    o0, o1, o2, o_vt, o_x, o_cot, o_qkv, o_p, o_mix, o_n1, o_r1, o_u, o_f, o_dg, o_n2, o_r2, o_y, o_root,
    w0, w1, w2, tok_in, cot_in, vec_in, tok_s, cot_s,
    vt, qkv, P, mix, n1, r1, x1, u, fa, dg, n2, r2, yo, xT, mT, uT, feat, stg, rb,
    wl, zs, zr, xs, xr, ys, yr, ds, dr, cs, cr, ls, ts, tr, os, ks,
):
    low, f32 = jnp.bfloat16, jnp.float32
    here = Here()
    wait_all = here.greet()
    x, y, z, c, f = here.x, here.y, here.z, here.c, here.f
    whole = [w0, w1, w2]
    whole_out = [o0, o1, o2]
    wide = GCOLS // 2
    sent = []
    outs = []
    count = [0]

    def keep(src, dst):
        outs.append(local(src, dst, os.at[count[0]]))
        count[0] += 1

    def narrow(g):
        def one(i, _):
            h, part = lax.div(i, 4), lax.rem(i, 4)
            at = cols(g * GCOLS + part * D, D)
            wl[h, :, at] = wf[h, :, at].astype(low)
            return 0

        lax.fori_loop(0, 8, one, 0)
        return local(wl.at[:, :, g * GCOLS : (g + 1) * GCOLS], whole[g].at[z, c], ls.at[g])

    def z_send(g):
        out = []
        for step in (1, 2, 3):
            out.append(
                send(
                    wl.at[x, :, cols(g * GCOLS + y * wide, wide)],
                    whole[g].at[z, c, x, :, cols(y * wide, wide)],
                    zs.at[g, step - 1],
                    zr.at[g, step - 1],
                    here.along(step),
                )
            )
        sent.extend(out)
        return out

    def rows_out(table, landing, number):
        out = []
        for step in range(1, 8):
            to = here.peer(step)
            src = table if number == 2 else table.at[to]
            out.append(
                send(src, landing.at[f], ts.at[number, step - 1], tr.at[number, step - 1], (here.r, to))
            )
        sent.extend(out)
        return out

    def plane(g, copies):
        out = []
        for step in (1, 2, 3):
            copies[step - 1].wait_recv()
            src = lax.rem(z + 4 - step, 4)
            part = whole[g].at[src, c, x, :, cols(y * wide, wide)]
            xc = send(part, part, xs.at[g, step - 1], xr.at[g, step - 1], here.to_x)
            yc = send(part, part, ys.at[g, step - 1], yr.at[g, step - 1], here.to_y)
            out.append((xc, yc))
            sent.extend([xc, yc])
        core(g, 0, x, y)
        return out

    cores = {0: [], 1: [], 2: []}

    def core(g, number, h, j):
        part = whole[g].at[:, c, h, :, cols(j * wide, wide)]
        copy = send(part, part, cs.at[g, number], cr.at[g, number], here.to_core)
        sent.append(copy)
        cores[g].append(copy)

    def turn(g, copies):
        out = []
        for step in (1, 2, 3):
            src = lax.rem(z + 4 - step, 4)
            xc, yc = copies[step - 1]
            xc.wait_recv()
            part = whole[g].at[src, c, 1 - x, :, cols(y * wide, wide // 2)]
            out.append(send(part, part, ds.at[g, 0, step - 1], dr.at[g, 0, step - 1], here.to_y))
            yc.wait_recv()
            part = whole[g].at[src, c, x, :, cols((1 - y) * wide + wide // 2, wide // 2)]
            out.append(send(part, part, ds.at[g, 1, step - 1], dr.at[g, 1, step - 1], here.to_x))
        sent.extend(out)
        core(g, 1, 1 - x, y)
        core(g, 2, x, 1 - y)
        return out

    def last(g, copies):
        for copy in copies:
            copy.wait_recv()
        core(g, 3, 1 - x, 1 - y)

    def ready(g):
        for copy in cores[g]:
            copy.wait_recv()
        keep(whole[g], whole_out[g])

    def square(ref, at):
        return ref[:, :, :, :, at].reshape(D, at.size)

    def order(source, target):
        hot = (lax.broadcasted_iota(jnp.int32, (TOK_DEV, TOK_DEV), 0) == outrow[...]).astype(f32).astype(low)
        target[...] = jnp.dot(hot, source[...], preferred_element_type=f32).astype(low).reshape(8, 64, D)

    def project():
        for part in range(3):

            def one(i, _, part=part):
                at = cols(i * 256, 256)
                to = cols(part * D + i * 256, 256)
                acc = jnp.dot(tok_in[...].reshape(TOK_DEV, D), square(w0, to), preferred_element_type=f32)
                if part == 0:
                    acc = (acc + vt[0:1, at]) * (HD ** (-0.5))
                if part == 2:
                    acc = acc + vt[1:2, at]
                qkv[:, to] = acc.astype(low)
                return 0

            lax.fori_loop(0, 3, one, 0)

    def features():
        def one(i, _):
            gap = jnp.zeros((BLK - 8, TOK_DEV), f32)
            rows = bias[i]
            feat[i] = jnp.transpose(jnp.concatenate([rows, gap, rows, gap], axis=0)).astype(low)
            return 0

        lax.fori_loop(0, H, one, 0)

    def roots():
        for number, (ref, t) in enumerate([(root_l, 0), (root_l, 1), (root_r, 0), (root_r, 1)]):
            load = local(ref.at[t], stg, ks.at[0])
            load.wait()
            if number:
                out.wait()

            def one(i, _):
                at = pl.ds(pl.multiple_of(i * 96, 96), 96)
                part = stg[at, :].astype(low).reshape(2, HALF, D)
                rb[lax.div(i, 2), lax.rem(i, 2)] = part
                return 0

            lax.fori_loop(0, 8, one, 0)
            out = local(rb, o_root.at[number], ks.at[1])
        out.wait()

    def attend(start, stop):
        def pair(i, _):
            at = cols(i * 128, 128)
            q2, k2 = qkv[:, at], qkv[:, cols(D + i * 128, 128)]
            v2 = qkv[:, cols(2 * D + i * 128, 128)]
            lane = lax.broadcasted_iota(jnp.int32, (TOK_DEV, 128), 1)
            row = lax.broadcasted_iota(jnp.int32, (TOK_DEV, 128), 0)
            spot = (lax.rem(lane, BLK) == lax.div(row, BLK)).astype(f32).astype(low)
            vT = jnp.transpose(v2)
            parts = []
            for half in range(2):
                mine = (lane < HD) if half == 0 else (lane >= HD)
                qm = jnp.where(mine, q2, spot)
                km = jnp.where(mine, k2, feat[2 * i + half])
                s = lax.dot_general(km, qm, (((1,), (1,)), ((), ())), preferred_element_type=f32)
                e = jnp.exp(s - jnp.max(s, axis=0, keepdims=True))
                p = (e * (use_row[...] / jnp.sum(e, axis=0, keepdims=True))).astype(low)
                P[2 * i + half] = p
                parts.append(jnp.dot(vT[half * HD : (half + 1) * HD], p, preferred_element_type=f32))
            total = jnp.where(use_row[...] > 0, jnp.concatenate(parts, axis=0), vT.astype(f32)).astype(low)
            mT[cols(i * 128, 128), :] = total
            mix[:, at] = jnp.transpose(total)
            return 0

        lax.fori_loop(start, stop, pair, 0)

    def flip(source, target):
        def one(i, _):
            at = cols(i * 128, 128)
            target[at, :] = jnp.transpose(source(at))
            return 0

        lax.fori_loop(0, 6, one, 0)

    def join():
        def one(i, _):
            at = cols(i * 256, 256)
            acc = jnp.dot(mix[...], square(w0, cols(3 * D + i * 256, 256)), preferred_element_type=f32)
            x1[:, at] = tok_in[:, :, at].reshape(TOK_DEV, 256).astype(f32) + (acc + vt[2:3, at])
            return 0

        lax.fori_loop(0, 3, one, 0)

    def norm(ref, i):
        at = pl.ds(pl.multiple_of(i * 64, 64), 64)
        h = ref[at, :]
        center = h - jnp.mean(h, axis=1, keepdims=True)
        r = lax.rsqrt(jnp.mean(center * center, axis=1, keepdims=True) + NORM_EPS)
        return at, center * r, r

    def norm_one():
        def one(i, _):
            at, n, r = norm(x1, i)
            n1[at, :] = n
            r1[at, :] = jnp.broadcast_to(r, (64, 128))
            out = n * vt[4:5, :] + vt[5:6, :]
            u[at, :] = out.astype(low)
            x1[at, :] = out
            return 0

        lax.fori_loop(0, 8, one, 0)

    def lift():
        for row in range(4):

            def one(i, _, row=row):
                at = cols(i * 256, 256)
                to = cols(row * D + i * 256, 256)
                pre = jnp.dot(u[...], square(w1, to), preferred_element_type=f32) + vt[8 + row : 9 + row, at]
                sq = pre * pre
                t = jnp.tanh(0.7978845608028654 * pre * (1.0 + 0.044715 * sq))
                half = 0.5 * (1.0 + t)
                fa[:, to] = (pre * half).astype(low)
                slope = 0.7978845608028654 * (1.0 + 0.134145 * sq)
                dg[:, to] = (half + 0.5 * pre * (1.0 - t * t) * slope).astype(low)
                return 0

            lax.fori_loop(0, 3, one, 0)

    def drop():
        def one(i, _):
            at = cols(i * 512, 512)
            acc = lax.dot_general(
                fa[:, at], square(w2, at), (((1,), (1,)), ((), ())), preferred_element_type=f32
            )
            x1[...] += acc
            return 0

        lax.fori_loop(0, 6, one, 0)

    def norm_two():
        def one(i, _):
            at = pl.ds(pl.multiple_of(i * 64, 64), 64)
            x1[at, :] = x1[at, :] + vt[3:4, :]
            at, n, r = norm(x1, i)
            n2[at, :] = n
            r2[at, :] = jnp.broadcast_to(r, (64, 128))
            out = (n * vt[6:7, :] + vt[7:8, :]) * use[at, 0:1]
            yo[at, :] = out.astype(low)
            return 0

        lax.fori_loop(0, 8, one, 0)

    stays = [narrow(0)]
    order(tok, tok_s)
    wait_all()
    z0 = z_send(0)
    small = rows_out(vec, vec_in, 2)
    own = [local(vec, vec_in.at[f], ls.at[5]), local(tok_s.at[f], tok_in.at[f], ls.at[3])]
    t0 = rows_out(tok_s, tok_in, 0)
    stays.append(narrow(1))
    z1 = z_send(1)
    stays.append(narrow(2))
    order(cot, cot_s)
    own.append(local(cot_s.at[f], cot_in.at[f], ls.at[4]))
    for copy in stays + own:
        copy.wait()
    features()
    p0 = plane(0, z0)
    for copy in small:
        copy.wait_recv()
    wide_vec = jnp.transpose(vec_in[...].reshape(D, 128).astype(f32))
    vt[...] = wide_vec[:16, :]
    keep(vt, o_vt)
    roots()
    d0 = turn(0, p0)
    z2 = z_send(2)
    t1 = rows_out(cot_s, cot_in, 1)
    last(0, d0)
    for copy in t0:
        copy.wait_recv()
    ready(0)
    project()
    keep(qkv, o_qkv)
    flip(lambda at: tok_in[:, :, at].reshape(TOK_DEV, 128), xT)
    keep(xT, o_x)
    p1 = plane(1, z1)
    attend(0, 2)
    d1 = turn(1, p1)
    attend(2, 4)
    last(1, d1)
    p2 = plane(2, z2)
    attend(4, 6)
    keep(P, o_p)
    keep(mT, o_mix)
    join()
    norm_one()
    keep(n1, o_n1)
    keep(r1, o_r1)
    d2 = turn(2, p2)
    flip(lambda at: u[:, at], uT)
    keep(uT, o_u)
    ready(1)
    lift()
    keep(fa, o_f)
    keep(dg, o_dg)
    last(2, d2)
    ready(2)
    drop()
    norm_two()
    keep(n2, o_n2)
    keep(r2, o_r2)
    keep(yo, o_y)
    for copy in t1:
        copy.wait_recv()
    keep(cot_in, o_cot)
    for copy in sent:
        copy.wait_send()
    for copy in outs:
        copy.wait()


def forward_all(outrow, tok, cot, flat_weights, vec, bias, use, use_row, root_l, root_r):
    any_spec = pl.BlockSpec(memory_space=pl.ANY)
    vmem = pl.BlockSpec(memory_space=pltpu.VMEM)
    dma = pltpu.SemaphoreType.DMA
    shape = jax.ShapeDtypeStruct
    low, f32 = jnp.bfloat16, jnp.float32
    square = (4, 2, 2, HALF, GCOLS)
    saved = [
        ((16, D), f32), ((D, TOK_DEV), low), ((8, 64, D), low), ((TOK_DEV, 3 * D), low),
        ((H, TOK_DEV, TOK_DEV), low), ((D, TOK_DEV), low), ((TOK_DEV, D), f32), ((TOK_DEV, 128), f32),
        ((D, TOK_DEV), low), ((TOK_DEV, FF), low), ((TOK_DEV, FF), low), ((TOK_DEV, D), f32),
        ((TOK_DEV, 128), f32), ((TOK_DEV, D), low), ((4, 4, 2, 2, HALF, D), low),
    ]
    return pl.pallas_call(
        forward_kernel,
        out_shape=[shape(square, low)] * 3 + [shape(*s) for s in saved],
        in_specs=[vmem] * 8 + [any_spec] * 2,
        out_specs=[any_spec] * 18,
        scratch_shapes=[
            pltpu.VMEM(square, low), pltpu.VMEM(square, low), pltpu.VMEM(square, low),
            pltpu.VMEM((8, 64, D), low), pltpu.VMEM((8, 64, D), low), pltpu.VMEM((8, 96, 128), low),
            pltpu.VMEM((8, 64, D), low), pltpu.VMEM((8, 64, D), low),
            pltpu.VMEM((16, D), f32),
            pltpu.VMEM((TOK_DEV, 3 * D), low),
            pltpu.VMEM((H, TOK_DEV, TOK_DEV), low),
            pltpu.VMEM((TOK_DEV, D), low),
            pltpu.VMEM((TOK_DEV, D), f32),
            pltpu.VMEM((TOK_DEV, 128), f32),
            pltpu.VMEM((TOK_DEV, D), f32),
            pltpu.VMEM((TOK_DEV, D), low),
            pltpu.VMEM((TOK_DEV, FF), low),
            pltpu.VMEM((TOK_DEV, FF), low),
            pltpu.VMEM((TOK_DEV, D), f32),
            pltpu.VMEM((TOK_DEV, 128), f32),
            pltpu.VMEM((TOK_DEV, D), low),
            pltpu.VMEM((D, TOK_DEV), low), pltpu.VMEM((D, TOK_DEV), low), pltpu.VMEM((D, TOK_DEV), low),
            pltpu.VMEM((H, TOK_DEV, 128), low),
            pltpu.VMEM((D, D), f32),
            pltpu.VMEM((4, 2, 2, HALF, D), low),
            pltpu.VMEM((2, HALF, 3 * GCOLS), low),
            dma((3, 3)), dma((3, 3)), dma((3, 3)), dma((3, 3)), dma((3, 3)), dma((3, 3)),
            dma((3, 2, 3)), dma((3, 2, 3)), dma((3, 4)), dma((3, 4)),
            dma((6,)), dma((3, 7)), dma((3, 7)), dma((17,)), dma((2,)),
        ],
        compiler_params=pltpu.CompilerParams(
            collective_id=0, has_side_effects=True, vmem_limit_bytes=60 * MIB
        ),
        name="forward_all",
    )(outrow, tok, cot, flat_weights.reshape(2, HALF, 3 * GCOLS), vec, bias, use, use_row, root_l, root_r)


def backward_kernel(
    block_of, vt, use, use_row,
    h_w0, h_w1, h_w2, h_xT, h_cot, h_qkv, h_p, h_mT, h_n1, h_r1, h_uT, h_f, h_dg, h_n2, h_r2, h_y, h_root,
    o_back, o_grad, WR, UA, SC, o_gs, o_vec,
    G, Rc, A1, A2, B1, B2, ZR, F, SO, Gs, wa, wb, fb, gb, low_g, LT, LU, hb, nb, PT, r1, r2, gi,
    PQ, sq, sr_in, sc_out, vb, vr,
    ld, pd, cs, cr, a1s, a1r, b1s, b1r, a2s, a2r, b2s, b2r, zs, zr,
    fs, fr, ts, tr, ss, sr, ps, pr, us, ur, qs, qr, es, er, ms, mr, vs, vrs, ls,
):
    low, f32 = jnp.bfloat16, jnp.float32
    here = Here(True)
    wait_all = here.greet()
    x, y, z, c, f, r = here.x, here.y, here.z, here.c, here.f, here.r
    W = GCOLS // 2
    sent = []

    class Load:
        def __init__(self, number, src, dst):
            self.copy, self.done = local(src, dst, ld.at[number]), False

        def wait(self):
            if not self.done:
                self.copy.wait()
                self.done = True

    cot_l = Load(0, h_cot, gi)
    n2_l = Load(1, h_n2, hb)
    r2_l = Load(2, h_r2, r2)
    f_l = Load(3, h_f, fb)
    wd_l = Load(4, h_w2, wa)
    dg_l = Load(5, h_dg, gb)
    uT_l = Load(6, h_uT, LU)
    wu_l = Load(7, h_w1, wb)
    n1_l = Load(8, h_n1, nb)
    r1_l = Load(9, h_r1, r1)
    vb[...] = jnp.zeros_like(vb)
    wait_all()

    def span(g):
        return pl.ds(g * W, W)

    def c_send(g):
        copy = send(
            G.at[:, :, 1 - c, :, :, span(g)], Rc.at[:, :, :, :, span(g)],
            cs.at[g], cr.at[g], here.to_core,
        )
        sent.append(copy)
        return copy

    def first(g, copy):
        copy.wait_recv()

        def add(i, _):
            j, zz, h = lax.div(i, 8), lax.rem(lax.div(i, 2), 4), lax.rem(i, 2)
            G[j, zz, c, h, :, span(g)] = (
                G[j, zz, c, h, :, span(g)].astype(f32) + Rc[j, zz, h, :, span(g)].astype(f32)
            ).astype(low)
            return 0

        lax.fori_loop(0, 16, add, 0)
        a = send(
            G.at[:, 0:2, c, 1 - x, :, span(g)], A1.at[:, :, :, span(g)], a1s.at[g], a1r.at[g], here.to_x
        )
        b = send(
            G.at[1 - y, 2:4, c, :, :, span(g)], B1.at[:, :, :, span(g)], b1s.at[g], b1r.at[g], here.to_y
        )
        sent.extend([a, b])
        return a, b

    def second(g, copies):
        copies[0].wait_recv()

        def add_a(i, _):
            j, zz = lax.div(i, 2), lax.rem(i, 2)
            G[j, zz, c, x, :, span(g)] = (
                G[j, zz, c, x, :, span(g)].astype(f32) + A1[j, zz, :, span(g)].astype(f32)
            ).astype(low)
            return 0

        lax.fori_loop(0, 4, add_a, 0)
        a = send(
            G.at[1 - y, 0:2, c, x, :, span(g)], A2.at[:, :, span(g)], a2s.at[g], a2r.at[g], here.to_y
        )
        copies[1].wait_recv()

        def add_b(i, _):
            zz, h = lax.div(i, 2), lax.rem(i, 2)
            G[y, zz + 2, c, h, :, span(g)] = (
                G[y, zz + 2, c, h, :, span(g)].astype(f32) + B1[zz, h, :, span(g)].astype(f32)
            ).astype(low)
            return 0

        lax.fori_loop(0, 4, add_b, 0)
        b = send(
            G.at[y, 2:4, c, 1 - x, :, span(g)], B2.at[:, :, span(g)], b2s.at[g], b2r.at[g], here.to_x
        )
        sent.extend([a, b])
        return a, b

    def third(g, copies):
        for number, (copy, part) in enumerate(zip(copies, (A2, B2))):
            copy.wait_recv()

            def add(i, _, number=number, part=part):
                zz = 2 * number + i
                G[y, zz, c, x, :, span(g)] = (
                    G[y, zz, c, x, :, span(g)].astype(f32) + part[i, :, span(g)].astype(f32)
                ).astype(low)
                return 0

            lax.fori_loop(0, 2, add, 0)
        out = []
        for step in (1, 2, 3):
            out.append(
                send(
                    G.at[y, here.z_plus(step), c, x, :, span(g)], ZR.at[step - 1, :, span(g)],
                    zs.at[g, step - 1], zr.at[g, step - 1], here.along(step),
                )
            )
        sent.extend(out)
        return out

    def final(g, copies):
        for copy in copies:
            copy.wait_recv()
        for b in range(4 * g, 4 * g + 4):
            at = pl.ds(b * JCOLS, JCOLS)
            total = G[y, z, c, x, :, at].astype(f32)
            for step in range(3):
                total = total + ZR[step, :, at].astype(f32)
            F[b] = total.astype(low)

    homes = []

    def spread(g):
        at = pl.ds(4 * g, 4)
        to = WR.at[x, y, at]
        a = send(F.at[at], to, fs.at[g, 0], fr.at[g, 0], here.to_x)
        b = send(F.at[at], to, fs.at[g, 1], fr.at[g, 1], here.to_y)
        homes.append(local(F.at[at], to, ls.at[g]))
        sent.extend([a, b])
        return a, b

    def spread_on(g, copies):
        a, b = copies
        a.wait_recv()
        part = WR.at[1 - x, y, pl.ds(4 * g, 2)]
        da = send(part, part, fs.at[g, 2], fr.at[g, 2], here.to_y)
        b.wait_recv()
        part = WR.at[x, 1 - y, pl.ds(4 * g + 2, 2)]
        db = send(part, part, fs.at[g, 3], fr.at[g, 3], here.to_x)
        sent.extend([da, db])
        return da, db

    def token_send(source, landing, number):
        out = []
        for step in range(1, 8):
            to = here.peer(step)
            out.append(
                send(source(to), landing.at[f], ts.at[number, step - 1], tr.at[number, step - 1], (r, to))
            )
        homes.append(local(source(f), landing.at[f], ls.at[3 + number]))
        sent.extend(out)
        return out

    def square(ref, at):
        return ref[:, :, :, :, at].reshape(D, at.size)

    def own_rows(ref, core):
        return jnp.concatenate(
            [ref[pl.ds(pl.multiple_of((2 * zz + core) * 96, 96), 96), :] for zz in range(4)], axis=0
        )

    def gradient(left, right, block, start, count, core):
        rows = own_rows(left, core)

        def one(i, _):
            out = jnp.dot(rows, right[:, cols(start + i * D, D)], preferred_element_type=f32)
            out = out.astype(low).reshape(4, 2, HALF, D)
            for j in range(2):
                at = cols((block + i) * JCOLS, JCOLS)
                G[j, :, core, :, :, at] = out[:, :, :, j * JCOLS : (j + 1) * JCOLS]
            return 0

        lax.fori_loop(0, count, one, 0)

    def eight(v):
        return jnp.sum(v.reshape(8, 8, v.shape[1]), axis=0)

    def norm_back(i, carry, grad, n, rr, gain):
        zed = grad * gain
        back = rr * (
            zed - jnp.mean(zed, axis=1, keepdims=True) - n * jnp.mean(zed * n, axis=1, keepdims=True)
        )
        rounded = back.astype(low)
        return back, rounded, (
            carry[0] + eight(grad * n), carry[1] + eight(grad), carry[2] + eight(rounded.astype(f32))
        )

    zero = jnp.zeros((8, D), f32)

    def put(row, total):
        vb[0, row : row + 1, :] = jnp.sum(total, axis=0, keepdims=True)

    def flip(source, target, count):
        def one(i, _):
            at = cols(i * 128, 128)
            target[at, :] = jnp.transpose(source[:, at])
            return 0

        lax.fori_loop(0, count, one, 0)

    ta = token_send(lambda to: h_y.at[to], o_back, 0)
    cot_l.wait()
    n2_l.wait()
    r2_l.wait()

    def back_two(i, carry):
        at = pl.ds(pl.multiple_of(i * 64, 64), 64)
        grad = gi[i].astype(f32) * use[at, 0:1]
        back, rounded, carry = norm_back(i, carry, grad, hb[at, :], r2[at, 0:1], vt[6:7, :])
        hb[at, :] = back
        low_g[at, :] = rounded
        return carry

    sums = lax.fori_loop(0, 8, back_two, (zero, zero, zero))
    put(6, sums[0])
    put(7, sums[1])
    put(3, sums[2])
    flip(low_g, LT, 6)
    f_l.wait()
    gradient(LT, fb, 8, 0, 4, 1 - c)
    c2 = c_send(2)
    gradient(LT, fb, 8, 0, 4, c)
    qkv_l = Load(10, h_qkv, fb.at[:, : 3 * D])
    mT_l = Load(11, h_mT, LT)
    wd_l.wait()
    dg_l.wait()

    def back_up(i, _):
        at = cols(i * 256, 256)
        acc = jnp.dot(low_g[...], square(wa, at), preferred_element_type=f32)
        gb[:, at] = (acc * gb[:, at].astype(f32)).astype(low)
        return 0

    lax.fori_loop(0, 12, back_up, 0)
    wq_l = Load(12, h_w0, wa)
    f2 = first(2, c2)
    uT_l.wait()
    gradient(LU, gb, 4, 0, 4, 1 - c)
    c1 = c_send(1)
    gradient(LU, gb, 4, 0, 4, c)
    xT_l = Load(13, h_xT, LU)
    wu_l.wait()

    def back_x1(i, _):
        at = cols(i * 512, 512)
        hb[...] += lax.dot_general(
            gb[:, at], square(wb, at), (((1,), (1,)), ((), ())), preferred_element_type=f32
        )
        return 0

    lax.fori_loop(0, 6, back_x1, 0)
    root_l = [Load(14 + n, h_root.at[n], wb.at[:, :, :, :, n * D : (n + 1) * D]) for n in range(4)]
    for row in range(4):

        def total(i, acc, row=row):
            at = pl.ds(pl.multiple_of(i * 64, 64), 64)
            return acc + eight(gb[at, row * D : (row + 1) * D].astype(f32))

        put(8 + row, lax.fori_loop(0, 8, total, zero))
    f1 = first(1, c1)
    n1_l.wait()
    r1_l.wait()

    def back_one(i, carry):
        at = pl.ds(pl.multiple_of(i * 64, 64), 64)
        back, rounded, carry = norm_back(i, carry, hb[at, :], nb[at, :], r1[at, 0:1], vt[4:5, :])
        hb[at, :] = back
        low_g[at, :] = rounded
        return carry

    sums = lax.fori_loop(0, 8, back_one, (zero, zero, zero))
    put(4, sums[0])
    put(5, sums[1])
    put(2, sums[2])
    s2 = second(2, f2)
    mT_l.wait()
    gradient(LT, low_g, 3, 0, 1, 1 - c)
    gradient(LT, low_g, 3, 0, 1, c)
    wq_l.wait()

    def back_mix(i, _):
        out = lax.dot_general(
            low_g[...], wa[pl.ds(2 * i, 2), :, :, :, 3 * D : 4 * D].reshape(JCOLS, D),
            (((1,), (1,)), ((), ())), preferred_element_type=f32,
        )
        gb[:, cols(3 * D + i * JCOLS, JCOLS)] = out.astype(low)
        return 0

    lax.fori_loop(0, 2, back_mix, 0)
    qkv_l.wait()

    def fetch(i):
        return pltpu.make_async_copy(h_p.at[pl.ds(2 * i, 2)], PT.at[lax.rem(i, 2)], pd.at[lax.rem(i, 2)])

    fetch(0).start()

    def attend(i, _):
        slot = lax.rem(i, 2)

        @pl.when(i < 5)
        def _():
            fetch(i + 1).start()

        q2, k2 = fb[:, cols(i * 128, 128)], fb[:, cols(D + i * 128, 128)]
        v2, go2 = fb[:, cols(2 * D + i * 128, 128)], gb[:, cols(3 * D + i * 128, 128)]
        kT = jnp.transpose(k2)
        lane = lax.broadcasted_iota(jnp.int32, (TOK_DEV, 128), 1)
        fetch(i).wait()
        parts = []
        gk = jnp.zeros((TOK_DEV, 128), f32)
        gv = jnp.where(use[:, :] > 0, 0.0, go2.astype(f32))
        for half in range(2):
            mine = (lane < HD) if half == 0 else (lane >= HD)
            none = jnp.zeros_like(v2)
            p = PT[slot, half]
            gp = lax.dot_general(
                jnp.where(mine, v2, none), go2, (((1,), (1,)), ((), ())), preferred_element_type=f32
            )
            pf = p.astype(f32)
            gs = (pf * (gp - jnp.sum(pf * gp, axis=0, keepdims=True))).astype(low)
            gk = gk + jnp.dot(gs, jnp.where(mine, q2, none), preferred_element_type=f32)
            gv = gv + jnp.dot(p, jnp.where(mine, go2, none), preferred_element_type=f32)
            parts.append(jnp.dot(kT[half * HD : (half + 1) * HD], gs, preferred_element_type=f32))
        gq = jnp.transpose(jnp.concatenate(parts, axis=0)) * (HD ** (-0.5))
        gb[:, cols(i * 128, 128)] = gq.astype(low)
        gb[:, cols(D + i * 128, 128)] = gk.astype(low)
        gb[:, cols(2 * D + i * 128, 128)] = gv.astype(low)
        return 0

    lax.fori_loop(0, 2, attend, 0)
    s1 = second(1, f1)
    t2 = third(2, s2)
    lax.fori_loop(2, 4, attend, 0)
    t1 = third(1, s1)
    lax.fori_loop(4, 6, attend, 0)
    xT_l.wait()
    gradient(LU, gb, 0, 0, 3, 1 - c)
    c0 = c_send(0)
    gradient(LU, gb, 0, 0, 3, c)
    for row, start in ((0, 0), (1, 2 * D)):

        def total(i, acc, start=start):
            at = pl.ds(pl.multiple_of(i * 64, 64), 64)
            return acc + eight(gb[at, start : start + D].astype(f32))

        put(row, lax.fori_loop(0, 8, total, zero))
    f0 = first(0, c0)
    vec_copy = send(vb.at[0], vr.at[0], vs.at[0], vrs.at[0], here.to_core)
    sent.append(vec_copy)
    final(2, t2)
    e2 = spread(2)

    def back_x(i, _):
        at = cols(i * D, D)
        hb[...] += lax.dot_general(
            gb[:, at], square(wa, at), (((1,), (1,)), ((), ())), preferred_element_type=f32
        )
        return 0

    lax.fori_loop(0, 3, back_x, 0)

    def rows_low(i, _):
        gi[i] = hb[pl.ds(pl.multiple_of(i * 64, 64), 64), :].astype(low)
        return 0

    lax.fori_loop(0, 8, rows_low, 0)
    vec_copy.wait_recv()
    vb[1] = vb[0] + vr[0]
    vec_copy = send(vb.at[1], vr.at[1], vs.at[1], vrs.at[1], here.to_x)
    sent.append(vec_copy)
    s0 = second(0, f0)
    final(1, t1)
    e1 = spread(1)
    vec_copy.wait_recv()
    vb[2] = vb[1] + vr[1]
    vec_copy = send(vb.at[2], vr.at[2], vs.at[2], vrs.at[2], here.to_y)
    sent.append(vec_copy)
    d2 = spread_on(2, e2)
    t0 = third(0, s0)
    final(0, t0)
    jc = cols(y * JCOLS, JCOLS)
    other = cols((1 - y) * JCOLS, JCOLS)
    slot_copies = []
    for step in range(1, 9):
        to = here.peer(step)
        for t in range(2):
            b = block_of[2 * to + t]
            flag = (b >= 0).astype(f32)
            SO[step - 1, t] = (F[jnp.maximum(b, 0)].astype(f32) * flag).astype(low)
        if step < 8:
            slot_copies.append(
                send(SO.at[step - 1], Gs.at[:, f, x, :, jc], ss.at[step - 1], sr.at[step - 1], (r, to))
            )
    sent.extend(slot_copies)
    own = local(SO.at[7], Gs.at[:, f, x, :, jc], ls.at[5])
    hops = []
    for step in range(8):
        src = lax.rem(f + 8 - step, 8)
        if step == 0:
            own.wait()
        else:
            slot_copies[step - 1].wait_recv()
        part = Gs.at[:, src, x, :, jc]
        hops.append(
            (
                send(part, part, ps.at[0, step], pr.at[0, step], here.to_x),
                send(part, part, ps.at[1, step], pr.at[1, step], here.to_y),
            )
        )
    ends = []
    for step in range(8):
        src = lax.rem(f + 8 - step, 8)
        hops[step][0].wait_recv()
        part = Gs.at[0, src, 1 - x, :, jc]
        ends.append(send(part, part, ps.at[2, step], pr.at[2, step], here.to_y))
        hops[step][1].wait_recv()
        part = Gs.at[1, src, x, :, other]
        ends.append(send(part, part, ps.at[3, step], pr.at[3, step], here.to_x))
        sent.extend(hops[step])
    sent.extend(ends)
    vec_copy.wait_recv()
    vb[3] = vb[2] + vr[2]
    vec_copies = []
    for step in (1, 2, 3):
        vec_copies.append(
            send(vb.at[3], vr.at[2 + step], vs.at[2 + step], vrs.at[2 + step], here.along(step))
        )
    sent.extend(vec_copies)
    e0 = spread(0)
    d1 = spread_on(1, e1)
    for load in root_l:
        load.wait()
    for copy in ends:
        copy.wait_recv()
    homes.append(local(Gs, o_gs, ls.at[6]))
    for t in range(2):
        whole = Gs[t].reshape(D, D)
        rows = wb[:, :, x, :, t * D : (t + 1) * D].reshape(JCOLS, D)
        half = jnp.dot(rows, whole, preferred_element_type=f32).astype(low)
        right = square(wb, cols((2 + t) * D + y * JCOLS, JCOLS))
        part = jnp.dot(half, right, preferred_element_type=f32)
        PQ[t] = part.astype(low).reshape(8, HALF, JCOLS)
        sq[t] = jnp.sum((part * part).reshape(48, 8, JCOLS), axis=0)
    ucopies = []
    for step in range(1, 8):
        to = here.peer(step)
        ucopies.append(
            send(PQ.at[:, to], UA.at[x, y, pl.ds(2 * f, 2)], us.at[step - 1], ur.at[step - 1], (r, to))
        )
    sent.extend(ucopies)
    own = local(PQ.at[:, f], UA.at[x, y, pl.ds(2 * f, 2)], ls.at[7])
    squares = []
    for number, to in enumerate((here.to_x, here.to_y, here.to_d)):
        squares.append(send(sq, sr_in.at[number], es.at[number], er.at[number], to))
    sent.extend(squares)
    uhops = []
    for step in range(8):
        src = lax.rem(f + 8 - step, 8)
        if step == 0:
            own.wait()
        else:
            ucopies[step - 1].wait_recv()
        part = UA.at[x, y, pl.ds(2 * src, 2)]
        uhops.append(
            (
                send(part, part, qs.at[0, step], qr.at[0, step], here.to_x),
                send(part, part, qs.at[1, step], qr.at[1, step], here.to_y),
            )
        )
        if step == 0:
            for copy in squares:
                copy.wait_recv()
            for t in range(2):
                total = sq[t] + sr_in[0, t] + sr_in[1, t] + sr_in[2, t]
                mean = jnp.sum(jnp.sum(total, axis=1, keepdims=True), axis=0, keepdims=True) * (1.0 / (D * D))
                sc_out[t] = jnp.broadcast_to(lax.rsqrt(mean + RMS_EPS), (8, 128))
            scales = []
            for number in range(1, 8):
                to = here.peer(number)
                scales.append(
                    send(
                        sc_out, SC.at[pl.ds(2 * f, 2)], ms.at[number - 1], mr.at[number - 1], (r, to)
                    )
                )
            sent.extend(scales)
            homes.append(local(sc_out, SC.at[pl.ds(2 * f, 2)], ls.at[8]))
            tb = token_send(lambda to: gi.at[to], o_grad, 1)
    uends = []
    for step in range(8):
        src = lax.rem(f + 8 - step, 8)
        uhops[step][0].wait_recv()
        part = UA.at[1 - x, y, 2 * src]
        uends.append(send(part, part, qs.at[2, step], qr.at[2, step], here.to_y))
        uhops[step][1].wait_recv()
        part = UA.at[x, 1 - y, 2 * src + 1]
        uends.append(send(part, part, qs.at[3, step], qr.at[3, step], here.to_x))
        sent.extend(uhops[step])
    sent.extend(uends)
    d0 = spread_on(0, e0)
    total = vb[3]
    for copy in vec_copies:
        copy.wait_recv()
    for step in range(3):
        total = total + vr[3 + step]
    vb[4] = total
    homes.append(local(vb.at[4], o_vec, ls.at[9]))
    for copy in list(d2) + list(d1) + list(d0) + uends + scales + ta + tb:
        copy.wait_recv()
    for copy in homes:
        copy.wait()
    for copy in sent:
        copy.wait_send()


def backward_all(block_of, vt, use, use_row, saved):
    any_spec = pl.BlockSpec(memory_space=pl.ANY)
    vmem = pl.BlockSpec(memory_space=pltpu.VMEM)
    smem = pl.BlockSpec(memory_space=pltpu.SMEM)
    dma = pltpu.SemaphoreType.DMA
    shape = jax.ShapeDtypeStruct
    low, f32 = jnp.bfloat16, jnp.float32
    JW = 12 * JCOLS
    square = (4, 2, 2, HALF, GCOLS)
    return pl.pallas_call(
        backward_kernel,
        out_shape=[
            shape((8, 64, D), low), shape((8, 64, D), low),
            shape((2, 2, 12, HALF, JCOLS), low), shape((2, 2, 16, HALF, JCOLS), low),
            shape((16, 8, 128), f32), shape((2, 8, 2, HALF, D), low), shape((16, D), f32),
        ],
        in_specs=[smem, vmem, vmem, vmem] + [any_spec] * 17,
        out_specs=[any_spec] * 7,
        scratch_shapes=[
            pltpu.VMEM((2, 4, 2, 2, HALF, JW), low),
            pltpu.VMEM((2, 4, 2, HALF, JW), low),
            pltpu.VMEM((2, 2, HALF, JW), low),
            pltpu.VMEM((2, HALF, JW), low),
            pltpu.VMEM((2, 2, HALF, JW), low),
            pltpu.VMEM((2, HALF, JW), low),
            pltpu.VMEM((3, HALF, JW), low),
            pltpu.VMEM((12, HALF, JCOLS), low),
            pltpu.VMEM((8, 2, HALF, JCOLS), low),
            pltpu.VMEM((2, 8, 2, HALF, D), low),
            pltpu.VMEM(square, low),
            pltpu.VMEM(square, low),
            pltpu.VMEM((TOK_DEV, FF), low),
            pltpu.VMEM((TOK_DEV, FF), low),
            pltpu.VMEM((TOK_DEV, D), low),
            pltpu.VMEM((D, TOK_DEV), low),
            pltpu.VMEM((D, TOK_DEV), low),
            pltpu.VMEM((TOK_DEV, D), f32),
            pltpu.VMEM((TOK_DEV, D), f32),
            pltpu.VMEM((2, 2, TOK_DEV, TOK_DEV), low),
            pltpu.VMEM((TOK_DEV, 128), f32),
            pltpu.VMEM((TOK_DEV, 128), f32),
            pltpu.VMEM((8, 64, D), low),
            pltpu.VMEM((2, 8, HALF, JCOLS), low),
            pltpu.VMEM((2, 8, JCOLS), f32),
            pltpu.VMEM((3, 2, 8, JCOLS), f32),
            pltpu.VMEM((2, 8, 128), f32),
            pltpu.VMEM((5, 16, D), f32),
            pltpu.VMEM((6, 16, D), f32),
            dma((18,)), dma((2,)), dma((3,)), dma((3,)),
            dma((3,)), dma((3,)), dma((3,)), dma((3,)), dma((3,)), dma((3,)), dma((3,)), dma((3,)),
            dma((3, 3)), dma((3, 3)), dma((3, 4)), dma((3, 4)),
            dma((2, 7)), dma((2, 7)), dma((7,)), dma((7,)), dma((4, 8)), dma((4, 8)),
            dma((7,)), dma((7,)), dma((4, 8)), dma((4, 8)), dma((3,)), dma((3,)), dma((7,)), dma((7,)),
            dma((6,)), dma((6,)), dma((10,)),
        ],
        compiler_params=pltpu.CompilerParams(
            collective_id=1, has_side_effects=True, vmem_limit_bytes=60 * MIB
        ),
        name="backward_all",
    )(block_of, vt, use, use_row, *saved)


def finish_kernel(
    owner, outrow, back, grad, wr, ua, sc, gs, vec, stat_l, stat_r, wf, vecs, mom1, mom2,
    layer_out, input_grad, wg, nw, new_l, new_r, out1, out2, outv,
    gb, sl, sr, ub, rb, wb, nb, gg, tb, to, ls, os,
):
    low, f32 = jnp.bfloat16, jnp.float32
    f = lax.axis_index("fsdp")
    loads = [
        local(back, tb.at[0], ls.at[0]), local(grad, tb.at[1], ls.at[1]),
        local(wr, rb, ls.at[2]), local(ua, ub, ls.at[3]), local(wf, wb, ls.at[4]),
        local(gs, gb, ls.at[5]),
    ]
    stats = [
        (local(stat_l.at[t], sl.at[t], ls.at[6 + 2 * t]), local(stat_r.at[t], sr.at[t], ls.at[7 + 2 * t]))
        for t in range(2)
    ]
    outs = []
    hot = (outrow[...] == lax.broadcasted_iota(jnp.int32, (TOK_DEV, TOK_DEV), 1)).astype(f32).astype(low)
    for number, target in enumerate((layer_out, input_grad)):
        loads[number].wait()
        to[number] = jnp.dot(
            hot, tb[number].reshape(TOK_DEV, D), preferred_element_type=f32
        ).astype(low)
        outs.append(local(to.at[number], target, os.at[number]))
    loads[2].wait()

    def one(i, _):
        h, b = lax.rem(i, 2), lax.div(i, 2)
        for j in range(2):
            gg[h, :, cols(b * D + j * JCOLS, JCOLS)] = rb[h, j, b].astype(f32)
        return 0

    lax.fori_loop(0, 24, one, 0)
    outs.append(local(gg, wg, os.at[2]))
    loads[3].wait()
    loads[4].wait()
    for b in range(NBLK):
        slot = owner[b]
        scale = LR_MATRIX * sc[slot, 0:1, 0:1]
        for h in range(2):
            for j in range(2):
                at = pl.ds(b * D + j * JCOLS, JCOLS)
                nb[h, :, at] = wb[h, :, at] - scale * ub[h, j, slot].astype(f32)
    outs.append(local(nb, nw, os.at[3]))
    loads[5].wait()
    for t in range(2):
        stats[t][0].wait()

        def left(i, _, t=t):
            at = pl.ds(pl.multiple_of(i * 192, 192), 192)
            rows = gb[t, pl.ds(2 * i, 2)].reshape(192, D)
            part = lax.dot_general(
                rows, gb[t].reshape(D, D), (((1,), (1,)), ((), ())), preferred_element_type=f32
            )
            sl[t, at, :] = STAT_DECAY * sl[t, at, :] + (1.0 - STAT_DECAY) * part
            return 0

        lax.fori_loop(0, 4, left, 0)
        outs.append(local(sl.at[t], new_l.at[t], os.at[4 + 2 * t]))
        stats[t][1].wait()
        for i in range(3):
            at = pl.ds(i * 256, 256)
            part = lax.dot_general(
                gb[t, :, :, :, at].reshape(D, 256), gb[t].reshape(D, D), (((0,), (0,)), ((), ())),
                preferred_element_type=f32,
            )
            sr[t, at, :] = STAT_DECAY * sr[t, at, :] + (1.0 - STAT_DECAY) * part
        outs.append(local(sr.at[t], new_r.at[t], os.at[5 + 2 * t]))
    tall = jnp.transpose(jnp.concatenate([vec[...], jnp.zeros((112, D), f32)], axis=0))
    gi = to.at[0]
    mine = jnp.zeros((96, NBLK), f32)
    for number in range(8):
        part = tall[number * 96 : (number + 1) * 96, :NBLK]
        mine = jnp.where(f == number, part, mine)
    fresh1 = BETA_ONE * mom1[...] + (1.0 - BETA_ONE) * mine
    fresh2 = BETA_TWO * mom2[...] + (1.0 - BETA_TWO) * mine * mine
    out1[...] = fresh1
    out2[...] = fresh2
    outv[...] = vecs[...] - LR_VECTOR * (fresh1 / (1.0 - BETA_ONE**STEP)) / (
        jnp.sqrt(fresh2 / (1.0 - BETA_TWO**STEP)) + ADAM_EPS
    )
    for copy in outs:
        copy.wait()


def finish_all(owner, outrow, results, stat_l, stat_r, wf, vecs, mom1, mom2):
    any_spec = pl.BlockSpec(memory_space=pl.ANY)
    vmem = pl.BlockSpec(memory_space=pltpu.VMEM)
    smem = pl.BlockSpec(memory_space=pltpu.SMEM)
    dma = pltpu.SemaphoreType.DMA
    shape = jax.ShapeDtypeStruct
    low, f32 = jnp.bfloat16, jnp.float32
    wide = (2, HALF, 3 * GCOLS)
    back, grad, wr, ua, sc, gs, vec = results
    return pl.pallas_call(
        finish_kernel,
        out_shape=[
            shape((TOK_DEV, D), low), shape((TOK_DEV, D), low), shape(wide, f32), shape(wide, f32),
            shape((2, D, D), f32), shape((2, D, D), f32),
            shape((96, NBLK), f32), shape((96, NBLK), f32), shape((96, NBLK), f32),
        ],
        in_specs=[smem, vmem] + [any_spec] * 4 + [vmem, any_spec, vmem] + [any_spec] * 3 + [vmem] * 3,
        out_specs=[any_spec] * 6 + [vmem] * 3,
        scratch_shapes=[
            pltpu.VMEM((2, 8, 2, HALF, D), low),
            pltpu.VMEM((2, D, D), f32),
            pltpu.VMEM((2, D, D), f32),
            pltpu.VMEM((2, 2, 16, HALF, JCOLS), low),
            pltpu.VMEM((2, 2, 12, HALF, JCOLS), low),
            pltpu.VMEM(wide, f32),
            pltpu.VMEM(wide, f32),
            pltpu.VMEM(wide, f32),
            pltpu.VMEM((2, 8, 64, D), low),
            pltpu.VMEM((2, TOK_DEV, D), low),
            dma((10,)), dma((8,)),
        ],
        compiler_params=pltpu.CompilerParams(vmem_limit_bytes=56 * MIB),
        name="finish_all",
    )(
        owner, outrow, back, grad, wr, ua, sc, gs, vec, stat_l, stat_r, wf.reshape(wide), vecs, mom1, mom2
    )


def masks(seq_lengths, random_blocks):
    seq_id, position, in_use, seq_blocks = layout(seq_lengths[0])
    picks = random_blocks % jnp.maximum(seq_blocks.reshape(TOK_DEV // BLK, BLK)[:, 0], 1)[:, None, None]
    rows = slice(None, None, BLK)
    row_seq, row_block = seq_id[rows], position[rows] // BLK
    key_block = position // BLK
    same = (row_seq[:, None] == seq_id[None, :]) & in_use[None, :]
    near = (
        (row_block[:, None] < NGLOB)
        | (key_block[None, :] < NGLOB)
        | (jnp.abs(row_block[:, None] - key_block[None, :]) <= 1)
    )
    chosen = jnp.any(picks[:, :, :, None] == key_block[None, None, None, :], axis=2)
    keep = same[:, None, :] & (near[:, None, :] | chosen)
    bias = jnp.where(jnp.transpose(keep, (1, 0, 2)), 0.0, MASKED_SCORE).astype(jnp.float32)
    use = jnp.broadcast_to(in_use.astype(jnp.float32)[:, None], (TOK_DEV, 128))
    use_row = in_use.astype(jnp.float32)[None, :]
    return bias, use, use_row


def fast_body(
    tokens,
    cotangent,
    place,
    seq_lengths,
    random_blocks,
    owner_slot,
    flat_weights,
    vectors,
    moment_first,
    moment_second,
    stat_left,
    stat_right,
    root_left,
    root_right,
):
    peers = lax.axis_size("fsdp")
    share_rows = TOK_DEV // peers
    me = lax.axis_index("fsdp")
    outrow = (place // TOK_DEV) * share_rows + place % TOK_DEV - me * share_rows
    vec_pad = jnp.pad(vectors.astype(jnp.bfloat16), ((0, 0), (0, 128 - NBLK)))
    bias, use, use_row = masks(seq_lengths, random_blocks)
    slots = jnp.arange(2 * peers, dtype=jnp.int32)
    hits = slots[:, None] == owner_slot[None, :]
    block_of = jnp.sum(jnp.where(hits, jnp.arange(NBLK, dtype=jnp.int32)[None, :] + 1, 0), axis=1) - 1
    w0, w1, w2, vt, *saved = forward_all(
        outrow[None, :], tokens, cotangent, flat_weights, vec_pad, bias, use, use_row, root_left, root_right
    )
    saved[-2] = saved[-2].reshape(peers, share_rows, D)
    results = backward_all(block_of.astype(jnp.int32), vt, use, use_row, [w0, w1, w2] + saved)
    layer_out, input_grad, weight_grads, new_weights, *others = finish_all(
        owner_slot, outrow[:, None], results, stat_left, stat_right, flat_weights, vectors, moment_first,
        moment_second,
    )
    return (
        layer_out,
        input_grad,
        weight_grads.reshape(flat_weights.shape),
        new_weights.reshape(flat_weights.shape),
        *others,
    )


def plain_body(
    tokens,
    cotangent,
    place,
    seq_lengths,
    random_blocks,
    owner_slot,
    flat_weights,
    vectors,
    moment_first,
    moment_second,
    stat_left,
    stat_right,
    root_left,
    root_right,
):
    peers = lax.axis_size("fsdp")
    share_rows = TOK_DEV // peers
    order_ids = jnp.argsort(place)
    outgoing = (
        tokens[order_ids].reshape(peers, share_rows, D),
        cotangent[order_ids].reshape(peers, share_rows, D),
    )
    arrived = (
        lax.all_to_all(outgoing[0], "fsdp", split_axis=0, concat_axis=0, tiled=True),
        lax.all_to_all(outgoing[1], "fsdp", split_axis=0, concat_axis=0, tiled=True),
    )
    inputs = arrived[0].reshape(TOK_DEV, D)
    upstream = arrived[1].reshape(TOK_DEV, D).astype(jnp.float32)
    weight_copy, vector_copy = (
        lax.all_gather(flat_weights.astype(jnp.bfloat16), "fsdp", axis=0, tiled=True),
        lax.all_gather(vectors.astype(jnp.bfloat16), "fsdp", axis=0, tiled=True),
    )
    vecs_full = vector_copy.astype(jnp.float32)
    b_up = jnp.transpose(vecs_full[:, 8:]).reshape(FF)
    seq_id, position, in_use, seq_blocks = layout(seq_lengths[0])
    picks = random_keys(random_blocks, seq_blocks)
    slot_ids = jnp.arange(TOK_DEV, dtype=jnp.int32)
    real_rows = in_use.astype(jnp.float32)[:, None]
    bias_qkv = jnp.concatenate([vecs_full[:, 0], jnp.zeros((D,), jnp.float32), vecs_full[:, 1]])
    qkv_low = (
        jnp.dot(inputs, weight_copy[:, : 3 * D], preferred_element_type=jnp.float32) + bias_qkv
    ).astype(jnp.bfloat16)
    qkv_heads = qkv_low.reshape(TOK_DEV, 3, H, HD)
    queries = qkv_heads[:, 0]
    key_heads = qkv_heads[:, 1]
    value_heads = qkv_heads[:, 2]
    block_rows = min(512, TOK_DEV)
    block_count = TOK_DEV // block_rows
    score_scale = HD ** (-0.5)

    def split_blocks(array):
        return array.reshape((block_count, block_rows) + array.shape[1:])

    block_inputs = (
        split_blocks(queries),
        split_blocks(seq_id),
        split_blocks(position),
        split_blocks(in_use),
        split_blocks(picks),
        split_blocks(slot_ids),
    )

    def scores_of(query_block, q_seq, q_pos, q_use, q_pick, q_slot):
        raw_scores = (
            jnp.einsum("qhd,khd->hqk", query_block, key_heads, preferred_element_type=jnp.float32)
            * score_scale
        )
        keep_mask = allowed(q_seq, q_pos, q_use, q_pick, q_slot, seq_id, position, in_use, slot_ids)
        return jnp.where(keep_mask, raw_scores, MASKED_SCORE)

    def forward_block(pieces):
        scores = scores_of(pieces[0], pieces[1], pieces[2], pieces[3], pieces[4], pieces[5])
        row_max = jnp.max(scores, axis=-1, keepdims=True)
        expo = jnp.exp(scores - row_max)
        row_total = jnp.sum(expo, axis=-1, keepdims=True)
        probs_low = (expo / row_total).astype(jnp.bfloat16)
        mixed_block = jnp.einsum(
            "hqk,khd->qhd", probs_low, value_heads, preferred_element_type=jnp.float32
        )
        return (mixed_block.reshape(block_rows, D), (row_max + jnp.log(row_total))[:, :, 0])

    attended, log_totals = lax.map(forward_block, block_inputs)
    mixed = attended.reshape(TOK_DEV, D).astype(jnp.bfloat16)
    branch = (
        jnp.dot(mixed, weight_copy[:, 3 * D : 4 * D], preferred_element_type=jnp.float32)
        + vecs_full[:, 2]
    )
    hidden_one = inputs.astype(jnp.float32) + branch
    x_one, norm_one_back = jax.vjp(layer_norm, hidden_one, vecs_full[:, 4], vecs_full[:, 5])
    x_one_low = x_one.astype(jnp.bfloat16)
    pre_act = (
        jnp.dot(x_one_low, weight_copy[:, 4 * D : 4 * D + FF], preferred_element_type=jnp.float32)
        + b_up
    )
    act, gelu_back = jax.vjp(gelu_tanh, pre_act)
    act_low = act.astype(jnp.bfloat16)
    ffn = contract_cols(act_low, weight_copy[:, 4 * D + FF :]) + vecs_full[:, 3]
    hidden_two = x_one + ffn
    result, norm_two_back = jax.vjp(layer_norm, hidden_two, vecs_full[:, 6], vecs_full[:, 7])
    layer_rows = (result * real_rows).astype(jnp.bfloat16)
    weight_copy = lax.all_gather(flat_weights.astype(jnp.bfloat16), "fsdp", axis=0, tiled=True)
    d_result = upstream * real_rows
    d_two, d_gain_two, d_shift_two = norm_two_back(d_result)
    d_ffn = d_two.astype(jnp.bfloat16)
    d_act = jnp.dot(d_ffn, weight_copy[:, 4 * D + FF :], preferred_element_type=jnp.float32)
    (d_pre,) = gelu_back(d_act)
    d_pre_low = d_pre.astype(jnp.bfloat16)
    grad_down = contract_rows(d_ffn, act_low)
    grad_up = contract_rows(x_one_low, d_pre_low)
    d_x_one = d_two + contract_cols(d_pre_low, weight_copy[:, 4 * D : 4 * D + FF])
    d_one, d_gain_one, d_shift_one = norm_one_back(d_x_one)
    up_sums = jnp.transpose(jnp.sum(d_pre_low.astype(jnp.float32), axis=0).reshape(FF // D, D))
    ffn_vec = jnp.concatenate(
        [
            jnp.sum(d_ffn.astype(jnp.float32), axis=0)[:, None],
            d_gain_one[:, None],
            d_shift_one[:, None],
            d_gain_two[:, None],
            d_shift_two[:, None],
            up_sums,
        ],
        axis=1,
    )
    ffn_mats = jnp.concatenate([grad_up, grad_down], axis=1)
    d_branch = d_one.astype(jnp.bfloat16)
    grad_out = contract_rows(mixed, d_branch)
    d_mixed = (
        contract_cols(d_branch, weight_copy[:, 3 * D : 4 * D])
        .astype(jnp.bfloat16)
        .reshape(TOK_DEV, H, HD)
    )

    def backward_block(carry, pieces):
        key_grad, value_grad = carry
        query_block = pieces[0]
        log_total = pieces[6]
        out_grad = pieces[7]
        scores = scores_of(pieces[0], pieces[1], pieces[2], pieces[3], pieces[4], pieces[5])
        probs = jnp.exp(scores - log_total[:, :, None])
        probs_low = probs.astype(jnp.bfloat16)
        value_grad = value_grad + jnp.einsum(
            "hqk,qhd->khd", probs_low, out_grad, preferred_element_type=jnp.float32
        )
        prob_grad = jnp.einsum(
            "qhd,khd->hqk", out_grad, value_heads, preferred_element_type=jnp.float32
        )
        score_grad = (
            probs * (prob_grad - jnp.sum(probs * prob_grad, axis=-1, keepdims=True))
        ).astype(jnp.bfloat16)
        query_grad = (
            jnp.einsum("hqk,khd->qhd", score_grad, key_heads, preferred_element_type=jnp.float32)
            * score_scale
        )
        key_grad = (
            key_grad
            + jnp.einsum(
                "hqk,qhd->khd", score_grad, query_block, preferred_element_type=jnp.float32
            )
            * score_scale
        )
        return ((key_grad, value_grad), query_grad)

    zero_heads = jnp.zeros((TOK_DEV, H, HD), jnp.float32)
    (key_grad, value_grad), query_grad = lax.scan(
        backward_block, (zero_heads, zero_heads), block_inputs + (log_totals, split_blocks(d_mixed))
    )
    d_qkv = jnp.concatenate(
        [
            query_grad.reshape(TOK_DEV, D),
            key_grad.reshape(TOK_DEV, D),
            value_grad.reshape(TOK_DEV, D),
        ],
        axis=1,
    ).astype(jnp.bfloat16)
    grad_qkv = contract_rows(inputs, d_qkv)
    d_inputs = d_one + contract_cols(d_qkv, weight_copy[:, : 3 * D])
    qkv_sums = jnp.sum(d_qkv.astype(jnp.float32), axis=0)
    attn_vec = jnp.stack(
        [qkv_sums[:D], qkv_sums[2 * D :], jnp.sum(d_branch.astype(jnp.float32), axis=0)], axis=1
    )
    attn_mats = jnp.concatenate([grad_qkv, grad_out], axis=1)
    mat_shard, vec_shard = (
        lax.psum_scatter(
            jnp.concatenate([attn_mats, ffn_mats], axis=1), "fsdp", scatter_dimension=0, tiled=True
        ),
        lax.psum_scatter(
            jnp.concatenate([attn_vec, ffn_vec], axis=1), "fsdp", scatter_dimension=0, tiled=True
        ),
    )
    mat_part = lax.psum_scatter(
        mat_shard.astype(jnp.bfloat16), "rep", scatter_dimension=1, tiled=True
    ).astype(jnp.float32)
    vec_shard = lax.psum(vec_shard, "rep")
    mat_shard = lax.all_gather(mat_part.astype(jnp.bfloat16), "rep", axis=1, tiled=True).astype(
        mat_part.dtype
    )
    grad_rows = d_inputs.astype(jnp.bfloat16)
    back_pair = (
        lax.all_to_all(
            layer_rows.reshape(peers, share_rows, D),
            "fsdp",
            split_axis=0,
            concat_axis=0,
            tiled=True,
        ),
        lax.all_to_all(
            grad_rows.reshape(peers, share_rows, D), "fsdp", split_axis=0, concat_axis=0, tiled=True
        ),
    )
    layer_out = (
        jnp.zeros((TOK_DEV, D), jnp.bfloat16).at[order_ids].set(back_pair[0].reshape(TOK_DEV, D))
    )
    input_grad = (
        jnp.zeros((TOK_DEV, D), jnp.bfloat16).at[order_ids].set(back_pair[1].reshape(TOK_DEV, D))
    )
    slot_count = stat_left.shape[0]
    rows_dev = flat_weights.shape[0]
    targets = (
        jnp.arange(slot_count, dtype=jnp.int32)[:, None, None]
        + slot_count * jnp.arange(peers, dtype=jnp.int32)[None, :, None]
    )
    select = (owner_slot[None, None, :] == targets).astype(jnp.float32)
    grad_pieces = mat_shard.reshape(rows_dev, NBLK, D)
    outbound = jnp.einsum("snb,rbc->snrc", select, grad_pieces, precision=PRECISE)
    inbound = lax.all_to_all(
        outbound.astype(jnp.bfloat16), "fsdp", split_axis=1, concat_axis=1, tiled=True
    ).astype(outbound.dtype)
    grad_blocks = inbound.reshape(slot_count, D, D)
    new_left = STAT_DECAY * stat_left + (1.0 - STAT_DECAY) * jnp.einsum(
        "sij,skj->sik", grad_blocks, grad_blocks, precision=PRECISE
    )
    new_right = STAT_DECAY * stat_right + (1.0 - STAT_DECAY) * jnp.einsum(
        "sji,sjk->sik", grad_blocks, grad_blocks, precision=PRECISE
    )
    left_applied = jnp.einsum("sij,sjk->sik", root_left, grad_blocks, precision=PRECISE)
    direction = jnp.einsum("sij,sjk->sik", left_applied, root_right, precision=PRECISE)
    update = direction * lax.rsqrt(
        jnp.mean(direction * direction, axis=(1, 2), keepdims=True) + RMS_EPS
    )
    returned = lax.all_to_all(
        update.reshape(slot_count, peers, rows_dev, D).astype(jnp.bfloat16),
        "fsdp",
        split_axis=1,
        concat_axis=1,
        tiled=True,
    ).astype(jnp.float32)
    step_matrix = jnp.einsum("snb,snrc->rbc", select, returned, precision=PRECISE).reshape(
        rows_dev, NBLK * D
    )
    new_weights = flat_weights - LR_MATRIX * step_matrix
    first_bias = 1.0 - BETA_ONE**STEP
    second_bias = 1.0 - BETA_TWO**STEP
    new_first = BETA_ONE * moment_first + (1.0 - BETA_ONE) * vec_shard
    new_second = BETA_TWO * moment_second + (1.0 - BETA_TWO) * vec_shard * vec_shard
    first_fixed = new_first / first_bias
    second_fixed = new_second / second_bias
    new_vectors = vectors - LR_VECTOR * first_fixed / (jnp.sqrt(second_fixed) + ADAM_EPS)
    return (
        layer_out,
        input_grad,
        mat_shard,
        new_weights,
        new_left,
        new_right,
        new_first,
        new_second,
        new_vectors,
    )


def solution(mesh):
    in_specs = (
        P(("rep", "fsdp"), None),
        P(("rep", "fsdp"), None),
        P(("rep", "fsdp")),
        P(("rep", "fsdp"), None),
        P(("rep", "fsdp"), None, None),
        P(),
        P("fsdp", None),
        P("fsdp", None),
        P("fsdp", None),
        P("fsdp", None),
        P("fsdp", None, None),
        P("fsdp", None, None),
        P("fsdp", None, None),
        P("fsdp", None, None),
    )
    out_specs = (
        P(("rep", "fsdp"), None),
        P(("rep", "fsdp"), None),
        P("fsdp", None),
        P("fsdp", None),
        P("fsdp", None, None),
        P("fsdp", None, None),
        P("fsdp", None),
        P("fsdp", None),
        P("fsdp", None),
    )
    shaped = mesh.shape["fsdp"] == 8 and mesh.shape["rep"] == 4
    body = fast_body if shaped else plain_body
    return jax.shard_map(body, mesh=mesh, in_specs=in_specs, out_specs=out_specs, check_vma=False)
```

```python
import functools

import jax
import jax.numpy as jnp
from jax import lax
from jax.experimental import pallas as pl
from jax.experimental.pallas import tpu as pltpu
from jax.sharding import PartitionSpec as P

D = 768
H = 12
HD = 64
FF = 3072
BLK = 64
NGLOB = 2
NRAND = 3
STEP = 10
SEQ_DEV = 4
TOK_DEV = 512
NBLK = 12


NORM_EPS = 1e-12
MASKED_SCORE = -1e30
STAT_DECAY = 0.5
LR_MATRIX = 0.02
LR_VECTOR = 0.1
BETA_ONE = 0.9
BETA_TWO = 0.999
ADAM_EPS = 1e-08
RMS_EPS = 1e-12
PRECISE = lax.Precision.HIGHEST


def layout(lengths):
    blocks = (lengths + (BLK - 1)) // BLK
    block_ends = jnp.cumsum(blocks)
    starts = (block_ends - blocks) * BLK
    slot_ids = jnp.arange(TOK_DEV, dtype=jnp.int32)
    seq_id = jnp.sum((slot_ids // BLK)[:, None] >= block_ends[None, :], axis=1)
    member = seq_id[:, None] == jnp.arange(SEQ_DEV, dtype=jnp.int32)[None, :]
    seq_start = jnp.sum(jnp.where(member, starts[None, :], 0), axis=1)
    length = jnp.sum(jnp.where(member, lengths[None, :], 0), axis=1)
    seq_blocks = jnp.sum(jnp.where(member, blocks[None, :], 0), axis=1)
    position = slot_ids - seq_start
    in_use = position < length
    return (seq_id, position, in_use, seq_blocks)


def random_keys(raw_picks, seq_blocks):
    per_block = seq_blocks.reshape(TOK_DEV // BLK, BLK)[:, 0]
    picked = raw_picks % jnp.maximum(per_block, 1)[:, None, None]
    return jnp.repeat(picked, BLK, axis=0)


def allowed(q_seq, q_pos, q_use, q_pick, q_slot, k_seq, k_pos, k_use, k_slot):
    q_block = q_pos // BLK
    k_block = k_pos // BLK
    same_seq = (q_seq[:, None] == k_seq[None, :]) & q_use[:, None] & k_use[None, :]
    nearby = (
        (q_block[:, None] < NGLOB)
        | (k_block[None, :] < NGLOB)
        | (jnp.abs(q_block[:, None] - k_block[None, :]) <= 1)
    )
    chosen = jnp.zeros((H, q_seq.shape[0], k_seq.shape[0]), dtype=jnp.bool_)
    for number in range(NRAND):
        chosen = chosen | (
            k_block[None, None, :] == jnp.transpose(q_pick[:, :, number])[:, :, None]
        )
    alone = jnp.logical_not(q_use)[:, None] & (q_slot[:, None] == k_slot[None, :])
    return (same_seq & nearby)[None] | same_seq[None] & chosen | alone[None]


def layer_norm(hidden, gain, shift):
    center = hidden - jnp.mean(hidden, axis=-1, keepdims=True)
    spread = jnp.mean(center * center, axis=-1, keepdims=True)
    return center * lax.rsqrt(spread + NORM_EPS) * gain + shift


def gelu_tanh(pre_act):
    return jax.nn.gelu(pre_act, approximate=True)


def contract_rows(left, right):
    return lax.dot_general(
        left, right, (((0,), (0,)), ((), ())), preferred_element_type=jnp.float32
    )


def contract_cols(left, right):
    return lax.dot_general(
        left, right, (((1,), (1,)), ((), ())), preferred_element_type=jnp.float32
    )


MESH = pl.DeviceIdType.MESH
HALF = 48
GCOLS = 3072
JCOLS = 384
MIB = 2**20


class Here:
    def __init__(self, corner=False):
        r, f = lax.axis_index("rep"), lax.axis_index("fsdp")
        self.r, self.f = r, f
        self.x, self.y = lax.rem(r, 2), lax.div(r, 2)
        self.z, self.c = lax.div(f, 2), lax.rem(f, 2)
        self.to_x = (r + 1 - 2 * self.x, f)
        self.to_y = (r + 2 - 4 * self.y, f)
        self.to_d = (3 - r, f)
        self.corner = corner
        self.to_core = (r, f + 1 - 2 * self.c)

    def z_plus(self, step):
        return lax.rem(self.z + step, 4)

    def along(self, step):
        return (self.r, 2 * self.z_plus(step) + self.c)

    def peer(self, step):
        return lax.rem(self.f + step, 8)

    def greet(self):
        barrier = pltpu.get_barrier_semaphore()
        friends = [self.to_x, self.to_y] + [self.to_d] * self.corner
        friends += [(self.r, self.peer(s)) for s in range(1, 8)]
        for friend in friends:
            pl.semaphore_signal(barrier, inc=1, device_id=friend, device_id_type=MESH)
        return lambda: pl.semaphore_wait(barrier, len(friends))


def send(src, dst, send_sem, recv_sem, device):
    copy = pltpu.make_async_remote_copy(
        src_ref=src,
        dst_ref=dst,
        send_sem=send_sem,
        recv_sem=recv_sem,
        device_id=device,
        device_id_type=MESH,
    )
    copy.start()
    return copy


def local(src, dst, sem):
    copy = pltpu.make_async_copy(src, dst, sem)
    copy.start()
    return copy


def cols(start, width):
    return pl.ds(pl.multiple_of(start, 128), width)


def forward_kernel(
    lengths, place, tok, cot, wf, vec, raw, root_l, root_r,
    o0, o1, o2, o_vt, o_x, o_cot, o_qkv, o_p, o_mix, o_n1, o_r1, o_u, o_f, o_dg, o_n2, o_r2, o_y, o_root, o_use, o_hot,
    w0, w1, w2, tok_in, cot_in, vec_in, tok_s, cot_s,
    hot, use, use_row, wide_w, vec_s, vt, qkv, P, mix, n1, r1, x1, u, fa, dg, n2, r2, yo, xT, mT, uT, feat, stg, rb,
    wl, zs, zr, xs, xr, ys, yr, ds, dr, cs, cr, ls, ts, tr, os, ks,
):
    low, f32 = jnp.bfloat16, jnp.float32
    here = Here()
    wait_all = here.greet()
    x, y, z, c, f = here.x, here.y, here.z, here.c, here.f
    whole = [w0, w1, w2]
    whole_out = [o0, o1, o2]
    wide = GCOLS // 2
    sent = []
    outs = []
    count = [0]

    def keep(src, dst):
        outs.append(local(src, dst, os.at[count[0]]))
        count[0] += 1

    fetched = [
        local(wf.at[:, :, g * GCOLS : (g + 1) * GCOLS], wide_w.at[:, :, g * GCOLS : (g + 1) * GCOLS], ks.at[2 + g])
        for g in range(3)
    ]

    def narrow(g):
        fetched[g].wait()

        def one(i, _):
            h, part = lax.div(i, 4), lax.rem(i, 4)
            at = cols(g * GCOLS + part * D, D)
            wl[h, :, at] = wide_w[h, :, at].astype(low)
            return 0

        lax.fori_loop(0, 8, one, 0)
        return local(wl.at[:, :, g * GCOLS : (g + 1) * GCOLS], whole[g].at[z, c], ls.at[g])

    inner = lax.rem(lax.div(z + 1, 2), 2)
    upper = lax.div(z, 2)
    end = 3 * upper

    def source(step):
        near = step - inner if step == 1 else step
        return near + upper * (3 - 2 * near)

    def line(zz):
        return (here.r, 2 * zz + c)

    def own_part(g):
        return wl.at[x, :, cols(g * GCOLS + y * wide, wide)]

    def landed(g, src):
        return whole[g].at[src, c, x, :, cols(y * wide, wide)]

    def z_own(g, second):
        first_to = 1 + upper + inner * (1 - 2 * upper)
        second_to = inner * end + (1 - inner) * (2 - upper)
        return pltpu.make_async_remote_copy(
            src_ref=own_part(g), dst_ref=landed(g, z), send_sem=zs.at[g, int(second)], recv_sem=zr.at[g, z],
            device_id=line(second_to if second else first_to), device_id_type=MESH,
        )

    def z_pass(g, step):
        part = landed(g, source(step))
        return pltpu.make_async_remote_copy(
            src_ref=part, dst_ref=part, send_sem=zs.at[g, 1 + step], recv_sem=zr.at[g, source(step)],
            device_id=line(end), device_id_type=MESH,
        )

    def z_send(g):
        z_own(g, False).start()
        z_own(g, True).start()

    def z_finish(g):
        z_own(g, False).wait_send()
        z_own(g, True).wait_send()

        @pl.when(inner == 1)
        def _():
            for step in (2, 3):
                z_pass(g, step).wait_send()

    def rows_out(table, landing, number):
        out = []
        for step in range(1, 8):
            to = here.peer(step)
            src = table if number == 2 else table.at[to]
            out.append(
                send(src, landing.at[f], ts.at[number, step - 1], tr.at[number, step - 1], (here.r, to))
            )
        sent.extend(out)
        return out

    planes = {0: {}, 1: {}, 2: {}}

    def plane(g, step):
        moving = z_pass(g, step)
        moving.wait_recv()

        if step > 1:

            @pl.when(inner == 1)
            def _():
                moving.start()

        src = source(step)
        part = landed(g, src)
        xc = send(part, part, xs.at[g, src], xr.at[g, src], here.to_x)
        yc = send(part, part, ys.at[g, src], yr.at[g, src], here.to_y)
        planes[g][step] = (xc, yc)
        sent.extend([xc, yc])
        if step == 3:
            core(g, 0, x, y)

    cores = {0: [], 1: [], 2: []}

    def core(g, number, h, j):
        part = whole[g].at[:, c, h, :, cols(j * wide, wide)]
        copy = send(part, part, cs.at[g, number], cr.at[g, number], here.to_core)
        sent.append(copy)
        cores[g].append(copy)

    turns = {0: [], 1: [], 2: []}

    def turn(g, step):
        src = source(step)
        xc, yc = planes[g][step]
        xc.wait_recv()
        part = whole[g].at[src, c, 1 - x, :, cols(y * wide, wide // 2)]
        one = send(part, part, ds.at[g, 0, src], dr.at[g, 0, src], here.to_y)
        yc.wait_recv()
        part = whole[g].at[src, c, x, :, cols((1 - y) * wide + wide // 2, wide // 2)]
        two = send(part, part, ds.at[g, 1, src], dr.at[g, 1, src], here.to_x)
        sent.extend([one, two])
        turns[g].extend([one, two])
        if step == 3:
            core(g, 1, 1 - x, y)
            core(g, 2, x, 1 - y)

    def last(g):
        for copy in turns[g]:
            copy.wait_recv()
        core(g, 3, 1 - x, 1 - y)

    def ready(g):
        for copy in cores[g]:
            copy.wait_recv()
        keep(whole[g], whole_out[g])

    def square(ref, at):
        return ref[:, :, :, :, at].reshape(D, at.size)

    def order(source, target):
        target[...] = jnp.dot(hot[...], source[...], preferred_element_type=f32).astype(low).reshape(8, 64, D)

    def layout_rows():
        sizes = [lengths[0, s] for s in range(SEQ_DEV)]
        blocks = [lax.div(size + (BLK - 1), BLK) for size in sizes]
        ends = [blocks[0]]
        for s in range(1, SEQ_DEV):
            ends.append(ends[-1] + blocks[s])

        def where_is(number):
            seq = jnp.zeros_like(number)
            for s in range(SEQ_DEV):
                seq = seq + (number >= ends[s]).astype(jnp.int32)
            first, size, count = jnp.zeros_like(number), jnp.zeros_like(number), jnp.zeros_like(number)
            for s in range(SEQ_DEV):
                first = jnp.where(seq == s, ends[s] - blocks[s], first)
                size = jnp.where(seq == s, sizes[s], size)
                count = jnp.where(seq == s, blocks[s], count)
            return seq, number - first, size, count

        slot = lax.broadcasted_iota(jnp.int32, (8, TOK_DEV), 1)
        key_seq, key_block, size, _ = where_is(lax.div(slot, BLK))
        used = key_block * BLK + lax.rem(slot, BLK) < size
        used_f = used.astype(f32)
        use_row[...] = used_f
        use[...] = jnp.transpose(jnp.concatenate([used_f] * 16, axis=0))
        row_seq, row_block, _, count = where_is(lax.broadcasted_iota(jnp.int32, (8, 128), 0))
        row_seq, row_block, count = row_seq[:, 0:1], row_block[:, 0:1], jnp.maximum(count[:, 0:1], 1)
        same = (row_seq == key_seq) & used
        near = (row_block < NGLOB) | (key_block < NGLOB) | (jnp.abs(row_block - key_block) <= 1)
        picks = []
        for number in range(NRAND):
            pick = raw[number]
            for _ in range(7):
                pick = jnp.where(pick >= count, pick - count, pick)
            picks.append(pick)
        gap = jnp.zeros((BLK - 8, TOK_DEV), f32)
        for head in range(H):
            keep_it = near
            for pick in picks:
                keep_it = keep_it | (key_block == pick[:, head : head + 1])
            rows = jnp.where(same & keep_it, 0.0, MASKED_SCORE)
            feat[head] = jnp.transpose(jnp.concatenate([rows, gap, rows, gap], axis=0)).astype(low)

    def places():
        spot = (
            lax.div(place[...], TOK_DEV) * 64 + lax.rem(place[...], TOK_DEV) - f * 64
        )
        hot[...] = (
            (lax.broadcasted_iota(jnp.int32, (TOK_DEV, TOK_DEV), 0) == spot).astype(f32).astype(low)
        )
        return spot

    def places_back(spot):
        tall = jnp.transpose(jnp.broadcast_to(spot.astype(f32), (128, TOK_DEV)))
        lane = lax.broadcasted_iota(jnp.int32, (TOK_DEV, TOK_DEV), 1).astype(f32)
        hot[...] = (tall[:, 0:1] == lane).astype(f32).astype(low)
        keep(hot, o_hot)

    def project():
        for part in range(3):

            def one(i, _, part=part):
                at = cols(i * 256, 256)
                to = cols(part * D + i * 256, 256)
                acc = jnp.dot(tok_in[...].reshape(TOK_DEV, D), square(w0, to), preferred_element_type=f32)
                if part == 0:
                    acc = (acc + vt[0:1, at]) * (HD ** (-0.5))
                if part == 2:
                    acc = acc + vt[1:2, at]
                qkv[:, to] = acc.astype(low)
                return 0

            lax.fori_loop(0, 3, one, 0)

    root_load = []

    def root_fetch(number):
        ref = (root_l, root_r)[number // 2]
        root_load.append(local(ref.at[number % 2], stg, ks.at[0]))

    def roots(number):
        root_load[number].wait()
        if number:
            root_out[number - 1].wait()

        def one(i, _):
            at = pl.ds(pl.multiple_of(i * 96, 96), 96)
            rb[lax.div(i, 2), lax.rem(i, 2)] = stg[at, :].astype(low).reshape(2, HALF, D)
            return 0

        lax.fori_loop(0, 8, one, 0)
        root_out.append(local(rb, o_root.at[number], ks.at[1]))
        if number < 3:
            root_fetch(number + 1)
        else:
            root_out[3].wait()

    root_out = []
    root_fetch(0)

    def attend(start, stop):
        def pair(i, _):
            at = cols(i * 128, 128)
            q2, k2 = qkv[:, at], qkv[:, cols(D + i * 128, 128)]
            v2 = qkv[:, cols(2 * D + i * 128, 128)]
            lane = lax.broadcasted_iota(jnp.int32, (TOK_DEV, 128), 1)
            row = lax.broadcasted_iota(jnp.int32, (TOK_DEV, 128), 0)
            spot = (lax.rem(lane, BLK) == lax.div(row, BLK)).astype(f32).astype(low)
            vT = jnp.transpose(v2)
            parts = []
            for half in range(2):
                mine = (lane < HD) if half == 0 else (lane >= HD)
                qm = jnp.where(mine, q2, spot)
                km = jnp.where(mine, k2, feat[2 * i + half])
                s = lax.dot_general(km, qm, (((1,), (1,)), ((), ())), preferred_element_type=f32)
                e = jnp.exp(s - jnp.max(s, axis=0, keepdims=True))
                p = (e * (use_row[0:1, :] / jnp.sum(e, axis=0, keepdims=True))).astype(low)
                P[2 * i + half] = p
                parts.append(jnp.dot(vT[half * HD : (half + 1) * HD], p, preferred_element_type=f32))
            total = jnp.where(use_row[0:1, :] > 0, jnp.concatenate(parts, axis=0), vT.astype(f32)).astype(low)
            mT[cols(i * 128, 128), :] = total
            mix[:, at] = jnp.transpose(total)
            return 0

        if stop - start == 1:
            pair(start, 0)
        else:
            lax.fori_loop(start, stop, pair, 0)

    def flip(source, target):
        def one(i, _):
            at = cols(i * 128, 128)
            target[at, :] = jnp.transpose(source(at))
            return 0

        lax.fori_loop(0, 6, one, 0)

    def join():
        def one(i, _):
            at = cols(i * 256, 256)
            acc = jnp.dot(mix[...], square(w0, cols(3 * D + i * 256, 256)), preferred_element_type=f32)
            x1[:, at] = tok_in[:, :, at].reshape(TOK_DEV, 256).astype(f32) + (acc + vt[2:3, at])
            return 0

        lax.fori_loop(0, 3, one, 0)

    def norm(ref, i):
        at = pl.ds(pl.multiple_of(i * 64, 64), 64)
        h = ref[at, :]
        center = h - jnp.mean(h, axis=1, keepdims=True)
        r = lax.rsqrt(jnp.mean(center * center, axis=1, keepdims=True) + NORM_EPS)
        return at, center * r, r

    def norm_one():
        def one(i, _):
            at, n, r = norm(x1, i)
            n1[at, :] = n
            r1[at, :] = jnp.broadcast_to(r, (64, 128))
            out = n * vt[4:5, :] + vt[5:6, :]
            u[at, :] = out.astype(low)
            x1[at, :] = out
            return 0

        lax.fori_loop(0, 8, one, 0)

    def lift(begin):
        for row in range(begin, begin + 2):

            def one(i, _, row=row):
                at = cols(i * 256, 256)
                to = cols(row * D + i * 256, 256)
                pre = jnp.dot(u[...], square(w1, to), preferred_element_type=f32) + vt[8 + row : 9 + row, at]
                sq = pre * pre
                t = jnp.tanh(0.7978845608028654 * pre * (1.0 + 0.044715 * sq))
                half = 0.5 * (1.0 + t)
                fa[:, to] = (pre * half).astype(low)
                slope = 0.7978845608028654 * (1.0 + 0.134145 * sq)
                dg[:, to] = (half + 0.5 * pre * (1.0 - t * t) * slope).astype(low)
                return 0

            lax.fori_loop(0, 3, one, 0)

    def drop():
        def one(i, _):
            at = cols(i * 512, 512)
            acc = lax.dot_general(
                fa[:, at], square(w2, at), (((1,), (1,)), ((), ())), preferred_element_type=f32
            )
            x1[...] += acc
            return 0

        lax.fori_loop(0, 6, one, 0)

    def norm_two():
        def one(i, _):
            at = pl.ds(pl.multiple_of(i * 64, 64), 64)
            x1[at, :] = x1[at, :] + vt[3:4, :]
            at, n, r = norm(x1, i)
            n2[at, :] = n
            r2[at, :] = jnp.broadcast_to(r, (64, 128))
            out = (n * vt[6:7, :] + vt[7:8, :]) * use[at, 0:1]
            yo[at, :] = out.astype(low)
            return 0

        lax.fori_loop(0, 8, one, 0)

    stays = [narrow(0)]
    wait_all()
    z_send(0)
    vec_s[...] = jnp.zeros_like(vec_s)
    vec_s[:NBLK, :96] = vec[...].astype(low)
    small = rows_out(vec_s, vec_in, 2)
    own = [local(vec_s, vec_in.at[f], ls.at[5])]
    spot = places()
    order(tok, tok_s)
    own.append(local(tok_s.at[f], tok_in.at[f], ls.at[3]))
    plane(0, 1)
    stays.append(narrow(1))
    plane(0, 2)
    order(cot, cot_s)
    own.append(local(cot_s.at[f], cot_in.at[f], ls.at[4]))
    stays.append(narrow(2))
    stays[0].wait()
    plane(0, 3)
    z_send(1)
    t0 = rows_out(tok_s, tok_in, 0)
    for copy in stays[1:] + own:
        copy.wait()
    layout_rows()
    keep(use, o_use)
    turn(0, 1)
    for copy in small:
        copy.wait_recv()
    for n in range(8):
        vt[:, n * 96 : (n + 1) * 96] = vec_in[n, :, :96].astype(f32)
    keep(vt, o_vt)
    places_back(spot)
    turn(0, 2)
    roots(0)
    turn(0, 3)
    plane(1, 1)
    roots(1)
    last(0)
    roots(2)
    plane(1, 2)
    ready(0)
    plane(1, 3)
    z_send(2)
    for copy in t0:
        copy.wait_recv()
    project()
    keep(qkv, o_qkv)
    turn(1, 1)
    attend(0, 1)
    turn(1, 2)
    attend(1, 2)
    turn(1, 3)
    attend(2, 3)
    plane(2, 1)
    attend(3, 4)
    last(1)
    plane(2, 2)
    attend(4, 5)
    plane(2, 3)
    t1 = rows_out(cot_s, cot_in, 1)
    attend(5, 6)
    keep(P, o_p)
    keep(mT, o_mix)
    join()
    norm_one()
    keep(n1, o_n1)
    keep(r1, o_r1)
    ready(1)
    turn(2, 1)
    lift(0)
    turn(2, 2)
    lift(2)
    turn(2, 3)
    keep(fa, o_f)
    keep(dg, o_dg)
    flip(lambda at: tok_in[:, :, at].reshape(TOK_DEV, 128), xT)
    keep(xT, o_x)
    flip(lambda at: u[:, at], uT)
    keep(uT, o_u)
    last(2)
    roots(3)
    ready(2)
    drop()
    norm_two()
    keep(n2, o_n2)
    keep(r2, o_r2)
    keep(yo, o_y)
    for copy in t1:
        copy.wait_recv()
    keep(cot_in, o_cot)
    for g in range(3):
        z_finish(g)
    for copy in sent:
        copy.wait_send()
    for copy in outs:
        copy.wait()


def forward_all(lengths, place, tok, cot, flat_weights, vec, raw, root_l, root_r):
    any_spec = pl.BlockSpec(memory_space=pl.ANY)
    vmem = pl.BlockSpec(memory_space=pltpu.VMEM)
    dma = pltpu.SemaphoreType.DMA
    shape = jax.ShapeDtypeStruct
    low, f32 = jnp.bfloat16, jnp.float32
    square = (4, 2, 2, HALF, GCOLS)
    saved = [
        ((16, D), f32), ((D, TOK_DEV), low), ((8, 64, D), low), ((TOK_DEV, 3 * D), low),
        ((H, TOK_DEV, TOK_DEV), low), ((D, TOK_DEV), low), ((TOK_DEV, D), f32), ((TOK_DEV, 128), f32),
        ((D, TOK_DEV), low), ((TOK_DEV, FF), low), ((TOK_DEV, FF), low), ((TOK_DEV, D), f32),
        ((TOK_DEV, 128), f32), ((TOK_DEV, D), low), ((4, 4, 2, 2, HALF, D), low),
        ((TOK_DEV, 128), f32), ((TOK_DEV, TOK_DEV), low),
    ]
    return pl.pallas_call(
        forward_kernel,
        out_shape=[shape(square, low)] * 3 + [shape(*s) for s in saved],
        in_specs=[pl.BlockSpec(memory_space=pltpu.SMEM)] + [vmem] * 3 + [any_spec] + [vmem] * 2 + [any_spec] * 2,
        out_specs=[any_spec] * 20,
        scratch_shapes=[
            pltpu.VMEM(square, low), pltpu.VMEM(square, low), pltpu.VMEM(square, low),
            pltpu.VMEM((8, 64, D), low), pltpu.VMEM((8, 64, D), low), pltpu.VMEM((8, 16, 128), low),
            pltpu.VMEM((8, 64, D), low), pltpu.VMEM((8, 64, D), low),
            pltpu.VMEM((TOK_DEV, TOK_DEV), low),
            pltpu.VMEM((TOK_DEV, 128), f32),
            pltpu.VMEM((8, TOK_DEV), f32),
            pltpu.VMEM((2, HALF, 3 * GCOLS), f32),
            pltpu.VMEM((16, 128), low),
            pltpu.VMEM((16, D), f32),
            pltpu.VMEM((TOK_DEV, 3 * D), low),
            pltpu.VMEM((H, TOK_DEV, TOK_DEV), low),
            pltpu.VMEM((TOK_DEV, D), low),
            pltpu.VMEM((TOK_DEV, D), f32),
            pltpu.VMEM((TOK_DEV, 128), f32),
            pltpu.VMEM((TOK_DEV, D), f32),
            pltpu.VMEM((TOK_DEV, D), low),
            pltpu.VMEM((TOK_DEV, FF), low),
            pltpu.VMEM((TOK_DEV, FF), low),
            pltpu.VMEM((TOK_DEV, D), f32),
            pltpu.VMEM((TOK_DEV, 128), f32),
            pltpu.VMEM((TOK_DEV, D), low),
            pltpu.VMEM((D, TOK_DEV), low), pltpu.VMEM((D, TOK_DEV), low), pltpu.VMEM((D, TOK_DEV), low),
            pltpu.VMEM((H, TOK_DEV, 128), low),
            pltpu.VMEM((D, D), f32),
            pltpu.VMEM((4, 2, 2, HALF, D), low),
            pltpu.VMEM((2, HALF, 3 * GCOLS), low),
            dma((3, 5)), dma((3, 4)), dma((3, 4)), dma((3, 4)), dma((3, 4)), dma((3, 4)),
            dma((3, 2, 4)), dma((3, 2, 4)), dma((3, 4)), dma((3, 4)),
            dma((6,)), dma((3, 7)), dma((3, 7)), dma((19,)), dma((5,)),
        ],
        compiler_params=pltpu.CompilerParams(
            collective_id=0, has_side_effects=True, vmem_limit_bytes=60 * MIB
        ),
        name="forward_all",
    )(lengths, place, tok, cot, flat_weights.reshape(2, HALF, 3 * GCOLS), vec, raw, root_l, root_r)


def backward_kernel(
    owner, vt, use,
    h_w0, h_w1, h_w2, h_xT, h_cot, h_qkv, h_p, h_mT, h_n1, h_r1, h_uT, h_f, h_dg, h_n2, h_r2, h_y, h_root,
    o_back, o_grad, WR, UA, SC, o_gs, o_vec,
    G, Rc, A1, A2, B1, B2, ZR, ZP, F, SO, Gs, wa, wb, fb, gb, low_g, LT, LU, hb, nb, PT, r1, r2, gi,
    PQ, sq, sr_in, sc_out, vb, vr,
    ld, pd, cs, cr, a1s, a1r, b1s, b1r, a2s, a2r, b2s, b2r, zs, zr,
    fs, fr, ts, tr, ss, sr, ps, pr, us, ur, qs, qr, es, er, ms, mr, vs, vrs, ls,
):
    low, f32 = jnp.bfloat16, jnp.float32
    here = Here(True)
    wait_all = here.greet()
    x, y, z, c, f, r = here.x, here.y, here.z, here.c, here.f, here.r
    W = GCOLS // 2
    sent = []

    class Load:
        def __init__(self, number, src, dst):
            self.copy, self.done = local(src, dst, ld.at[number]), False

        def wait(self):
            if not self.done:
                self.copy.wait()
                self.done = True

    cot_l = Load(0, h_cot, gi)
    n2_l = Load(1, h_n2, hb)
    r2_l = Load(2, h_r2, r2)
    f_l = Load(3, h_f, fb)
    wd_l = Load(4, h_w2, wa)
    dg_l = Load(5, h_dg, gb)
    uT_l = Load(6, h_uT, LU)
    wu_l = Load(7, h_w1, wb)
    n1_l = Load(8, h_n1, nb)
    r1_l = Load(9, h_r1, r1)
    vb[...] = jnp.zeros_like(vb)
    wait_all()

    chunks = [(8, 2), (10, 2), (4, 2), (6, 2), (3, 1), (0, 1), (1, 1), (2, 1)]

    def span(n):
        block, count = chunks[n]
        return pl.ds(block * JCOLS, count * JCOLS)

    ways = {}

    def c_send(n):
        at = span(n)
        ways[n] = [
            send(G.at[:, :, 1 - c, :, :, at], Rc.at[:, :, :, :, at], cs.at[n], cr.at[n], here.to_core)
        ]
        sent.extend(ways[n])

    def first(n):
        at = span(n)
        ways[n][0].wait_recv()

        def add(j, zz, h):
            G[j, zz, c, h, :, at] = (
                G[j, zz, c, h, :, at].astype(f32) + Rc[j, zz, h, :, at].astype(f32)
            ).astype(low)

        def add_a(i, _):
            add(lax.div(i, 2), lax.rem(i, 2), 1 - x)
            return 0

        def add_b(i, _):
            add(1 - y, 2 + lax.div(i, 2), lax.rem(i, 2))
            return 0

        def add_rest(i, _):
            add(lax.div(i, 2), lax.rem(i, 2), x)
            add(y, 2 + lax.div(i, 2), lax.rem(i, 2))
            return 0

        lax.fori_loop(0, 4, add_a, 0)
        a = send(G.at[:, 0:2, c, 1 - x, :, at], A1.at[:, :, :, at], a1s.at[n], a1r.at[n], here.to_x)
        lax.fori_loop(0, 4, add_b, 0)
        b = send(G.at[1 - y, 2:4, c, :, :, at], B1.at[:, :, :, at], b1s.at[n], b1r.at[n], here.to_y)
        lax.fori_loop(0, 4, add_rest, 0)
        ways[n] = [a, b]
        sent.extend(ways[n])

    def second(n):
        at = span(n)
        ways[n][0].wait_recv()

        def add_a(i, _):
            for j in (1 - y, y):
                G[j, i, c, x, :, at] = (
                    G[j, i, c, x, :, at].astype(f32) + A1[j, i, :, at].astype(f32)
                ).astype(low)
            return 0

        lax.fori_loop(0, 2, add_a, 0)
        a = send(G.at[1 - y, 0:2, c, x, :, at], A2.at[:, :, at], a2s.at[n], a2r.at[n], here.to_y)
        ways[n][1].wait_recv()

        def add_b(i, _):
            for h in (1 - x, x):
                G[y, i + 2, c, h, :, at] = (
                    G[y, i + 2, c, h, :, at].astype(f32) + B1[i, h, :, at].astype(f32)
                ).astype(low)
            return 0

        lax.fori_loop(0, 2, add_b, 0)
        b = send(G.at[y, 2:4, c, 1 - x, :, at], B2.at[:, :, at], b2s.at[n], b2r.at[n], here.to_x)
        ways[n] = [a, b]
        sent.extend(ways[n])

    def third(n):
        at = span(n)
        for number, (copy, part) in enumerate(zip(ways[n], (A2, B2))):
            copy.wait_recv()

            def add(i, _, number=number, part=part):
                zz = 2 * number + i
                G[y, zz, c, x, :, at] = (
                    G[y, zz, c, x, :, at].astype(f32) + part[i, :, at].astype(f32)
                ).astype(low)
                return 0

            lax.fori_loop(0, 2, add, 0)
        partner = z + 1 - 2 * lax.rem(z, 2)
        near = send(
            G.at[y, partner, c, x, :, at], ZR.at[0, :, at], zs.at[n, 0], zr.at[n, 0],
            (r, 2 * partner + c),
        )
        sent.append(near)
        ways[n] = [near]

        @pl.when(inner == 0)
        def _():
            passing(n).start()

    inner = lax.rem(lax.div(z + 1, 2), 2)
    far = 2 - 2 * lax.div(z, 2)

    def passing(n):
        at = span(n)
        return pltpu.make_async_remote_copy(
            src_ref=G.at[y, pl.ds(far, 2), c, x, :, at], dst_ref=ZP.at[:, :, at], send_sem=zs.at[n, 1],
            recv_sem=zr.at[n, 1], device_id=(r, 2 * (z + 1 - 2 * lax.rem(z, 2)) + c), device_id_type=MESH,
        )

    def crossing(n, i):
        at = span(n)
        return pltpu.make_async_remote_copy(
            src_ref=G.at[y, far + i, c, x, :, at], dst_ref=ZR.at[1, :, at], send_sem=zs.at[n, 2 + i],
            recv_sem=zr.at[n, 2], device_id=(r, 2 * (far + i) + c), device_id_type=MESH,
        )

    def fourth(n):
        at = span(n)

        @pl.when(inner == 1)
        def _():
            passing(n).wait_recv()
            for i in range(2):
                G[y, far + i, c, x, :, at] = (
                    G[y, far + i, c, x, :, at].astype(f32) + ZP[i, :, at].astype(f32)
                ).astype(low)
                crossing(n, i).start()

    def z_finish():
        for n in range(8):

            @pl.when(inner == 0)
            def _():
                passing(n).wait_send()

            @pl.when(inner == 1)
            def _():
                for i in range(2):
                    crossing(n, i).wait_send()

    def final(n):
        ways[n][0].wait_recv()
        crossing(n, 0).wait_recv()
        block, count = chunks[n]
        for b in range(block, block + count):
            at = pl.ds(b * JCOLS, JCOLS)
            total = G[y, z, c, x, :, at].astype(f32)
            for step in range(2):
                total = total + ZR[step, :, at].astype(f32)
            F[b] = total.astype(low)

    homes = []

    spreads = {}
    diagonals = []

    def spread(g):
        at = pl.ds(4 * g, 4)
        to = WR.at[x, y, at]
        a = send(F.at[at], to, fs.at[g, 0], fr.at[g, 0], here.to_x)
        b = send(F.at[at], to, fs.at[g, 1], fr.at[g, 1], here.to_y)
        homes.append(local(F.at[at], to, ls.at[g]))
        sent.extend([a, b])
        spreads[g] = (a, b)

    def spread_on(g):
        a, b = spreads[g]
        a.wait_recv()
        part = WR.at[1 - x, y, pl.ds(4 * g, 2)]
        da = send(part, part, fs.at[g, 2], fr.at[g, 2], here.to_y)
        b.wait_recv()
        part = WR.at[x, 1 - y, pl.ds(4 * g + 2, 2)]
        db = send(part, part, fs.at[g, 3], fr.at[g, 3], here.to_x)
        sent.extend([da, db])
        diagonals.extend([da, db])

    def token_send(source, landing, number):
        out = []
        for step in range(1, 8):
            to = here.peer(step)
            out.append(
                send(source(to), landing.at[f], ts.at[number, step - 1], tr.at[number, step - 1], (r, to))
            )
        homes.append(local(source(f), landing.at[f], ls.at[3 + number]))
        sent.extend(out)
        return out

    def square(ref, at):
        return ref[:, :, :, :, at].reshape(D, at.size)

    def own_rows(ref, core):
        return jnp.concatenate(
            [ref[pl.ds(pl.multiple_of((2 * zz + core) * 96, 96), 96), :] for zz in range(4)], axis=0
        )

    def gradient(left, right, block, start, count, core):
        rows = own_rows(left, core)

        def one(i, _):
            out = jnp.dot(rows, right[:, cols(start + i * D, D)], preferred_element_type=f32)
            out = out.astype(low).reshape(4, 2, HALF, D)
            for j in range(2):
                at = cols((block + i) * JCOLS, JCOLS)
                G[j, :, core, :, :, at] = out[:, :, :, j * JCOLS : (j + 1) * JCOLS]
            return 0

        lax.fori_loop(0, count, one, 0)

    def eight(v):
        return jnp.sum(v.reshape(8, 8, v.shape[1]), axis=0)

    def norm_back(i, carry, grad, n, rr, gain):
        zed = grad * gain
        back = rr * (
            zed - jnp.mean(zed, axis=1, keepdims=True) - n * jnp.mean(zed * n, axis=1, keepdims=True)
        )
        rounded = back.astype(low)
        return back, rounded, (
            carry[0] + eight(grad * n), carry[1] + eight(grad), carry[2] + eight(rounded.astype(f32))
        )

    zero = jnp.zeros((8, D), f32)

    def put(row, total):
        vb[0, row : row + 1, :] = jnp.sum(total, axis=0, keepdims=True)

    def flip(source, target, count):
        def one(i, _):
            at = cols(i * 128, 128)
            target[at, :] = jnp.transpose(source[:, at])
            return 0

        lax.fori_loop(0, count, one, 0)

    ta = token_send(lambda to: h_y.at[to], o_back, 0)
    cot_l.wait()
    n2_l.wait()
    r2_l.wait()

    def back_two(i, carry):
        at = pl.ds(pl.multiple_of(i * 64, 64), 64)
        grad = gi[i].astype(f32) * use[at, 0:1]
        back, rounded, carry = norm_back(i, carry, grad, hb[at, :], r2[at, 0:1], vt[6:7, :])
        hb[at, :] = back
        low_g[at, :] = rounded
        return carry

    sums = lax.fori_loop(0, 8, back_two, (zero, zero, zero))
    put(6, sums[0])
    put(7, sums[1])
    put(3, sums[2])
    flip(low_g, LT, 6)
    f_l.wait()
    gradient(LT, fb, 8, 0, 2, 1 - c)
    c_send(0)
    gradient(LT, fb, 10, 2 * D, 2, 1 - c)
    c_send(1)
    gradient(LT, fb, 8, 0, 4, c)
    qkv_l = Load(10, h_qkv, fb.at[:, : 3 * D])
    mT_l = Load(11, h_mT, LT)
    wd_l.wait()
    dg_l.wait()

    def back_up(i, _):
        at = cols(i * 256, 256)
        acc = jnp.dot(low_g[...], square(wa, at), preferred_element_type=f32)
        gb[:, at] = (acc * gb[:, at].astype(f32)).astype(low)
        return 0

    first(0)
    lax.fori_loop(0, 6, back_up, 0)
    first(1)
    uT_l.wait()
    gradient(LU, gb, 4, 0, 2, 1 - c)
    c_send(2)
    lax.fori_loop(6, 12, back_up, 0)
    wq_l = Load(12, h_w0, wa)
    gradient(LU, gb, 4, 0, 2, c)
    first(2)
    gradient(LU, gb, 6, 2 * D, 2, 1 - c)
    c_send(3)
    gradient(LU, gb, 6, 2 * D, 2, c)
    xT_l = Load(13, h_xT, LU)
    second(0)
    first(3)
    wu_l.wait()

    def back_x1(i, _):
        at = cols(i * 512, 512)
        hb[...] += lax.dot_general(
            gb[:, at], square(wb, at), (((1,), (1,)), ((), ())), preferred_element_type=f32
        )
        return 0

    lax.fori_loop(0, 6, back_x1, 0)
    second(1)
    root_l = [Load(14 + n, h_root.at[n], wb.at[:, :, :, :, n * D : (n + 1) * D]) for n in range(4)]
    n1_l.wait()
    r1_l.wait()

    def back_one(i, carry):
        at = pl.ds(pl.multiple_of(i * 64, 64), 64)
        back, rounded, carry = norm_back(i, carry, hb[at, :], nb[at, :], r1[at, 0:1], vt[4:5, :])
        hb[at, :] = back
        low_g[at, :] = rounded
        return carry

    sums = lax.fori_loop(0, 8, back_one, (zero, zero, zero))
    put(4, sums[0])
    put(5, sums[1])
    put(2, sums[2])
    third(0)
    mT_l.wait()
    gradient(LT, low_g, 3, 0, 1, 1 - c)
    c_send(4)
    gradient(LT, low_g, 3, 0, 1, c)
    wq_l.wait()

    def back_mix(i, _):
        out = lax.dot_general(
            low_g[...], wa[pl.ds(2 * i, 2), :, :, :, 3 * D : 4 * D].reshape(JCOLS, D),
            (((1,), (1,)), ((), ())), preferred_element_type=f32,
        )
        gb[:, cols(3 * D + i * JCOLS, JCOLS)] = out.astype(low)
        return 0

    for row in range(4):

        def total(i, acc, row=row):
            at = pl.ds(pl.multiple_of(i * 64, 64), 64)
            return acc + eight(gb[at, row * D : (row + 1) * D].astype(f32))

        put(8 + row, lax.fori_loop(0, 8, total, zero))
    lax.fori_loop(0, 2, back_mix, 0)
    second(2)
    first(4)
    qkv_l.wait()

    def fetch(i):
        return pltpu.make_async_copy(h_p.at[pl.ds(2 * i, 2)], PT.at[i % 2], pd.at[i % 2])

    fetch(0).start()

    def attend(i):
        slot = i % 2
        if i < 5:
            fetch(i + 1).start()
        q2, k2 = fb[:, cols(i * 128, 128)], fb[:, cols(D + i * 128, 128)]
        v2, go2 = fb[:, cols(2 * D + i * 128, 128)], gb[:, cols(3 * D + i * 128, 128)]
        kT = jnp.transpose(k2)
        lane = lax.broadcasted_iota(jnp.int32, (TOK_DEV, 128), 1)
        fetch(i).wait()
        parts = []
        gk = jnp.zeros((TOK_DEV, 128), f32)
        gv = jnp.where(use[:, :] > 0, 0.0, go2.astype(f32))
        for half in range(2):
            mine = (lane < HD) if half == 0 else (lane >= HD)
            none = jnp.zeros_like(v2)
            p = PT[slot, half]
            gp = lax.dot_general(
                jnp.where(mine, v2, none), go2, (((1,), (1,)), ((), ())), preferred_element_type=f32
            )
            pf = p.astype(f32)
            gs = (pf * (gp - jnp.sum(pf * gp, axis=0, keepdims=True))).astype(low)
            gk = gk + jnp.dot(gs, jnp.where(mine, q2, none), preferred_element_type=f32)
            gv = gv + jnp.dot(p, jnp.where(mine, go2, none), preferred_element_type=f32)
            parts.append(jnp.dot(kT[half * HD : (half + 1) * HD], gs, preferred_element_type=f32))
        gq = jnp.transpose(jnp.concatenate(parts, axis=0)) * (HD ** (-0.5))
        gb[:, cols(i * 128, 128)] = gq.astype(low)
        gb[:, cols(D + i * 128, 128)] = gk.astype(low)
        gb[:, cols(2 * D + i * 128, 128)] = gv.astype(low)

    attend(0)
    attend(1)
    third(1)
    fourth(0)
    attend(2)
    attend(3)
    second(3)
    attend(4)
    fourth(1)
    attend(5)
    third(2)

    def back_x(i, _):
        at = cols(i * D, D)
        hb[...] += lax.dot_general(
            gb[:, at], square(wa, at), (((1,), (1,)), ((), ())), preferred_element_type=f32
        )
        return 0

    lax.fori_loop(0, 3, back_x, 0)

    def rows_low(i, _):
        gi[i] = hb[pl.ds(pl.multiple_of(i * 64, 64), 64), :].astype(low)
        return 0

    lax.fori_loop(0, 8, rows_low, 0)
    tb = token_send(lambda to: gi.at[to], o_grad, 1)
    second(4)
    xT_l.wait()
    for n in range(3):
        gradient(LU, gb, n, n * D, 1, 1 - c)
        c_send(5 + n)
    fourth(2)
    gradient(LU, gb, 0, 0, 1, c)
    first(5)
    gradient(LU, gb, 1, D, 1, c)
    first(6)
    gradient(LU, gb, 2, 2 * D, 1, c)
    first(7)
    third(3)
    for row, start in ((0, 0), (1, 2 * D)):

        def total(i, acc, start=start):
            at = pl.ds(pl.multiple_of(i * 64, 64), 64)
            return acc + eight(gb[at, start : start + D].astype(f32))

        put(row, lax.fori_loop(0, 8, total, zero))
    vec_copy = send(vb.at[0], vr.at[0], vs.at[0], vrs.at[0], here.to_core)
    sent.append(vec_copy)
    third(4)
    second(5)
    fourth(3)
    vec_copy.wait_recv()
    vb[1] = vb[0] + vr[0]
    vec_copy = send(vb.at[1], vr.at[1], vs.at[1], vrs.at[1], here.to_x)
    sent.append(vec_copy)
    second(6)
    third(5)
    fourth(4)
    vec_copy.wait_recv()
    vb[2] = vb[1] + vr[1]
    vec_copy = send(vb.at[2], vr.at[2], vs.at[2], vrs.at[2], here.to_y)
    sent.append(vec_copy)
    second(7)
    final(0)
    final(1)
    spread(2)
    fourth(5)
    third(6)
    final(2)
    final(3)
    spread(1)
    fourth(6)
    third(7)
    final(4)
    fourth(7)
    final(5)
    final(6)
    final(7)
    jc = cols(y * JCOLS, JCOLS)
    other = cols((1 - y) * JCOLS, JCOLS)
    slot_copies = []
    for step in range(1, 9):
        to = here.peer(step)
        for t in range(2):
            b = jnp.int32(-1)
            for k in range(NBLK):
                b = jnp.where(owner[k] == 2 * to + t, k, b)
            flag = (b >= 0).astype(f32)
            SO[step - 1, t] = (F[jnp.maximum(b, 0)].astype(f32) * flag).astype(low)
        if step < 8:
            slot_copies.append(
                send(SO.at[step - 1], Gs.at[:, f, x, :, jc], ss.at[step - 1], sr.at[step - 1], (r, to))
            )
    sent.extend(slot_copies)
    own = local(SO.at[7], Gs.at[:, f, x, :, jc], ls.at[5])
    hops = []
    for step in range(8):
        src = lax.rem(f + 8 - step, 8)
        if step == 0:
            own.wait()
        else:
            slot_copies[step - 1].wait_recv()
        part = Gs.at[:, src, x, :, jc]
        hops.append(
            (
                send(part, part, ps.at[0, step], pr.at[0, step], here.to_x),
                send(part, part, ps.at[1, step], pr.at[1, step], here.to_y),
            )
        )
    ends = []
    for step in range(8):
        src = lax.rem(f + 8 - step, 8)
        hops[step][0].wait_recv()
        part = Gs.at[0, src, 1 - x, :, jc]
        ends.append(send(part, part, ps.at[2, step], pr.at[2, step], here.to_y))
        hops[step][1].wait_recv()
        part = Gs.at[1, src, x, :, other]
        ends.append(send(part, part, ps.at[3, step], pr.at[3, step], here.to_x))
        sent.extend(hops[step])
    sent.extend(ends)
    vec_copy.wait_recv()
    vb[3] = vb[2] + vr[2]
    vec_copies = []
    for step in (1, 2, 3):
        vec_copies.append(
            send(vb.at[3], vr.at[2 + step], vs.at[2 + step], vrs.at[2 + step], here.along(step))
        )
    sent.extend(vec_copies)
    spread_on(2)
    spread_on(1)
    spread(0)
    for load in root_l:
        load.wait()
    for copy in ends:
        copy.wait_recv()
    homes.append(local(Gs, o_gs, ls.at[6]))
    for t in range(2):
        whole = Gs[t].reshape(D, D)
        rows = wb[:, :, x, :, t * D : (t + 1) * D].reshape(JCOLS, D)
        half = jnp.dot(rows, whole, preferred_element_type=f32).astype(low)
        right = square(wb, cols((2 + t) * D + y * JCOLS, JCOLS))
        part = jnp.dot(half, right, preferred_element_type=f32)
        PQ[t] = part.astype(low).reshape(8, HALF, JCOLS)
        sq[t] = jnp.sum((part * part).reshape(48, 8, JCOLS), axis=0)
    ucopies = []
    for step in range(1, 8):
        to = here.peer(step)
        ucopies.append(
            send(PQ.at[:, to], UA.at[x, y, pl.ds(2 * f, 2)], us.at[step - 1], ur.at[step - 1], (r, to))
        )
    sent.extend(ucopies)
    own = local(PQ.at[:, f], UA.at[x, y, pl.ds(2 * f, 2)], ls.at[7])
    squares = []
    for number, to in enumerate((here.to_x, here.to_y, here.to_d)):
        squares.append(send(sq, sr_in.at[number], es.at[number], er.at[number], to))
    sent.extend(squares)
    uhops = []
    for step in range(8):
        src = lax.rem(f + 8 - step, 8)
        if step == 0:
            own.wait()
        else:
            ucopies[step - 1].wait_recv()
        part = UA.at[x, y, pl.ds(2 * src, 2)]
        uhops.append(
            (
                send(part, part, qs.at[0, step], qr.at[0, step], here.to_x),
                send(part, part, qs.at[1, step], qr.at[1, step], here.to_y),
            )
        )
        if step == 0:
            for copy in squares:
                copy.wait_recv()
            for t in range(2):
                total = sq[t] + sr_in[0, t] + sr_in[1, t] + sr_in[2, t]
                mean = jnp.sum(jnp.sum(total, axis=1, keepdims=True), axis=0, keepdims=True) * (1.0 / (D * D))
                sc_out[t] = jnp.broadcast_to(lax.rsqrt(mean + RMS_EPS), (8, 128))
            scales = []
            for number in range(1, 8):
                to = here.peer(number)
                scales.append(
                    send(
                        sc_out, SC.at[pl.ds(2 * f, 2)], ms.at[number - 1], mr.at[number - 1], (r, to)
                    )
                )
            sent.extend(scales)
            homes.append(local(sc_out, SC.at[pl.ds(2 * f, 2)], ls.at[8]))
    uends = []
    for step in range(8):
        src = lax.rem(f + 8 - step, 8)
        uhops[step][0].wait_recv()
        part = UA.at[1 - x, y, 2 * src]
        uends.append(send(part, part, qs.at[2, step], qr.at[2, step], here.to_y))
        uhops[step][1].wait_recv()
        part = UA.at[x, 1 - y, 2 * src + 1]
        uends.append(send(part, part, qs.at[3, step], qr.at[3, step], here.to_x))
        sent.extend(uhops[step])
    sent.extend(uends)
    spread_on(0)
    total = vb[3]
    for copy in vec_copies:
        copy.wait_recv()
    for step in range(3):
        total = total + vr[3 + step]
    vb[4] = total
    homes.append(local(vb.at[4], o_vec, ls.at[9]))
    for copy in diagonals + uends + scales + ta + tb:
        copy.wait_recv()
    for copy in homes:
        copy.wait()
    z_finish()
    for copy in sent:
        copy.wait_send()


def backward_all(owner, vt, use, saved):
    any_spec = pl.BlockSpec(memory_space=pl.ANY)
    vmem = pl.BlockSpec(memory_space=pltpu.VMEM)
    smem = pl.BlockSpec(memory_space=pltpu.SMEM)
    dma = pltpu.SemaphoreType.DMA
    shape = jax.ShapeDtypeStruct
    low, f32 = jnp.bfloat16, jnp.float32
    JW = 12 * JCOLS
    square = (4, 2, 2, HALF, GCOLS)
    return pl.pallas_call(
        backward_kernel,
        out_shape=[
            shape((8, 64, D), low), shape((8, 64, D), low),
            shape((2, 2, 12, HALF, JCOLS), low), shape((2, 2, 16, HALF, JCOLS), low),
            shape((16, 8, 128), f32), shape((2, 8, 2, HALF, D), low), shape((16, D), f32),
        ],
        in_specs=[smem, vmem, vmem] + [any_spec] * 17,
        out_specs=[any_spec] * 7,
        scratch_shapes=[
            pltpu.VMEM((2, 4, 2, 2, HALF, JW), low),
            pltpu.VMEM((2, 4, 2, HALF, JW), low),
            pltpu.VMEM((2, 2, HALF, JW), low),
            pltpu.VMEM((2, HALF, JW), low),
            pltpu.VMEM((2, 2, HALF, JW), low),
            pltpu.VMEM((2, HALF, JW), low),
            pltpu.VMEM((2, HALF, JW), low),
            pltpu.VMEM((2, HALF, JW), low),
            pltpu.VMEM((12, HALF, JCOLS), low),
            pltpu.VMEM((8, 2, HALF, JCOLS), low),
            pltpu.VMEM((2, 8, 2, HALF, D), low),
            pltpu.VMEM(square, low),
            pltpu.VMEM(square, low),
            pltpu.VMEM((TOK_DEV, FF), low),
            pltpu.VMEM((TOK_DEV, FF), low),
            pltpu.VMEM((TOK_DEV, D), low),
            pltpu.VMEM((D, TOK_DEV), low),
            pltpu.VMEM((D, TOK_DEV), low),
            pltpu.VMEM((TOK_DEV, D), f32),
            pltpu.VMEM((TOK_DEV, D), f32),
            pltpu.VMEM((2, 2, TOK_DEV, TOK_DEV), low),
            pltpu.VMEM((TOK_DEV, 128), f32),
            pltpu.VMEM((TOK_DEV, 128), f32),
            pltpu.VMEM((8, 64, D), low),
            pltpu.VMEM((2, 8, HALF, JCOLS), low),
            pltpu.VMEM((2, 8, JCOLS), f32),
            pltpu.VMEM((3, 2, 8, JCOLS), f32),
            pltpu.VMEM((2, 8, 128), f32),
            pltpu.VMEM((5, 16, D), f32),
            pltpu.VMEM((6, 16, D), f32),
            dma((18,)), dma((2,)), dma((8,)), dma((8,)),
            dma((8,)), dma((8,)), dma((8,)), dma((8,)), dma((8,)), dma((8,)), dma((8,)), dma((8,)),
            dma((8, 4)), dma((8, 3)), dma((3, 4)), dma((3, 4)),
            dma((2, 7)), dma((2, 7)), dma((7,)), dma((7,)), dma((4, 8)), dma((4, 8)),
            dma((7,)), dma((7,)), dma((4, 8)), dma((4, 8)), dma((3,)), dma((3,)), dma((7,)), dma((7,)),
            dma((6,)), dma((6,)), dma((10,)),
        ],
        compiler_params=pltpu.CompilerParams(
            collective_id=1, has_side_effects=True, vmem_limit_bytes=60 * MIB
        ),
        name="backward_all",
    )(owner, vt, use, *saved)


def finish_kernel(
    owner, hot, back, grad, wr, ua, sc, gs, vec, stat_l, stat_r, wf, vecs, mom1, mom2,
    layer_out, input_grad, wg, nw, new_l, new_r, out1, out2, outv,
    gb, sl, sr, ub, rb, wb, nb, gg, tb, to, ls, os,
):
    low, f32 = jnp.bfloat16, jnp.float32
    f = lax.axis_index("fsdp")
    loads = [
        local(back, tb.at[0], ls.at[0]), local(grad, tb.at[1], ls.at[1]),
        local(wr, rb, ls.at[2]), local(ua, ub, ls.at[3]), local(wf, wb, ls.at[4]),
        local(gs, gb, ls.at[5]),
    ]
    stats = [
        (local(stat_l.at[t], sl.at[t], ls.at[6 + 2 * t]), local(stat_r.at[t], sr.at[t], ls.at[7 + 2 * t]))
        for t in range(2)
    ]
    outs = []
    for number, target in enumerate((layer_out, input_grad)):
        loads[number].wait()
        to[number] = jnp.dot(
            hot[...], tb[number].reshape(TOK_DEV, D), preferred_element_type=f32
        ).astype(low)
        outs.append(local(to.at[number], target, os.at[number]))
    loads[2].wait()

    def one(i, _):
        h, b = lax.rem(i, 2), lax.div(i, 2)
        for j in range(2):
            gg[h, :, cols(b * D + j * JCOLS, JCOLS)] = rb[h, j, b].astype(f32)
        return 0

    lax.fori_loop(0, 24, one, 0)
    outs.append(local(gg, wg, os.at[2]))
    loads[3].wait()
    loads[4].wait()
    for b in range(NBLK):
        slot = owner[b]
        scale = LR_MATRIX * sc[slot, 0:1, 0:1]
        for h in range(2):
            for j in range(2):
                at = pl.ds(b * D + j * JCOLS, JCOLS)
                nb[h, :, at] = wb[h, :, at] - scale * ub[h, j, slot].astype(f32)
    outs.append(local(nb, nw, os.at[3]))
    loads[5].wait()
    for t in range(2):
        stats[t][0].wait()

        def left(i, _, t=t):
            at = pl.ds(pl.multiple_of(i * 192, 192), 192)
            rows = gb[t, pl.ds(2 * i, 2)].reshape(192, D)
            part = lax.dot_general(
                rows, gb[t].reshape(D, D), (((1,), (1,)), ((), ())), preferred_element_type=f32
            )
            sl[t, at, :] = STAT_DECAY * sl[t, at, :] + (1.0 - STAT_DECAY) * part
            return 0

        lax.fori_loop(0, 4, left, 0)
        outs.append(local(sl.at[t], new_l.at[t], os.at[4 + 2 * t]))
        stats[t][1].wait()
        for i in range(3):
            at = pl.ds(i * 256, 256)
            part = lax.dot_general(
                gb[t, :, :, :, at].reshape(D, 256), gb[t].reshape(D, D), (((0,), (0,)), ((), ())),
                preferred_element_type=f32,
            )
            sr[t, at, :] = STAT_DECAY * sr[t, at, :] + (1.0 - STAT_DECAY) * part
        outs.append(local(sr.at[t], new_r.at[t], os.at[5 + 2 * t]))
    mine = jnp.zeros((NBLK, 96), f32)
    for number in range(8):
        mine = jnp.where(f == number, vec[:NBLK, number * 96 : (number + 1) * 96], mine)
    fresh1 = BETA_ONE * mom1[...] + (1.0 - BETA_ONE) * mine
    fresh2 = BETA_TWO * mom2[...] + (1.0 - BETA_TWO) * mine * mine
    out1[...] = fresh1
    out2[...] = fresh2
    outv[...] = vecs[...] - LR_VECTOR * (fresh1 / (1.0 - BETA_ONE**STEP)) / (
        jnp.sqrt(fresh2 / (1.0 - BETA_TWO**STEP)) + ADAM_EPS
    )
    for copy in outs:
        copy.wait()


def finish_all(owner, hot, results, stat_l, stat_r, wf, vecs, mom1, mom2):
    any_spec = pl.BlockSpec(memory_space=pl.ANY)
    vmem = pl.BlockSpec(memory_space=pltpu.VMEM)
    smem = pl.BlockSpec(memory_space=pltpu.SMEM)
    dma = pltpu.SemaphoreType.DMA
    shape = jax.ShapeDtypeStruct
    low, f32 = jnp.bfloat16, jnp.float32
    wide = (2, HALF, 3 * GCOLS)
    back, grad, wr, ua, sc, gs, vec = results
    return pl.pallas_call(
        finish_kernel,
        out_shape=[
            shape((TOK_DEV, D), low), shape((TOK_DEV, D), low), shape(wide, f32), shape(wide, f32),
            shape((2, D, D), f32), shape((2, D, D), f32),
            shape((NBLK, 96), f32), shape((NBLK, 96), f32), shape((NBLK, 96), f32),
        ],
        in_specs=[smem, vmem] + [any_spec] * 4 + [vmem, any_spec, vmem] + [any_spec] * 3 + [vmem] * 3,
        out_specs=[any_spec] * 6 + [vmem] * 3,
        scratch_shapes=[
            pltpu.VMEM((2, 8, 2, HALF, D), low),
            pltpu.VMEM((2, D, D), f32),
            pltpu.VMEM((2, D, D), f32),
            pltpu.VMEM((2, 2, 16, HALF, JCOLS), low),
            pltpu.VMEM((2, 2, 12, HALF, JCOLS), low),
            pltpu.VMEM(wide, f32),
            pltpu.VMEM(wide, f32),
            pltpu.VMEM(wide, f32),
            pltpu.VMEM((2, 8, 64, D), low),
            pltpu.VMEM((2, TOK_DEV, D), low),
            dma((10,)), dma((8,)),
        ],
        compiler_params=pltpu.CompilerParams(vmem_limit_bytes=56 * MIB),
        name="finish_all",
    )(
        owner, hot, back, grad, wr, ua, sc, gs, vec, stat_l, stat_r, wf.reshape(wide), vecs, mom1, mom2
    )


def fast_body(
    tokens,
    cotangent,
    place,
    seq_lengths,
    random_blocks,
    owner_slot,
    flat_weights,
    vectors,
    moment_first,
    moment_second,
    stat_left,
    stat_right,
    root_left,
    root_right,
):
    peers = lax.axis_size("fsdp")
    share_rows = TOK_DEV // peers
    w0, w1, w2, vt, *saved = forward_all(
        seq_lengths, place[None, :], tokens, cotangent, flat_weights, vectors.T,
        jnp.transpose(random_blocks, (2, 0, 1)), root_left, root_right,
    )
    *saved, use, hot = saved
    saved[-2] = saved[-2].reshape(peers, share_rows, D)
    results = backward_all(owner_slot, vt, use, [w0, w1, w2] + saved)
    layer_out, input_grad, weight_grads, new_weights, *others = finish_all(
        owner_slot, hot, results, stat_left, stat_right, flat_weights, vectors.T, moment_first.T,
        moment_second.T,
    )
    return (
        layer_out,
        input_grad,
        weight_grads.reshape(flat_weights.shape),
        new_weights.reshape(flat_weights.shape),
        *others[:2],
        *[vec.T for vec in others[2:]],
    )


def plain_body(
    tokens,
    cotangent,
    place,
    seq_lengths,
    random_blocks,
    owner_slot,
    flat_weights,
    vectors,
    moment_first,
    moment_second,
    stat_left,
    stat_right,
    root_left,
    root_right,
):
    peers = lax.axis_size("fsdp")
    share_rows = TOK_DEV // peers
    order_ids = jnp.argsort(place)
    outgoing = (
        tokens[order_ids].reshape(peers, share_rows, D),
        cotangent[order_ids].reshape(peers, share_rows, D),
    )
    arrived = (
        lax.all_to_all(outgoing[0], "fsdp", split_axis=0, concat_axis=0, tiled=True),
        lax.all_to_all(outgoing[1], "fsdp", split_axis=0, concat_axis=0, tiled=True),
    )
    inputs = arrived[0].reshape(TOK_DEV, D)
    upstream = arrived[1].reshape(TOK_DEV, D).astype(jnp.float32)
    weight_copy, vector_copy = (
        lax.all_gather(flat_weights.astype(jnp.bfloat16), "fsdp", axis=0, tiled=True),
        lax.all_gather(vectors.astype(jnp.bfloat16), "fsdp", axis=0, tiled=True),
    )
    vecs_full = vector_copy.astype(jnp.float32)
    b_up = jnp.transpose(vecs_full[:, 8:]).reshape(FF)
    seq_id, position, in_use, seq_blocks = layout(seq_lengths[0])
    picks = random_keys(random_blocks, seq_blocks)
    slot_ids = jnp.arange(TOK_DEV, dtype=jnp.int32)
    real_rows = in_use.astype(jnp.float32)[:, None]
    bias_qkv = jnp.concatenate([vecs_full[:, 0], jnp.zeros((D,), jnp.float32), vecs_full[:, 1]])
    qkv_low = (
        jnp.dot(inputs, weight_copy[:, : 3 * D], preferred_element_type=jnp.float32) + bias_qkv
    ).astype(jnp.bfloat16)
    qkv_heads = qkv_low.reshape(TOK_DEV, 3, H, HD)
    queries = qkv_heads[:, 0]
    key_heads = qkv_heads[:, 1]
    value_heads = qkv_heads[:, 2]
    block_rows = min(512, TOK_DEV)
    block_count = TOK_DEV // block_rows
    score_scale = HD ** (-0.5)

    def split_blocks(array):
        return array.reshape((block_count, block_rows) + array.shape[1:])

    block_inputs = (
        split_blocks(queries),
        split_blocks(seq_id),
        split_blocks(position),
        split_blocks(in_use),
        split_blocks(picks),
        split_blocks(slot_ids),
    )

    def scores_of(query_block, q_seq, q_pos, q_use, q_pick, q_slot):
        raw_scores = (
            jnp.einsum("qhd,khd->hqk", query_block, key_heads, preferred_element_type=jnp.float32)
            * score_scale
        )
        keep_mask = allowed(q_seq, q_pos, q_use, q_pick, q_slot, seq_id, position, in_use, slot_ids)
        return jnp.where(keep_mask, raw_scores, MASKED_SCORE)

    def forward_block(pieces):
        scores = scores_of(pieces[0], pieces[1], pieces[2], pieces[3], pieces[4], pieces[5])
        row_max = jnp.max(scores, axis=-1, keepdims=True)
        expo = jnp.exp(scores - row_max)
        row_total = jnp.sum(expo, axis=-1, keepdims=True)
        probs_low = (expo / row_total).astype(jnp.bfloat16)
        mixed_block = jnp.einsum(
            "hqk,khd->qhd", probs_low, value_heads, preferred_element_type=jnp.float32
        )
        return (mixed_block.reshape(block_rows, D), (row_max + jnp.log(row_total))[:, :, 0])

    attended, log_totals = lax.map(forward_block, block_inputs)
    mixed = attended.reshape(TOK_DEV, D).astype(jnp.bfloat16)
    branch = (
        jnp.dot(mixed, weight_copy[:, 3 * D : 4 * D], preferred_element_type=jnp.float32)
        + vecs_full[:, 2]
    )
    hidden_one = inputs.astype(jnp.float32) + branch
    x_one, norm_one_back = jax.vjp(layer_norm, hidden_one, vecs_full[:, 4], vecs_full[:, 5])
    x_one_low = x_one.astype(jnp.bfloat16)
    pre_act = (
        jnp.dot(x_one_low, weight_copy[:, 4 * D : 4 * D + FF], preferred_element_type=jnp.float32)
        + b_up
    )
    act, gelu_back = jax.vjp(gelu_tanh, pre_act)
    act_low = act.astype(jnp.bfloat16)
    ffn = contract_cols(act_low, weight_copy[:, 4 * D + FF :]) + vecs_full[:, 3]
    hidden_two = x_one + ffn
    result, norm_two_back = jax.vjp(layer_norm, hidden_two, vecs_full[:, 6], vecs_full[:, 7])
    layer_rows = (result * real_rows).astype(jnp.bfloat16)
    weight_copy = lax.all_gather(flat_weights.astype(jnp.bfloat16), "fsdp", axis=0, tiled=True)
    d_result = upstream * real_rows
    d_two, d_gain_two, d_shift_two = norm_two_back(d_result)
    d_ffn = d_two.astype(jnp.bfloat16)
    d_act = jnp.dot(d_ffn, weight_copy[:, 4 * D + FF :], preferred_element_type=jnp.float32)
    (d_pre,) = gelu_back(d_act)
    d_pre_low = d_pre.astype(jnp.bfloat16)
    grad_down = contract_rows(d_ffn, act_low)
    grad_up = contract_rows(x_one_low, d_pre_low)
    d_x_one = d_two + contract_cols(d_pre_low, weight_copy[:, 4 * D : 4 * D + FF])
    d_one, d_gain_one, d_shift_one = norm_one_back(d_x_one)
    up_sums = jnp.transpose(jnp.sum(d_pre_low.astype(jnp.float32), axis=0).reshape(FF // D, D))
    ffn_vec = jnp.concatenate(
        [
            jnp.sum(d_ffn.astype(jnp.float32), axis=0)[:, None],
            d_gain_one[:, None],
            d_shift_one[:, None],
            d_gain_two[:, None],
            d_shift_two[:, None],
            up_sums,
        ],
        axis=1,
    )
    ffn_mats = jnp.concatenate([grad_up, grad_down], axis=1)
    d_branch = d_one.astype(jnp.bfloat16)
    grad_out = contract_rows(mixed, d_branch)
    d_mixed = (
        contract_cols(d_branch, weight_copy[:, 3 * D : 4 * D])
        .astype(jnp.bfloat16)
        .reshape(TOK_DEV, H, HD)
    )

    def backward_block(carry, pieces):
        key_grad, value_grad = carry
        query_block = pieces[0]
        log_total = pieces[6]
        out_grad = pieces[7]
        scores = scores_of(pieces[0], pieces[1], pieces[2], pieces[3], pieces[4], pieces[5])
        probs = jnp.exp(scores - log_total[:, :, None])
        probs_low = probs.astype(jnp.bfloat16)
        value_grad = value_grad + jnp.einsum(
            "hqk,qhd->khd", probs_low, out_grad, preferred_element_type=jnp.float32
        )
        prob_grad = jnp.einsum(
            "qhd,khd->hqk", out_grad, value_heads, preferred_element_type=jnp.float32
        )
        score_grad = (
            probs * (prob_grad - jnp.sum(probs * prob_grad, axis=-1, keepdims=True))
        ).astype(jnp.bfloat16)
        query_grad = (
            jnp.einsum("hqk,khd->qhd", score_grad, key_heads, preferred_element_type=jnp.float32)
            * score_scale
        )
        key_grad = (
            key_grad
            + jnp.einsum(
                "hqk,qhd->khd", score_grad, query_block, preferred_element_type=jnp.float32
            )
            * score_scale
        )
        return ((key_grad, value_grad), query_grad)

    zero_heads = jnp.zeros((TOK_DEV, H, HD), jnp.float32)
    (key_grad, value_grad), query_grad = lax.scan(
        backward_block, (zero_heads, zero_heads), block_inputs + (log_totals, split_blocks(d_mixed))
    )
    d_qkv = jnp.concatenate(
        [
            query_grad.reshape(TOK_DEV, D),
            key_grad.reshape(TOK_DEV, D),
            value_grad.reshape(TOK_DEV, D),
        ],
        axis=1,
    ).astype(jnp.bfloat16)
    grad_qkv = contract_rows(inputs, d_qkv)
    d_inputs = d_one + contract_cols(d_qkv, weight_copy[:, : 3 * D])
    qkv_sums = jnp.sum(d_qkv.astype(jnp.float32), axis=0)
    attn_vec = jnp.stack(
        [qkv_sums[:D], qkv_sums[2 * D :], jnp.sum(d_branch.astype(jnp.float32), axis=0)], axis=1
    )
    attn_mats = jnp.concatenate([grad_qkv, grad_out], axis=1)
    mat_shard, vec_shard = (
        lax.psum_scatter(
            jnp.concatenate([attn_mats, ffn_mats], axis=1), "fsdp", scatter_dimension=0, tiled=True
        ),
        lax.psum_scatter(
            jnp.concatenate([attn_vec, ffn_vec], axis=1), "fsdp", scatter_dimension=0, tiled=True
        ),
    )
    mat_part = lax.psum_scatter(
        mat_shard.astype(jnp.bfloat16), "rep", scatter_dimension=1, tiled=True
    ).astype(jnp.float32)
    vec_shard = lax.psum(vec_shard, "rep")
    mat_shard = lax.all_gather(mat_part.astype(jnp.bfloat16), "rep", axis=1, tiled=True).astype(
        mat_part.dtype
    )
    grad_rows = d_inputs.astype(jnp.bfloat16)
    back_pair = (
        lax.all_to_all(
            layer_rows.reshape(peers, share_rows, D),
            "fsdp",
            split_axis=0,
            concat_axis=0,
            tiled=True,
        ),
        lax.all_to_all(
            grad_rows.reshape(peers, share_rows, D), "fsdp", split_axis=0, concat_axis=0, tiled=True
        ),
    )
    layer_out = (
        jnp.zeros((TOK_DEV, D), jnp.bfloat16).at[order_ids].set(back_pair[0].reshape(TOK_DEV, D))
    )
    input_grad = (
        jnp.zeros((TOK_DEV, D), jnp.bfloat16).at[order_ids].set(back_pair[1].reshape(TOK_DEV, D))
    )
    slot_count = stat_left.shape[0]
    rows_dev = flat_weights.shape[0]
    targets = (
        jnp.arange(slot_count, dtype=jnp.int32)[:, None, None]
        + slot_count * jnp.arange(peers, dtype=jnp.int32)[None, :, None]
    )
    select = (owner_slot[None, None, :] == targets).astype(jnp.float32)
    grad_pieces = mat_shard.reshape(rows_dev, NBLK, D)
    outbound = jnp.einsum("snb,rbc->snrc", select, grad_pieces, precision=PRECISE)
    inbound = lax.all_to_all(
        outbound.astype(jnp.bfloat16), "fsdp", split_axis=1, concat_axis=1, tiled=True
    ).astype(outbound.dtype)
    grad_blocks = inbound.reshape(slot_count, D, D)
    new_left = STAT_DECAY * stat_left + (1.0 - STAT_DECAY) * jnp.einsum(
        "sij,skj->sik", grad_blocks, grad_blocks, precision=PRECISE
    )
    new_right = STAT_DECAY * stat_right + (1.0 - STAT_DECAY) * jnp.einsum(
        "sji,sjk->sik", grad_blocks, grad_blocks, precision=PRECISE
    )
    left_applied = jnp.einsum("sij,sjk->sik", root_left, grad_blocks, precision=PRECISE)
    direction = jnp.einsum("sij,sjk->sik", left_applied, root_right, precision=PRECISE)
    update = direction * lax.rsqrt(
        jnp.mean(direction * direction, axis=(1, 2), keepdims=True) + RMS_EPS
    )
    returned = lax.all_to_all(
        update.reshape(slot_count, peers, rows_dev, D).astype(jnp.bfloat16),
        "fsdp",
        split_axis=1,
        concat_axis=1,
        tiled=True,
    ).astype(jnp.float32)
    step_matrix = jnp.einsum("snb,snrc->rbc", select, returned, precision=PRECISE).reshape(
        rows_dev, NBLK * D
    )
    new_weights = flat_weights - LR_MATRIX * step_matrix
    first_bias = 1.0 - BETA_ONE**STEP
    second_bias = 1.0 - BETA_TWO**STEP
    new_first = BETA_ONE * moment_first + (1.0 - BETA_ONE) * vec_shard
    new_second = BETA_TWO * moment_second + (1.0 - BETA_TWO) * vec_shard * vec_shard
    first_fixed = new_first / first_bias
    second_fixed = new_second / second_bias
    new_vectors = vectors - LR_VECTOR * first_fixed / (jnp.sqrt(second_fixed) + ADAM_EPS)
    return (
        layer_out,
        input_grad,
        mat_shard,
        new_weights,
        new_left,
        new_right,
        new_first,
        new_second,
        new_vectors,
    )


def solution(mesh):
    in_specs = (
        P(("rep", "fsdp"), None),
        P(("rep", "fsdp"), None),
        P(("rep", "fsdp")),
        P(("rep", "fsdp"), None),
        P(("rep", "fsdp"), None, None),
        P(),
        P("fsdp", None),
        P("fsdp", None),
        P("fsdp", None),
        P("fsdp", None),
        P("fsdp", None, None),
        P("fsdp", None, None),
        P("fsdp", None, None),
        P("fsdp", None, None),
    )
    out_specs = (
        P(("rep", "fsdp"), None),
        P(("rep", "fsdp"), None),
        P("fsdp", None),
        P("fsdp", None),
        P("fsdp", None, None),
        P("fsdp", None, None),
        P("fsdp", None),
        P("fsdp", None),
        P("fsdp", None),
    )
    shaped = mesh.shape["fsdp"] == 8 and mesh.shape["rep"] == 4
    body = fast_body if shaped else plain_body
    return jax.shard_map(body, mesh=mesh, in_specs=in_specs, out_specs=out_specs, check_vma=False)
```

```python
import functools

import jax
import jax.numpy as jnp
from jax import lax
from jax.experimental import pallas as pl
from jax.experimental.pallas import tpu as pltpu
from jax.sharding import PartitionSpec as P

D = 768
H = 12
HD = 64
FF = 3072
BLK = 64
NGLOB = 2
NRAND = 3
STEP = 10
SEQ_DEV = 4
TOK_DEV = 512
NBLK = 12


NORM_EPS = 1e-12
MASKED_SCORE = -1e30
STAT_DECAY = 0.5
LR_MATRIX = 0.02
LR_VECTOR = 0.1
BETA_ONE = 0.9
BETA_TWO = 0.999
ADAM_EPS = 1e-08
RMS_EPS = 1e-12
PRECISE = lax.Precision.HIGHEST


def layout(lengths):
    blocks = (lengths + (BLK - 1)) // BLK
    block_ends = jnp.cumsum(blocks)
    starts = (block_ends - blocks) * BLK
    slot_ids = jnp.arange(TOK_DEV, dtype=jnp.int32)
    seq_id = jnp.sum((slot_ids // BLK)[:, None] >= block_ends[None, :], axis=1)
    member = seq_id[:, None] == jnp.arange(SEQ_DEV, dtype=jnp.int32)[None, :]
    seq_start = jnp.sum(jnp.where(member, starts[None, :], 0), axis=1)
    length = jnp.sum(jnp.where(member, lengths[None, :], 0), axis=1)
    seq_blocks = jnp.sum(jnp.where(member, blocks[None, :], 0), axis=1)
    position = slot_ids - seq_start
    in_use = position < length
    return (seq_id, position, in_use, seq_blocks)


def random_keys(raw_picks, seq_blocks):
    per_block = seq_blocks.reshape(TOK_DEV // BLK, BLK)[:, 0]
    picked = raw_picks % jnp.maximum(per_block, 1)[:, None, None]
    return jnp.repeat(picked, BLK, axis=0)


def allowed(q_seq, q_pos, q_use, q_pick, q_slot, k_seq, k_pos, k_use, k_slot):
    q_block = q_pos // BLK
    k_block = k_pos // BLK
    same_seq = (q_seq[:, None] == k_seq[None, :]) & q_use[:, None] & k_use[None, :]
    nearby = (
        (q_block[:, None] < NGLOB)
        | (k_block[None, :] < NGLOB)
        | (jnp.abs(q_block[:, None] - k_block[None, :]) <= 1)
    )
    chosen = jnp.zeros((H, q_seq.shape[0], k_seq.shape[0]), dtype=jnp.bool_)
    for number in range(NRAND):
        chosen = chosen | (
            k_block[None, None, :] == jnp.transpose(q_pick[:, :, number])[:, :, None]
        )
    alone = jnp.logical_not(q_use)[:, None] & (q_slot[:, None] == k_slot[None, :])
    return (same_seq & nearby)[None] | same_seq[None] & chosen | alone[None]


def layer_norm(hidden, gain, shift):
    center = hidden - jnp.mean(hidden, axis=-1, keepdims=True)
    spread = jnp.mean(center * center, axis=-1, keepdims=True)
    return center * lax.rsqrt(spread + NORM_EPS) * gain + shift


def gelu_tanh(pre_act):
    return jax.nn.gelu(pre_act, approximate=True)


def contract_rows(left, right):
    return lax.dot_general(
        left, right, (((0,), (0,)), ((), ())), preferred_element_type=jnp.float32
    )


def contract_cols(left, right):
    return lax.dot_general(
        left, right, (((1,), (1,)), ((), ())), preferred_element_type=jnp.float32
    )


MESH = pl.DeviceIdType.MESH
HALF = 48
GCOLS = 3072
JCOLS = 384
MIB = 2**20


class Here:
    def __init__(self, corner=False):
        r, f = lax.axis_index("rep"), lax.axis_index("fsdp")
        self.r, self.f = r, f
        self.x, self.y = lax.rem(r, 2), lax.div(r, 2)
        self.z, self.c = lax.div(f, 2), lax.rem(f, 2)
        self.to_x = (r + 1 - 2 * self.x, f)
        self.to_y = (r + 2 - 4 * self.y, f)
        self.to_d = (3 - r, f)
        self.corner = corner
        self.to_core = (r, f + 1 - 2 * self.c)

    def z_plus(self, step):
        return lax.rem(self.z + step, 4)

    def along(self, step):
        return (self.r, 2 * self.z_plus(step) + self.c)

    def peer(self, step):
        return lax.rem(self.f + step, 8)

    def pair(self, step):
        zz = (self.z, self.z + 1 - 2 * lax.rem(self.z, 2), lax.rem(self.z + 2, 4), 3 - self.z)[step // 2 % 4]
        return 2 * zz + (1 - self.c if step % 2 else self.c)

    def greet(self):
        barrier = pltpu.get_barrier_semaphore()
        friends = [self.to_x, self.to_y] + [self.to_d] * self.corner
        friends += [(self.r, self.peer(s)) for s in range(1, 8)]
        for friend in friends:
            pl.semaphore_signal(barrier, inc=1, device_id=friend, device_id_type=MESH)
        return lambda: pl.semaphore_wait(barrier, len(friends))


def send(src, dst, send_sem, recv_sem, device):
    copy = pltpu.make_async_remote_copy(
        src_ref=src,
        dst_ref=dst,
        send_sem=send_sem,
        recv_sem=recv_sem,
        device_id=device,
        device_id_type=MESH,
    )
    copy.start()
    return copy


def local(src, dst, sem):
    copy = pltpu.make_async_copy(src, dst, sem)
    copy.start()
    return copy


def cols(start, width):
    return pl.ds(pl.multiple_of(start, 128), width)


def forward_kernel(
    lengths, place, tok, cot, wf, vec, raw, root_l, root_r,
    o0, o1, o2, o_vt, o_x, o_cot, o_qkv, o_p, o_mix, o_n1, o_r1, o_u, o_f, o_dg, o_n2, o_r2, o_y, o_root, o_use, o_hot,
    w0, w1, w2, tok_in, cot_in, vec_in, tok_s, cot_s,
    tok_v, cot_v, pre_a, pre_b, hot, use, use_row, wide_w, vec_s, vt, qkv, P, mix, n1, r1, x1, u, fa, dg, n2, r2, yo, xT, mT, uT, feat, stg, rb,
    wl, zs, zr, xs, xr, ys, yr, ds, dr, cs, cr, ls, ts, tr, os, ks,
):
    low, f32 = jnp.bfloat16, jnp.float32
    here = Here()
    wait_all = here.greet()
    x, y, z, c, f = here.x, here.y, here.z, here.c, here.f
    whole = [w0, w1, w2]
    whole_out = [o0, o1, o2]
    wide = GCOLS // 2
    sent = []
    outs = []
    count = [0]

    def keep(src, dst):
        outs.append(local(src, dst, os.at[count[0]]))
        count[0] += 1

    tok_load = local(tok, tok_v, ks.at[5])
    cot_load = local(cot, cot_v, ks.at[6])
    fetched = [
        local(wf.at[:, :, g * GCOLS : (g + 1) * GCOLS], wide_w.at[:, :, g * GCOLS : (g + 1) * GCOLS], ks.at[2 + g])
        for g in range(3)
    ]

    def narrow(g):
        fetched[g].wait()

        def one(i, _):
            h, part = lax.div(i, 4), lax.rem(i, 4)
            at = cols(g * GCOLS + part * D, D)
            wl[h, :, at] = wide_w[h, :, at].astype(low)
            return 0

        lax.fori_loop(0, 8, one, 0)
        return local(wl.at[:, :, g * GCOLS : (g + 1) * GCOLS], whole[g].at[z, c], ls.at[g])

    inner = lax.rem(lax.div(z + 1, 2), 2)
    upper = lax.div(z, 2)
    end = 3 * upper

    def source(step):
        near = step - inner if step == 1 else step
        return near + upper * (3 - 2 * near)

    def line(zz):
        return (here.r, 2 * zz + c)

    def own_part(g):
        return wl.at[x, :, cols(g * GCOLS + y * wide, wide)]

    def landed(g, src):
        return whole[g].at[src, c, x, :, cols(y * wide, wide)]

    def z_own(g, second):
        first_to = 1 + upper + inner * (1 - 2 * upper)
        second_to = inner * end + (1 - inner) * (2 - upper)
        return pltpu.make_async_remote_copy(
            src_ref=own_part(g), dst_ref=landed(g, z), send_sem=zs.at[g, int(second)], recv_sem=zr.at[g, z],
            device_id=line(second_to if second else first_to), device_id_type=MESH,
        )

    def z_pass(g, step):
        part = landed(g, source(step))
        return pltpu.make_async_remote_copy(
            src_ref=part, dst_ref=part, send_sem=zs.at[g, 1 + step], recv_sem=zr.at[g, source(step)],
            device_id=line(end), device_id_type=MESH,
        )

    def z_send(g):
        z_own(g, False).start()
        z_own(g, True).start()

    def z_finish(g):
        z_own(g, False).wait_send()
        z_own(g, True).wait_send()

        @pl.when(inner == 1)
        def _():
            for step in (2, 3):
                z_pass(g, step).wait_send()

    def rows_out(table, landing, number):
        out = []
        for step in range(1, 8):
            to = here.pair(step)
            src = table if number == 2 else table.at[to]
            out.append(
                send(src, landing.at[f], ts.at[number, step - 1], tr.at[number, step - 1], (here.r, to))
            )
        sent.extend(out)
        return out

    planes = {0: {}, 1: {}, 2: {}}

    def plane(g, step):
        moving = z_pass(g, step)
        moving.wait_recv()

        if step > 1:

            @pl.when(inner == 1)
            def _():
                moving.start()

        src = source(step)
        part = landed(g, src)
        xc = send(part, part, xs.at[g, src], xr.at[g, src], here.to_x)
        yc = send(part, part, ys.at[g, src], yr.at[g, src], here.to_y)
        planes[g][step] = (xc, yc)
        sent.extend([xc, yc])
        if step == 3:
            core(g, 0, x, y)

    cores = {0: [], 1: [], 2: []}

    def core(g, number, h, j):
        part = whole[g].at[:, c, h, :, cols(j * wide, wide)]
        copy = send(part, part, cs.at[g, number], cr.at[g, number], here.to_core)
        sent.append(copy)
        cores[g].append(copy)

    turns = {0: [], 1: [], 2: []}

    def turn(g, step):
        src = source(step)
        xc, yc = planes[g][step]
        xc.wait_recv()
        part = whole[g].at[src, c, 1 - x, :, cols(y * wide, wide // 2)]
        one = send(part, part, ds.at[g, 0, src], dr.at[g, 0, src], here.to_y)
        yc.wait_recv()
        part = whole[g].at[src, c, x, :, cols((1 - y) * wide + wide // 2, wide // 2)]
        two = send(part, part, ds.at[g, 1, src], dr.at[g, 1, src], here.to_x)
        sent.extend([one, two])
        turns[g].extend([one, two])
        if step == 3:
            core(g, 1, 1 - x, y)
            core(g, 2, x, 1 - y)

    def last(g):
        for copy in turns[g]:
            copy.wait_recv()
        core(g, 3, 1 - x, 1 - y)

    def ready(g):
        for copy in cores[g]:
            copy.wait_recv()
        keep(whole[g], whole_out[g])

    def square(ref, at):
        return ref[:, :, :, :, at].reshape(D, at.size)

    def order(source, target):
        target[...] = jnp.dot(hot[...], source[...], preferred_element_type=f32).astype(low).reshape(8, 64, D)

    def layout_rows():
        sizes = [lengths[0, s] for s in range(SEQ_DEV)]
        blocks = [lax.div(size + (BLK - 1), BLK) for size in sizes]
        ends = [blocks[0]]
        for s in range(1, SEQ_DEV):
            ends.append(ends[-1] + blocks[s])

        def where_is(number):
            seq = jnp.zeros_like(number)
            for s in range(SEQ_DEV):
                seq = seq + (number >= ends[s]).astype(jnp.int32)
            first, size, count = jnp.zeros_like(number), jnp.zeros_like(number), jnp.zeros_like(number)
            for s in range(SEQ_DEV):
                first = jnp.where(seq == s, ends[s] - blocks[s], first)
                size = jnp.where(seq == s, sizes[s], size)
                count = jnp.where(seq == s, blocks[s], count)
            return seq, number - first, size, count

        slot = lax.broadcasted_iota(jnp.int32, (8, TOK_DEV), 1)
        key_seq, key_block, size, _ = where_is(lax.div(slot, BLK))
        used = key_block * BLK + lax.rem(slot, BLK) < size
        used_f = used.astype(f32)
        use_row[...] = used_f
        use[...] = jnp.transpose(jnp.concatenate([used_f] * 16, axis=0))
        row_seq, row_block, _, count = where_is(lax.broadcasted_iota(jnp.int32, (8, 128), 0))
        row_seq, row_block, count = row_seq[:, 0:1], row_block[:, 0:1], jnp.maximum(count[:, 0:1], 1)
        same = (row_seq == key_seq) & used
        near = (row_block < NGLOB) | (key_block < NGLOB) | (jnp.abs(row_block - key_block) <= 1)
        picks = []
        for number in range(NRAND):
            pick = raw[number]
            for _ in range(7):
                pick = jnp.where(pick >= count, pick - count, pick)
            picks.append(pick)
        gap = jnp.zeros((BLK - 8, TOK_DEV), f32)
        for head in range(H):
            keep_it = near
            for pick in picks:
                keep_it = keep_it | (key_block == pick[:, head : head + 1])
            rows = jnp.where(same & keep_it, 0.0, MASKED_SCORE)
            feat[head] = jnp.transpose(jnp.concatenate([rows, gap, rows, gap], axis=0)).astype(low)

    def places():
        spot = (
            lax.div(place[...], TOK_DEV) * 64 + lax.rem(place[...], TOK_DEV) - f * 64
        )
        hot[...] = (
            (lax.broadcasted_iota(jnp.int32, (TOK_DEV, TOK_DEV), 0) == spot).astype(f32).astype(low)
        )
        return spot

    def places_back(spot):
        tall = jnp.transpose(jnp.broadcast_to(spot.astype(f32), (128, TOK_DEV)))
        lane = lax.broadcasted_iota(jnp.int32, (TOK_DEV, TOK_DEV), 1).astype(f32)
        hot[...] = (tall[:, 0:1] == lane).astype(f32).astype(low)
        keep(hot, o_hot)

    def project():
        for part in range(3):
            to = pl.ds(part * D, D)
            acc = jnp.dot(tok_in[...].reshape(TOK_DEV, D), square(w0, to), preferred_element_type=f32)
            if part == 0:
                acc = (acc + vt[0:1, :]) * (HD ** (-0.5))
            if part == 2:
                acc = acc + vt[1:2, :]
            qkv[:, to] = acc.astype(low)

    root_load = []

    def root_fetch(number):
        ref = (root_l, root_r)[number // 2]
        root_load.append(local(ref.at[number % 2], stg, ks.at[0]))

    def roots(number):
        root_load[number].wait()
        if number:
            root_out[number - 1].wait()

        def one(i, _):
            at = pl.ds(pl.multiple_of(i * 96, 96), 96)
            rb[lax.div(i, 2), lax.rem(i, 2)] = stg[at, :].astype(low).reshape(2, HALF, D)
            return 0

        lax.fori_loop(0, 8, one, 0)
        root_out.append(local(rb, o_root.at[number], ks.at[1]))
        if number < 3:
            root_fetch(number + 1)
        else:
            root_out[3].wait()

    root_out = []
    root_fetch(0)

    def attend(start, stop):
        def pair(i, _):
            at = cols(i * 128, 128)
            q2, k2 = qkv[:, at], qkv[:, cols(D + i * 128, 128)]
            v2 = qkv[:, cols(2 * D + i * 128, 128)]
            lane = lax.broadcasted_iota(jnp.int32, (TOK_DEV, 128), 1)
            row = lax.broadcasted_iota(jnp.int32, (TOK_DEV, 128), 0)
            spot = (lax.rem(lane, BLK) == lax.div(row, BLK)).astype(f32).astype(low)
            vT = jnp.transpose(v2)
            parts = []
            for half in range(2):
                mine = (lane < HD) if half == 0 else (lane >= HD)
                qm = jnp.where(mine, q2, spot)
                km = jnp.where(mine, k2, feat[2 * i + half])
                s = lax.dot_general(km, qm, (((1,), (1,)), ((), ())), preferred_element_type=f32)
                e = jnp.exp(s - jnp.max(s, axis=0, keepdims=True))
                p = (e * (use_row[0:1, :] / jnp.sum(e, axis=0, keepdims=True))).astype(low)
                P[2 * i + half] = p
                parts.append(jnp.dot(vT[half * HD : (half + 1) * HD], p, preferred_element_type=f32))
            total = jnp.where(use_row[0:1, :] > 0, jnp.concatenate(parts, axis=0), vT.astype(f32)).astype(low)
            mT[cols(i * 128, 128), :] = total
            mix[:, at] = jnp.transpose(total)
            return 0

        if stop - start == 1:
            pair(start, 0)
        else:
            lax.fori_loop(start, stop, pair, 0)

    def flip(source, target):
        def one(i, _):
            at = cols(i * 128, 128)
            target[at, :] = jnp.transpose(source(at))
            return 0

        lax.fori_loop(0, 6, one, 0)

    def join():
        def one(i, _):
            at = cols(i * 256, 256)
            acc = jnp.dot(mix[...], square(w0, cols(3 * D + i * 256, 256)), preferred_element_type=f32)
            x1[:, at] = tok_in[:, :, at].reshape(TOK_DEV, 256).astype(f32) + (acc + vt[2:3, at])
            return 0

        lax.fori_loop(0, 3, one, 0)

    def norm(ref, i):
        at = pl.ds(pl.multiple_of(i * 128, 128), 128)
        h = ref[at, :]
        center = h - jnp.mean(h, axis=1, keepdims=True)
        r = lax.rsqrt(jnp.mean(center * center, axis=1, keepdims=True) + NORM_EPS)
        return at, center * r, r

    def norm_one():
        def one(i, _):
            at, n, r = norm(x1, i)
            n1[at, :] = n
            r1[at, :] = jnp.broadcast_to(r, (128, 128))
            out = n * vt[4:5, :] + vt[5:6, :]
            u[at, :] = out.astype(low)
            x1[at, :] = out
            return 0

        lax.fori_loop(0, 4, one, 0)

    def lift(begin):
        def raise_to(target, i):
            target[...] = jnp.dot(u[...], square(w1, cols(i * 256, 256)), preferred_element_type=f32)

        def bend(source, i):
            row = lax.div(i, 3)
            pre = source[...] + vt[pl.ds(8 + row, 1), cols((i - 3 * row) * 256, 256)]
            sq = pre * pre
            half = 0.5 * jnp.tanh(pre * (0.7978845608028654 + 0.035677408136300125 * sq)) + 0.5
            act = pre * half
            to = cols(i * 256, 256)
            fa[:, to] = act.astype(low)
            slope = 1.5957691216057308 + 0.21406444881780075 * sq
            dg[:, to] = (half + act * (1.0 - half) * slope).astype(low)

        raise_to(pre_a, begin)

        def two(k, _):
            i = begin + 2 * k
            raise_to(pre_b, i + 1)
            bend(pre_a, i)
            raise_to(pre_a, jnp.minimum(i + 2, 11))
            bend(pre_b, i + 1)
            return 0

        lax.fori_loop(0, 3, two, 0)

    def drop():
        def one(i, _):
            at = cols(i * 512, 512)
            acc = lax.dot_general(
                fa[:, at], square(w2, at), (((1,), (1,)), ((), ())), preferred_element_type=f32
            )
            x1[...] += acc
            return 0

        lax.fori_loop(0, 6, one, 0)

    def norm_two():
        def one(i, _):
            at = pl.ds(pl.multiple_of(i * 128, 128), 128)
            x1[at, :] = x1[at, :] + vt[3:4, :]
            at, n, r = norm(x1, i)
            n2[at, :] = n
            r2[at, :] = jnp.broadcast_to(r, (128, 128))
            out = (n * vt[6:7, :] + vt[7:8, :]) * use[at, 0:1]
            yo[at, :] = out.astype(low)
            return 0

        lax.fori_loop(0, 4, one, 0)

    stays = [narrow(0)]
    wait_all()
    z_send(0)
    vec_s[...] = jnp.zeros_like(vec_s)
    vec_s[:NBLK, :96] = vec[...].astype(low)
    small = rows_out(vec_s, vec_in, 2)
    own = [local(vec_s, vec_in.at[f], ls.at[5])]
    stays.append(narrow(1))
    z_send(1)
    spot = places()
    plane(0, 1)
    tok_load.wait()
    order(tok_v, tok_s)
    own.append(local(tok_s.at[f], tok_in.at[f], ls.at[3]))
    plane(0, 2)
    cot_load.wait()
    order(cot_v, cot_s)
    own.append(local(cot_s.at[f], cot_in.at[f], ls.at[4]))
    stays.append(narrow(2))
    stays[0].wait()
    plane(0, 3)
    t0 = rows_out(tok_s, tok_in, 0)
    for copy in stays[1:] + own:
        copy.wait()
    layout_rows()
    keep(use, o_use)
    turn(0, 1)
    plane(1, 1)
    for copy in small:
        copy.wait_recv()
    for n in range(8):
        vt[:, n * 96 : (n + 1) * 96] = vec_in[n, :, :96].astype(f32)
    keep(vt, o_vt)
    places_back(spot)
    turn(0, 2)
    plane(1, 2)
    roots(0)
    turn(0, 3)
    plane(1, 3)
    roots(1)
    last(0)
    z_send(2)
    roots(2)
    roots(3)
    ready(0)
    turn(1, 1)
    for copy in t0:
        copy.wait_recv()
    project()
    keep(qkv, o_qkv)
    turn(1, 2)
    plane(2, 1)
    attend(0, 1)
    turn(1, 3)
    plane(2, 2)
    attend(1, 2)
    last(1)
    attend(2, 3)
    plane(2, 3)
    t1 = rows_out(cot_s, cot_in, 1)
    attend(3, 4)
    turn(2, 1)
    attend(4, 5)
    attend(5, 6)
    keep(P, o_p)
    keep(mT, o_mix)
    turn(2, 2)
    join()
    norm_one()
    turn(2, 3)
    keep(n1, o_n1)
    keep(r1, o_r1)
    ready(1)
    lift(0)
    last(2)
    lift(6)
    keep(fa, o_f)
    keep(dg, o_dg)
    flip(lambda at: tok_in[:, :, at].reshape(TOK_DEV, 128), xT)
    keep(xT, o_x)
    flip(lambda at: u[:, at], uT)
    keep(uT, o_u)
    ready(2)
    drop()
    norm_two()
    keep(n2, o_n2)
    keep(r2, o_r2)
    keep(yo, o_y)
    for copy in t1:
        copy.wait_recv()
    keep(cot_in, o_cot)
    for g in range(3):
        z_finish(g)
    for copy in sent:
        copy.wait_send()
    for copy in outs:
        copy.wait()


def forward_all(lengths, place, tok, cot, flat_weights, vec, raw, root_l, root_r):
    any_spec = pl.BlockSpec(memory_space=pl.ANY)
    vmem = pl.BlockSpec(memory_space=pltpu.VMEM)
    dma = pltpu.SemaphoreType.DMA
    shape = jax.ShapeDtypeStruct
    low, f32 = jnp.bfloat16, jnp.float32
    square = (4, 2, 2, HALF, GCOLS)
    saved = [
        ((16, D), f32), ((D, TOK_DEV), low), ((8, 64, D), low), ((TOK_DEV, 3 * D), low),
        ((H, TOK_DEV, TOK_DEV), low), ((D, TOK_DEV), low), ((TOK_DEV, D), f32), ((TOK_DEV, 128), f32),
        ((D, TOK_DEV), low), ((TOK_DEV, FF), low), ((TOK_DEV, FF), low), ((TOK_DEV, D), f32),
        ((TOK_DEV, 128), f32), ((TOK_DEV, D), low), ((4, 4, 2, 2, HALF, D), low),
        ((TOK_DEV, 128), f32), ((TOK_DEV, TOK_DEV), low),
    ]
    return pl.pallas_call(
        forward_kernel,
        out_shape=[shape(square, low)] * 3 + [shape(*s) for s in saved],
        in_specs=[pl.BlockSpec(memory_space=pltpu.SMEM)] + [vmem] + [any_spec] * 3 + [vmem] * 2 + [any_spec] * 2,
        out_specs=[any_spec] * 20,
        scratch_shapes=[
            pltpu.VMEM(square, low), pltpu.VMEM(square, low), pltpu.VMEM(square, low),
            pltpu.VMEM((8, 64, D), low), pltpu.VMEM((8, 64, D), low), pltpu.VMEM((8, 16, 128), low),
            pltpu.VMEM((8, 64, D), low), pltpu.VMEM((8, 64, D), low),
            pltpu.VMEM((TOK_DEV, D), low),
            pltpu.VMEM((TOK_DEV, D), low),
            pltpu.VMEM((TOK_DEV, 256), f32),
            pltpu.VMEM((TOK_DEV, 256), f32),
            pltpu.VMEM((TOK_DEV, TOK_DEV), low),
            pltpu.VMEM((TOK_DEV, 128), f32),
            pltpu.VMEM((8, TOK_DEV), f32),
            pltpu.VMEM((2, HALF, 3 * GCOLS), f32),
            pltpu.VMEM((16, 128), low),
            pltpu.VMEM((16, D), f32),
            pltpu.VMEM((TOK_DEV, 3 * D), low),
            pltpu.VMEM((H, TOK_DEV, TOK_DEV), low),
            pltpu.VMEM((TOK_DEV, D), low),
            pltpu.VMEM((TOK_DEV, D), f32),
            pltpu.VMEM((TOK_DEV, 128), f32),
            pltpu.VMEM((TOK_DEV, D), f32),
            pltpu.VMEM((TOK_DEV, D), low),
            pltpu.VMEM((TOK_DEV, FF), low),
            pltpu.VMEM((TOK_DEV, FF), low),
            pltpu.VMEM((TOK_DEV, D), f32),
            pltpu.VMEM((TOK_DEV, 128), f32),
            pltpu.VMEM((TOK_DEV, D), low),
            pltpu.VMEM((D, TOK_DEV), low), pltpu.VMEM((D, TOK_DEV), low), pltpu.VMEM((D, TOK_DEV), low),
            pltpu.VMEM((H, TOK_DEV, 128), low),
            pltpu.VMEM((D, D), f32),
            pltpu.VMEM((4, 2, 2, HALF, D), low),
            pltpu.VMEM((2, HALF, 3 * GCOLS), low),
            dma((3, 5)), dma((3, 4)), dma((3, 4)), dma((3, 4)), dma((3, 4)), dma((3, 4)),
            dma((3, 2, 4)), dma((3, 2, 4)), dma((3, 4)), dma((3, 4)),
            dma((6,)), dma((3, 7)), dma((3, 7)), dma((19,)), dma((7,)),
        ],
        compiler_params=pltpu.CompilerParams(
            collective_id=0, has_side_effects=True, vmem_limit_bytes=60 * MIB
        ),
        name="forward_all",
    )(lengths, place, tok, cot, flat_weights.reshape(2, HALF, 3 * GCOLS), vec, raw, root_l, root_r)


def backward_kernel(
    owner, vt, use,
    h_w0, h_w1, h_w2, h_xT, h_cot, h_qkv, h_p, h_mT, h_n1, h_r1, h_uT, h_f, h_dg, h_n2, h_r2, h_y, h_root,
    o_back, o_grad, WR, UA, SC, o_gs, o_vec,
    G, Rc, A1, A2, B1, B2, ZR, ZP, F, SO, Gs, wa, wb, fb, gb, low_g, LT, LU, hb, nb, PT, r1, r2, gi,
    PQ, sq, sr_in, sc_out, vb, vr,
    ld, pd, cs, cr, a1s, a1r, b1s, b1r, a2s, a2r, b2s, b2r, zs, zr,
    fs, fr, ts, tr, ss, sr, ps, pr, us, ur, qs, qr, es, er, ms, mr, vs, vrs, ls,
):
    low, f32 = jnp.bfloat16, jnp.float32
    here = Here(True)
    wait_all = here.greet()
    x, y, z, c, f, r = here.x, here.y, here.z, here.c, here.f, here.r
    W = GCOLS // 2
    sent = []

    class Load:
        def __init__(self, number, src, dst):
            self.copy, self.done = local(src, dst, ld.at[number]), False

        def wait(self):
            if not self.done:
                self.copy.wait()
                self.done = True

    cot_l = Load(0, h_cot, gi)
    n2_l = Load(1, h_n2, hb)
    r2_l = Load(2, h_r2, r2)
    f_l = Load(3, h_f, fb)
    wd_l = Load(4, h_w2, wa)
    dg_l = Load(5, h_dg, gb)
    uT_l = Load(6, h_uT, LU)
    wu_l = Load(7, h_w1, wb)
    n1_l = Load(8, h_n1, nb)
    r1_l = Load(9, h_r1, r1)
    vb[...] = jnp.zeros_like(vb)
    wait_all()

    chunks = [(8, 2), (10, 2), (4, 2), (6, 2), (3, 1), (0, 1), (1, 1), (2, 1)]

    def span(n):
        block, count = chunks[n]
        return pl.ds(block * JCOLS, count * JCOLS)

    ways = {}

    def c_send(n):
        at = span(n)
        ways[n] = [
            send(G.at[:, :, 1 - c, :, :, at], Rc.at[:, :, :, :, at], cs.at[n], cr.at[n], here.to_core)
        ]
        sent.extend(ways[n])

    def first(n):
        at = span(n)
        ways[n][0].wait_recv()

        def add(j, zz, h):
            G[j, zz, c, h, :, at] = (
                G[j, zz, c, h, :, at].astype(f32) + Rc[j, zz, h, :, at].astype(f32)
            ).astype(low)

        def add_a(i, _):
            add(lax.div(i, 2), lax.rem(i, 2), 1 - x)
            return 0

        def add_b(i, _):
            add(1 - y, 2 + lax.div(i, 2), lax.rem(i, 2))
            return 0

        def add_rest(i, _):
            add(lax.div(i, 2), lax.rem(i, 2), x)
            add(y, 2 + lax.div(i, 2), lax.rem(i, 2))
            return 0

        lax.fori_loop(0, 4, add_a, 0)
        a = send(G.at[:, 0:2, c, 1 - x, :, at], A1.at[:, :, :, at], a1s.at[n], a1r.at[n], here.to_x)
        lax.fori_loop(0, 4, add_b, 0)
        b = send(G.at[1 - y, 2:4, c, :, :, at], B1.at[:, :, :, at], b1s.at[n], b1r.at[n], here.to_y)
        lax.fori_loop(0, 4, add_rest, 0)
        ways[n] = [a, b]
        sent.extend(ways[n])

    def second(n):
        at = span(n)
        ways[n][0].wait_recv()

        def add_a(i, _):
            for j in (1 - y, y):
                G[j, i, c, x, :, at] = (
                    G[j, i, c, x, :, at].astype(f32) + A1[j, i, :, at].astype(f32)
                ).astype(low)
            return 0

        lax.fori_loop(0, 2, add_a, 0)
        a = send(G.at[1 - y, 0:2, c, x, :, at], A2.at[:, :, at], a2s.at[n], a2r.at[n], here.to_y)
        ways[n][1].wait_recv()

        def add_b(i, _):
            for h in (1 - x, x):
                G[y, i + 2, c, h, :, at] = (
                    G[y, i + 2, c, h, :, at].astype(f32) + B1[i, h, :, at].astype(f32)
                ).astype(low)
            return 0

        lax.fori_loop(0, 2, add_b, 0)
        b = send(G.at[y, 2:4, c, 1 - x, :, at], B2.at[:, :, at], b2s.at[n], b2r.at[n], here.to_x)
        ways[n] = [a, b]
        sent.extend(ways[n])

    def third(n):
        at = span(n)
        for number, (copy, part) in enumerate(zip(ways[n], (A2, B2))):
            copy.wait_recv()

            def add(i, _, number=number, part=part):
                zz = 2 * number + i
                G[y, zz, c, x, :, at] = (
                    G[y, zz, c, x, :, at].astype(f32) + part[i, :, at].astype(f32)
                ).astype(low)
                return 0

            lax.fori_loop(0, 2, add, 0)
        partner = z + 1 - 2 * lax.rem(z, 2)
        near = send(
            G.at[y, partner, c, x, :, at], ZR.at[0, :, at], zs.at[n, 0], zr.at[n, 0],
            (r, 2 * partner + c),
        )
        sent.append(near)
        ways[n] = [near]

        @pl.when(inner == 0)
        def _():
            passing(n).start()

    inner = lax.rem(lax.div(z + 1, 2), 2)
    far = 2 - 2 * lax.div(z, 2)

    def passing(n):
        at = span(n)
        return pltpu.make_async_remote_copy(
            src_ref=G.at[y, pl.ds(far, 2), c, x, :, at], dst_ref=ZP.at[:, :, at], send_sem=zs.at[n, 1],
            recv_sem=zr.at[n, 1], device_id=(r, 2 * (z + 1 - 2 * lax.rem(z, 2)) + c), device_id_type=MESH,
        )

    def crossing(n, i):
        at = span(n)
        return pltpu.make_async_remote_copy(
            src_ref=G.at[y, far + i, c, x, :, at], dst_ref=ZR.at[1, :, at], send_sem=zs.at[n, 2 + i],
            recv_sem=zr.at[n, 2], device_id=(r, 2 * (far + i) + c), device_id_type=MESH,
        )

    def fourth(n):
        at = span(n)

        @pl.when(inner == 1)
        def _():
            passing(n).wait_recv()
            for i in range(2):
                G[y, far + i, c, x, :, at] = (
                    G[y, far + i, c, x, :, at].astype(f32) + ZP[i, :, at].astype(f32)
                ).astype(low)
                crossing(n, i).start()

    def z_finish():
        for n in range(8):

            @pl.when(inner == 0)
            def _():
                passing(n).wait_send()

            @pl.when(inner == 1)
            def _():
                for i in range(2):
                    crossing(n, i).wait_send()

    def final(n):
        ways[n][0].wait_recv()
        crossing(n, 0).wait_recv()
        block, count = chunks[n]
        for b in range(block, block + count):
            at = pl.ds(b * JCOLS, JCOLS)
            total = G[y, z, c, x, :, at].astype(f32)
            for step in range(2):
                total = total + ZR[step, :, at].astype(f32)
            F[b] = total.astype(low)

    homes = []

    spreads = {}
    diagonals = []

    def spread(g):
        at = pl.ds(4 * g, 4)
        to = WR.at[x, y, at]
        a = send(F.at[at], to, fs.at[g, 0], fr.at[g, 0], here.to_x)
        b = send(F.at[at], to, fs.at[g, 1], fr.at[g, 1], here.to_y)
        homes.append(local(F.at[at], to, ls.at[g]))
        sent.extend([a, b])
        spreads[g] = (a, b)

    def spread_on(g):
        a, b = spreads[g]
        a.wait_recv()
        part = WR.at[1 - x, y, pl.ds(4 * g, 2)]
        da = send(part, part, fs.at[g, 2], fr.at[g, 2], here.to_y)
        b.wait_recv()
        part = WR.at[x, 1 - y, pl.ds(4 * g + 2, 2)]
        db = send(part, part, fs.at[g, 3], fr.at[g, 3], here.to_x)
        sent.extend([da, db])
        diagonals.extend([da, db])

    def token_send(source, landing, number):
        out = []
        for step in range(1, 8):
            to = here.pair(step)
            out.append(
                send(source(to), landing.at[f], ts.at[number, step - 1], tr.at[number, step - 1], (r, to))
            )
        homes.append(local(source(f), landing.at[f], ls.at[3 + number]))
        sent.extend(out)
        return out

    def square(ref, at):
        return ref[:, :, :, :, at].reshape(D, at.size)

    def own_rows(ref, core):
        return jnp.concatenate(
            [ref[pl.ds(pl.multiple_of((2 * zz + core) * 96, 96), 96), :] for zz in range(4)], axis=0
        )

    def gradient(left, right, block, start, count, core):
        rows = own_rows(left, core)

        def one(i, _):
            out = jnp.dot(rows, right[:, cols(start + i * D, D)], preferred_element_type=f32)
            out = out.astype(low).reshape(4, 2, HALF, D)
            for j in range(2):
                at = cols((block + i) * JCOLS, JCOLS)
                G[j, :, core, :, :, at] = out[:, :, :, j * JCOLS : (j + 1) * JCOLS]
            return 0

        lax.fori_loop(0, count, one, 0)

    def eight(v):
        return jnp.sum(v.reshape(8, 8, v.shape[1]), axis=0)

    def norm_back(i, carry, grad, n, rr, gain):
        zed = grad * gain
        back = rr * (
            zed - jnp.mean(zed, axis=1, keepdims=True) - n * jnp.mean(zed * n, axis=1, keepdims=True)
        )
        rounded = back.astype(low)
        return back, rounded, (
            carry[0] + eight(grad * n), carry[1] + eight(grad), carry[2] + eight(rounded.astype(f32))
        )

    zero = jnp.zeros((8, D), f32)

    def put(row, total):
        vb[0, row : row + 1, :] = jnp.sum(total, axis=0, keepdims=True)

    def flip(source, target, count):
        def one(i, _):
            at = cols(i * 128, 128)
            target[at, :] = jnp.transpose(source[:, at])
            return 0

        lax.fori_loop(0, count, one, 0)

    ta = token_send(lambda to: h_y.at[to], o_back, 0)
    cot_l.wait()
    n2_l.wait()
    r2_l.wait()

    def back_two(i, carry):
        at = pl.ds(pl.multiple_of(i * 64, 64), 64)
        grad = gi[i].astype(f32) * use[at, 0:1]
        back, rounded, carry = norm_back(i, carry, grad, hb[at, :], r2[at, 0:1], vt[6:7, :])
        hb[at, :] = back
        low_g[at, :] = rounded
        return carry

    sums = lax.fori_loop(0, 8, back_two, (zero, zero, zero))
    put(6, sums[0])
    put(7, sums[1])
    put(3, sums[2])
    flip(low_g, LT, 6)
    f_l.wait()
    gradient(LT, fb, 8, 0, 2, 1 - c)
    c_send(0)
    gradient(LT, fb, 10, 2 * D, 2, 1 - c)
    c_send(1)
    gradient(LT, fb, 8, 0, 4, c)
    qkv_l = Load(10, h_qkv, fb.at[:, : 3 * D])
    mT_l = Load(11, h_mT, LT)
    wd_l.wait()
    dg_l.wait()

    def back_up(i, _):
        at = cols(i * 256, 256)
        acc = jnp.dot(low_g[...], square(wa, at), preferred_element_type=f32)
        gb[:, at] = (acc * gb[:, at].astype(f32)).astype(low)
        return 0

    first(0)
    lax.fori_loop(0, 6, back_up, 0)
    first(1)
    uT_l.wait()
    gradient(LU, gb, 4, 0, 2, 1 - c)
    c_send(2)
    lax.fori_loop(6, 12, back_up, 0)
    wq_l = Load(12, h_w0, wa)
    gradient(LU, gb, 4, 0, 2, c)
    first(2)
    gradient(LU, gb, 6, 2 * D, 2, 1 - c)
    c_send(3)
    gradient(LU, gb, 6, 2 * D, 2, c)
    xT_l = Load(13, h_xT, LU)
    second(0)
    first(3)
    wu_l.wait()

    def back_x1(i, _):
        at = cols(i * 512, 512)
        hb[...] += lax.dot_general(
            gb[:, at], square(wb, at), (((1,), (1,)), ((), ())), preferred_element_type=f32
        )
        return 0

    lax.fori_loop(0, 6, back_x1, 0)
    second(1)
    root_l = [Load(14 + n, h_root.at[n], wb.at[:, :, :, :, n * D : (n + 1) * D]) for n in range(4)]
    n1_l.wait()
    r1_l.wait()

    def back_one(i, carry):
        at = pl.ds(pl.multiple_of(i * 64, 64), 64)
        back, rounded, carry = norm_back(i, carry, hb[at, :], nb[at, :], r1[at, 0:1], vt[4:5, :])
        hb[at, :] = back
        low_g[at, :] = rounded
        return carry

    sums = lax.fori_loop(0, 8, back_one, (zero, zero, zero))
    put(4, sums[0])
    put(5, sums[1])
    put(2, sums[2])
    third(0)
    mT_l.wait()
    gradient(LT, low_g, 3, 0, 1, 1 - c)
    c_send(4)
    gradient(LT, low_g, 3, 0, 1, c)
    wq_l.wait()

    def back_mix(i, _):
        out = lax.dot_general(
            low_g[...], wa[pl.ds(2 * i, 2), :, :, :, 3 * D : 4 * D].reshape(JCOLS, D),
            (((1,), (1,)), ((), ())), preferred_element_type=f32,
        )
        gb[:, cols(3 * D + i * JCOLS, JCOLS)] = out.astype(low)
        return 0

    for row in range(4):

        def total(i, acc, row=row):
            at = pl.ds(pl.multiple_of(i * 64, 64), 64)
            return acc + eight(gb[at, row * D : (row + 1) * D].astype(f32))

        put(8 + row, lax.fori_loop(0, 8, total, zero))
    lax.fori_loop(0, 2, back_mix, 0)
    second(2)
    first(4)
    qkv_l.wait()

    def fetch(i):
        return pltpu.make_async_copy(h_p.at[pl.ds(2 * i, 2)], PT.at[i % 2], pd.at[i % 2])

    fetch(0).start()

    def attend(i):
        slot = i % 2
        if i < 5:
            fetch(i + 1).start()
        q2, k2 = fb[:, cols(i * 128, 128)], fb[:, cols(D + i * 128, 128)]
        v2, go2 = fb[:, cols(2 * D + i * 128, 128)], gb[:, cols(3 * D + i * 128, 128)]
        kT = jnp.transpose(k2)
        lane = lax.broadcasted_iota(jnp.int32, (TOK_DEV, 128), 1)
        fetch(i).wait()
        parts = []
        gk = jnp.zeros((TOK_DEV, 128), f32)
        gv = jnp.where(use[:, :] > 0, 0.0, go2.astype(f32))
        for half in range(2):
            mine = (lane < HD) if half == 0 else (lane >= HD)
            none = jnp.zeros_like(v2)
            p = PT[slot, half]
            gp = lax.dot_general(
                jnp.where(mine, v2, none), go2, (((1,), (1,)), ((), ())), preferred_element_type=f32
            )
            pf = p.astype(f32)
            gs = (pf * (gp - jnp.sum(pf * gp, axis=0, keepdims=True))).astype(low)
            gk = gk + jnp.dot(gs, jnp.where(mine, q2, none), preferred_element_type=f32)
            gv = gv + jnp.dot(p, jnp.where(mine, go2, none), preferred_element_type=f32)
            parts.append(jnp.dot(kT[half * HD : (half + 1) * HD], gs, preferred_element_type=f32))
        gq = jnp.transpose(jnp.concatenate(parts, axis=0)) * (HD ** (-0.5))
        gb[:, cols(i * 128, 128)] = gq.astype(low)
        gb[:, cols(D + i * 128, 128)] = gk.astype(low)
        gb[:, cols(2 * D + i * 128, 128)] = gv.astype(low)

    attend(0)
    attend(1)
    third(1)
    fourth(0)
    attend(2)
    attend(3)
    second(3)
    attend(4)
    fourth(1)
    attend(5)
    third(2)

    def back_x(i, _):
        at = cols(i * D, D)
        hb[...] += lax.dot_general(
            gb[:, at], square(wa, at), (((1,), (1,)), ((), ())), preferred_element_type=f32
        )
        return 0

    lax.fori_loop(0, 3, back_x, 0)

    def rows_low(i, _):
        gi[i] = hb[pl.ds(pl.multiple_of(i * 64, 64), 64), :].astype(low)
        return 0

    lax.fori_loop(0, 8, rows_low, 0)
    tb = token_send(lambda to: gi.at[to], o_grad, 1)
    second(4)
    xT_l.wait()
    for n in range(3):
        gradient(LU, gb, n, n * D, 1, 1 - c)
        c_send(5 + n)
    fourth(2)
    gradient(LU, gb, 0, 0, 1, c)
    first(5)
    gradient(LU, gb, 1, D, 1, c)
    first(6)
    gradient(LU, gb, 2, 2 * D, 1, c)
    first(7)
    third(3)
    for row, start in ((0, 0), (1, 2 * D)):

        def total(i, acc, start=start):
            at = pl.ds(pl.multiple_of(i * 64, 64), 64)
            return acc + eight(gb[at, start : start + D].astype(f32))

        put(row, lax.fori_loop(0, 8, total, zero))
    vec_copy = send(vb.at[0], vr.at[0], vs.at[0], vrs.at[0], here.to_core)
    sent.append(vec_copy)
    third(4)
    second(5)
    fourth(3)
    vec_copy.wait_recv()
    vb[1] = vb[0] + vr[0]
    vec_copy = send(vb.at[1], vr.at[1], vs.at[1], vrs.at[1], here.to_x)
    sent.append(vec_copy)
    second(6)
    third(5)
    fourth(4)
    vec_copy.wait_recv()
    vb[2] = vb[1] + vr[1]
    vec_copy = send(vb.at[2], vr.at[2], vs.at[2], vrs.at[2], here.to_y)
    sent.append(vec_copy)
    second(7)
    final(0)
    final(1)
    spread(2)
    fourth(5)
    third(6)
    final(2)
    final(3)
    spread(1)
    fourth(6)
    third(7)
    final(4)
    fourth(7)
    final(5)
    final(6)
    final(7)
    jc = cols(y * JCOLS, JCOLS)
    other = cols((1 - y) * JCOLS, JCOLS)
    slot_copies = []
    for step in range(1, 9):
        to = here.pair(step)
        for t in range(2):
            b = jnp.int32(-1)
            for k in range(NBLK):
                b = jnp.where(owner[k] == 2 * to + t, k, b)
            flag = (b >= 0).astype(f32)
            SO[step - 1, t] = (F[jnp.maximum(b, 0)].astype(f32) * flag).astype(low)
        if step < 8:
            slot_copies.append(
                send(SO.at[step - 1], Gs.at[:, f, x, :, jc], ss.at[step - 1], sr.at[step - 1], (r, to))
            )
    sent.extend(slot_copies)
    own = local(SO.at[7], Gs.at[:, f, x, :, jc], ls.at[5])
    hops = []
    for step in range(8):
        src = here.pair(step)
        if step == 0:
            own.wait()
        else:
            slot_copies[step - 1].wait_recv()
        part = Gs.at[:, src, x, :, jc]
        hops.append(
            (
                send(part, part, ps.at[0, step], pr.at[0, step], here.to_x),
                send(part, part, ps.at[1, step], pr.at[1, step], here.to_y),
            )
        )
    ends = []
    for step in range(8):
        src = here.pair(step)
        hops[step][0].wait_recv()
        part = Gs.at[0, src, 1 - x, :, jc]
        ends.append(send(part, part, ps.at[2, step], pr.at[2, step], here.to_y))
        hops[step][1].wait_recv()
        part = Gs.at[1, src, x, :, other]
        ends.append(send(part, part, ps.at[3, step], pr.at[3, step], here.to_x))
        sent.extend(hops[step])
    sent.extend(ends)
    vec_copy.wait_recv()
    vb[3] = vb[2] + vr[2]
    vec_copies = []
    for step in (1, 2, 3):
        vec_copies.append(
            send(vb.at[3], vr.at[2 + step], vs.at[2 + step], vrs.at[2 + step], here.along(step))
        )
    sent.extend(vec_copies)
    spread_on(2)
    spread_on(1)
    spread(0)
    for load in root_l:
        load.wait()
    for copy in ends:
        copy.wait_recv()
    homes.append(local(Gs, o_gs, ls.at[6]))
    for t in range(2):
        whole = Gs[t].reshape(D, D)
        rows = wb[:, :, x, :, t * D : (t + 1) * D].reshape(JCOLS, D)
        half = jnp.dot(rows, whole, preferred_element_type=f32).astype(low)
        right = square(wb, cols((2 + t) * D + y * JCOLS, JCOLS))
        part = jnp.dot(half, right, preferred_element_type=f32)
        PQ[t] = part.astype(low).reshape(8, HALF, JCOLS)
        sq[t] = jnp.sum((part * part).reshape(48, 8, JCOLS), axis=0)
    ucopies = []
    for step in range(1, 8):
        to = here.pair(step)
        ucopies.append(
            send(PQ.at[:, to], UA.at[x, y, pl.ds(2 * f, 2)], us.at[step - 1], ur.at[step - 1], (r, to))
        )
    sent.extend(ucopies)
    own = local(PQ.at[:, f], UA.at[x, y, pl.ds(2 * f, 2)], ls.at[7])
    squares = []
    for number, to in enumerate((here.to_x, here.to_y, here.to_d)):
        squares.append(send(sq, sr_in.at[number], es.at[number], er.at[number], to))
    sent.extend(squares)
    uhops = []
    for step in range(8):
        src = here.pair(step)
        if step == 0:
            own.wait()
        else:
            ucopies[step - 1].wait_recv()
        part = UA.at[x, y, pl.ds(2 * src, 2)]
        uhops.append(
            (
                send(part, part, qs.at[0, step], qr.at[0, step], here.to_x),
                send(part, part, qs.at[1, step], qr.at[1, step], here.to_y),
            )
        )
        if step == 0:
            for copy in squares:
                copy.wait_recv()
            for t in range(2):
                total = sq[t] + sr_in[0, t] + sr_in[1, t] + sr_in[2, t]
                mean = jnp.sum(jnp.sum(total, axis=1, keepdims=True), axis=0, keepdims=True) * (1.0 / (D * D))
                sc_out[t] = jnp.broadcast_to(lax.rsqrt(mean + RMS_EPS), (8, 128))
            scales = []
            for number in range(1, 8):
                to = here.pair(number)
                scales.append(
                    send(
                        sc_out, SC.at[pl.ds(2 * f, 2)], ms.at[number - 1], mr.at[number - 1], (r, to)
                    )
                )
            sent.extend(scales)
            homes.append(local(sc_out, SC.at[pl.ds(2 * f, 2)], ls.at[8]))
    uends = []
    for step in range(8):
        src = here.pair(step)
        uhops[step][0].wait_recv()
        part = UA.at[1 - x, y, 2 * src]
        uends.append(send(part, part, qs.at[2, step], qr.at[2, step], here.to_y))
        uhops[step][1].wait_recv()
        part = UA.at[x, 1 - y, 2 * src + 1]
        uends.append(send(part, part, qs.at[3, step], qr.at[3, step], here.to_x))
        sent.extend(uhops[step])
    sent.extend(uends)
    spread_on(0)
    total = vb[3]
    for copy in vec_copies:
        copy.wait_recv()
    for step in range(3):
        total = total + vr[3 + step]
    vb[4] = total
    homes.append(local(vb.at[4], o_vec, ls.at[9]))
    for copy in diagonals + uends + scales + ta + tb:
        copy.wait_recv()
    for copy in homes:
        copy.wait()
    z_finish()
    for copy in sent:
        copy.wait_send()


def backward_all(owner, vt, use, saved):
    any_spec = pl.BlockSpec(memory_space=pl.ANY)
    vmem = pl.BlockSpec(memory_space=pltpu.VMEM)
    smem = pl.BlockSpec(memory_space=pltpu.SMEM)
    dma = pltpu.SemaphoreType.DMA
    shape = jax.ShapeDtypeStruct
    low, f32 = jnp.bfloat16, jnp.float32
    JW = 12 * JCOLS
    square = (4, 2, 2, HALF, GCOLS)
    return pl.pallas_call(
        backward_kernel,
        out_shape=[
            shape((8, 64, D), low), shape((8, 64, D), low),
            shape((2, 2, 12, HALF, JCOLS), low), shape((2, 2, 16, HALF, JCOLS), low),
            shape((16, 8, 128), f32), shape((2, 8, 2, HALF, D), low), shape((16, D), f32),
        ],
        in_specs=[smem, vmem, vmem] + [any_spec] * 17,
        out_specs=[any_spec] * 7,
        scratch_shapes=[
            pltpu.VMEM((2, 4, 2, 2, HALF, JW), low),
            pltpu.VMEM((2, 4, 2, HALF, JW), low),
            pltpu.VMEM((2, 2, HALF, JW), low),
            pltpu.VMEM((2, HALF, JW), low),
            pltpu.VMEM((2, 2, HALF, JW), low),
            pltpu.VMEM((2, HALF, JW), low),
            pltpu.VMEM((2, HALF, JW), low),
            pltpu.VMEM((2, HALF, JW), low),
            pltpu.VMEM((12, HALF, JCOLS), low),
            pltpu.VMEM((8, 2, HALF, JCOLS), low),
            pltpu.VMEM((2, 8, 2, HALF, D), low),
            pltpu.VMEM(square, low),
            pltpu.VMEM(square, low),
            pltpu.VMEM((TOK_DEV, FF), low),
            pltpu.VMEM((TOK_DEV, FF), low),
            pltpu.VMEM((TOK_DEV, D), low),
            pltpu.VMEM((D, TOK_DEV), low),
            pltpu.VMEM((D, TOK_DEV), low),
            pltpu.VMEM((TOK_DEV, D), f32),
            pltpu.VMEM((TOK_DEV, D), f32),
            pltpu.VMEM((2, 2, TOK_DEV, TOK_DEV), low),
            pltpu.VMEM((TOK_DEV, 128), f32),
            pltpu.VMEM((TOK_DEV, 128), f32),
            pltpu.VMEM((8, 64, D), low),
            pltpu.VMEM((2, 8, HALF, JCOLS), low),
            pltpu.VMEM((2, 8, JCOLS), f32),
            pltpu.VMEM((3, 2, 8, JCOLS), f32),
            pltpu.VMEM((2, 8, 128), f32),
            pltpu.VMEM((5, 16, D), f32),
            pltpu.VMEM((6, 16, D), f32),
            dma((18,)), dma((2,)), dma((8,)), dma((8,)),
            dma((8,)), dma((8,)), dma((8,)), dma((8,)), dma((8,)), dma((8,)), dma((8,)), dma((8,)),
            dma((8, 4)), dma((8, 3)), dma((3, 4)), dma((3, 4)),
            dma((2, 7)), dma((2, 7)), dma((7,)), dma((7,)), dma((4, 8)), dma((4, 8)),
            dma((7,)), dma((7,)), dma((4, 8)), dma((4, 8)), dma((3,)), dma((3,)), dma((7,)), dma((7,)),
            dma((6,)), dma((6,)), dma((10,)),
        ],
        compiler_params=pltpu.CompilerParams(
            collective_id=1, has_side_effects=True, vmem_limit_bytes=60 * MIB
        ),
        name="backward_all",
    )(owner, vt, use, *saved)


def finish_kernel(
    owner, hot, back, grad, wr, ua, sc, gs, vec, stat_l, stat_r, wf, vecs, mom1, mom2,
    layer_out, input_grad, wg, nw, new_l, new_r, out1, out2, outv,
    gb, sl, sr, ub, rb, wb, nb, gg, tb, to, ls, os,
):
    low, f32 = jnp.bfloat16, jnp.float32
    f = lax.axis_index("fsdp")
    gs_load = local(gs, gb, ls.at[5])
    stats = [
        (local(stat_l.at[t], sl.at[t], ls.at[6 + 2 * t]), local(stat_r.at[t], sr.at[t], ls.at[7 + 2 * t]))
        for t in range(2)
    ]
    loads = [
        local(back, tb.at[0], ls.at[0]), local(grad, tb.at[1], ls.at[1]),
        local(wr, rb, ls.at[2]), local(ua, ub, ls.at[3]), local(wf, wb, ls.at[4]),
    ]
    outs = []
    gs_load.wait()
    for t in range(2):
        stats[t][0].wait()

        def left(i, _, t=t):
            at = pl.ds(pl.multiple_of(i * 384, 384), 384)
            rows = gb[t, pl.ds(4 * i, 4)].reshape(384, D)
            part = lax.dot_general(
                rows, gb[t].reshape(D, D), (((1,), (1,)), ((), ())), preferred_element_type=f32
            )
            sl[t, at, :] = STAT_DECAY * sl[t, at, :] + (1.0 - STAT_DECAY) * part
            return 0

        lax.fori_loop(0, 2, left, 0)
        outs.append(local(sl.at[t], new_l.at[t], os.at[4 + 2 * t]))
        stats[t][1].wait()
        for i in range(3):
            at = pl.ds(i * 256, 256)
            part = lax.dot_general(
                gb[t, :, :, :, at].reshape(D, 256), gb[t].reshape(D, D), (((0,), (0,)), ((), ())),
                preferred_element_type=f32,
            )
            sr[t, at, :] = STAT_DECAY * sr[t, at, :] + (1.0 - STAT_DECAY) * part
        outs.append(local(sr.at[t], new_r.at[t], os.at[5 + 2 * t]))
    for number, target in enumerate((layer_out, input_grad)):
        loads[number].wait()
        to[number] = jnp.dot(
            hot[...], tb[number].reshape(TOK_DEV, D), preferred_element_type=f32
        ).astype(low)
        outs.append(local(to.at[number], target, os.at[number]))
    loads[3].wait()
    loads[4].wait()
    for b in range(NBLK):
        slot = owner[b]
        scale = LR_MATRIX * sc[slot, 0:1, 0:1]
        for h in range(2):
            for j in range(2):
                at = pl.ds(b * D + j * JCOLS, JCOLS)
                nb[h, :, at] = wb[h, :, at] - scale * ub[h, j, slot].astype(f32)
    outs.append(local(nb, nw, os.at[3]))
    loads[2].wait()

    def one(i, _):
        h, b = lax.rem(i, 2), lax.div(i, 2)
        for j in range(2):
            gg[h, :, cols(b * D + j * JCOLS, JCOLS)] = rb[h, j, b].astype(f32)
        return 0

    lax.fori_loop(0, 24, one, 0)
    outs.append(local(gg, wg, os.at[2]))
    mine = jnp.zeros((NBLK, 96), f32)
    for number in range(8):
        mine = jnp.where(f == number, vec[:NBLK, number * 96 : (number + 1) * 96], mine)
    fresh1 = BETA_ONE * mom1[...] + (1.0 - BETA_ONE) * mine
    fresh2 = BETA_TWO * mom2[...] + (1.0 - BETA_TWO) * mine * mine
    out1[...] = fresh1
    out2[...] = fresh2
    outv[...] = vecs[...] - LR_VECTOR * (fresh1 / (1.0 - BETA_ONE**STEP)) / (
        jnp.sqrt(fresh2 / (1.0 - BETA_TWO**STEP)) + ADAM_EPS
    )
    for copy in outs:
        copy.wait()


def finish_all(owner, hot, results, stat_l, stat_r, wf, vecs, mom1, mom2):
    any_spec = pl.BlockSpec(memory_space=pl.ANY)
    vmem = pl.BlockSpec(memory_space=pltpu.VMEM)
    smem = pl.BlockSpec(memory_space=pltpu.SMEM)
    dma = pltpu.SemaphoreType.DMA
    shape = jax.ShapeDtypeStruct
    low, f32 = jnp.bfloat16, jnp.float32
    wide = (2, HALF, 3 * GCOLS)
    back, grad, wr, ua, sc, gs, vec = results
    return pl.pallas_call(
        finish_kernel,
        out_shape=[
            shape((TOK_DEV, D), low), shape((TOK_DEV, D), low), shape(wide, f32), shape(wide, f32),
            shape((2, D, D), f32), shape((2, D, D), f32),
            shape((NBLK, 96), f32), shape((NBLK, 96), f32), shape((NBLK, 96), f32),
        ],
        in_specs=[smem, vmem] + [any_spec] * 4 + [vmem, any_spec, vmem] + [any_spec] * 3 + [vmem] * 3,
        out_specs=[any_spec] * 6 + [vmem] * 3,
        scratch_shapes=[
            pltpu.VMEM((2, 8, 2, HALF, D), low),
            pltpu.VMEM((2, D, D), f32),
            pltpu.VMEM((2, D, D), f32),
            pltpu.VMEM((2, 2, 16, HALF, JCOLS), low),
            pltpu.VMEM((2, 2, 12, HALF, JCOLS), low),
            pltpu.VMEM(wide, f32),
            pltpu.VMEM(wide, f32),
            pltpu.VMEM(wide, f32),
            pltpu.VMEM((2, 8, 64, D), low),
            pltpu.VMEM((2, TOK_DEV, D), low),
            dma((10,)), dma((8,)),
        ],
        compiler_params=pltpu.CompilerParams(vmem_limit_bytes=56 * MIB),
        name="finish_all",
    )(
        owner, hot, back, grad, wr, ua, sc, gs, vec, stat_l, stat_r, wf.reshape(wide), vecs, mom1, mom2
    )


def fast_body(
    tokens,
    cotangent,
    place,
    seq_lengths,
    random_blocks,
    owner_slot,
    flat_weights,
    vectors,
    moment_first,
    moment_second,
    stat_left,
    stat_right,
    root_left,
    root_right,
):
    peers = lax.axis_size("fsdp")
    share_rows = TOK_DEV // peers
    w0, w1, w2, vt, *saved = forward_all(
        seq_lengths, place[None, :], tokens, cotangent, flat_weights, vectors.T,
        jnp.transpose(random_blocks, (2, 0, 1)), root_left, root_right,
    )
    *saved, use, hot = saved
    saved[-2] = saved[-2].reshape(peers, share_rows, D)
    results = backward_all(owner_slot, vt, use, [w0, w1, w2] + saved)
    layer_out, input_grad, weight_grads, new_weights, *others = finish_all(
        owner_slot, hot, results, stat_left, stat_right, flat_weights, vectors.T, moment_first.T,
        moment_second.T,
    )
    return (
        layer_out,
        input_grad,
        weight_grads.reshape(flat_weights.shape),
        new_weights.reshape(flat_weights.shape),
        *others[:2],
        *[vec.T for vec in others[2:]],
    )


def plain_body(
    tokens,
    cotangent,
    place,
    seq_lengths,
    random_blocks,
    owner_slot,
    flat_weights,
    vectors,
    moment_first,
    moment_second,
    stat_left,
    stat_right,
    root_left,
    root_right,
):
    peers = lax.axis_size("fsdp")
    share_rows = TOK_DEV // peers
    order_ids = jnp.argsort(place)
    outgoing = (
        tokens[order_ids].reshape(peers, share_rows, D),
        cotangent[order_ids].reshape(peers, share_rows, D),
    )
    arrived = (
        lax.all_to_all(outgoing[0], "fsdp", split_axis=0, concat_axis=0, tiled=True),
        lax.all_to_all(outgoing[1], "fsdp", split_axis=0, concat_axis=0, tiled=True),
    )
    inputs = arrived[0].reshape(TOK_DEV, D)
    upstream = arrived[1].reshape(TOK_DEV, D).astype(jnp.float32)
    weight_copy, vector_copy = (
        lax.all_gather(flat_weights.astype(jnp.bfloat16), "fsdp", axis=0, tiled=True),
        lax.all_gather(vectors.astype(jnp.bfloat16), "fsdp", axis=0, tiled=True),
    )
    vecs_full = vector_copy.astype(jnp.float32)
    b_up = jnp.transpose(vecs_full[:, 8:]).reshape(FF)
    seq_id, position, in_use, seq_blocks = layout(seq_lengths[0])
    picks = random_keys(random_blocks, seq_blocks)
    slot_ids = jnp.arange(TOK_DEV, dtype=jnp.int32)
    real_rows = in_use.astype(jnp.float32)[:, None]
    bias_qkv = jnp.concatenate([vecs_full[:, 0], jnp.zeros((D,), jnp.float32), vecs_full[:, 1]])
    qkv_low = (
        jnp.dot(inputs, weight_copy[:, : 3 * D], preferred_element_type=jnp.float32) + bias_qkv
    ).astype(jnp.bfloat16)
    qkv_heads = qkv_low.reshape(TOK_DEV, 3, H, HD)
    queries = qkv_heads[:, 0]
    key_heads = qkv_heads[:, 1]
    value_heads = qkv_heads[:, 2]
    block_rows = min(512, TOK_DEV)
    block_count = TOK_DEV // block_rows
    score_scale = HD ** (-0.5)

    def split_blocks(array):
        return array.reshape((block_count, block_rows) + array.shape[1:])

    block_inputs = (
        split_blocks(queries),
        split_blocks(seq_id),
        split_blocks(position),
        split_blocks(in_use),
        split_blocks(picks),
        split_blocks(slot_ids),
    )

    def scores_of(query_block, q_seq, q_pos, q_use, q_pick, q_slot):
        raw_scores = (
            jnp.einsum("qhd,khd->hqk", query_block, key_heads, preferred_element_type=jnp.float32)
            * score_scale
        )
        keep_mask = allowed(q_seq, q_pos, q_use, q_pick, q_slot, seq_id, position, in_use, slot_ids)
        return jnp.where(keep_mask, raw_scores, MASKED_SCORE)

    def forward_block(pieces):
        scores = scores_of(pieces[0], pieces[1], pieces[2], pieces[3], pieces[4], pieces[5])
        row_max = jnp.max(scores, axis=-1, keepdims=True)
        expo = jnp.exp(scores - row_max)
        row_total = jnp.sum(expo, axis=-1, keepdims=True)
        probs_low = (expo / row_total).astype(jnp.bfloat16)
        mixed_block = jnp.einsum(
            "hqk,khd->qhd", probs_low, value_heads, preferred_element_type=jnp.float32
        )
        return (mixed_block.reshape(block_rows, D), (row_max + jnp.log(row_total))[:, :, 0])

    attended, log_totals = lax.map(forward_block, block_inputs)
    mixed = attended.reshape(TOK_DEV, D).astype(jnp.bfloat16)
    branch = (
        jnp.dot(mixed, weight_copy[:, 3 * D : 4 * D], preferred_element_type=jnp.float32)
        + vecs_full[:, 2]
    )
    hidden_one = inputs.astype(jnp.float32) + branch
    x_one, norm_one_back = jax.vjp(layer_norm, hidden_one, vecs_full[:, 4], vecs_full[:, 5])
    x_one_low = x_one.astype(jnp.bfloat16)
    pre_act = (
        jnp.dot(x_one_low, weight_copy[:, 4 * D : 4 * D + FF], preferred_element_type=jnp.float32)
        + b_up
    )
    act, gelu_back = jax.vjp(gelu_tanh, pre_act)
    act_low = act.astype(jnp.bfloat16)
    ffn = contract_cols(act_low, weight_copy[:, 4 * D + FF :]) + vecs_full[:, 3]
    hidden_two = x_one + ffn
    result, norm_two_back = jax.vjp(layer_norm, hidden_two, vecs_full[:, 6], vecs_full[:, 7])
    layer_rows = (result * real_rows).astype(jnp.bfloat16)
    weight_copy = lax.all_gather(flat_weights.astype(jnp.bfloat16), "fsdp", axis=0, tiled=True)
    d_result = upstream * real_rows
    d_two, d_gain_two, d_shift_two = norm_two_back(d_result)
    d_ffn = d_two.astype(jnp.bfloat16)
    d_act = jnp.dot(d_ffn, weight_copy[:, 4 * D + FF :], preferred_element_type=jnp.float32)
    (d_pre,) = gelu_back(d_act)
    d_pre_low = d_pre.astype(jnp.bfloat16)
    grad_down = contract_rows(d_ffn, act_low)
    grad_up = contract_rows(x_one_low, d_pre_low)
    d_x_one = d_two + contract_cols(d_pre_low, weight_copy[:, 4 * D : 4 * D + FF])
    d_one, d_gain_one, d_shift_one = norm_one_back(d_x_one)
    up_sums = jnp.transpose(jnp.sum(d_pre_low.astype(jnp.float32), axis=0).reshape(FF // D, D))
    ffn_vec = jnp.concatenate(
        [
            jnp.sum(d_ffn.astype(jnp.float32), axis=0)[:, None],
            d_gain_one[:, None],
            d_shift_one[:, None],
            d_gain_two[:, None],
            d_shift_two[:, None],
            up_sums,
        ],
        axis=1,
    )
    ffn_mats = jnp.concatenate([grad_up, grad_down], axis=1)
    d_branch = d_one.astype(jnp.bfloat16)
    grad_out = contract_rows(mixed, d_branch)
    d_mixed = (
        contract_cols(d_branch, weight_copy[:, 3 * D : 4 * D])
        .astype(jnp.bfloat16)
        .reshape(TOK_DEV, H, HD)
    )

    def backward_block(carry, pieces):
        key_grad, value_grad = carry
        query_block = pieces[0]
        log_total = pieces[6]
        out_grad = pieces[7]
        scores = scores_of(pieces[0], pieces[1], pieces[2], pieces[3], pieces[4], pieces[5])
        probs = jnp.exp(scores - log_total[:, :, None])
        probs_low = probs.astype(jnp.bfloat16)
        value_grad = value_grad + jnp.einsum(
            "hqk,qhd->khd", probs_low, out_grad, preferred_element_type=jnp.float32
        )
        prob_grad = jnp.einsum(
            "qhd,khd->hqk", out_grad, value_heads, preferred_element_type=jnp.float32
        )
        score_grad = (
            probs * (prob_grad - jnp.sum(probs * prob_grad, axis=-1, keepdims=True))
        ).astype(jnp.bfloat16)
        query_grad = (
            jnp.einsum("hqk,khd->qhd", score_grad, key_heads, preferred_element_type=jnp.float32)
            * score_scale
        )
        key_grad = (
            key_grad
            + jnp.einsum(
                "hqk,qhd->khd", score_grad, query_block, preferred_element_type=jnp.float32
            )
            * score_scale
        )
        return ((key_grad, value_grad), query_grad)

    zero_heads = jnp.zeros((TOK_DEV, H, HD), jnp.float32)
    (key_grad, value_grad), query_grad = lax.scan(
        backward_block, (zero_heads, zero_heads), block_inputs + (log_totals, split_blocks(d_mixed))
    )
    d_qkv = jnp.concatenate(
        [
            query_grad.reshape(TOK_DEV, D),
            key_grad.reshape(TOK_DEV, D),
            value_grad.reshape(TOK_DEV, D),
        ],
        axis=1,
    ).astype(jnp.bfloat16)
    grad_qkv = contract_rows(inputs, d_qkv)
    d_inputs = d_one + contract_cols(d_qkv, weight_copy[:, : 3 * D])
    qkv_sums = jnp.sum(d_qkv.astype(jnp.float32), axis=0)
    attn_vec = jnp.stack(
        [qkv_sums[:D], qkv_sums[2 * D :], jnp.sum(d_branch.astype(jnp.float32), axis=0)], axis=1
    )
    attn_mats = jnp.concatenate([grad_qkv, grad_out], axis=1)
    mat_shard, vec_shard = (
        lax.psum_scatter(
            jnp.concatenate([attn_mats, ffn_mats], axis=1), "fsdp", scatter_dimension=0, tiled=True
        ),
        lax.psum_scatter(
            jnp.concatenate([attn_vec, ffn_vec], axis=1), "fsdp", scatter_dimension=0, tiled=True
        ),
    )
    mat_part = lax.psum_scatter(
        mat_shard.astype(jnp.bfloat16), "rep", scatter_dimension=1, tiled=True
    ).astype(jnp.float32)
    vec_shard = lax.psum(vec_shard, "rep")
    mat_shard = lax.all_gather(mat_part.astype(jnp.bfloat16), "rep", axis=1, tiled=True).astype(
        mat_part.dtype
    )
    grad_rows = d_inputs.astype(jnp.bfloat16)
    back_pair = (
        lax.all_to_all(
            layer_rows.reshape(peers, share_rows, D),
            "fsdp",
            split_axis=0,
            concat_axis=0,
            tiled=True,
        ),
        lax.all_to_all(
            grad_rows.reshape(peers, share_rows, D), "fsdp", split_axis=0, concat_axis=0, tiled=True
        ),
    )
    layer_out = (
        jnp.zeros((TOK_DEV, D), jnp.bfloat16).at[order_ids].set(back_pair[0].reshape(TOK_DEV, D))
    )
    input_grad = (
        jnp.zeros((TOK_DEV, D), jnp.bfloat16).at[order_ids].set(back_pair[1].reshape(TOK_DEV, D))
    )
    slot_count = stat_left.shape[0]
    rows_dev = flat_weights.shape[0]
    targets = (
        jnp.arange(slot_count, dtype=jnp.int32)[:, None, None]
        + slot_count * jnp.arange(peers, dtype=jnp.int32)[None, :, None]
    )
    select = (owner_slot[None, None, :] == targets).astype(jnp.float32)
    grad_pieces = mat_shard.reshape(rows_dev, NBLK, D)
    outbound = jnp.einsum("snb,rbc->snrc", select, grad_pieces, precision=PRECISE)
    inbound = lax.all_to_all(
        outbound.astype(jnp.bfloat16), "fsdp", split_axis=1, concat_axis=1, tiled=True
    ).astype(outbound.dtype)
    grad_blocks = inbound.reshape(slot_count, D, D)
    new_left = STAT_DECAY * stat_left + (1.0 - STAT_DECAY) * jnp.einsum(
        "sij,skj->sik", grad_blocks, grad_blocks, precision=PRECISE
    )
    new_right = STAT_DECAY * stat_right + (1.0 - STAT_DECAY) * jnp.einsum(
        "sji,sjk->sik", grad_blocks, grad_blocks, precision=PRECISE
    )
    left_applied = jnp.einsum("sij,sjk->sik", root_left, grad_blocks, precision=PRECISE)
    direction = jnp.einsum("sij,sjk->sik", left_applied, root_right, precision=PRECISE)
    update = direction * lax.rsqrt(
        jnp.mean(direction * direction, axis=(1, 2), keepdims=True) + RMS_EPS
    )
    returned = lax.all_to_all(
        update.reshape(slot_count, peers, rows_dev, D).astype(jnp.bfloat16),
        "fsdp",
        split_axis=1,
        concat_axis=1,
        tiled=True,
    ).astype(jnp.float32)
    step_matrix = jnp.einsum("snb,snrc->rbc", select, returned, precision=PRECISE).reshape(
        rows_dev, NBLK * D
    )
    new_weights = flat_weights - LR_MATRIX * step_matrix
    first_bias = 1.0 - BETA_ONE**STEP
    second_bias = 1.0 - BETA_TWO**STEP
    new_first = BETA_ONE * moment_first + (1.0 - BETA_ONE) * vec_shard
    new_second = BETA_TWO * moment_second + (1.0 - BETA_TWO) * vec_shard * vec_shard
    first_fixed = new_first / first_bias
    second_fixed = new_second / second_bias
    new_vectors = vectors - LR_VECTOR * first_fixed / (jnp.sqrt(second_fixed) + ADAM_EPS)
    return (
        layer_out,
        input_grad,
        mat_shard,
        new_weights,
        new_left,
        new_right,
        new_first,
        new_second,
        new_vectors,
    )


def solution(mesh):
    in_specs = (
        P(("rep", "fsdp"), None),
        P(("rep", "fsdp"), None),
        P(("rep", "fsdp")),
        P(("rep", "fsdp"), None),
        P(("rep", "fsdp"), None, None),
        P(),
        P("fsdp", None),
        P("fsdp", None),
        P("fsdp", None),
        P("fsdp", None),
        P("fsdp", None, None),
        P("fsdp", None, None),
        P("fsdp", None, None),
        P("fsdp", None, None),
    )
    out_specs = (
        P(("rep", "fsdp"), None),
        P(("rep", "fsdp"), None),
        P("fsdp", None),
        P("fsdp", None),
        P("fsdp", None, None),
        P("fsdp", None, None),
        P("fsdp", None),
        P("fsdp", None),
        P("fsdp", None),
    )
    shaped = mesh.shape["fsdp"] == 8 and mesh.shape["rep"] == 4
    body = fast_body if shaped else plain_body
    return jax.shard_map(body, mesh=mesh, in_specs=in_specs, out_specs=out_specs, check_vma=False)
```

```python
import functools

import jax
import jax.numpy as jnp
from jax import lax
from jax.experimental import pallas as pl
from jax.experimental.pallas import tpu as pltpu
from jax.sharding import PartitionSpec as P

D = 768
H = 12
HD = 64
FF = 3072
BLK = 64
NGLOB = 2
NRAND = 3
STEP = 10
SEQ_DEV = 4
TOK_DEV = 512
NBLK = 12


NORM_EPS = 1e-12
MASKED_SCORE = -1e30
STAT_DECAY = 0.5
LR_MATRIX = 0.02
LR_VECTOR = 0.1
BETA_ONE = 0.9
BETA_TWO = 0.999
ADAM_EPS = 1e-08
RMS_EPS = 1e-12
PRECISE = lax.Precision.HIGHEST


def layout(lengths):
    blocks = (lengths + (BLK - 1)) // BLK
    block_ends = jnp.cumsum(blocks)
    starts = (block_ends - blocks) * BLK
    slot_ids = jnp.arange(TOK_DEV, dtype=jnp.int32)
    seq_id = jnp.sum((slot_ids // BLK)[:, None] >= block_ends[None, :], axis=1)
    member = seq_id[:, None] == jnp.arange(SEQ_DEV, dtype=jnp.int32)[None, :]
    seq_start = jnp.sum(jnp.where(member, starts[None, :], 0), axis=1)
    length = jnp.sum(jnp.where(member, lengths[None, :], 0), axis=1)
    seq_blocks = jnp.sum(jnp.where(member, blocks[None, :], 0), axis=1)
    position = slot_ids - seq_start
    in_use = position < length
    return (seq_id, position, in_use, seq_blocks)


def random_keys(raw_picks, seq_blocks):
    per_block = seq_blocks.reshape(TOK_DEV // BLK, BLK)[:, 0]
    picked = raw_picks % jnp.maximum(per_block, 1)[:, None, None]
    return jnp.repeat(picked, BLK, axis=0)


def allowed(q_seq, q_pos, q_use, q_pick, q_slot, k_seq, k_pos, k_use, k_slot):
    q_block = q_pos // BLK
    k_block = k_pos // BLK
    same_seq = (q_seq[:, None] == k_seq[None, :]) & q_use[:, None] & k_use[None, :]
    nearby = (
        (q_block[:, None] < NGLOB)
        | (k_block[None, :] < NGLOB)
        | (jnp.abs(q_block[:, None] - k_block[None, :]) <= 1)
    )
    chosen = jnp.zeros((H, q_seq.shape[0], k_seq.shape[0]), dtype=jnp.bool_)
    for number in range(NRAND):
        chosen = chosen | (
            k_block[None, None, :] == jnp.transpose(q_pick[:, :, number])[:, :, None]
        )
    alone = jnp.logical_not(q_use)[:, None] & (q_slot[:, None] == k_slot[None, :])
    return (same_seq & nearby)[None] | same_seq[None] & chosen | alone[None]


def layer_norm(hidden, gain, shift):
    center = hidden - jnp.mean(hidden, axis=-1, keepdims=True)
    spread = jnp.mean(center * center, axis=-1, keepdims=True)
    return center * lax.rsqrt(spread + NORM_EPS) * gain + shift


def gelu_tanh(pre_act):
    return jax.nn.gelu(pre_act, approximate=True)


def contract_rows(left, right):
    return lax.dot_general(
        left, right, (((0,), (0,)), ((), ())), preferred_element_type=jnp.float32
    )


def contract_cols(left, right):
    return lax.dot_general(
        left, right, (((1,), (1,)), ((), ())), preferred_element_type=jnp.float32
    )


MESH = pl.DeviceIdType.MESH
HALF = 48
GCOLS = 3072
JCOLS = 384
MIB = 2**20


class Here:
    def __init__(self, corner=False):
        r, f = lax.axis_index("rep"), lax.axis_index("fsdp")
        self.r, self.f = r, f
        self.x, self.y = lax.rem(r, 2), lax.div(r, 2)
        self.z, self.c = lax.div(f, 2), lax.rem(f, 2)
        self.to_x = (r + 1 - 2 * self.x, f)
        self.to_y = (r + 2 - 4 * self.y, f)
        self.to_d = (3 - r, f)
        self.corner = corner
        self.to_core = (r, f + 1 - 2 * self.c)

    def z_plus(self, step):
        return lax.rem(self.z + step, 4)

    def along(self, step):
        return (self.r, 2 * self.z_plus(step) + self.c)

    def peer(self, step):
        return lax.rem(self.f + step, 8)

    def pair(self, step):
        zz = (self.z, self.z + 1 - 2 * lax.rem(self.z, 2), lax.rem(self.z + 2, 4), 3 - self.z)[step // 2 % 4]
        return 2 * zz + (1 - self.c if step % 2 else self.c)

    def greet(self):
        barrier = pltpu.get_barrier_semaphore()
        friends = [self.to_x, self.to_y] + [self.to_d] * self.corner
        friends += [(self.r, self.peer(s)) for s in range(1, 8)]
        for friend in friends:
            pl.semaphore_signal(barrier, inc=1, device_id=friend, device_id_type=MESH)
        return lambda: pl.semaphore_wait(barrier, len(friends))


def send(src, dst, send_sem, recv_sem, device):
    copy = pltpu.make_async_remote_copy(
        src_ref=src,
        dst_ref=dst,
        send_sem=send_sem,
        recv_sem=recv_sem,
        device_id=device,
        device_id_type=MESH,
    )
    copy.start()
    return copy


def local(src, dst, sem):
    copy = pltpu.make_async_copy(src, dst, sem)
    copy.start()
    return copy


def cols(start, width):
    return pl.ds(pl.multiple_of(start, 128), width)


def forward_kernel(
    lengths, place, tok, cot, wf, vec, raw, root_l, root_r,
    o0, o1, o2, o_vt, o_x, o_cot, o_qkv, o_p, o_mix, o_n1, o_r1, o_u, o_f, o_dg, o_n2, o_r2, o_y, o_root, o_use, o_hot,
    w0, w1, w2, tok_in, cot_in, vec_in, tok_s, cot_s,
    tok_v, cot_v, pre_a, pre_b, hot, use, use_row, wide_w, vec_s, vt, qkv, P, mix, n1, r1, x1, u, fa, dg, n2, r2, yo, xT, mT, uT, feat, stg, rb,
    wl, zs, zr, xs, xr, ys, yr, ds, dr, cs, cr, ls, ts, tr, os, ks,
):
    low, f32 = jnp.bfloat16, jnp.float32
    here = Here()
    wait_all = here.greet()
    x, y, z, c, f = here.x, here.y, here.z, here.c, here.f
    whole = [w0, w1, w2]
    whole_out = [o0, o1, o2]
    wide = GCOLS // 2
    sent = []
    outs = []
    count = [0]

    def keep(src, dst):
        outs.append(local(src, dst, os.at[count[0]]))
        count[0] += 1

    tok_load = local(tok, tok_v, ks.at[5])
    cot_load = local(cot, cot_v, ks.at[6])
    fetched = [
        local(wf.at[:, :, g * GCOLS : (g + 1) * GCOLS], wide_w.at[:, :, g * GCOLS : (g + 1) * GCOLS], ks.at[2 + g])
        for g in range(3)
    ]

    def narrow(g):
        fetched[g].wait()

        def one(i, _):
            h, part = lax.div(i, 4), lax.rem(i, 4)
            at = cols(g * GCOLS + part * D, D)
            wl[h, :, at] = wide_w[h, :, at].astype(low)
            return 0

        lax.fori_loop(0, 8, one, 0)
        return local(wl.at[:, :, g * GCOLS : (g + 1) * GCOLS], whole[g].at[z, c], ls.at[g])

    inner = lax.rem(lax.div(z + 1, 2), 2)
    upper = lax.div(z, 2)
    end = 3 * upper

    def source(step):
        near = step - inner if step == 1 else step
        return near + upper * (3 - 2 * near)

    def line(zz):
        return (here.r, 2 * zz + c)

    def own_part(g):
        return wl.at[x, :, cols(g * GCOLS + y * wide, wide)]

    def landed(g, src):
        return whole[g].at[src, c, x, :, cols(y * wide, wide)]

    def z_own(g, second):
        first_to = 1 + upper + inner * (1 - 2 * upper)
        second_to = inner * end + (1 - inner) * (2 - upper)
        return pltpu.make_async_remote_copy(
            src_ref=own_part(g), dst_ref=landed(g, z), send_sem=zs.at[g, int(second)], recv_sem=zr.at[g, z],
            device_id=line(second_to if second else first_to), device_id_type=MESH,
        )

    def z_pass(g, step):
        part = landed(g, source(step))
        return pltpu.make_async_remote_copy(
            src_ref=part, dst_ref=part, send_sem=zs.at[g, 1 + step], recv_sem=zr.at[g, source(step)],
            device_id=line(end), device_id_type=MESH,
        )

    def z_send(g):
        z_own(g, False).start()
        z_own(g, True).start()

    def z_finish(g):
        z_own(g, False).wait_send()
        z_own(g, True).wait_send()

        @pl.when(inner == 1)
        def _():
            for step in (2, 3):
                z_pass(g, step).wait_send()

    def rows_out(table, landing, number):
        out = []
        for step in range(1, 8):
            to = here.pair(step)
            src = table if number == 2 else table.at[to]
            out.append(
                send(src, landing.at[f], ts.at[number, step - 1], tr.at[number, step - 1], (here.r, to))
            )
        sent.extend(out)
        return out

    planes = {0: {}, 1: {}, 2: {}}

    def plane(g, step):
        moving = z_pass(g, step)
        moving.wait_recv()

        if step > 1:

            @pl.when(inner == 1)
            def _():
                moving.start()

        src = source(step)
        part = landed(g, src)
        xc = send(part, part, xs.at[g, src], xr.at[g, src], here.to_x)
        yc = send(part, part, ys.at[g, src], yr.at[g, src], here.to_y)
        planes[g][step] = (xc, yc)
        sent.extend([xc, yc])
        if step == 3:
            core(g, 0, x, y)

    cores = {0: [], 1: [], 2: []}

    def core(g, number, h, j):
        part = whole[g].at[:, c, h, :, cols(j * wide, wide)]
        copy = send(part, part, cs.at[g, number], cr.at[g, number], here.to_core)
        sent.append(copy)
        cores[g].append(copy)

    turns = {0: [], 1: [], 2: []}

    def turn(g, step):
        src = source(step)
        xc, yc = planes[g][step]
        xc.wait_recv()
        part = whole[g].at[src, c, 1 - x, :, cols(y * wide, wide // 2)]
        one = send(part, part, ds.at[g, 0, src], dr.at[g, 0, src], here.to_y)
        yc.wait_recv()
        part = whole[g].at[src, c, x, :, cols((1 - y) * wide + wide // 2, wide // 2)]
        two = send(part, part, ds.at[g, 1, src], dr.at[g, 1, src], here.to_x)
        sent.extend([one, two])
        turns[g].extend([one, two])
        if step == 3:
            core(g, 1, 1 - x, y)
            core(g, 2, x, 1 - y)

    def last(g):
        for copy in turns[g]:
            copy.wait_recv()
        core(g, 3, 1 - x, 1 - y)

    def ready(g):
        for copy in cores[g]:
            copy.wait_recv()
        keep(whole[g], whole_out[g])

    def square(ref, at):
        return ref[:, :, :, :, at].reshape(D, at.size)

    def order(source, target):
        target[...] = jnp.dot(hot[...], source[...], preferred_element_type=f32).astype(low).reshape(8, 64, D)

    def layout_rows():
        sizes = [lengths[0, s] for s in range(SEQ_DEV)]
        blocks = [lax.div(size + (BLK - 1), BLK) for size in sizes]
        ends = [blocks[0]]
        for s in range(1, SEQ_DEV):
            ends.append(ends[-1] + blocks[s])

        def where_is(number):
            seq = jnp.zeros_like(number)
            for s in range(SEQ_DEV):
                seq = seq + (number >= ends[s]).astype(jnp.int32)
            first, size, count = jnp.zeros_like(number), jnp.zeros_like(number), jnp.zeros_like(number)
            for s in range(SEQ_DEV):
                first = jnp.where(seq == s, ends[s] - blocks[s], first)
                size = jnp.where(seq == s, sizes[s], size)
                count = jnp.where(seq == s, blocks[s], count)
            return seq, number - first, size, count

        slot = lax.broadcasted_iota(jnp.int32, (8, TOK_DEV), 1)
        key_seq, key_block, size, _ = where_is(lax.div(slot, BLK))
        used = key_block * BLK + lax.rem(slot, BLK) < size
        used_f = used.astype(f32)
        use_row[...] = used_f
        use[...] = jnp.transpose(jnp.concatenate([used_f] * 16, axis=0))
        row_seq, row_block, _, count = where_is(lax.broadcasted_iota(jnp.int32, (8, 128), 0))
        row_seq, row_block, count = row_seq[:, 0:1], row_block[:, 0:1], jnp.maximum(count[:, 0:1], 1)
        same = (row_seq == key_seq) & used
        near = (row_block < NGLOB) | (key_block < NGLOB) | (jnp.abs(row_block - key_block) <= 1)
        picks = []
        for number in range(NRAND):
            pick = raw[number]
            for _ in range(7):
                pick = jnp.where(pick >= count, pick - count, pick)
            picks.append(pick)
        gap = jnp.zeros((BLK - 8, TOK_DEV), f32)
        for head in range(H):
            keep_it = near
            for pick in picks:
                keep_it = keep_it | (key_block == pick[:, head : head + 1])
            rows = jnp.where(same & keep_it, 0.0, MASKED_SCORE)
            feat[head] = jnp.transpose(jnp.concatenate([rows, gap, rows, gap], axis=0)).astype(low)

    def places():
        spot = (
            lax.div(place[...], TOK_DEV) * 64 + lax.rem(place[...], TOK_DEV) - f * 64
        )
        hot[...] = (
            (lax.broadcasted_iota(jnp.int32, (TOK_DEV, TOK_DEV), 0) == spot).astype(f32).astype(low)
        )
        return spot

    def places_back(spot):
        tall = jnp.transpose(jnp.broadcast_to(spot.astype(f32), (128, TOK_DEV)))
        lane = lax.broadcasted_iota(jnp.int32, (TOK_DEV, TOK_DEV), 1).astype(f32)
        hot[...] = (tall[:, 0:1] == lane).astype(f32).astype(low)
        keep(hot, o_hot)

    def project():
        for part in range(3):
            to = pl.ds(part * D, D)
            acc = jnp.dot(tok_in[...].reshape(TOK_DEV, D), square(w0, to), preferred_element_type=f32)
            if part == 0:
                acc = (acc + vt[0:1, :]) * (HD ** (-0.5))
            if part == 2:
                acc = acc + vt[1:2, :]
            qkv[:, to] = acc.astype(low)

    root_load = []

    def root_fetch(number):
        ref = (root_l, root_r)[number // 2]
        root_load.append(local(ref.at[number % 2], stg, ks.at[0]))

    def roots(number):
        root_load[number].wait()
        if number:
            root_out[number - 1].wait()

        def one(i, _):
            at = pl.ds(pl.multiple_of(i * 96, 96), 96)
            rb[lax.div(i, 2), lax.rem(i, 2)] = stg[at, :].astype(low).reshape(2, HALF, D)
            return 0

        lax.fori_loop(0, 8, one, 0)
        root_out.append(local(rb, o_root.at[number], ks.at[1]))
        if number < 3:
            root_fetch(number + 1)
        else:
            root_out[3].wait()

    root_out = []
    root_fetch(0)

    def attend(start, stop):
        def pair(i, _):
            at = cols(i * 128, 128)
            q2, k2 = qkv[:, at], qkv[:, cols(D + i * 128, 128)]
            v2 = qkv[:, cols(2 * D + i * 128, 128)]
            lane = lax.broadcasted_iota(jnp.int32, (TOK_DEV, 128), 1)
            row = lax.broadcasted_iota(jnp.int32, (TOK_DEV, 128), 0)
            spot = (lax.rem(lane, BLK) == lax.div(row, BLK)).astype(f32).astype(low)
            vT = jnp.transpose(v2)
            parts = []
            for half in range(2):
                mine = (lane < HD) if half == 0 else (lane >= HD)
                qm = jnp.where(mine, q2, spot)
                km = jnp.where(mine, k2, feat[2 * i + half])
                s = lax.dot_general(km, qm, (((1,), (1,)), ((), ())), preferred_element_type=f32)
                e = jnp.exp(s - jnp.max(s, axis=0, keepdims=True))
                p = (e * (use_row[0:1, :] / jnp.sum(e, axis=0, keepdims=True))).astype(low)
                P[2 * i + half] = p
                parts.append(jnp.dot(vT[half * HD : (half + 1) * HD], p, preferred_element_type=f32))
            total = jnp.where(use_row[0:1, :] > 0, jnp.concatenate(parts, axis=0), vT.astype(f32)).astype(low)
            mT[cols(i * 128, 128), :] = total
            mix[:, at] = jnp.transpose(total)
            return 0

        if stop - start == 1:
            pair(start, 0)
        else:
            lax.fori_loop(start, stop, pair, 0)

    def flip(source, target):
        def one(i, _):
            at = cols(i * 128, 128)
            target[at, :] = jnp.transpose(source(at))
            return 0

        lax.fori_loop(0, 6, one, 0)

    def join():
        def one(i, _):
            at = cols(i * 256, 256)
            acc = jnp.dot(mix[...], square(w0, cols(3 * D + i * 256, 256)), preferred_element_type=f32)
            x1[:, at] = tok_in[:, :, at].reshape(TOK_DEV, 256).astype(f32) + (acc + vt[2:3, at])
            return 0

        lax.fori_loop(0, 3, one, 0)

    def norm(ref, i):
        at = pl.ds(pl.multiple_of(i * 128, 128), 128)
        h = ref[at, :]
        center = h - jnp.mean(h, axis=1, keepdims=True)
        r = lax.rsqrt(jnp.mean(center * center, axis=1, keepdims=True) + NORM_EPS)
        return at, center * r, r

    def norm_one():
        def one(i, _):
            at, n, r = norm(x1, i)
            n1[at, :] = n
            r1[at, :] = jnp.broadcast_to(r, (128, 128))
            out = n * vt[4:5, :] + vt[5:6, :]
            u[at, :] = out.astype(low)
            x1[at, :] = out
            return 0

        lax.fori_loop(0, 4, one, 0)

    def lift(begin):
        def raise_to(target, i):
            target[...] = jnp.dot(u[...], square(w1, cols(i * 256, 256)), preferred_element_type=f32)

        def bend(source, i):
            row = lax.div(i, 3)
            pre = source[...] + vt[pl.ds(8 + row, 1), cols((i - 3 * row) * 256, 256)]
            sq = pre * pre
            half = 0.5 * jnp.tanh(pre * (0.7978845608028654 + 0.035677408136300125 * sq)) + 0.5
            act = pre * half
            to = cols(i * 256, 256)
            fa[:, to] = act.astype(low)
            slope = 1.5957691216057308 + 0.21406444881780075 * sq
            dg[:, to] = (half + act * (1.0 - half) * slope).astype(low)

        raise_to(pre_a, begin)

        def two(k, _):
            i = begin + 2 * k
            raise_to(pre_b, i + 1)
            bend(pre_a, i)
            raise_to(pre_a, jnp.minimum(i + 2, 11))
            bend(pre_b, i + 1)
            return 0

        lax.fori_loop(0, 3, two, 0)

    def drop():
        def one(i, _):
            at = cols(i * 512, 512)
            acc = lax.dot_general(
                fa[:, at], square(w2, at), (((1,), (1,)), ((), ())), preferred_element_type=f32
            )
            x1[...] += acc
            return 0

        lax.fori_loop(0, 6, one, 0)

    def norm_two():
        def one(i, _):
            at = pl.ds(pl.multiple_of(i * 128, 128), 128)
            x1[at, :] = x1[at, :] + vt[3:4, :]
            at, n, r = norm(x1, i)
            n2[at, :] = n
            r2[at, :] = jnp.broadcast_to(r, (128, 128))
            out = (n * vt[6:7, :] + vt[7:8, :]) * use[at, 0:1]
            yo[at, :] = out.astype(low)
            return 0

        lax.fori_loop(0, 4, one, 0)

    stays = [narrow(0)]
    wait_all()
    z_send(0)
    vec_s[...] = jnp.zeros_like(vec_s)
    vec_s[:NBLK, :96] = vec[...].astype(low)
    small = rows_out(vec_s, vec_in, 2)
    own = [local(vec_s, vec_in.at[f], ls.at[5])]
    stays.append(narrow(1))
    z_send(1)
    spot = places()
    plane(0, 1)
    tok_load.wait()
    order(tok_v, tok_s)
    own.append(local(tok_s.at[f], tok_in.at[f], ls.at[3]))
    plane(0, 2)
    cot_load.wait()
    order(cot_v, cot_s)
    own.append(local(cot_s.at[f], o_cot.at[f], ls.at[4]))
    stays.append(narrow(2))
    stays[0].wait()
    plane(0, 3)
    t0 = rows_out(tok_s, tok_in, 0)
    for copy in stays[1:] + own:
        copy.wait()
    layout_rows()
    keep(use, o_use)
    turn(0, 1)
    plane(1, 1)
    for copy in small:
        copy.wait_recv()
    for n in range(8):
        vt[:, n * 96 : (n + 1) * 96] = vec_in[n, :, :96].astype(f32)
    keep(vt, o_vt)
    places_back(spot)
    turn(0, 2)
    plane(1, 2)
    roots(0)
    turn(0, 3)
    plane(1, 3)
    roots(1)
    last(0)
    z_send(2)
    roots(2)
    roots(3)
    ready(0)
    turn(1, 1)
    for copy in t0:
        copy.wait_recv()
    project()
    keep(qkv, o_qkv)
    turn(1, 2)
    plane(2, 1)
    attend(0, 1)
    turn(1, 3)
    plane(2, 2)
    attend(1, 2)
    last(1)
    attend(2, 3)
    plane(2, 3)
    t1 = rows_out(cot_s, o_cot, 1)
    attend(3, 4)
    turn(2, 1)
    attend(4, 5)
    attend(5, 6)
    keep(P, o_p)
    keep(mT, o_mix)
    turn(2, 2)
    join()
    norm_one()
    turn(2, 3)
    keep(n1, o_n1)
    keep(r1, o_r1)
    ready(1)
    lift(0)
    last(2)
    lift(6)
    keep(fa, o_f)
    keep(dg, o_dg)
    flip(lambda at: tok_in[:, :, at].reshape(TOK_DEV, 128), xT)
    keep(xT, o_x)
    flip(lambda at: u[:, at], uT)
    keep(uT, o_u)
    ready(2)
    drop()
    norm_two()
    keep(n2, o_n2)
    keep(r2, o_r2)
    keep(yo, o_y)
    for copy in t1:
        copy.wait_recv()
    for g in range(3):
        z_finish(g)
    for copy in sent:
        copy.wait_send()
    for copy in outs:
        copy.wait()


def forward_all(lengths, place, tok, cot, flat_weights, vec, raw, root_l, root_r):
    any_spec = pl.BlockSpec(memory_space=pl.ANY)
    vmem = pl.BlockSpec(memory_space=pltpu.VMEM)
    dma = pltpu.SemaphoreType.DMA
    shape = jax.ShapeDtypeStruct
    low, f32 = jnp.bfloat16, jnp.float32
    square = (4, 2, 2, HALF, GCOLS)
    saved = [
        ((16, D), f32), ((D, TOK_DEV), low), ((8, 64, D), low), ((TOK_DEV, 3 * D), low),
        ((H, TOK_DEV, TOK_DEV), low), ((D, TOK_DEV), low), ((TOK_DEV, D), f32), ((TOK_DEV, 128), f32),
        ((D, TOK_DEV), low), ((TOK_DEV, FF), low), ((TOK_DEV, FF), low), ((TOK_DEV, D), f32),
        ((TOK_DEV, 128), f32), ((TOK_DEV, D), low), ((4, 4, 2, 2, HALF, D), low),
        ((TOK_DEV, 128), f32), ((TOK_DEV, TOK_DEV), low),
    ]
    return pl.pallas_call(
        forward_kernel,
        out_shape=[shape(square, low)] * 3 + [shape(*s) for s in saved],
        in_specs=[pl.BlockSpec(memory_space=pltpu.SMEM)] + [vmem] + [any_spec] * 3 + [vmem] * 2 + [any_spec] * 2,
        out_specs=[any_spec] * 20,
        scratch_shapes=[
            pltpu.VMEM(square, low), pltpu.VMEM(square, low), pltpu.VMEM(square, low),
            pltpu.VMEM((8, 64, D), low), pltpu.VMEM((8, 64, D), low), pltpu.VMEM((8, 16, 128), low),
            pltpu.VMEM((8, 64, D), low), pltpu.VMEM((8, 64, D), low),
            pltpu.VMEM((TOK_DEV, D), low),
            pltpu.VMEM((TOK_DEV, D), low),
            pltpu.VMEM((TOK_DEV, 256), f32),
            pltpu.VMEM((TOK_DEV, 256), f32),
            pltpu.VMEM((TOK_DEV, TOK_DEV), low),
            pltpu.VMEM((TOK_DEV, 128), f32),
            pltpu.VMEM((8, TOK_DEV), f32),
            pltpu.VMEM((2, HALF, 3 * GCOLS), f32),
            pltpu.VMEM((16, 128), low),
            pltpu.VMEM((16, D), f32),
            pltpu.VMEM((TOK_DEV, 3 * D), low),
            pltpu.VMEM((H, TOK_DEV, TOK_DEV), low),
            pltpu.VMEM((TOK_DEV, D), low),
            pltpu.VMEM((TOK_DEV, D), f32),
            pltpu.VMEM((TOK_DEV, 128), f32),
            pltpu.VMEM((TOK_DEV, D), f32),
            pltpu.VMEM((TOK_DEV, D), low),
            pltpu.VMEM((TOK_DEV, FF), low),
            pltpu.VMEM((TOK_DEV, FF), low),
            pltpu.VMEM((TOK_DEV, D), f32),
            pltpu.VMEM((TOK_DEV, 128), f32),
            pltpu.VMEM((TOK_DEV, D), low),
            pltpu.VMEM((D, TOK_DEV), low), pltpu.VMEM((D, TOK_DEV), low), pltpu.VMEM((D, TOK_DEV), low),
            pltpu.VMEM((H, TOK_DEV, 128), low),
            pltpu.VMEM((D, D), f32),
            pltpu.VMEM((4, 2, 2, HALF, D), low),
            pltpu.VMEM((2, HALF, 3 * GCOLS), low),
            dma((3, 5)), dma((3, 4)), dma((3, 4)), dma((3, 4)), dma((3, 4)), dma((3, 4)),
            dma((3, 2, 4)), dma((3, 2, 4)), dma((3, 4)), dma((3, 4)),
            dma((6,)), dma((3, 7)), dma((3, 7)), dma((19,)), dma((7,)),
        ],
        compiler_params=pltpu.CompilerParams(
            collective_id=0, has_side_effects=True, vmem_limit_bytes=60 * MIB
        ),
        name="forward_all",
    )(lengths, place, tok, cot, flat_weights.reshape(2, HALF, 3 * GCOLS), vec, raw, root_l, root_r)


def backward_kernel(
    owner, vt, use,
    h_w0, h_w1, h_w2, h_xT, h_cot, h_qkv, h_p, h_mT, h_n1, h_r1, h_uT, h_f, h_dg, h_n2, h_r2, h_y, h_root,
    o_back, o_grad, WR, UA, SC, o_gs, o_vec,
    G, Rc, A1, A2, B1, B2, ZR, ZP, F, SO, Gs, wa, wb, fb, gb, low_g, LT, LU, hb, nb, PT, r1, r2, gi,
    PQ, sq, sr_in, sc_out, vb, vr,
    ld, pd, cs, cr, a1s, a1r, b1s, b1r, a2s, a2r, b2s, b2r, zs, zr,
    fs, fr, ts, tr, ss, sr, ps, pr, us, ur, qs, qr, es, er, ms, mr, vs, vrs, ls,
):
    low, f32 = jnp.bfloat16, jnp.float32
    here = Here(True)
    wait_all = here.greet()
    x, y, z, c, f, r = here.x, here.y, here.z, here.c, here.f, here.r
    W = GCOLS // 2
    sent = []

    class Load:
        def __init__(self, number, src, dst):
            self.copy, self.done = local(src, dst, ld.at[number]), False

        def wait(self):
            if not self.done:
                self.copy.wait()
                self.done = True

    cot_l = Load(0, h_cot, gi)
    n2_l = Load(1, h_n2, hb)
    r2_l = Load(2, h_r2, r2)
    f_l = Load(3, h_f, fb)
    wd_l = Load(4, h_w2, wa)
    dg_l = Load(5, h_dg, gb)
    uT_l = Load(6, h_uT, LU)
    wu_l = Load(7, h_w1, wb)
    n1_l = Load(8, h_n1, nb)
    r1_l = Load(9, h_r1, r1)
    vb[...] = jnp.zeros_like(vb)
    wait_all()

    chunks = [(8, 2), (10, 2), (4, 2), (6, 2), (3, 1), (0, 1), (1, 1), (2, 1)]

    def span(n):
        block, count = chunks[n]
        return pl.ds(block * JCOLS, count * JCOLS)

    ways = {}

    def c_send(n):
        at = span(n)
        ways[n] = [
            send(G.at[:, :, 1 - c, :, :, at], Rc.at[:, :, :, :, at], cs.at[n], cr.at[n], here.to_core)
        ]
        sent.extend(ways[n])

    def first(n):
        at = span(n)
        ways[n][0].wait_recv()

        def add(j, zz, h):
            G[j, zz, c, h, :, at] = G[j, zz, c, h, :, at] + Rc[j, zz, h, :, at]

        def add_a(i, _):
            add(lax.div(i, 2), lax.rem(i, 2), 1 - x)
            return 0

        def add_b(i, _):
            add(1 - y, 2 + lax.div(i, 2), lax.rem(i, 2))
            return 0

        def add_rest(i, _):
            add(lax.div(i, 2), lax.rem(i, 2), x)
            add(y, 2 + lax.div(i, 2), lax.rem(i, 2))
            return 0

        lax.fori_loop(0, 4, add_a, 0)
        a = send(G.at[:, 0:2, c, 1 - x, :, at], A1.at[:, :, :, at], a1s.at[n], a1r.at[n], here.to_x)
        lax.fori_loop(0, 4, add_b, 0)
        b = send(G.at[1 - y, 2:4, c, :, :, at], B1.at[:, :, :, at], b1s.at[n], b1r.at[n], here.to_y)
        lax.fori_loop(0, 4, add_rest, 0)
        ways[n] = [a, b]
        sent.extend(ways[n])

    def second(n):
        at = span(n)
        ways[n][0].wait_recv()

        def add_a(i, _):
            for j in (1 - y, y):
                G[j, i, c, x, :, at] = G[j, i, c, x, :, at] + A1[j, i, :, at]
            return 0

        lax.fori_loop(0, 2, add_a, 0)
        a = send(G.at[1 - y, 0:2, c, x, :, at], A2.at[:, :, at], a2s.at[n], a2r.at[n], here.to_y)
        ways[n][1].wait_recv()

        def add_b(i, _):
            for h in (1 - x, x):
                G[y, i + 2, c, h, :, at] = G[y, i + 2, c, h, :, at] + B1[i, h, :, at]
            return 0

        lax.fori_loop(0, 2, add_b, 0)
        b = send(G.at[y, 2:4, c, 1 - x, :, at], B2.at[:, :, at], b2s.at[n], b2r.at[n], here.to_x)
        ways[n] = [a, b]
        sent.extend(ways[n])

    def third(n):
        at = span(n)
        for number, (copy, part) in enumerate(zip(ways[n], (A2, B2))):
            copy.wait_recv()

            def add(i, _, number=number, part=part):
                zz = 2 * number + i
                G[y, zz, c, x, :, at] = G[y, zz, c, x, :, at] + part[i, :, at]
                return 0

            lax.fori_loop(0, 2, add, 0)
        partner = z + 1 - 2 * lax.rem(z, 2)
        near = send(
            G.at[y, partner, c, x, :, at], ZR.at[0, :, at], zs.at[n, 0], zr.at[n, 0],
            (r, 2 * partner + c),
        )
        sent.append(near)
        ways[n] = [near]

        @pl.when(inner == 0)
        def _():
            passing(n).start()

    inner = lax.rem(lax.div(z + 1, 2), 2)
    far = 2 - 2 * lax.div(z, 2)

    def passing(n):
        at = span(n)
        return pltpu.make_async_remote_copy(
            src_ref=G.at[y, pl.ds(far, 2), c, x, :, at], dst_ref=ZP.at[:, :, at], send_sem=zs.at[n, 1],
            recv_sem=zr.at[n, 1], device_id=(r, 2 * (z + 1 - 2 * lax.rem(z, 2)) + c), device_id_type=MESH,
        )

    def crossing(n, i):
        at = span(n)
        return pltpu.make_async_remote_copy(
            src_ref=G.at[y, far + i, c, x, :, at], dst_ref=ZR.at[1, :, at], send_sem=zs.at[n, 2 + i],
            recv_sem=zr.at[n, 2], device_id=(r, 2 * (far + i) + c), device_id_type=MESH,
        )

    def fourth(n):
        at = span(n)

        @pl.when(inner == 1)
        def _():
            passing(n).wait_recv()
            for i in range(2):
                G[y, far + i, c, x, :, at] = G[y, far + i, c, x, :, at] + ZP[i, :, at]
                crossing(n, i).start()

    def z_finish():
        for n in range(8):

            @pl.when(inner == 0)
            def _():
                passing(n).wait_send()

            @pl.when(inner == 1)
            def _():
                for i in range(2):
                    crossing(n, i).wait_send()

    def final(n):
        ways[n][0].wait_recv()
        crossing(n, 0).wait_recv()
        block, count = chunks[n]
        for b in range(block, block + count):
            at = pl.ds(b * JCOLS, JCOLS)
            total = G[y, z, c, x, :, at].astype(f32)
            for step in range(2):
                total = total + ZR[step, :, at].astype(f32)
            F[b] = total.astype(low)

    homes = []

    spreads = {}
    diagonals = []

    def spread(g):
        at = pl.ds(4 * g, 4)
        to = WR.at[x, y, at]
        a = send(F.at[at], to, fs.at[g, 0], fr.at[g, 0], here.to_x)
        b = send(F.at[at], to, fs.at[g, 1], fr.at[g, 1], here.to_y)
        homes.append(local(F.at[at], to, ls.at[g]))
        sent.extend([a, b])
        spreads[g] = (a, b)

    def spread_on(g):
        a, b = spreads[g]
        a.wait_recv()
        part = WR.at[1 - x, y, pl.ds(4 * g, 2)]
        da = send(part, part, fs.at[g, 2], fr.at[g, 2], here.to_y)
        b.wait_recv()
        part = WR.at[x, 1 - y, pl.ds(4 * g + 2, 2)]
        db = send(part, part, fs.at[g, 3], fr.at[g, 3], here.to_x)
        sent.extend([da, db])
        diagonals.extend([da, db])

    def token_send(source, landing, number):
        out = []
        for step in range(1, 8):
            to = here.pair(step)
            out.append(
                send(source(to), landing.at[f], ts.at[number, step - 1], tr.at[number, step - 1], (r, to))
            )
        homes.append(local(source(f), landing.at[f], ls.at[3 + number]))
        sent.extend(out)
        return out

    def square(ref, at):
        return ref[:, :, :, :, at].reshape(D, at.size)

    def own_rows(ref, core):
        return jnp.concatenate(
            [ref[pl.ds(pl.multiple_of((2 * zz + core) * 96, 96), 96), :] for zz in range(4)], axis=0
        )

    def gradient(left, right, block, start, count, core):
        rows = own_rows(left, core)

        def one(i, _):
            out = jnp.dot(rows, right[:, cols(start + i * D, D)], preferred_element_type=f32)
            out = out.astype(low).reshape(4, 2, HALF, D)
            for j in range(2):
                at = cols((block + i) * JCOLS, JCOLS)
                G[j, :, core, :, :, at] = out[:, :, :, j * JCOLS : (j + 1) * JCOLS]
            return 0

        lax.fori_loop(0, count, one, 0)

    def eight(v):
        return jnp.sum(v.reshape(8, 8, v.shape[1]), axis=0)

    def norm_back(i, carry, grad, n, rr, gain):
        zed = grad * gain
        back = rr * (
            zed - jnp.mean(zed, axis=1, keepdims=True) - n * jnp.mean(zed * n, axis=1, keepdims=True)
        )
        rounded = back.astype(low)
        return back, rounded, (
            carry[0] + eight(grad * n), carry[1] + eight(grad), carry[2] + eight(rounded.astype(f32))
        )

    zero = jnp.zeros((8, D), f32)

    def put(row, total):
        vb[0, row : row + 1, :] = jnp.sum(total, axis=0, keepdims=True)

    def flip(source, target, count):
        def one(i, _):
            at = cols(i * 128, 128)
            target[at, :] = jnp.transpose(source[:, at])
            return 0

        lax.fori_loop(0, count, one, 0)

    ta = token_send(lambda to: h_y.at[to], o_back, 0)
    cot_l.wait()
    n2_l.wait()
    r2_l.wait()

    def back_two(i, carry):
        at = pl.ds(pl.multiple_of(i * 64, 64), 64)
        grad = gi[i].astype(f32) * use[at, 0:1]
        back, rounded, carry = norm_back(i, carry, grad, hb[at, :], r2[at, 0:1], vt[6:7, :])
        hb[at, :] = back
        low_g[at, :] = rounded
        return carry

    sums = lax.fori_loop(0, 8, back_two, (zero, zero, zero))
    put(6, sums[0])
    put(7, sums[1])
    put(3, sums[2])
    flip(low_g, LT, 6)
    f_l.wait()
    gradient(LT, fb, 8, 0, 2, 1 - c)
    c_send(0)
    gradient(LT, fb, 10, 2 * D, 2, 1 - c)
    c_send(1)
    gradient(LT, fb, 8, 0, 4, c)
    qkv_l = Load(10, h_qkv, fb.at[:, : 3 * D])
    mT_l = Load(11, h_mT, LT)
    wd_l.wait()
    dg_l.wait()

    def back_up(i, _):
        at = cols(i * 256, 256)
        acc = jnp.dot(low_g[...], square(wa, at), preferred_element_type=f32)
        gb[:, at] = (acc * gb[:, at].astype(f32)).astype(low)
        return 0

    first(0)
    lax.fori_loop(0, 6, back_up, 0)
    first(1)
    uT_l.wait()
    gradient(LU, gb, 4, 0, 2, 1 - c)
    c_send(2)
    lax.fori_loop(6, 12, back_up, 0)
    wq_l = Load(12, h_w0, wa)
    gradient(LU, gb, 4, 0, 2, c)
    first(2)
    gradient(LU, gb, 6, 2 * D, 2, 1 - c)
    c_send(3)
    gradient(LU, gb, 6, 2 * D, 2, c)
    xT_l = Load(13, h_xT, LU)
    second(0)
    first(3)
    wu_l.wait()

    def back_x1(i, _):
        at = cols(i * 512, 512)
        hb[...] += lax.dot_general(
            gb[:, at], square(wb, at), (((1,), (1,)), ((), ())), preferred_element_type=f32
        )
        return 0

    lax.fori_loop(0, 6, back_x1, 0)
    second(1)
    root_l = [Load(14 + n, h_root.at[n], wb.at[:, :, :, :, n * D : (n + 1) * D]) for n in range(4)]
    n1_l.wait()
    r1_l.wait()

    def back_one(i, carry):
        at = pl.ds(pl.multiple_of(i * 64, 64), 64)
        back, rounded, carry = norm_back(i, carry, hb[at, :], nb[at, :], r1[at, 0:1], vt[4:5, :])
        hb[at, :] = back
        low_g[at, :] = rounded
        return carry

    sums = lax.fori_loop(0, 8, back_one, (zero, zero, zero))
    put(4, sums[0])
    put(5, sums[1])
    put(2, sums[2])
    third(0)
    mT_l.wait()
    gradient(LT, low_g, 3, 0, 1, 1 - c)
    c_send(4)
    gradient(LT, low_g, 3, 0, 1, c)
    wq_l.wait()

    def back_mix(i, _):
        out = lax.dot_general(
            low_g[...], wa[pl.ds(2 * i, 2), :, :, :, 3 * D : 4 * D].reshape(JCOLS, D),
            (((1,), (1,)), ((), ())), preferred_element_type=f32,
        )
        gb[:, cols(3 * D + i * JCOLS, JCOLS)] = out.astype(low)
        return 0

    for row in range(4):

        def total(i, acc, row=row):
            at = pl.ds(pl.multiple_of(i * 64, 64), 64)
            return acc + eight(gb[at, row * D : (row + 1) * D].astype(f32))

        put(8 + row, lax.fori_loop(0, 8, total, zero))
    lax.fori_loop(0, 2, back_mix, 0)
    second(2)
    first(4)
    qkv_l.wait()

    def fetch(i):
        return pltpu.make_async_copy(h_p.at[pl.ds(2 * i, 2)], PT.at[i % 2], pd.at[i % 2])

    fetch(0).start()

    def attend(i):
        slot = i % 2
        if i < 5:
            fetch(i + 1).start()
        q2, k2 = fb[:, cols(i * 128, 128)], fb[:, cols(D + i * 128, 128)]
        v2, go2 = fb[:, cols(2 * D + i * 128, 128)], gb[:, cols(3 * D + i * 128, 128)]
        kT = jnp.transpose(k2)
        lane = lax.broadcasted_iota(jnp.int32, (TOK_DEV, 128), 1)
        fetch(i).wait()
        parts = []
        gk = jnp.zeros((TOK_DEV, 128), f32)
        gv = jnp.where(use[:, :] > 0, 0.0, go2.astype(f32))
        for half in range(2):
            mine = (lane < HD) if half == 0 else (lane >= HD)
            none = jnp.zeros_like(v2)
            p = PT[slot, half]
            gp = lax.dot_general(
                jnp.where(mine, v2, none), go2, (((1,), (1,)), ((), ())), preferred_element_type=f32
            )
            pf = p.astype(f32)
            gs = (pf * (gp - jnp.sum(pf * gp, axis=0, keepdims=True))).astype(low)
            gk = gk + jnp.dot(gs, jnp.where(mine, q2, none), preferred_element_type=f32)
            gv = gv + jnp.dot(p, jnp.where(mine, go2, none), preferred_element_type=f32)
            parts.append(jnp.dot(kT[half * HD : (half + 1) * HD], gs, preferred_element_type=f32))
        gq = jnp.transpose(jnp.concatenate(parts, axis=0)) * (HD ** (-0.5))
        gb[:, cols(i * 128, 128)] = gq.astype(low)
        gb[:, cols(D + i * 128, 128)] = gk.astype(low)
        gb[:, cols(2 * D + i * 128, 128)] = gv.astype(low)

    attend(0)
    attend(1)
    third(1)
    fourth(0)
    attend(2)
    attend(3)
    second(3)
    attend(4)
    fourth(1)
    attend(5)
    third(2)

    def back_x(i, _):
        at = cols(i * D, D)
        hb[...] += lax.dot_general(
            gb[:, at], square(wa, at), (((1,), (1,)), ((), ())), preferred_element_type=f32
        )
        return 0

    lax.fori_loop(0, 3, back_x, 0)

    def rows_low(i, _):
        gi[i] = hb[pl.ds(pl.multiple_of(i * 64, 64), 64), :].astype(low)
        return 0

    lax.fori_loop(0, 8, rows_low, 0)
    tb = token_send(lambda to: gi.at[to], o_grad, 1)
    second(4)
    xT_l.wait()
    for n in range(3):
        gradient(LU, gb, n, n * D, 1, 1 - c)
        c_send(5 + n)
    fourth(2)
    gradient(LU, gb, 0, 0, 1, c)
    first(5)
    gradient(LU, gb, 1, D, 1, c)
    first(6)
    gradient(LU, gb, 2, 2 * D, 1, c)
    first(7)
    third(3)
    for row, start in ((0, 0), (1, 2 * D)):

        def total(i, acc, start=start):
            at = pl.ds(pl.multiple_of(i * 64, 64), 64)
            return acc + eight(gb[at, start : start + D].astype(f32))

        put(row, lax.fori_loop(0, 8, total, zero))
    vec_copy = send(vb.at[0], vr.at[0], vs.at[0], vrs.at[0], here.to_core)
    sent.append(vec_copy)
    third(4)
    second(5)
    fourth(3)
    vec_copy.wait_recv()
    vb[1] = vb[0] + vr[0]
    vec_copy = send(vb.at[1], vr.at[1], vs.at[1], vrs.at[1], here.to_x)
    sent.append(vec_copy)
    second(6)
    third(5)
    fourth(4)
    vec_copy.wait_recv()
    vb[2] = vb[1] + vr[1]
    vec_copy = send(vb.at[2], vr.at[2], vs.at[2], vrs.at[2], here.to_y)
    sent.append(vec_copy)
    second(7)
    final(0)
    final(1)
    spread(2)
    fourth(5)
    third(6)
    final(2)
    final(3)
    spread(1)
    fourth(6)
    third(7)
    final(4)
    fourth(7)
    final(5)
    final(6)
    spread_on(2)
    spread_on(1)
    final(7)
    spread(0)
    jc = cols(y * JCOLS, JCOLS)
    other = cols((1 - y) * JCOLS, JCOLS)
    slot_copies = []
    for step in range(1, 9):
        to = here.pair(step)
        for t in range(2):
            b = jnp.int32(-1)
            for k in range(NBLK):
                b = jnp.where(owner[k] == 2 * to + t, k, b)
            flag = (b >= 0).astype(f32)
            SO[step - 1, t] = (F[jnp.maximum(b, 0)].astype(f32) * flag).astype(low)
        if step < 8:
            slot_copies.append(
                send(SO.at[step - 1], Gs.at[:, f, x, :, jc], ss.at[step - 1], sr.at[step - 1], (r, to))
            )
    sent.extend(slot_copies)
    own = local(SO.at[7], Gs.at[:, f, x, :, jc], ls.at[5])
    hops = []
    for step in range(8):
        src = here.pair(step)
        if step == 0:
            own.wait()
        else:
            slot_copies[step - 1].wait_recv()
        part = Gs.at[:, src, x, :, jc]
        hops.append(
            (
                send(part, part, ps.at[0, step], pr.at[0, step], here.to_x),
                send(part, part, ps.at[1, step], pr.at[1, step], here.to_y),
            )
        )
    ends = []
    for step in range(8):
        src = here.pair(step)
        hops[step][0].wait_recv()
        part = Gs.at[0, src, 1 - x, :, jc]
        ends.append(send(part, part, ps.at[2, step], pr.at[2, step], here.to_y))
        hops[step][1].wait_recv()
        part = Gs.at[1, src, x, :, other]
        ends.append(send(part, part, ps.at[3, step], pr.at[3, step], here.to_x))
        sent.extend(hops[step])
    sent.extend(ends)
    vec_copy.wait_recv()
    vb[3] = vb[2] + vr[2]
    vec_copies = []
    for step in (1, 2, 3):
        vec_copies.append(
            send(vb.at[3], vr.at[2 + step], vs.at[2 + step], vrs.at[2 + step], here.along(step))
        )
    sent.extend(vec_copies)
    for load in root_l:
        load.wait()
    for copy in ends:
        copy.wait_recv()
    spread_on(0)
    homes.append(local(Gs, o_gs, ls.at[6]))
    for t in range(2):
        whole = Gs[t].reshape(D, D)
        rows = wb[:, :, x, :, t * D : (t + 1) * D].reshape(JCOLS, D)
        half = jnp.dot(rows, whole, preferred_element_type=f32).astype(low)
        right = square(wb, cols((2 + t) * D + y * JCOLS, JCOLS))
        part = jnp.dot(half, right, preferred_element_type=f32)
        PQ[t] = part.astype(low).reshape(8, HALF, JCOLS)
        sq[t] = jnp.sum((part * part).reshape(48, 8, JCOLS), axis=0)
    ucopies = []
    for step in range(1, 8):
        to = here.pair(step)
        ucopies.append(
            send(PQ.at[:, to], UA.at[x, y, pl.ds(2 * f, 2)], us.at[step - 1], ur.at[step - 1], (r, to))
        )
    sent.extend(ucopies)
    own = local(PQ.at[:, f], UA.at[x, y, pl.ds(2 * f, 2)], ls.at[7])
    squares = []
    for number, to in enumerate((here.to_x, here.to_y, here.to_d)):
        squares.append(send(sq, sr_in.at[number], es.at[number], er.at[number], to))
    sent.extend(squares)
    uhops = []
    for step in range(8):
        src = here.pair(step)
        if step == 0:
            own.wait()
        else:
            ucopies[step - 1].wait_recv()
        part = UA.at[x, y, pl.ds(2 * src, 2)]
        uhops.append(
            (
                send(part, part, qs.at[0, step], qr.at[0, step], here.to_x),
                send(part, part, qs.at[1, step], qr.at[1, step], here.to_y),
            )
        )
        if step == 3:
            for copy in squares:
                copy.wait_recv()
            for t in range(2):
                total = sq[t] + sr_in[0, t] + sr_in[1, t] + sr_in[2, t]
                mean = jnp.sum(jnp.sum(total, axis=1, keepdims=True), axis=0, keepdims=True) * (1.0 / (D * D))
                sc_out[t] = jnp.broadcast_to(lax.rsqrt(mean + RMS_EPS), (8, 128))
            scales = []
            for number in range(1, 8):
                to = here.pair(number)
                scales.append(
                    send(
                        sc_out, SC.at[pl.ds(2 * f, 2)], ms.at[number - 1], mr.at[number - 1], (r, to)
                    )
                )
            sent.extend(scales)
            homes.append(local(sc_out, SC.at[pl.ds(2 * f, 2)], ls.at[8]))
    uends = []
    for step in range(8):
        src = here.pair(step)
        uhops[step][0].wait_recv()
        part = UA.at[1 - x, y, 2 * src]
        uends.append(send(part, part, qs.at[2, step], qr.at[2, step], here.to_y))
        uhops[step][1].wait_recv()
        part = UA.at[x, 1 - y, 2 * src + 1]
        uends.append(send(part, part, qs.at[3, step], qr.at[3, step], here.to_x))
        sent.extend(uhops[step])
    sent.extend(uends)
    total = vb[3]
    for copy in vec_copies:
        copy.wait_recv()
    for step in range(3):
        total = total + vr[3 + step]
    vb[4] = total
    homes.append(local(vb.at[4], o_vec, ls.at[9]))
    for copy in diagonals + uends + scales + ta + tb:
        copy.wait_recv()
    for copy in homes:
        copy.wait()
    z_finish()
    for copy in sent:
        copy.wait_send()


def backward_all(owner, vt, use, saved):
    any_spec = pl.BlockSpec(memory_space=pl.ANY)
    vmem = pl.BlockSpec(memory_space=pltpu.VMEM)
    smem = pl.BlockSpec(memory_space=pltpu.SMEM)
    dma = pltpu.SemaphoreType.DMA
    shape = jax.ShapeDtypeStruct
    low, f32 = jnp.bfloat16, jnp.float32
    JW = 12 * JCOLS
    square = (4, 2, 2, HALF, GCOLS)
    return pl.pallas_call(
        backward_kernel,
        out_shape=[
            shape((8, 64, D), low), shape((8, 64, D), low),
            shape((2, 2, 12, HALF, JCOLS), low), shape((2, 2, 16, HALF, JCOLS), low),
            shape((16, 8, 128), f32), shape((2, 8, 2, HALF, D), low), shape((16, D), f32),
        ],
        in_specs=[smem, vmem, vmem] + [any_spec] * 17,
        out_specs=[any_spec] * 7,
        scratch_shapes=[
            pltpu.VMEM((2, 4, 2, 2, HALF, JW), low),
            pltpu.VMEM((2, 4, 2, HALF, JW), low),
            pltpu.VMEM((2, 2, HALF, JW), low),
            pltpu.VMEM((2, HALF, JW), low),
            pltpu.VMEM((2, 2, HALF, JW), low),
            pltpu.VMEM((2, HALF, JW), low),
            pltpu.VMEM((2, HALF, JW), low),
            pltpu.VMEM((2, HALF, JW), low),
            pltpu.VMEM((12, HALF, JCOLS), low),
            pltpu.VMEM((8, 2, HALF, JCOLS), low),
            pltpu.VMEM((2, 8, 2, HALF, D), low),
            pltpu.VMEM(square, low),
            pltpu.VMEM(square, low),
            pltpu.VMEM((TOK_DEV, FF), low),
            pltpu.VMEM((TOK_DEV, FF), low),
            pltpu.VMEM((TOK_DEV, D), low),
            pltpu.VMEM((D, TOK_DEV), low),
            pltpu.VMEM((D, TOK_DEV), low),
            pltpu.VMEM((TOK_DEV, D), f32),
            pltpu.VMEM((TOK_DEV, D), f32),
            pltpu.VMEM((2, 2, TOK_DEV, TOK_DEV), low),
            pltpu.VMEM((TOK_DEV, 128), f32),
            pltpu.VMEM((TOK_DEV, 128), f32),
            pltpu.VMEM((8, 64, D), low),
            pltpu.VMEM((2, 8, HALF, JCOLS), low),
            pltpu.VMEM((2, 8, JCOLS), f32),
            pltpu.VMEM((3, 2, 8, JCOLS), f32),
            pltpu.VMEM((2, 8, 128), f32),
            pltpu.VMEM((5, 16, D), f32),
            pltpu.VMEM((6, 16, D), f32),
            dma((18,)), dma((2,)), dma((8,)), dma((8,)),
            dma((8,)), dma((8,)), dma((8,)), dma((8,)), dma((8,)), dma((8,)), dma((8,)), dma((8,)),
            dma((8, 4)), dma((8, 3)), dma((3, 4)), dma((3, 4)),
            dma((2, 7)), dma((2, 7)), dma((7,)), dma((7,)), dma((4, 8)), dma((4, 8)),
            dma((7,)), dma((7,)), dma((4, 8)), dma((4, 8)), dma((3,)), dma((3,)), dma((7,)), dma((7,)),
            dma((6,)), dma((6,)), dma((10,)),
        ],
        compiler_params=pltpu.CompilerParams(
            collective_id=1, has_side_effects=True, vmem_limit_bytes=60 * MIB
        ),
        name="backward_all",
    )(owner, vt, use, *saved)


def finish_kernel(
    owner, hot, back, grad, wr, ua, sc, gs, vec, stat_l, stat_r, wf, vecs, mom1, mom2,
    layer_out, input_grad, wg, nw, new_l, new_r, out1, out2, outv,
    gb, sl, sr, ub, rb, wb, nb, gg, tb, to, ls, os,
):
    low, f32 = jnp.bfloat16, jnp.float32
    f = lax.axis_index("fsdp")
    gs_load = local(gs, gb, ls.at[5])
    stats = [
        (local(stat_l.at[t], sl.at[t], ls.at[6 + 2 * t]), local(stat_r.at[t], sr.at[t], ls.at[7 + 2 * t]))
        for t in range(2)
    ]
    loads = [
        local(back, tb.at[0], ls.at[0]), local(grad, tb.at[1], ls.at[1]),
        local(wr, rb, ls.at[2]), local(ua, ub, ls.at[3]), local(wf, wb, ls.at[4]),
    ]
    outs = []
    gs_load.wait()
    for t in range(2):
        stats[t][0].wait()

        def left(i, _, t=t):
            at = pl.ds(pl.multiple_of(i * 384, 384), 384)
            rows = gb[t, pl.ds(4 * i, 4)].reshape(384, D)
            part = lax.dot_general(
                rows, gb[t].reshape(D, D), (((1,), (1,)), ((), ())), preferred_element_type=f32
            )
            sl[t, at, :] = STAT_DECAY * sl[t, at, :] + (1.0 - STAT_DECAY) * part
            return 0

        lax.fori_loop(0, 2, left, 0)
        outs.append(local(sl.at[t], new_l.at[t], os.at[4 + 2 * t]))
        stats[t][1].wait()
        for i in range(3):
            at = pl.ds(i * 256, 256)
            part = lax.dot_general(
                gb[t, :, :, :, at].reshape(D, 256), gb[t].reshape(D, D), (((0,), (0,)), ((), ())),
                preferred_element_type=f32,
            )
            sr[t, at, :] = STAT_DECAY * sr[t, at, :] + (1.0 - STAT_DECAY) * part
        outs.append(local(sr.at[t], new_r.at[t], os.at[5 + 2 * t]))
    for number, target in enumerate((layer_out, input_grad)):
        loads[number].wait()
        to[number] = jnp.dot(
            hot[...], tb[number].reshape(TOK_DEV, D), preferred_element_type=f32
        ).astype(low)
        outs.append(local(to.at[number], target, os.at[number]))
    loads[3].wait()
    loads[4].wait()
    for h in range(2):
        for b in range(NBLK):
            slot = owner[b]
            scale = LR_MATRIX * sc[slot, 0:1, 0:1]
            for j in range(2):
                at = pl.ds(b * D + j * JCOLS, JCOLS)
                nb[h, :, at] = wb[h, :, at] - scale * ub[h, j, slot].astype(f32)
        outs.append(local(nb.at[h], nw.at[h], os.at[3 + 5 * h]))
    loads[2].wait()
    for h in range(2):

        def one(b, _, h=h):
            for j in range(2):
                gg[h, :, cols(b * D + j * JCOLS, JCOLS)] = rb[h, j, b].astype(f32)
            return 0

        lax.fori_loop(0, 12, one, 0)
        outs.append(local(gg.at[h], wg.at[h], os.at[2 + 7 * h]))
    mine = jnp.zeros((NBLK, 96), f32)
    for number in range(8):
        mine = jnp.where(f == number, vec[:NBLK, number * 96 : (number + 1) * 96], mine)
    fresh1 = BETA_ONE * mom1[...] + (1.0 - BETA_ONE) * mine
    fresh2 = BETA_TWO * mom2[...] + (1.0 - BETA_TWO) * mine * mine
    out1[...] = fresh1
    out2[...] = fresh2
    outv[...] = vecs[...] - LR_VECTOR * (fresh1 / (1.0 - BETA_ONE**STEP)) / (
        jnp.sqrt(fresh2 / (1.0 - BETA_TWO**STEP)) + ADAM_EPS
    )
    for copy in outs:
        copy.wait()


def finish_all(owner, hot, results, stat_l, stat_r, wf, vecs, mom1, mom2):
    any_spec = pl.BlockSpec(memory_space=pl.ANY)
    vmem = pl.BlockSpec(memory_space=pltpu.VMEM)
    smem = pl.BlockSpec(memory_space=pltpu.SMEM)
    dma = pltpu.SemaphoreType.DMA
    shape = jax.ShapeDtypeStruct
    low, f32 = jnp.bfloat16, jnp.float32
    wide = (2, HALF, 3 * GCOLS)
    back, grad, wr, ua, sc, gs, vec = results
    return pl.pallas_call(
        finish_kernel,
        out_shape=[
            shape((TOK_DEV, D), low), shape((TOK_DEV, D), low), shape(wide, f32), shape(wide, f32),
            shape((2, D, D), f32), shape((2, D, D), f32),
            shape((NBLK, 96), f32), shape((NBLK, 96), f32), shape((NBLK, 96), f32),
        ],
        in_specs=[smem, vmem] + [any_spec] * 4 + [vmem, any_spec, vmem] + [any_spec] * 3 + [vmem] * 3,
        out_specs=[any_spec] * 6 + [vmem] * 3,
        scratch_shapes=[
            pltpu.VMEM((2, 8, 2, HALF, D), low),
            pltpu.VMEM((2, D, D), f32),
            pltpu.VMEM((2, D, D), f32),
            pltpu.VMEM((2, 2, 16, HALF, JCOLS), low),
            pltpu.VMEM((2, 2, 12, HALF, JCOLS), low),
            pltpu.VMEM(wide, f32),
            pltpu.VMEM(wide, f32),
            pltpu.VMEM(wide, f32),
            pltpu.VMEM((2, 8, 64, D), low),
            pltpu.VMEM((2, TOK_DEV, D), low),
            dma((10,)), dma((10,)),
        ],
        compiler_params=pltpu.CompilerParams(vmem_limit_bytes=56 * MIB),
        name="finish_all",
    )(
        owner, hot, back, grad, wr, ua, sc, gs, vec, stat_l, stat_r, wf.reshape(wide), vecs, mom1, mom2
    )


def fast_body(
    tokens,
    cotangent,
    place,
    seq_lengths,
    random_blocks,
    owner_slot,
    flat_weights,
    vectors,
    moment_first,
    moment_second,
    stat_left,
    stat_right,
    root_left,
    root_right,
):
    peers = lax.axis_size("fsdp")
    share_rows = TOK_DEV // peers
    w0, w1, w2, vt, *saved = forward_all(
        seq_lengths, place[None, :], tokens, cotangent, flat_weights, vectors.T,
        jnp.transpose(random_blocks, (2, 0, 1)), root_left, root_right,
    )
    *saved, use, hot = saved
    saved[-2] = saved[-2].reshape(peers, share_rows, D)
    results = backward_all(owner_slot, vt, use, [w0, w1, w2] + saved)
    layer_out, input_grad, weight_grads, new_weights, *others = finish_all(
        owner_slot, hot, results, stat_left, stat_right, flat_weights, vectors.T, moment_first.T,
        moment_second.T,
    )
    return (
        layer_out,
        input_grad,
        weight_grads.reshape(flat_weights.shape),
        new_weights.reshape(flat_weights.shape),
        *others[:2],
        *[vec.T for vec in others[2:]],
    )


def plain_body(
    tokens,
    cotangent,
    place,
    seq_lengths,
    random_blocks,
    owner_slot,
    flat_weights,
    vectors,
    moment_first,
    moment_second,
    stat_left,
    stat_right,
    root_left,
    root_right,
):
    peers = lax.axis_size("fsdp")
    share_rows = TOK_DEV // peers
    order_ids = jnp.argsort(place)
    outgoing = (
        tokens[order_ids].reshape(peers, share_rows, D),
        cotangent[order_ids].reshape(peers, share_rows, D),
    )
    arrived = (
        lax.all_to_all(outgoing[0], "fsdp", split_axis=0, concat_axis=0, tiled=True),
        lax.all_to_all(outgoing[1], "fsdp", split_axis=0, concat_axis=0, tiled=True),
    )
    inputs = arrived[0].reshape(TOK_DEV, D)
    upstream = arrived[1].reshape(TOK_DEV, D).astype(jnp.float32)
    weight_copy, vector_copy = (
        lax.all_gather(flat_weights.astype(jnp.bfloat16), "fsdp", axis=0, tiled=True),
        lax.all_gather(vectors.astype(jnp.bfloat16), "fsdp", axis=0, tiled=True),
    )
    vecs_full = vector_copy.astype(jnp.float32)
    b_up = jnp.transpose(vecs_full[:, 8:]).reshape(FF)
    seq_id, position, in_use, seq_blocks = layout(seq_lengths[0])
    picks = random_keys(random_blocks, seq_blocks)
    slot_ids = jnp.arange(TOK_DEV, dtype=jnp.int32)
    real_rows = in_use.astype(jnp.float32)[:, None]
    bias_qkv = jnp.concatenate([vecs_full[:, 0], jnp.zeros((D,), jnp.float32), vecs_full[:, 1]])
    qkv_low = (
        jnp.dot(inputs, weight_copy[:, : 3 * D], preferred_element_type=jnp.float32) + bias_qkv
    ).astype(jnp.bfloat16)
    qkv_heads = qkv_low.reshape(TOK_DEV, 3, H, HD)
    queries = qkv_heads[:, 0]
    key_heads = qkv_heads[:, 1]
    value_heads = qkv_heads[:, 2]
    block_rows = min(512, TOK_DEV)
    block_count = TOK_DEV // block_rows
    score_scale = HD ** (-0.5)

    def split_blocks(array):
        return array.reshape((block_count, block_rows) + array.shape[1:])

    block_inputs = (
        split_blocks(queries),
        split_blocks(seq_id),
        split_blocks(position),
        split_blocks(in_use),
        split_blocks(picks),
        split_blocks(slot_ids),
    )

    def scores_of(query_block, q_seq, q_pos, q_use, q_pick, q_slot):
        raw_scores = (
            jnp.einsum("qhd,khd->hqk", query_block, key_heads, preferred_element_type=jnp.float32)
            * score_scale
        )
        keep_mask = allowed(q_seq, q_pos, q_use, q_pick, q_slot, seq_id, position, in_use, slot_ids)
        return jnp.where(keep_mask, raw_scores, MASKED_SCORE)

    def forward_block(pieces):
        scores = scores_of(pieces[0], pieces[1], pieces[2], pieces[3], pieces[4], pieces[5])
        row_max = jnp.max(scores, axis=-1, keepdims=True)
        expo = jnp.exp(scores - row_max)
        row_total = jnp.sum(expo, axis=-1, keepdims=True)
        probs_low = (expo / row_total).astype(jnp.bfloat16)
        mixed_block = jnp.einsum(
            "hqk,khd->qhd", probs_low, value_heads, preferred_element_type=jnp.float32
        )
        return (mixed_block.reshape(block_rows, D), (row_max + jnp.log(row_total))[:, :, 0])

    attended, log_totals = lax.map(forward_block, block_inputs)
    mixed = attended.reshape(TOK_DEV, D).astype(jnp.bfloat16)
    branch = (
        jnp.dot(mixed, weight_copy[:, 3 * D : 4 * D], preferred_element_type=jnp.float32)
        + vecs_full[:, 2]
    )
    hidden_one = inputs.astype(jnp.float32) + branch
    x_one, norm_one_back = jax.vjp(layer_norm, hidden_one, vecs_full[:, 4], vecs_full[:, 5])
    x_one_low = x_one.astype(jnp.bfloat16)
    pre_act = (
        jnp.dot(x_one_low, weight_copy[:, 4 * D : 4 * D + FF], preferred_element_type=jnp.float32)
        + b_up
    )
    act, gelu_back = jax.vjp(gelu_tanh, pre_act)
    act_low = act.astype(jnp.bfloat16)
    ffn = contract_cols(act_low, weight_copy[:, 4 * D + FF :]) + vecs_full[:, 3]
    hidden_two = x_one + ffn
    result, norm_two_back = jax.vjp(layer_norm, hidden_two, vecs_full[:, 6], vecs_full[:, 7])
    layer_rows = (result * real_rows).astype(jnp.bfloat16)
    weight_copy = lax.all_gather(flat_weights.astype(jnp.bfloat16), "fsdp", axis=0, tiled=True)
    d_result = upstream * real_rows
    d_two, d_gain_two, d_shift_two = norm_two_back(d_result)
    d_ffn = d_two.astype(jnp.bfloat16)
    d_act = jnp.dot(d_ffn, weight_copy[:, 4 * D + FF :], preferred_element_type=jnp.float32)
    (d_pre,) = gelu_back(d_act)
    d_pre_low = d_pre.astype(jnp.bfloat16)
    grad_down = contract_rows(d_ffn, act_low)
    grad_up = contract_rows(x_one_low, d_pre_low)
    d_x_one = d_two + contract_cols(d_pre_low, weight_copy[:, 4 * D : 4 * D + FF])
    d_one, d_gain_one, d_shift_one = norm_one_back(d_x_one)
    up_sums = jnp.transpose(jnp.sum(d_pre_low.astype(jnp.float32), axis=0).reshape(FF // D, D))
    ffn_vec = jnp.concatenate(
        [
            jnp.sum(d_ffn.astype(jnp.float32), axis=0)[:, None],
            d_gain_one[:, None],
            d_shift_one[:, None],
            d_gain_two[:, None],
            d_shift_two[:, None],
            up_sums,
        ],
        axis=1,
    )
    ffn_mats = jnp.concatenate([grad_up, grad_down], axis=1)
    d_branch = d_one.astype(jnp.bfloat16)
    grad_out = contract_rows(mixed, d_branch)
    d_mixed = (
        contract_cols(d_branch, weight_copy[:, 3 * D : 4 * D])
        .astype(jnp.bfloat16)
        .reshape(TOK_DEV, H, HD)
    )

    def backward_block(carry, pieces):
        key_grad, value_grad = carry
        query_block = pieces[0]
        log_total = pieces[6]
        out_grad = pieces[7]
        scores = scores_of(pieces[0], pieces[1], pieces[2], pieces[3], pieces[4], pieces[5])
        probs = jnp.exp(scores - log_total[:, :, None])
        probs_low = probs.astype(jnp.bfloat16)
        value_grad = value_grad + jnp.einsum(
            "hqk,qhd->khd", probs_low, out_grad, preferred_element_type=jnp.float32
        )
        prob_grad = jnp.einsum(
            "qhd,khd->hqk", out_grad, value_heads, preferred_element_type=jnp.float32
        )
        score_grad = (
            probs * (prob_grad - jnp.sum(probs * prob_grad, axis=-1, keepdims=True))
        ).astype(jnp.bfloat16)
        query_grad = (
            jnp.einsum("hqk,khd->qhd", score_grad, key_heads, preferred_element_type=jnp.float32)
            * score_scale
        )
        key_grad = (
            key_grad
            + jnp.einsum(
                "hqk,qhd->khd", score_grad, query_block, preferred_element_type=jnp.float32
            )
            * score_scale
        )
        return ((key_grad, value_grad), query_grad)

    zero_heads = jnp.zeros((TOK_DEV, H, HD), jnp.float32)
    (key_grad, value_grad), query_grad = lax.scan(
        backward_block, (zero_heads, zero_heads), block_inputs + (log_totals, split_blocks(d_mixed))
    )
    d_qkv = jnp.concatenate(
        [
            query_grad.reshape(TOK_DEV, D),
            key_grad.reshape(TOK_DEV, D),
            value_grad.reshape(TOK_DEV, D),
        ],
        axis=1,
    ).astype(jnp.bfloat16)
    grad_qkv = contract_rows(inputs, d_qkv)
    d_inputs = d_one + contract_cols(d_qkv, weight_copy[:, : 3 * D])
    qkv_sums = jnp.sum(d_qkv.astype(jnp.float32), axis=0)
    attn_vec = jnp.stack(
        [qkv_sums[:D], qkv_sums[2 * D :], jnp.sum(d_branch.astype(jnp.float32), axis=0)], axis=1
    )
    attn_mats = jnp.concatenate([grad_qkv, grad_out], axis=1)
    mat_shard, vec_shard = (
        lax.psum_scatter(
            jnp.concatenate([attn_mats, ffn_mats], axis=1), "fsdp", scatter_dimension=0, tiled=True
        ),
        lax.psum_scatter(
            jnp.concatenate([attn_vec, ffn_vec], axis=1), "fsdp", scatter_dimension=0, tiled=True
        ),
    )
    mat_part = lax.psum_scatter(
        mat_shard.astype(jnp.bfloat16), "rep", scatter_dimension=1, tiled=True
    ).astype(jnp.float32)
    vec_shard = lax.psum(vec_shard, "rep")
    mat_shard = lax.all_gather(mat_part.astype(jnp.bfloat16), "rep", axis=1, tiled=True).astype(
        mat_part.dtype
    )
    grad_rows = d_inputs.astype(jnp.bfloat16)
    back_pair = (
        lax.all_to_all(
            layer_rows.reshape(peers, share_rows, D),
            "fsdp",
            split_axis=0,
            concat_axis=0,
            tiled=True,
        ),
        lax.all_to_all(
            grad_rows.reshape(peers, share_rows, D), "fsdp", split_axis=0, concat_axis=0, tiled=True
        ),
    )
    layer_out = (
        jnp.zeros((TOK_DEV, D), jnp.bfloat16).at[order_ids].set(back_pair[0].reshape(TOK_DEV, D))
    )
    input_grad = (
        jnp.zeros((TOK_DEV, D), jnp.bfloat16).at[order_ids].set(back_pair[1].reshape(TOK_DEV, D))
    )
    slot_count = stat_left.shape[0]
    rows_dev = flat_weights.shape[0]
    targets = (
        jnp.arange(slot_count, dtype=jnp.int32)[:, None, None]
        + slot_count * jnp.arange(peers, dtype=jnp.int32)[None, :, None]
    )
    select = (owner_slot[None, None, :] == targets).astype(jnp.float32)
    grad_pieces = mat_shard.reshape(rows_dev, NBLK, D)
    outbound = jnp.einsum("snb,rbc->snrc", select, grad_pieces, precision=PRECISE)
    inbound = lax.all_to_all(
        outbound.astype(jnp.bfloat16), "fsdp", split_axis=1, concat_axis=1, tiled=True
    ).astype(outbound.dtype)
    grad_blocks = inbound.reshape(slot_count, D, D)
    new_left = STAT_DECAY * stat_left + (1.0 - STAT_DECAY) * jnp.einsum(
        "sij,skj->sik", grad_blocks, grad_blocks, precision=PRECISE
    )
    new_right = STAT_DECAY * stat_right + (1.0 - STAT_DECAY) * jnp.einsum(
        "sji,sjk->sik", grad_blocks, grad_blocks, precision=PRECISE
    )
    left_applied = jnp.einsum("sij,sjk->sik", root_left, grad_blocks, precision=PRECISE)
    direction = jnp.einsum("sij,sjk->sik", left_applied, root_right, precision=PRECISE)
    update = direction * lax.rsqrt(
        jnp.mean(direction * direction, axis=(1, 2), keepdims=True) + RMS_EPS
    )
    returned = lax.all_to_all(
        update.reshape(slot_count, peers, rows_dev, D).astype(jnp.bfloat16),
        "fsdp",
        split_axis=1,
        concat_axis=1,
        tiled=True,
    ).astype(jnp.float32)
    step_matrix = jnp.einsum("snb,snrc->rbc", select, returned, precision=PRECISE).reshape(
        rows_dev, NBLK * D
    )
    new_weights = flat_weights - LR_MATRIX * step_matrix
    first_bias = 1.0 - BETA_ONE**STEP
    second_bias = 1.0 - BETA_TWO**STEP
    new_first = BETA_ONE * moment_first + (1.0 - BETA_ONE) * vec_shard
    new_second = BETA_TWO * moment_second + (1.0 - BETA_TWO) * vec_shard * vec_shard
    first_fixed = new_first / first_bias
    second_fixed = new_second / second_bias
    new_vectors = vectors - LR_VECTOR * first_fixed / (jnp.sqrt(second_fixed) + ADAM_EPS)
    return (
        layer_out,
        input_grad,
        mat_shard,
        new_weights,
        new_left,
        new_right,
        new_first,
        new_second,
        new_vectors,
    )


def solution(mesh):
    in_specs = (
        P(("rep", "fsdp"), None),
        P(("rep", "fsdp"), None),
        P(("rep", "fsdp")),
        P(("rep", "fsdp"), None),
        P(("rep", "fsdp"), None, None),
        P(),
        P("fsdp", None),
        P("fsdp", None),
        P("fsdp", None),
        P("fsdp", None),
        P("fsdp", None, None),
        P("fsdp", None, None),
        P("fsdp", None, None),
        P("fsdp", None, None),
    )
    out_specs = (
        P(("rep", "fsdp"), None),
        P(("rep", "fsdp"), None),
        P("fsdp", None),
        P("fsdp", None),
        P("fsdp", None, None),
        P("fsdp", None, None),
        P("fsdp", None),
        P("fsdp", None),
        P("fsdp", None),
    )
    shaped = mesh.shape["fsdp"] == 8 and mesh.shape["rep"] == 4
    body = fast_body if shaped else plain_body
    return jax.shard_map(body, mesh=mesh, in_specs=in_specs, out_specs=out_specs, check_vma=False)
```

```python
import functools

import jax
import jax.numpy as jnp
from jax import lax
from jax.experimental import pallas as pl
from jax.experimental.pallas import tpu as pltpu
from jax.sharding import PartitionSpec as P

D = 768
H = 12
HD = 64
FF = 3072
BLK = 64
NGLOB = 2
NRAND = 3
STEP = 10
SEQ_DEV = 4
TOK_DEV = 512
NBLK = 12


NORM_EPS = 1e-12
MASKED_SCORE = -1e30
STAT_DECAY = 0.5
LR_MATRIX = 0.02
LR_VECTOR = 0.1
BETA_ONE = 0.9
BETA_TWO = 0.999
ADAM_EPS = 1e-08
RMS_EPS = 1e-12
PRECISE = lax.Precision.HIGHEST


def layout(lengths):
    blocks = (lengths + (BLK - 1)) // BLK
    block_ends = jnp.cumsum(blocks)
    starts = (block_ends - blocks) * BLK
    slot_ids = jnp.arange(TOK_DEV, dtype=jnp.int32)
    seq_id = jnp.sum((slot_ids // BLK)[:, None] >= block_ends[None, :], axis=1)
    member = seq_id[:, None] == jnp.arange(SEQ_DEV, dtype=jnp.int32)[None, :]
    seq_start = jnp.sum(jnp.where(member, starts[None, :], 0), axis=1)
    length = jnp.sum(jnp.where(member, lengths[None, :], 0), axis=1)
    seq_blocks = jnp.sum(jnp.where(member, blocks[None, :], 0), axis=1)
    position = slot_ids - seq_start
    in_use = position < length
    return (seq_id, position, in_use, seq_blocks)


def random_keys(raw_picks, seq_blocks):
    per_block = seq_blocks.reshape(TOK_DEV // BLK, BLK)[:, 0]
    picked = raw_picks % jnp.maximum(per_block, 1)[:, None, None]
    return jnp.repeat(picked, BLK, axis=0)


def allowed(q_seq, q_pos, q_use, q_pick, q_slot, k_seq, k_pos, k_use, k_slot):
    q_block = q_pos // BLK
    k_block = k_pos // BLK
    same_seq = (q_seq[:, None] == k_seq[None, :]) & q_use[:, None] & k_use[None, :]
    nearby = (
        (q_block[:, None] < NGLOB)
        | (k_block[None, :] < NGLOB)
        | (jnp.abs(q_block[:, None] - k_block[None, :]) <= 1)
    )
    chosen = jnp.zeros((H, q_seq.shape[0], k_seq.shape[0]), dtype=jnp.bool_)
    for number in range(NRAND):
        chosen = chosen | (
            k_block[None, None, :] == jnp.transpose(q_pick[:, :, number])[:, :, None]
        )
    alone = jnp.logical_not(q_use)[:, None] & (q_slot[:, None] == k_slot[None, :])
    return (same_seq & nearby)[None] | same_seq[None] & chosen | alone[None]


def layer_norm(hidden, gain, shift):
    center = hidden - jnp.mean(hidden, axis=-1, keepdims=True)
    spread = jnp.mean(center * center, axis=-1, keepdims=True)
    return center * lax.rsqrt(spread + NORM_EPS) * gain + shift


def gelu_tanh(pre_act):
    return jax.nn.gelu(pre_act, approximate=True)


def contract_rows(left, right):
    return lax.dot_general(
        left, right, (((0,), (0,)), ((), ())), preferred_element_type=jnp.float32
    )


def contract_cols(left, right):
    return lax.dot_general(
        left, right, (((1,), (1,)), ((), ())), preferred_element_type=jnp.float32
    )


MESH = pl.DeviceIdType.MESH
HALF = 48
GCOLS = 3072
JCOLS = 384
MIB = 2**20


class Here:
    def __init__(self, corner=False):
        r, f = lax.axis_index("rep"), lax.axis_index("fsdp")
        self.r, self.f = r, f
        self.x, self.y = lax.rem(r, 2), lax.div(r, 2)
        self.z, self.c = lax.div(f, 2), lax.rem(f, 2)
        self.to_x = (r + 1 - 2 * self.x, f)
        self.to_y = (r + 2 - 4 * self.y, f)
        self.to_d = (3 - r, f)
        self.corner = corner
        self.to_core = (r, f + 1 - 2 * self.c)

    def z_plus(self, step):
        return lax.rem(self.z + step, 4)

    def along(self, step):
        return (self.r, 2 * self.z_plus(step) + self.c)

    def peer(self, step):
        return lax.rem(self.f + step, 8)

    def pair(self, step):
        zz = (self.z, self.z + 1 - 2 * lax.rem(self.z, 2), lax.rem(self.z + 2, 4), 3 - self.z)[step // 2 % 4]
        return 2 * zz + (1 - self.c if step % 2 else self.c)

    def greet(self):
        barrier = pltpu.get_barrier_semaphore()
        friends = [self.to_x, self.to_y] + [self.to_d] * self.corner
        friends += [(self.r, self.peer(s)) for s in range(1, 8)]
        for friend in friends:
            pl.semaphore_signal(barrier, inc=1, device_id=friend, device_id_type=MESH)
        return lambda: pl.semaphore_wait(barrier, len(friends))


def send(src, dst, send_sem, recv_sem, device):
    copy = pltpu.make_async_remote_copy(
        src_ref=src,
        dst_ref=dst,
        send_sem=send_sem,
        recv_sem=recv_sem,
        device_id=device,
        device_id_type=MESH,
    )
    copy.start()
    return copy


def local(src, dst, sem):
    copy = pltpu.make_async_copy(src, dst, sem)
    copy.start()
    return copy


def cols(start, width):
    return pl.ds(pl.multiple_of(start, 128), width)


def forward_kernel(
    lengths, place, tok, cot, wf, vec, raw, root_l, root_r,
    o0, o1, o2, o_vt, o_x, o_cot, o_qkv, o_p, o_mix, o_n1, o_r1, o_u, o_f, o_dg, o_n2, o_r2, o_y, o_root, o_use, o_hot,
    w0, w1, w2, tok_in, cot_in, vec_in, tok_s, cot_s,
    tok_v, cot_v, pre_a, pre_b, hot, use, use_row, wide_w, vec_s, vt, qkv, P, mix, n1, r1, x1, u, fa, dg, n2, r2, yo, xT, mT, uT, feat, stg, rb,
    wl, zs, zr, xs, xr, ys, yr, ds, dr, cs, cr, ls, ts, tr, os, ks,
):
    low, f32 = jnp.bfloat16, jnp.float32
    here = Here()
    wait_all = here.greet()
    x, y, z, c, f = here.x, here.y, here.z, here.c, here.f
    whole = [w0, w1, w2]
    whole_out = [o0, o1, o2]
    wide = GCOLS // 2
    sent = []
    outs = []
    count = [0]

    def keep(src, dst):
        outs.append(local(src, dst, os.at[count[0]]))
        count[0] += 1

    tok_load = local(tok, tok_v, ks.at[5])
    cot_load = local(cot, cot_v, ks.at[6])
    fetched = [
        local(wf.at[:, :, g * GCOLS : (g + 1) * GCOLS], wide_w.at[:, :, g * GCOLS : (g + 1) * GCOLS], ks.at[2 + g])
        for g in range(3)
    ]

    def narrow(g):
        fetched[g].wait()

        def one(i, _):
            h, part = lax.div(i, 4), lax.rem(i, 4)
            at = cols(g * GCOLS + part * D, D)
            wl[h, :, at] = wide_w[h, :, at].astype(low)
            return 0

        lax.fori_loop(0, 8, one, 0)
        return local(wl.at[:, :, g * GCOLS : (g + 1) * GCOLS], whole[g].at[z, c], ls.at[g])

    inner = lax.rem(lax.div(z + 1, 2), 2)
    upper = lax.div(z, 2)
    end = 3 * upper

    def source(step):
        near = step - inner if step == 1 else step
        return near + upper * (3 - 2 * near)

    def line(zz):
        return (here.r, 2 * zz + c)

    def own_part(g):
        return wl.at[x, :, cols(g * GCOLS + y * wide, wide)]

    def landed(g, src):
        return whole[g].at[src, c, x, :, cols(y * wide, wide)]

    def z_own(g, second):
        first_to = 1 + upper + inner * (1 - 2 * upper)
        second_to = inner * end + (1 - inner) * (2 - upper)
        return pltpu.make_async_remote_copy(
            src_ref=own_part(g), dst_ref=landed(g, z), send_sem=zs.at[g, int(second)], recv_sem=zr.at[g, z],
            device_id=line(second_to if second else first_to), device_id_type=MESH,
        )

    def z_pass(g, step):
        part = landed(g, source(step))
        return pltpu.make_async_remote_copy(
            src_ref=part, dst_ref=part, send_sem=zs.at[g, 1 + step], recv_sem=zr.at[g, source(step)],
            device_id=line(end), device_id_type=MESH,
        )

    def z_send(g):
        z_own(g, False).start()
        z_own(g, True).start()

    def z_finish(g):
        z_own(g, False).wait_send()
        z_own(g, True).wait_send()

        @pl.when(inner == 1)
        def _():
            for step in (2, 3):
                z_pass(g, step).wait_send()

    def rows_out(table, landing, number):
        out = []
        for step in range(1, 8):
            to = here.pair(step)
            src = table if number == 2 else table.at[to]
            out.append(
                send(src, landing.at[f], ts.at[number, step - 1], tr.at[number, step - 1], (here.r, to))
            )
        sent.extend(out)
        return out

    planes = {0: {}, 1: {}, 2: {}}

    def plane(g, step):
        moving = z_pass(g, step)
        moving.wait_recv()

        if step > 1:

            @pl.when(inner == 1)
            def _():
                moving.start()

        src = source(step)
        part = landed(g, src)
        xc = send(part, part, xs.at[g, src], xr.at[g, src], here.to_x)
        yc = send(part, part, ys.at[g, src], yr.at[g, src], here.to_y)
        planes[g][step] = (xc, yc)
        sent.extend([xc, yc])
        if step == 3:
            core(g, 0, x, y)

    cores = {0: [], 1: [], 2: []}

    def core(g, number, h, j):
        part = whole[g].at[:, c, h, :, cols(j * wide, wide)]
        copy = send(part, part, cs.at[g, number], cr.at[g, number], here.to_core)
        sent.append(copy)
        cores[g].append(copy)

    turns = {0: [], 1: [], 2: []}

    def turn(g, step):
        src = source(step)
        xc, yc = planes[g][step]
        xc.wait_recv()
        part = whole[g].at[src, c, 1 - x, :, cols(y * wide, wide // 2)]
        one = send(part, part, ds.at[g, 0, src], dr.at[g, 0, src], here.to_y)
        yc.wait_recv()
        part = whole[g].at[src, c, x, :, cols((1 - y) * wide + wide // 2, wide // 2)]
        two = send(part, part, ds.at[g, 1, src], dr.at[g, 1, src], here.to_x)
        sent.extend([one, two])
        turns[g].extend([one, two])
        if step == 3:
            core(g, 1, 1 - x, y)
            core(g, 2, x, 1 - y)

    def last(g):
        for copy in turns[g]:
            copy.wait_recv()
        core(g, 3, 1 - x, 1 - y)

    def ready(g):
        for copy in cores[g]:
            copy.wait_recv()
        keep(whole[g], whole_out[g])

    def square(ref, at):
        return ref[:, :, :, :, at].reshape(D, at.size)

    def order(source, target):
        target[...] = jnp.dot(hot[...], source[...], preferred_element_type=f32).astype(low).reshape(8, 64, D)

    def layout_rows():
        sizes = [lengths[0, s] for s in range(SEQ_DEV)]
        blocks = [lax.div(size + (BLK - 1), BLK) for size in sizes]
        ends = [blocks[0]]
        for s in range(1, SEQ_DEV):
            ends.append(ends[-1] + blocks[s])

        def where_is(number):
            seq = jnp.zeros_like(number)
            for s in range(SEQ_DEV):
                seq = seq + (number >= ends[s]).astype(jnp.int32)
            first, size, count = jnp.zeros_like(number), jnp.zeros_like(number), jnp.zeros_like(number)
            for s in range(SEQ_DEV):
                first = jnp.where(seq == s, ends[s] - blocks[s], first)
                size = jnp.where(seq == s, sizes[s], size)
                count = jnp.where(seq == s, blocks[s], count)
            return seq, number - first, size, count

        slot = lax.broadcasted_iota(jnp.int32, (8, TOK_DEV), 1)
        key_seq, key_block, size, _ = where_is(lax.div(slot, BLK))
        used = key_block * BLK + lax.rem(slot, BLK) < size
        used_f = used.astype(f32)
        use_row[...] = used_f
        use[...] = jnp.transpose(jnp.concatenate([used_f] * 16, axis=0))
        row_seq, row_block, _, count = where_is(lax.broadcasted_iota(jnp.int32, (8, 128), 0))
        row_seq, row_block, count = row_seq[:, 0:1], row_block[:, 0:1], jnp.maximum(count[:, 0:1], 1)
        same = (row_seq == key_seq) & used
        near = (row_block < NGLOB) | (key_block < NGLOB) | (jnp.abs(row_block - key_block) <= 1)
        picks = []
        for number in range(NRAND):
            pick = raw[number]
            for _ in range(7):
                pick = jnp.where(pick >= count, pick - count, pick)
            picks.append(pick)
        gap = jnp.zeros((BLK - 8, TOK_DEV), f32)
        for head in range(H):
            keep_it = near
            for pick in picks:
                keep_it = keep_it | (key_block == pick[:, head : head + 1])
            rows = jnp.where(same & keep_it, 0.0, MASKED_SCORE)
            feat[head] = jnp.transpose(jnp.concatenate([rows, gap, rows, gap], axis=0)).astype(low)

    def places():
        spot = (
            lax.div(place[...], TOK_DEV) * 64 + lax.rem(place[...], TOK_DEV) - f * 64
        )
        hot[...] = (
            (lax.broadcasted_iota(jnp.int32, (TOK_DEV, TOK_DEV), 0) == spot).astype(f32).astype(low)
        )
        return spot

    def places_back(spot):
        tall = jnp.transpose(jnp.broadcast_to(spot.astype(f32), (128, TOK_DEV)))
        lane = lax.broadcasted_iota(jnp.int32, (TOK_DEV, TOK_DEV), 1).astype(f32)
        hot[...] = (tall[:, 0:1] == lane).astype(f32).astype(low)
        keep(hot, o_hot)

    def project():
        for part in range(3):
            to = pl.ds(part * D, D)
            acc = jnp.dot(tok_in[...].reshape(TOK_DEV, D), square(w0, to), preferred_element_type=f32)
            if part == 0:
                acc = (acc + vt[0:1, :]) * (HD ** (-0.5))
            if part == 2:
                acc = acc + vt[1:2, :]
            qkv[:, to] = acc.astype(low)

    root_load = []

    def root_fetch(number):
        ref = (root_l, root_r)[number // 2]
        root_load.append(local(ref.at[number % 2], stg, ks.at[0]))

    def roots(number):
        root_load[number].wait()
        if number:
            root_out[number - 1].wait()

        def one(i, _):
            at = pl.ds(pl.multiple_of(i * 96, 96), 96)
            rb[lax.div(i, 2), lax.rem(i, 2)] = stg[at, :].astype(low).reshape(2, HALF, D)
            return 0

        lax.fori_loop(0, 8, one, 0)
        root_out.append(local(rb, o_root.at[number], ks.at[1]))
        if number < 3:
            root_fetch(number + 1)
        else:
            root_out[3].wait()

    root_out = []
    root_fetch(0)

    def attend(start, stop):
        def pair(i, _):
            at = cols(i * 128, 128)
            q2, k2 = qkv[:, at], qkv[:, cols(D + i * 128, 128)]
            v2 = qkv[:, cols(2 * D + i * 128, 128)]
            lane = lax.broadcasted_iota(jnp.int32, (TOK_DEV, 128), 1)
            row = lax.broadcasted_iota(jnp.int32, (TOK_DEV, 128), 0)
            spot = (lax.rem(lane, BLK) == lax.div(row, BLK)).astype(f32).astype(low)
            vT = jnp.transpose(v2)
            parts = []
            for half in range(2):
                mine = (lane < HD) if half == 0 else (lane >= HD)
                qm = jnp.where(mine, q2, spot)
                km = jnp.where(mine, k2, feat[2 * i + half])
                s = lax.dot_general(km, qm, (((1,), (1,)), ((), ())), preferred_element_type=f32)
                e = jnp.exp(s - jnp.max(s, axis=0, keepdims=True))
                p = (e * (use_row[0:1, :] / jnp.sum(e, axis=0, keepdims=True))).astype(low)
                P[2 * i + half] = p
                parts.append(jnp.dot(vT[half * HD : (half + 1) * HD], p, preferred_element_type=f32))
            total = jnp.where(use_row[0:1, :] > 0, jnp.concatenate(parts, axis=0), vT.astype(f32)).astype(low)
            mT[cols(i * 128, 128), :] = total
            mix[:, at] = jnp.transpose(total)
            return 0

        if stop - start == 1:
            pair(start, 0)
        else:
            lax.fori_loop(start, stop, pair, 0)

    def flip(source, target):
        def one(i, _):
            at = cols(i * 128, 128)
            target[at, :] = jnp.transpose(source(at))
            return 0

        lax.fori_loop(0, 6, one, 0)

    def join():
        def one(i, _):
            at = cols(i * 256, 256)
            acc = jnp.dot(mix[...], square(w0, cols(3 * D + i * 256, 256)), preferred_element_type=f32)
            x1[:, at] = tok_in[:, :, at].reshape(TOK_DEV, 256).astype(f32) + (acc + vt[2:3, at])
            return 0

        lax.fori_loop(0, 3, one, 0)

    def norm(ref, i):
        at = pl.ds(pl.multiple_of(i * 128, 128), 128)
        h = ref[at, :]
        center = h - jnp.mean(h, axis=1, keepdims=True)
        r = lax.rsqrt(jnp.mean(center * center, axis=1, keepdims=True) + NORM_EPS)
        return at, center * r, r

    def norm_one():
        def one(i, _):
            at, n, r = norm(x1, i)
            n1[at, :] = n
            r1[at, :] = jnp.broadcast_to(r, (128, 128))
            out = n * vt[4:5, :] + vt[5:6, :]
            u[at, :] = out.astype(low)
            x1[at, :] = out
            return 0

        lax.fori_loop(0, 4, one, 0)

    def lift(begin):
        def raise_to(target, i):
            target[...] = jnp.dot(u[...], square(w1, cols(i * 256, 256)), preferred_element_type=f32)

        def bend(source, i):
            row = lax.div(i, 3)
            pre = source[...] + vt[pl.ds(8 + row, 1), cols((i - 3 * row) * 256, 256)]
            sq = pre * pre
            half = 0.5 * jnp.tanh(pre * (0.7978845608028654 + 0.035677408136300125 * sq)) + 0.5
            act = pre * half
            to = cols(i * 256, 256)
            fa[:, to] = act.astype(low)
            slope = 1.5957691216057308 + 0.21406444881780075 * sq
            dg[:, to] = (half + act * (1.0 - half) * slope).astype(low)

        raise_to(pre_a, begin)

        def two(k, _):
            i = begin + 2 * k
            raise_to(pre_b, i + 1)
            bend(pre_a, i)
            raise_to(pre_a, jnp.minimum(i + 2, 11))
            bend(pre_b, i + 1)
            return 0

        lax.fori_loop(0, 3, two, 0)

    def drop():
        def one(i, _):
            at = cols(i * 512, 512)
            acc = lax.dot_general(
                fa[:, at], square(w2, at), (((1,), (1,)), ((), ())), preferred_element_type=f32
            )
            x1[...] += acc
            return 0

        lax.fori_loop(0, 6, one, 0)

    def norm_two():
        def one(i, _):
            at = pl.ds(pl.multiple_of(i * 128, 128), 128)
            x1[at, :] = x1[at, :] + vt[3:4, :]
            at, n, r = norm(x1, i)
            n2[at, :] = n
            r2[at, :] = jnp.broadcast_to(r, (128, 128))
            out = (n * vt[6:7, :] + vt[7:8, :]) * use[at, 0:1]
            yo[at, :] = out.astype(low)
            return 0

        lax.fori_loop(0, 4, one, 0)

    stays = [narrow(0)]
    wait_all()
    z_send(0)
    vec_s[...] = jnp.zeros_like(vec_s)
    vec_s[:NBLK, :96] = vec[...].astype(low)
    small = rows_out(vec_s, vec_in, 2)
    own = [local(vec_s, vec_in.at[f], ls.at[5])]
    stays.append(narrow(1))
    z_send(1)
    spot = places()
    plane(0, 1)
    tok_load.wait()
    order(tok_v, tok_s)
    own.append(local(tok_s.at[f], tok_in.at[f], ls.at[3]))
    plane(0, 2)
    cot_load.wait()
    order(cot_v, cot_s)
    own.append(local(cot_s.at[f], o_cot.at[f], ls.at[4]))
    stays.append(narrow(2))
    stays[0].wait()
    plane(0, 3)
    t0 = rows_out(tok_s, tok_in, 0)
    for copy in stays[1:] + own:
        copy.wait()
    layout_rows()
    keep(use, o_use)
    turn(0, 1)
    plane(1, 1)
    for copy in small:
        copy.wait_recv()
    for n in range(8):
        vt[:, n * 96 : (n + 1) * 96] = vec_in[n, :, :96].astype(f32)
    keep(vt, o_vt)
    places_back(spot)
    turn(0, 2)
    plane(1, 2)
    roots(0)
    turn(0, 3)
    plane(1, 3)
    roots(1)
    last(0)
    z_send(2)
    roots(2)
    roots(3)
    ready(0)
    turn(1, 1)
    for copy in t0:
        copy.wait_recv()
    project()
    keep(qkv, o_qkv)
    turn(1, 2)
    plane(2, 1)
    attend(0, 1)
    turn(1, 3)
    plane(2, 2)
    attend(1, 2)
    last(1)
    attend(2, 3)
    plane(2, 3)
    t1 = rows_out(cot_s, o_cot, 1)
    attend(3, 4)
    turn(2, 1)
    attend(4, 5)
    attend(5, 6)
    keep(P, o_p)
    keep(mT, o_mix)
    turn(2, 2)
    join()
    norm_one()
    turn(2, 3)
    keep(n1, o_n1)
    keep(r1, o_r1)
    ready(1)
    lift(0)
    last(2)
    lift(6)
    keep(fa, o_f)
    keep(dg, o_dg)
    flip(lambda at: tok_in[:, :, at].reshape(TOK_DEV, 128), xT)
    keep(xT, o_x)
    flip(lambda at: u[:, at], uT)
    keep(uT, o_u)
    ready(2)
    drop()
    norm_two()
    keep(n2, o_n2)
    keep(r2, o_r2)
    keep(yo, o_y)
    for copy in t1:
        copy.wait_recv()
    for g in range(3):
        z_finish(g)
    for copy in sent:
        copy.wait_send()
    for copy in outs:
        copy.wait()


def forward_all(lengths, place, tok, cot, flat_weights, vec, raw, root_l, root_r):
    any_spec = pl.BlockSpec(memory_space=pl.ANY)
    vmem = pl.BlockSpec(memory_space=pltpu.VMEM)
    dma = pltpu.SemaphoreType.DMA
    shape = jax.ShapeDtypeStruct
    low, f32 = jnp.bfloat16, jnp.float32
    square = (4, 2, 2, HALF, GCOLS)
    saved = [
        ((16, D), f32), ((D, TOK_DEV), low), ((8, 64, D), low), ((TOK_DEV, 3 * D), low),
        ((H, TOK_DEV, TOK_DEV), low), ((D, TOK_DEV), low), ((TOK_DEV, D), f32), ((TOK_DEV, 128), f32),
        ((D, TOK_DEV), low), ((TOK_DEV, FF), low), ((TOK_DEV, FF), low), ((TOK_DEV, D), f32),
        ((TOK_DEV, 128), f32), ((TOK_DEV, D), low), ((4, 4, 2, 2, HALF, D), low),
        ((TOK_DEV, 128), f32), ((TOK_DEV, TOK_DEV), low),
    ]
    return pl.pallas_call(
        forward_kernel,
        out_shape=[shape(square, low)] * 3 + [shape(*s) for s in saved],
        in_specs=[pl.BlockSpec(memory_space=pltpu.SMEM)] + [vmem] + [any_spec] * 3 + [vmem] * 2 + [any_spec] * 2,
        out_specs=[any_spec] * 20,
        scratch_shapes=[
            pltpu.VMEM(square, low), pltpu.VMEM(square, low), pltpu.VMEM(square, low),
            pltpu.VMEM((8, 64, D), low), pltpu.VMEM((8, 64, D), low), pltpu.VMEM((8, 16, 128), low),
            pltpu.VMEM((8, 64, D), low), pltpu.VMEM((8, 64, D), low),
            pltpu.VMEM((TOK_DEV, D), low),
            pltpu.VMEM((TOK_DEV, D), low),
            pltpu.VMEM((TOK_DEV, 256), f32),
            pltpu.VMEM((TOK_DEV, 256), f32),
            pltpu.VMEM((TOK_DEV, TOK_DEV), low),
            pltpu.VMEM((TOK_DEV, 128), f32),
            pltpu.VMEM((8, TOK_DEV), f32),
            pltpu.VMEM((2, HALF, 3 * GCOLS), f32),
            pltpu.VMEM((16, 128), low),
            pltpu.VMEM((16, D), f32),
            pltpu.VMEM((TOK_DEV, 3 * D), low),
            pltpu.VMEM((H, TOK_DEV, TOK_DEV), low),
            pltpu.VMEM((TOK_DEV, D), low),
            pltpu.VMEM((TOK_DEV, D), f32),
            pltpu.VMEM((TOK_DEV, 128), f32),
            pltpu.VMEM((TOK_DEV, D), f32),
            pltpu.VMEM((TOK_DEV, D), low),
            pltpu.VMEM((TOK_DEV, FF), low),
            pltpu.VMEM((TOK_DEV, FF), low),
            pltpu.VMEM((TOK_DEV, D), f32),
            pltpu.VMEM((TOK_DEV, 128), f32),
            pltpu.VMEM((TOK_DEV, D), low),
            pltpu.VMEM((D, TOK_DEV), low), pltpu.VMEM((D, TOK_DEV), low), pltpu.VMEM((D, TOK_DEV), low),
            pltpu.VMEM((H, TOK_DEV, 128), low),
            pltpu.VMEM((D, D), f32),
            pltpu.VMEM((4, 2, 2, HALF, D), low),
            pltpu.VMEM((2, HALF, 3 * GCOLS), low),
            dma((3, 5)), dma((3, 4)), dma((3, 4)), dma((3, 4)), dma((3, 4)), dma((3, 4)),
            dma((3, 2, 4)), dma((3, 2, 4)), dma((3, 4)), dma((3, 4)),
            dma((6,)), dma((3, 7)), dma((3, 7)), dma((19,)), dma((7,)),
        ],
        compiler_params=pltpu.CompilerParams(
            collective_id=0, has_side_effects=True, vmem_limit_bytes=60 * MIB
        ),
        name="forward_all",
    )(lengths, place, tok, cot, flat_weights.reshape(2, HALF, 3 * GCOLS), vec, raw, root_l, root_r)


def backward_kernel(
    owner, vt, use,
    h_w0, h_w1, h_w2, h_xT, h_cot, h_qkv, h_p, h_mT, h_n1, h_r1, h_uT, h_f, h_dg, h_n2, h_r2, h_y, h_root,
    o_back, o_grad, WR, UA, SC, o_gs, o_vec,
    G, Rc, A1, A2, B1, B2, ZR, ZP, F, SO, Gs, wa, wb, fb, gb, low_g, LT, LU, hb, nb, PT, r1, r2, gi,
    PQ, sq, sr_in, sc_out, vb, vr,
    ld, pd, cs, cr, a1s, a1r, b1s, b1r, a2s, a2r, b2s, b2r, zs, zr,
    fs, fr, ts, tr, ss, sr, ps, pr, us, ur, qs, qr, es, er, ms, mr, vs, vrs, ls,
):
    low, f32 = jnp.bfloat16, jnp.float32
    here = Here(True)
    wait_all = here.greet()
    x, y, z, c, f, r = here.x, here.y, here.z, here.c, here.f, here.r
    W = GCOLS // 2
    sent = []

    class Load:
        def __init__(self, number, src, dst):
            self.copy, self.done = local(src, dst, ld.at[number]), False

        def wait(self):
            if not self.done:
                self.copy.wait()
                self.done = True

    cot_l = Load(0, h_cot, gi)
    n2_l = Load(1, h_n2, hb)
    r2_l = Load(2, h_r2, r2)
    f_l = Load(3, h_f, fb)
    wd_l = Load(4, h_w2, wa)
    dg_l = Load(5, h_dg, gb)
    uT_l = Load(6, h_uT, LU)
    wu_l = Load(7, h_w1, wb)
    n1_l = Load(8, h_n1, nb)
    r1_l = Load(9, h_r1, r1)
    vb[...] = jnp.zeros_like(vb)

    chunks = [(8, 2), (10, 2), (4, 2), (6, 2), (3, 1), (0, 1), (1, 1), (2, 1)]

    def span(n):
        block, count = chunks[n]
        return pl.ds(block * JCOLS, count * JCOLS)

    ways = {}

    def c_send(n):
        at = span(n)
        ways[n] = [
            send(G.at[:, :, 1 - c, :, :, at], Rc.at[:, :, :, :, at], cs.at[n], cr.at[n], here.to_core)
        ]
        sent.extend(ways[n])

    def first(n):
        at = span(n)
        ways[n][0].wait_recv()

        def add(j, zz, h):
            G[j, zz, c, h, :, at] = G[j, zz, c, h, :, at] + Rc[j, zz, h, :, at]

        def add_a(i, _):
            add(lax.div(i, 2), lax.rem(i, 2), 1 - x)
            return 0

        def add_b(i, _):
            add(1 - y, 2 + lax.div(i, 2), lax.rem(i, 2))
            return 0

        def add_rest(i, _):
            add(lax.div(i, 2), lax.rem(i, 2), x)
            add(y, 2 + lax.div(i, 2), lax.rem(i, 2))
            return 0

        lax.fori_loop(0, 4, add_a, 0)
        a = send(G.at[:, 0:2, c, 1 - x, :, at], A1.at[:, :, :, at], a1s.at[n], a1r.at[n], here.to_x)
        lax.fori_loop(0, 4, add_b, 0)
        b = send(G.at[1 - y, 2:4, c, :, :, at], B1.at[:, :, :, at], b1s.at[n], b1r.at[n], here.to_y)
        lax.fori_loop(0, 4, add_rest, 0)
        ways[n] = [a, b]
        sent.extend(ways[n])

    def second(n):
        at = span(n)
        ways[n][0].wait_recv()

        def add_a(i, _):
            for j in (1 - y, y):
                G[j, i, c, x, :, at] = G[j, i, c, x, :, at] + A1[j, i, :, at]
            return 0

        lax.fori_loop(0, 2, add_a, 0)
        a = send(G.at[1 - y, 0:2, c, x, :, at], A2.at[:, :, at], a2s.at[n], a2r.at[n], here.to_y)
        ways[n][1].wait_recv()

        def add_b(i, _):
            for h in (1 - x, x):
                G[y, i + 2, c, h, :, at] = G[y, i + 2, c, h, :, at] + B1[i, h, :, at]
            return 0

        lax.fori_loop(0, 2, add_b, 0)
        b = send(G.at[y, 2:4, c, 1 - x, :, at], B2.at[:, :, at], b2s.at[n], b2r.at[n], here.to_x)
        ways[n] = [a, b]
        sent.extend(ways[n])

    def third(n):
        at = span(n)
        for number, (copy, part) in enumerate(zip(ways[n], (A2, B2))):
            copy.wait_recv()

            def add(i, _, number=number, part=part):
                zz = 2 * number + i
                G[y, zz, c, x, :, at] = G[y, zz, c, x, :, at] + part[i, :, at]
                return 0

            lax.fori_loop(0, 2, add, 0)
        partner = z + 1 - 2 * lax.rem(z, 2)
        near = send(
            G.at[y, partner, c, x, :, at], ZR.at[0, :, at], zs.at[n, 0], zr.at[n, 0],
            (r, 2 * partner + c),
        )
        sent.append(near)
        ways[n] = [near]

        @pl.when(inner == 0)
        def _():
            passing(n).start()

    inner = lax.rem(lax.div(z + 1, 2), 2)
    far = 2 - 2 * lax.div(z, 2)

    def passing(n):
        at = span(n)
        return pltpu.make_async_remote_copy(
            src_ref=G.at[y, pl.ds(far, 2), c, x, :, at], dst_ref=ZP.at[:, :, at], send_sem=zs.at[n, 1],
            recv_sem=zr.at[n, 1], device_id=(r, 2 * (z + 1 - 2 * lax.rem(z, 2)) + c), device_id_type=MESH,
        )

    def crossing(n, i):
        at = span(n)
        return pltpu.make_async_remote_copy(
            src_ref=G.at[y, far + i, c, x, :, at], dst_ref=ZR.at[1, :, at], send_sem=zs.at[n, 2 + i],
            recv_sem=zr.at[n, 2], device_id=(r, 2 * (far + i) + c), device_id_type=MESH,
        )

    def fourth(n):
        at = span(n)

        @pl.when(inner == 1)
        def _():
            passing(n).wait_recv()
            for i in range(2):
                G[y, far + i, c, x, :, at] = G[y, far + i, c, x, :, at] + ZP[i, :, at]
                crossing(n, i).start()

    def z_finish():
        for n in range(8):

            @pl.when(inner == 0)
            def _():
                passing(n).wait_send()

            @pl.when(inner == 1)
            def _():
                for i in range(2):
                    crossing(n, i).wait_send()

    def final(n):
        ways[n][0].wait_recv()
        crossing(n, 0).wait_recv()
        block, count = chunks[n]
        for b in range(block, block + count):
            at = pl.ds(b * JCOLS, JCOLS)
            total = G[y, z, c, x, :, at].astype(f32)
            for step in range(2):
                total = total + ZR[step, :, at].astype(f32)
            F[b] = total.astype(low)

    homes = []

    spreads = {}
    diagonals = []

    def spread(g):
        at = pl.ds(4 * g, 4)
        to = WR.at[x, y, at]
        a = send(F.at[at], to, fs.at[g, 0], fr.at[g, 0], here.to_x)
        b = send(F.at[at], to, fs.at[g, 1], fr.at[g, 1], here.to_y)
        homes.append(local(F.at[at], to, ls.at[g]))
        sent.extend([a, b])
        spreads[g] = (a, b)

    def spread_on(g):
        a, b = spreads[g]
        a.wait_recv()
        part = WR.at[1 - x, y, pl.ds(4 * g, 2)]
        da = send(part, part, fs.at[g, 2], fr.at[g, 2], here.to_y)
        b.wait_recv()
        part = WR.at[x, 1 - y, pl.ds(4 * g + 2, 2)]
        db = send(part, part, fs.at[g, 3], fr.at[g, 3], here.to_x)
        sent.extend([da, db])
        diagonals.extend([da, db])

    def token_send(source, landing, number):
        out = []
        for step in range(1, 8):
            to = here.pair(step)
            out.append(
                send(source(to), landing.at[f], ts.at[number, step - 1], tr.at[number, step - 1], (r, to))
            )
        homes.append(local(source(f), landing.at[f], ls.at[3 + number]))
        sent.extend(out)
        return out

    def square(ref, at):
        return ref[:, :, :, :, at].reshape(D, at.size)

    def own_rows(ref, core):
        return jnp.concatenate(
            [ref[pl.ds(pl.multiple_of((2 * zz + core) * 96, 96), 96), :] for zz in range(4)], axis=0
        )

    def gradient(left, right, block, start, count, core):
        rows = own_rows(left, core)

        def one(i, _):
            out = jnp.dot(rows, right[:, cols(start + i * D, D)], preferred_element_type=f32)
            out = out.astype(low).reshape(4, 2, HALF, D)
            for j in range(2):
                at = cols((block + i) * JCOLS, JCOLS)
                G[j, :, core, :, :, at] = out[:, :, :, j * JCOLS : (j + 1) * JCOLS]
            return 0

        lax.fori_loop(0, count, one, 0)

    def eight(v):
        return jnp.sum(v.reshape(8, 8, v.shape[1]), axis=0)

    def norm_back(i, carry, grad, n, rr, gain):
        zed = grad * gain
        back = rr * (
            zed - jnp.mean(zed, axis=1, keepdims=True) - n * jnp.mean(zed * n, axis=1, keepdims=True)
        )
        rounded = back.astype(low)
        return back, rounded, (
            carry[0] + eight(grad * n), carry[1] + eight(grad), carry[2] + eight(rounded.astype(f32))
        )

    zero = jnp.zeros((8, D), f32)

    def put(row, total):
        vb[0, row : row + 1, :] = jnp.sum(total, axis=0, keepdims=True)

    def flip(source, target, count):
        def one(i, _):
            at = cols(i * 128, 128)
            target[at, :] = jnp.transpose(source[:, at])
            return 0

        lax.fori_loop(0, count, one, 0)

    cot_l.wait()
    n2_l.wait()
    r2_l.wait()

    def back_two(i, carry):
        at = pl.ds(pl.multiple_of(i * 64, 64), 64)
        grad = gi[i].astype(f32) * use[at, 0:1]
        back, rounded, carry = norm_back(i, carry, grad, hb[at, :], r2[at, 0:1], vt[6:7, :])
        hb[at, :] = back
        low_g[at, :] = rounded
        return carry

    sums = lax.fori_loop(0, 8, back_two, (zero, zero, zero))
    put(6, sums[0])
    put(7, sums[1])
    put(3, sums[2])
    flip(low_g, LT, 6)
    f_l.wait()
    gradient(LT, fb, 8, 0, 2, 1 - c)
    wait_all()
    ta = token_send(lambda to: h_y.at[to], o_back, 0)
    c_send(0)
    gradient(LT, fb, 10, 2 * D, 2, 1 - c)
    c_send(1)
    gradient(LT, fb, 8, 0, 4, c)
    qkv_l = Load(10, h_qkv, fb.at[:, : 3 * D])
    mT_l = Load(11, h_mT, LT)
    wd_l.wait()
    dg_l.wait()

    def back_up(i, _):
        at = cols(i * 256, 256)
        acc = jnp.dot(low_g[...], square(wa, at), preferred_element_type=f32)
        gb[:, at] = (acc * gb[:, at].astype(f32)).astype(low)
        return 0

    first(0)
    lax.fori_loop(0, 6, back_up, 0)
    first(1)
    uT_l.wait()
    gradient(LU, gb, 4, 0, 2, 1 - c)
    c_send(2)
    lax.fori_loop(6, 12, back_up, 0)
    wq_l = Load(12, h_w0, wa)
    gradient(LU, gb, 4, 0, 2, c)
    first(2)
    gradient(LU, gb, 6, 2 * D, 2, 1 - c)
    c_send(3)
    gradient(LU, gb, 6, 2 * D, 2, c)
    xT_l = Load(13, h_xT, LU)
    second(0)
    first(3)
    wu_l.wait()

    def back_x1(i, _):
        at = cols(i * 512, 512)
        hb[...] += lax.dot_general(
            gb[:, at], square(wb, at), (((1,), (1,)), ((), ())), preferred_element_type=f32
        )
        return 0

    lax.fori_loop(0, 6, back_x1, 0)
    second(1)
    root_l = [Load(14 + n, h_root.at[n], wb.at[:, :, :, :, n * D : (n + 1) * D]) for n in range(4)]
    n1_l.wait()
    r1_l.wait()

    def back_one(i, carry):
        at = pl.ds(pl.multiple_of(i * 64, 64), 64)
        back, rounded, carry = norm_back(i, carry, hb[at, :], nb[at, :], r1[at, 0:1], vt[4:5, :])
        hb[at, :] = back
        low_g[at, :] = rounded
        return carry

    sums = lax.fori_loop(0, 8, back_one, (zero, zero, zero))
    put(4, sums[0])
    put(5, sums[1])
    put(2, sums[2])
    third(0)
    mT_l.wait()
    gradient(LT, low_g, 3, 0, 1, 1 - c)
    c_send(4)
    gradient(LT, low_g, 3, 0, 1, c)
    wq_l.wait()

    def back_mix(i, _):
        out = lax.dot_general(
            low_g[...], wa[pl.ds(2 * i, 2), :, :, :, 3 * D : 4 * D].reshape(JCOLS, D),
            (((1,), (1,)), ((), ())), preferred_element_type=f32,
        )
        gb[:, cols(3 * D + i * JCOLS, JCOLS)] = out.astype(low)
        return 0

    for row in range(4):

        def total(i, acc, row=row):
            at = pl.ds(pl.multiple_of(i * 64, 64), 64)
            return acc + eight(gb[at, row * D : (row + 1) * D].astype(f32))

        put(8 + row, lax.fori_loop(0, 8, total, zero))
    lax.fori_loop(0, 2, back_mix, 0)
    second(2)
    first(4)
    qkv_l.wait()

    def fetch(i):
        return pltpu.make_async_copy(h_p.at[pl.ds(2 * i, 2)], PT.at[i % 2], pd.at[i % 2])

    fetch(0).start()

    def attend(i):
        slot = i % 2
        if i < 5:
            fetch(i + 1).start()
        q2, k2 = fb[:, cols(i * 128, 128)], fb[:, cols(D + i * 128, 128)]
        v2, go2 = fb[:, cols(2 * D + i * 128, 128)], gb[:, cols(3 * D + i * 128, 128)]
        kT = jnp.transpose(k2)
        lane = lax.broadcasted_iota(jnp.int32, (TOK_DEV, 128), 1)
        fetch(i).wait()
        parts = []
        gk = jnp.zeros((TOK_DEV, 128), f32)
        gv = jnp.where(use[:, :] > 0, 0.0, go2.astype(f32))
        for half in range(2):
            mine = (lane < HD) if half == 0 else (lane >= HD)
            none = jnp.zeros_like(v2)
            p = PT[slot, half]
            gp = lax.dot_general(
                jnp.where(mine, v2, none), go2, (((1,), (1,)), ((), ())), preferred_element_type=f32
            )
            pf = p.astype(f32)
            gs = (pf * (gp - jnp.sum(pf * gp, axis=0, keepdims=True))).astype(low)
            gk = gk + jnp.dot(gs, jnp.where(mine, q2, none), preferred_element_type=f32)
            gv = gv + jnp.dot(p, jnp.where(mine, go2, none), preferred_element_type=f32)
            parts.append(jnp.dot(kT[half * HD : (half + 1) * HD], gs, preferred_element_type=f32))
        gq = jnp.transpose(jnp.concatenate(parts, axis=0)) * (HD ** (-0.5))
        gb[:, cols(i * 128, 128)] = gq.astype(low)
        gb[:, cols(D + i * 128, 128)] = gk.astype(low)
        gb[:, cols(2 * D + i * 128, 128)] = gv.astype(low)

    attend(0)
    attend(1)
    third(1)
    fourth(0)
    attend(2)
    attend(3)
    second(3)
    attend(4)
    fourth(1)
    attend(5)
    third(2)

    def back_x(i, _):
        at = cols(i * D, D)
        hb[...] += lax.dot_general(
            gb[:, at], square(wa, at), (((1,), (1,)), ((), ())), preferred_element_type=f32
        )
        return 0

    lax.fori_loop(0, 3, back_x, 0)

    def rows_low(i, _):
        gi[i] = hb[pl.ds(pl.multiple_of(i * 64, 64), 64), :].astype(low)
        return 0

    lax.fori_loop(0, 8, rows_low, 0)
    tb = token_send(lambda to: gi.at[to], o_grad, 1)
    second(4)
    xT_l.wait()
    for n in range(3):
        gradient(LU, gb, n, n * D, 1, 1 - c)
        c_send(5 + n)
    fourth(2)
    gradient(LU, gb, 0, 0, 1, c)
    first(5)
    gradient(LU, gb, 1, D, 1, c)
    first(6)
    gradient(LU, gb, 2, 2 * D, 1, c)
    first(7)
    third(3)
    for row, start in ((0, 0), (1, 2 * D)):

        def total(i, acc, start=start):
            at = pl.ds(pl.multiple_of(i * 64, 64), 64)
            return acc + eight(gb[at, start : start + D].astype(f32))

        put(row, lax.fori_loop(0, 8, total, zero))
    vec_copy = send(vb.at[0], vr.at[0], vs.at[0], vrs.at[0], here.to_core)
    sent.append(vec_copy)
    third(4)
    second(5)
    fourth(3)
    vec_copy.wait_recv()
    vb[1] = vb[0] + vr[0]
    vec_copy = send(vb.at[1], vr.at[1], vs.at[1], vrs.at[1], here.to_x)
    sent.append(vec_copy)
    second(6)
    third(5)
    fourth(4)
    vec_copy.wait_recv()
    vb[2] = vb[1] + vr[1]
    vec_copy = send(vb.at[2], vr.at[2], vs.at[2], vrs.at[2], here.to_y)
    sent.append(vec_copy)
    second(7)
    final(0)
    final(1)
    spread(2)
    fourth(5)
    third(6)
    final(2)
    final(3)
    spread(1)
    fourth(6)
    third(7)
    final(4)
    fourth(7)
    final(5)
    final(6)
    spread_on(2)
    spread_on(1)
    final(7)
    spread(0)
    jc = cols(y * JCOLS, JCOLS)
    other = cols((1 - y) * JCOLS, JCOLS)
    slot_copies = []
    for step in range(1, 9):
        to = here.pair(step)
        for t in range(2):
            b = jnp.int32(-1)
            for k in range(NBLK):
                b = jnp.where(owner[k] == 2 * to + t, k, b)
            flag = (b >= 0).astype(f32)
            SO[step - 1, t] = (F[jnp.maximum(b, 0)].astype(f32) * flag).astype(low)
        if step < 8:
            slot_copies.append(
                send(SO.at[step - 1], Gs.at[:, f, x, :, jc], ss.at[step - 1], sr.at[step - 1], (r, to))
            )
    sent.extend(slot_copies)
    own = local(SO.at[7], Gs.at[:, f, x, :, jc], ls.at[5])
    hops = []
    for step in range(8):
        src = here.pair(step)
        if step == 0:
            own.wait()
        else:
            slot_copies[step - 1].wait_recv()
        part = Gs.at[:, src, x, :, jc]
        hops.append(
            (
                send(part, part, ps.at[0, step], pr.at[0, step], here.to_x),
                send(part, part, ps.at[1, step], pr.at[1, step], here.to_y),
            )
        )
    ends = []
    for step in range(8):
        src = here.pair(step)
        hops[step][0].wait_recv()
        part = Gs.at[0, src, 1 - x, :, jc]
        ends.append(send(part, part, ps.at[2, step], pr.at[2, step], here.to_y))
        hops[step][1].wait_recv()
        part = Gs.at[1, src, x, :, other]
        ends.append(send(part, part, ps.at[3, step], pr.at[3, step], here.to_x))
        sent.extend(hops[step])
    sent.extend(ends)
    vec_copy.wait_recv()
    vb[3] = vb[2] + vr[2]
    vec_copies = []
    for step in (1, 2, 3):
        vec_copies.append(
            send(vb.at[3], vr.at[2 + step], vs.at[2 + step], vrs.at[2 + step], here.along(step))
        )
    sent.extend(vec_copies)
    for load in root_l:
        load.wait()
    for copy in ends:
        copy.wait_recv()
    spread_on(0)
    homes.append(local(Gs, o_gs, ls.at[6]))
    for t in range(2):
        whole = Gs[t].reshape(D, D)
        rows = wb[:, :, x, :, t * D : (t + 1) * D].reshape(JCOLS, D)
        half = jnp.dot(rows, whole, preferred_element_type=f32).astype(low)
        right = square(wb, cols((2 + t) * D + y * JCOLS, JCOLS))
        part = jnp.dot(half, right, preferred_element_type=f32)
        PQ[t] = part.astype(low).reshape(8, HALF, JCOLS)
        sq[t] = jnp.sum((part * part).reshape(48, 8, JCOLS), axis=0)
    ucopies = []
    for step in range(1, 8):
        to = here.pair(step)
        ucopies.append(
            send(PQ.at[:, to], UA.at[x, y, pl.ds(2 * f, 2)], us.at[step - 1], ur.at[step - 1], (r, to))
        )
    sent.extend(ucopies)
    own = local(PQ.at[:, f], UA.at[x, y, pl.ds(2 * f, 2)], ls.at[7])
    squares = []
    for number, to in enumerate((here.to_x, here.to_y, here.to_d)):
        squares.append(send(sq, sr_in.at[number], es.at[number], er.at[number], to))
    sent.extend(squares)
    uhops = []
    for step in range(8):
        src = here.pair(step)
        if step == 0:
            own.wait()
        else:
            ucopies[step - 1].wait_recv()
        part = UA.at[x, y, pl.ds(2 * src, 2)]
        uhops.append(
            (
                send(part, part, qs.at[0, step], qr.at[0, step], here.to_x),
                send(part, part, qs.at[1, step], qr.at[1, step], here.to_y),
            )
        )
        if step == 3:
            for copy in squares:
                copy.wait_recv()
            for t in range(2):
                total = sq[t] + sr_in[0, t] + sr_in[1, t] + sr_in[2, t]
                mean = jnp.sum(jnp.sum(total, axis=1, keepdims=True), axis=0, keepdims=True) * (1.0 / (D * D))
                sc_out[t] = jnp.broadcast_to(lax.rsqrt(mean + RMS_EPS), (8, 128))
            scales = []
            for number in range(1, 8):
                to = here.pair(number)
                scales.append(
                    send(
                        sc_out, SC.at[pl.ds(2 * f, 2)], ms.at[number - 1], mr.at[number - 1], (r, to)
                    )
                )
            sent.extend(scales)
            homes.append(local(sc_out, SC.at[pl.ds(2 * f, 2)], ls.at[8]))
    uends = []
    for step in range(8):
        src = here.pair(step)
        uhops[step][0].wait_recv()
        part = UA.at[1 - x, y, 2 * src]
        uends.append(send(part, part, qs.at[2, step], qr.at[2, step], here.to_y))
        uhops[step][1].wait_recv()
        part = UA.at[x, 1 - y, 2 * src + 1]
        uends.append(send(part, part, qs.at[3, step], qr.at[3, step], here.to_x))
        sent.extend(uhops[step])
    sent.extend(uends)
    total = vb[3]
    for copy in vec_copies:
        copy.wait_recv()
    for step in range(3):
        total = total + vr[3 + step]
    vb[4] = total
    homes.append(local(vb.at[4], o_vec, ls.at[9]))
    for copy in diagonals + uends + scales + ta + tb:
        copy.wait_recv()
    for copy in homes:
        copy.wait()
    z_finish()
    for copy in sent:
        copy.wait_send()


def backward_all(owner, vt, use, saved):
    any_spec = pl.BlockSpec(memory_space=pl.ANY)
    vmem = pl.BlockSpec(memory_space=pltpu.VMEM)
    smem = pl.BlockSpec(memory_space=pltpu.SMEM)
    dma = pltpu.SemaphoreType.DMA
    shape = jax.ShapeDtypeStruct
    low, f32 = jnp.bfloat16, jnp.float32
    JW = 12 * JCOLS
    square = (4, 2, 2, HALF, GCOLS)
    return pl.pallas_call(
        backward_kernel,
        out_shape=[
            shape((8, 64, D), low), shape((8, 64, D), low),
            shape((2, 2, 12, HALF, JCOLS), low), shape((2, 2, 16, HALF, JCOLS), low),
            shape((16, 8, 128), f32), shape((2, 8, 2, HALF, D), low), shape((16, D), f32),
        ],
        in_specs=[smem, vmem, vmem] + [any_spec] * 17,
        out_specs=[any_spec] * 7,
        scratch_shapes=[
            pltpu.VMEM((2, 4, 2, 2, HALF, JW), low),
            pltpu.VMEM((2, 4, 2, HALF, JW), low),
            pltpu.VMEM((2, 2, HALF, JW), low),
            pltpu.VMEM((2, HALF, JW), low),
            pltpu.VMEM((2, 2, HALF, JW), low),
            pltpu.VMEM((2, HALF, JW), low),
            pltpu.VMEM((2, HALF, JW), low),
            pltpu.VMEM((2, HALF, JW), low),
            pltpu.VMEM((12, HALF, JCOLS), low),
            pltpu.VMEM((8, 2, HALF, JCOLS), low),
            pltpu.VMEM((2, 8, 2, HALF, D), low),
            pltpu.VMEM(square, low),
            pltpu.VMEM(square, low),
            pltpu.VMEM((TOK_DEV, FF), low),
            pltpu.VMEM((TOK_DEV, FF), low),
            pltpu.VMEM((TOK_DEV, D), low),
            pltpu.VMEM((D, TOK_DEV), low),
            pltpu.VMEM((D, TOK_DEV), low),
            pltpu.VMEM((TOK_DEV, D), f32),
            pltpu.VMEM((TOK_DEV, D), f32),
            pltpu.VMEM((2, 2, TOK_DEV, TOK_DEV), low),
            pltpu.VMEM((TOK_DEV, 128), f32),
            pltpu.VMEM((TOK_DEV, 128), f32),
            pltpu.VMEM((8, 64, D), low),
            pltpu.VMEM((2, 8, HALF, JCOLS), low),
            pltpu.VMEM((2, 8, JCOLS), f32),
            pltpu.VMEM((3, 2, 8, JCOLS), f32),
            pltpu.VMEM((2, 8, 128), f32),
            pltpu.VMEM((5, 16, D), f32),
            pltpu.VMEM((6, 16, D), f32),
            dma((18,)), dma((2,)), dma((8,)), dma((8,)),
            dma((8,)), dma((8,)), dma((8,)), dma((8,)), dma((8,)), dma((8,)), dma((8,)), dma((8,)),
            dma((8, 4)), dma((8, 3)), dma((3, 4)), dma((3, 4)),
            dma((2, 7)), dma((2, 7)), dma((7,)), dma((7,)), dma((4, 8)), dma((4, 8)),
            dma((7,)), dma((7,)), dma((4, 8)), dma((4, 8)), dma((3,)), dma((3,)), dma((7,)), dma((7,)),
            dma((6,)), dma((6,)), dma((10,)),
        ],
        compiler_params=pltpu.CompilerParams(
            collective_id=1, has_side_effects=True, vmem_limit_bytes=60 * MIB
        ),
        name="backward_all",
    )(owner, vt, use, *saved)


def finish_kernel(
    owner, hot, back, grad, wr, ua, sc, gs, vec, stat_l, stat_r, wf, vecs, mom1, mom2,
    layer_out, input_grad, wg, nw, new_l, new_r, out1, out2, outv,
    gb, sl, sr, ub, rb, wb, nb, gg, tb, to, ls, os,
):
    low, f32 = jnp.bfloat16, jnp.float32
    f = lax.axis_index("fsdp")
    gs_load = local(gs, gb, ls.at[5])
    stats = [
        (local(stat_l.at[t], sl.at[t], ls.at[6 + 2 * t]), local(stat_r.at[t], sr.at[t], ls.at[7 + 2 * t]))
        for t in range(2)
    ]
    loads = [
        local(back, tb.at[0], ls.at[0]), local(grad, tb.at[1], ls.at[1]),
        local(wr, rb, ls.at[2]), local(ua, ub, ls.at[3]), local(wf, wb, ls.at[4]),
    ]
    outs = []
    gs_load.wait()
    for t in range(2):
        stats[t][0].wait()

        def left(i, _, t=t):
            at = pl.ds(pl.multiple_of(i * 384, 384), 384)
            rows = gb[t, pl.ds(4 * i, 4)].reshape(384, D)
            part = lax.dot_general(
                rows, gb[t].reshape(D, D), (((1,), (1,)), ((), ())), preferred_element_type=f32
            )
            sl[t, at, :] = STAT_DECAY * sl[t, at, :] + (1.0 - STAT_DECAY) * part
            return 0

        lax.fori_loop(0, 2, left, 0)
        outs.append(local(sl.at[t], new_l.at[t], os.at[4 + 2 * t]))
        stats[t][1].wait()
        for i in range(3):
            at = pl.ds(i * 256, 256)
            part = lax.dot_general(
                gb[t, :, :, :, at].reshape(D, 256), gb[t].reshape(D, D), (((0,), (0,)), ((), ())),
                preferred_element_type=f32,
            )
            sr[t, at, :] = STAT_DECAY * sr[t, at, :] + (1.0 - STAT_DECAY) * part
        outs.append(local(sr.at[t], new_r.at[t], os.at[5 + 2 * t]))
    for number, target in enumerate((layer_out, input_grad)):
        loads[number].wait()
        to[number] = jnp.dot(
            hot[...], tb[number].reshape(TOK_DEV, D), preferred_element_type=f32
        ).astype(low)
        outs.append(local(to.at[number], target, os.at[number]))
    loads[3].wait()
    loads[4].wait()
    for h in range(2):
        for b in range(NBLK):
            slot = owner[b]
            scale = LR_MATRIX * sc[slot, 0:1, 0:1]
            for j in range(2):
                at = pl.ds(b * D + j * JCOLS, JCOLS)
                nb[h, :, at] = wb[h, :, at] - scale * ub[h, j, slot].astype(f32)
        outs.append(local(nb.at[h], nw.at[h], os.at[3 + 5 * h]))
    loads[2].wait()
    for h in range(2):

        def one(b, _, h=h):
            for j in range(2):
                gg[h, :, cols(b * D + j * JCOLS, JCOLS)] = rb[h, j, b].astype(f32)
            return 0

        lax.fori_loop(0, 12, one, 0)
        outs.append(local(gg.at[h], wg.at[h], os.at[2 + 7 * h]))
    mine = jnp.zeros((NBLK, 96), f32)
    for number in range(8):
        mine = jnp.where(f == number, vec[:NBLK, number * 96 : (number + 1) * 96], mine)
    fresh1 = BETA_ONE * mom1[...] + (1.0 - BETA_ONE) * mine
    fresh2 = BETA_TWO * mom2[...] + (1.0 - BETA_TWO) * mine * mine
    out1[...] = fresh1
    out2[...] = fresh2
    outv[...] = vecs[...] - LR_VECTOR * (fresh1 / (1.0 - BETA_ONE**STEP)) / (
        jnp.sqrt(fresh2 / (1.0 - BETA_TWO**STEP)) + ADAM_EPS
    )
    for copy in outs:
        copy.wait()


def finish_all(owner, hot, results, stat_l, stat_r, wf, vecs, mom1, mom2):
    any_spec = pl.BlockSpec(memory_space=pl.ANY)
    vmem = pl.BlockSpec(memory_space=pltpu.VMEM)
    smem = pl.BlockSpec(memory_space=pltpu.SMEM)
    dma = pltpu.SemaphoreType.DMA
    shape = jax.ShapeDtypeStruct
    low, f32 = jnp.bfloat16, jnp.float32
    wide = (2, HALF, 3 * GCOLS)
    back, grad, wr, ua, sc, gs, vec = results
    return pl.pallas_call(
        finish_kernel,
        out_shape=[
            shape((TOK_DEV, D), low), shape((TOK_DEV, D), low), shape(wide, f32), shape(wide, f32),
            shape((2, D, D), f32), shape((2, D, D), f32),
            shape((NBLK, 96), f32), shape((NBLK, 96), f32), shape((NBLK, 96), f32),
        ],
        in_specs=[smem, vmem] + [any_spec] * 4 + [vmem, any_spec, vmem] + [any_spec] * 3 + [vmem] * 3,
        out_specs=[any_spec] * 6 + [vmem] * 3,
        scratch_shapes=[
            pltpu.VMEM((2, 8, 2, HALF, D), low),
            pltpu.VMEM((2, D, D), f32),
            pltpu.VMEM((2, D, D), f32),
            pltpu.VMEM((2, 2, 16, HALF, JCOLS), low),
            pltpu.VMEM((2, 2, 12, HALF, JCOLS), low),
            pltpu.VMEM(wide, f32),
            pltpu.VMEM(wide, f32),
            pltpu.VMEM(wide, f32),
            pltpu.VMEM((2, 8, 64, D), low),
            pltpu.VMEM((2, TOK_DEV, D), low),
            dma((10,)), dma((10,)),
        ],
        compiler_params=pltpu.CompilerParams(vmem_limit_bytes=56 * MIB),
        name="finish_all",
    )(
        owner, hot, back, grad, wr, ua, sc, gs, vec, stat_l, stat_r, wf.reshape(wide), vecs, mom1, mom2
    )


def fast_body(
    tokens,
    cotangent,
    place,
    seq_lengths,
    random_blocks,
    owner_slot,
    flat_weights,
    vectors,
    moment_first,
    moment_second,
    stat_left,
    stat_right,
    root_left,
    root_right,
):
    peers = lax.axis_size("fsdp")
    share_rows = TOK_DEV // peers
    w0, w1, w2, vt, *saved = forward_all(
        seq_lengths, place[None, :], tokens, cotangent, flat_weights, vectors.T,
        jnp.transpose(random_blocks, (2, 0, 1)), root_left, root_right,
    )
    *saved, use, hot = saved
    saved[-2] = saved[-2].reshape(peers, share_rows, D)
    results = backward_all(owner_slot, vt, use, [w0, w1, w2] + saved)
    layer_out, input_grad, weight_grads, new_weights, *others = finish_all(
        owner_slot, hot, results, stat_left, stat_right, flat_weights, vectors.T, moment_first.T,
        moment_second.T,
    )
    return (
        layer_out,
        input_grad,
        weight_grads.reshape(flat_weights.shape),
        new_weights.reshape(flat_weights.shape),
        *others[:2],
        *[vec.T for vec in others[2:]],
    )


def plain_body(
    tokens,
    cotangent,
    place,
    seq_lengths,
    random_blocks,
    owner_slot,
    flat_weights,
    vectors,
    moment_first,
    moment_second,
    stat_left,
    stat_right,
    root_left,
    root_right,
):
    peers = lax.axis_size("fsdp")
    share_rows = TOK_DEV // peers
    order_ids = jnp.argsort(place)
    outgoing = (
        tokens[order_ids].reshape(peers, share_rows, D),
        cotangent[order_ids].reshape(peers, share_rows, D),
    )
    arrived = (
        lax.all_to_all(outgoing[0], "fsdp", split_axis=0, concat_axis=0, tiled=True),
        lax.all_to_all(outgoing[1], "fsdp", split_axis=0, concat_axis=0, tiled=True),
    )
    inputs = arrived[0].reshape(TOK_DEV, D)
    upstream = arrived[1].reshape(TOK_DEV, D).astype(jnp.float32)
    weight_copy, vector_copy = (
        lax.all_gather(flat_weights.astype(jnp.bfloat16), "fsdp", axis=0, tiled=True),
        lax.all_gather(vectors.astype(jnp.bfloat16), "fsdp", axis=0, tiled=True),
    )
    vecs_full = vector_copy.astype(jnp.float32)
    b_up = jnp.transpose(vecs_full[:, 8:]).reshape(FF)
    seq_id, position, in_use, seq_blocks = layout(seq_lengths[0])
    picks = random_keys(random_blocks, seq_blocks)
    slot_ids = jnp.arange(TOK_DEV, dtype=jnp.int32)
    real_rows = in_use.astype(jnp.float32)[:, None]
    bias_qkv = jnp.concatenate([vecs_full[:, 0], jnp.zeros((D,), jnp.float32), vecs_full[:, 1]])
    qkv_low = (
        jnp.dot(inputs, weight_copy[:, : 3 * D], preferred_element_type=jnp.float32) + bias_qkv
    ).astype(jnp.bfloat16)
    qkv_heads = qkv_low.reshape(TOK_DEV, 3, H, HD)
    queries = qkv_heads[:, 0]
    key_heads = qkv_heads[:, 1]
    value_heads = qkv_heads[:, 2]
    block_rows = min(512, TOK_DEV)
    block_count = TOK_DEV // block_rows
    score_scale = HD ** (-0.5)

    def split_blocks(array):
        return array.reshape((block_count, block_rows) + array.shape[1:])

    block_inputs = (
        split_blocks(queries),
        split_blocks(seq_id),
        split_blocks(position),
        split_blocks(in_use),
        split_blocks(picks),
        split_blocks(slot_ids),
    )

    def scores_of(query_block, q_seq, q_pos, q_use, q_pick, q_slot):
        raw_scores = (
            jnp.einsum("qhd,khd->hqk", query_block, key_heads, preferred_element_type=jnp.float32)
            * score_scale
        )
        keep_mask = allowed(q_seq, q_pos, q_use, q_pick, q_slot, seq_id, position, in_use, slot_ids)
        return jnp.where(keep_mask, raw_scores, MASKED_SCORE)

    def forward_block(pieces):
        scores = scores_of(pieces[0], pieces[1], pieces[2], pieces[3], pieces[4], pieces[5])
        row_max = jnp.max(scores, axis=-1, keepdims=True)
        expo = jnp.exp(scores - row_max)
        row_total = jnp.sum(expo, axis=-1, keepdims=True)
        probs_low = (expo / row_total).astype(jnp.bfloat16)
        mixed_block = jnp.einsum(
            "hqk,khd->qhd", probs_low, value_heads, preferred_element_type=jnp.float32
        )
        return (mixed_block.reshape(block_rows, D), (row_max + jnp.log(row_total))[:, :, 0])

    attended, log_totals = lax.map(forward_block, block_inputs)
    mixed = attended.reshape(TOK_DEV, D).astype(jnp.bfloat16)
    branch = (
        jnp.dot(mixed, weight_copy[:, 3 * D : 4 * D], preferred_element_type=jnp.float32)
        + vecs_full[:, 2]
    )
    hidden_one = inputs.astype(jnp.float32) + branch
    x_one, norm_one_back = jax.vjp(layer_norm, hidden_one, vecs_full[:, 4], vecs_full[:, 5])
    x_one_low = x_one.astype(jnp.bfloat16)
    pre_act = (
        jnp.dot(x_one_low, weight_copy[:, 4 * D : 4 * D + FF], preferred_element_type=jnp.float32)
        + b_up
    )
    act, gelu_back = jax.vjp(gelu_tanh, pre_act)
    act_low = act.astype(jnp.bfloat16)
    ffn = contract_cols(act_low, weight_copy[:, 4 * D + FF :]) + vecs_full[:, 3]
    hidden_two = x_one + ffn
    result, norm_two_back = jax.vjp(layer_norm, hidden_two, vecs_full[:, 6], vecs_full[:, 7])
    layer_rows = (result * real_rows).astype(jnp.bfloat16)
    weight_copy = lax.all_gather(flat_weights.astype(jnp.bfloat16), "fsdp", axis=0, tiled=True)
    d_result = upstream * real_rows
    d_two, d_gain_two, d_shift_two = norm_two_back(d_result)
    d_ffn = d_two.astype(jnp.bfloat16)
    d_act = jnp.dot(d_ffn, weight_copy[:, 4 * D + FF :], preferred_element_type=jnp.float32)
    (d_pre,) = gelu_back(d_act)
    d_pre_low = d_pre.astype(jnp.bfloat16)
    grad_down = contract_rows(d_ffn, act_low)
    grad_up = contract_rows(x_one_low, d_pre_low)
    d_x_one = d_two + contract_cols(d_pre_low, weight_copy[:, 4 * D : 4 * D + FF])
    d_one, d_gain_one, d_shift_one = norm_one_back(d_x_one)
    up_sums = jnp.transpose(jnp.sum(d_pre_low.astype(jnp.float32), axis=0).reshape(FF // D, D))
    ffn_vec = jnp.concatenate(
        [
            jnp.sum(d_ffn.astype(jnp.float32), axis=0)[:, None],
            d_gain_one[:, None],
            d_shift_one[:, None],
            d_gain_two[:, None],
            d_shift_two[:, None],
            up_sums,
        ],
        axis=1,
    )
    ffn_mats = jnp.concatenate([grad_up, grad_down], axis=1)
    d_branch = d_one.astype(jnp.bfloat16)
    grad_out = contract_rows(mixed, d_branch)
    d_mixed = (
        contract_cols(d_branch, weight_copy[:, 3 * D : 4 * D])
        .astype(jnp.bfloat16)
        .reshape(TOK_DEV, H, HD)
    )

    def backward_block(carry, pieces):
        key_grad, value_grad = carry
        query_block = pieces[0]
        log_total = pieces[6]
        out_grad = pieces[7]
        scores = scores_of(pieces[0], pieces[1], pieces[2], pieces[3], pieces[4], pieces[5])
        probs = jnp.exp(scores - log_total[:, :, None])
        probs_low = probs.astype(jnp.bfloat16)
        value_grad = value_grad + jnp.einsum(
            "hqk,qhd->khd", probs_low, out_grad, preferred_element_type=jnp.float32
        )
        prob_grad = jnp.einsum(
            "qhd,khd->hqk", out_grad, value_heads, preferred_element_type=jnp.float32
        )
        score_grad = (
            probs * (prob_grad - jnp.sum(probs * prob_grad, axis=-1, keepdims=True))
        ).astype(jnp.bfloat16)
        query_grad = (
            jnp.einsum("hqk,khd->qhd", score_grad, key_heads, preferred_element_type=jnp.float32)
            * score_scale
        )
        key_grad = (
            key_grad
            + jnp.einsum(
                "hqk,qhd->khd", score_grad, query_block, preferred_element_type=jnp.float32
            )
            * score_scale
        )
        return ((key_grad, value_grad), query_grad)

    zero_heads = jnp.zeros((TOK_DEV, H, HD), jnp.float32)
    (key_grad, value_grad), query_grad = lax.scan(
        backward_block, (zero_heads, zero_heads), block_inputs + (log_totals, split_blocks(d_mixed))
    )
    d_qkv = jnp.concatenate(
        [
            query_grad.reshape(TOK_DEV, D),
            key_grad.reshape(TOK_DEV, D),
            value_grad.reshape(TOK_DEV, D),
        ],
        axis=1,
    ).astype(jnp.bfloat16)
    grad_qkv = contract_rows(inputs, d_qkv)
    d_inputs = d_one + contract_cols(d_qkv, weight_copy[:, : 3 * D])
    qkv_sums = jnp.sum(d_qkv.astype(jnp.float32), axis=0)
    attn_vec = jnp.stack(
        [qkv_sums[:D], qkv_sums[2 * D :], jnp.sum(d_branch.astype(jnp.float32), axis=0)], axis=1
    )
    attn_mats = jnp.concatenate([grad_qkv, grad_out], axis=1)
    mat_shard, vec_shard = (
        lax.psum_scatter(
            jnp.concatenate([attn_mats, ffn_mats], axis=1), "fsdp", scatter_dimension=0, tiled=True
        ),
        lax.psum_scatter(
            jnp.concatenate([attn_vec, ffn_vec], axis=1), "fsdp", scatter_dimension=0, tiled=True
        ),
    )
    mat_part = lax.psum_scatter(
        mat_shard.astype(jnp.bfloat16), "rep", scatter_dimension=1, tiled=True
    ).astype(jnp.float32)
    vec_shard = lax.psum(vec_shard, "rep")
    mat_shard = lax.all_gather(mat_part.astype(jnp.bfloat16), "rep", axis=1, tiled=True).astype(
        mat_part.dtype
    )
    grad_rows = d_inputs.astype(jnp.bfloat16)
    back_pair = (
        lax.all_to_all(
            layer_rows.reshape(peers, share_rows, D),
            "fsdp",
            split_axis=0,
            concat_axis=0,
            tiled=True,
        ),
        lax.all_to_all(
            grad_rows.reshape(peers, share_rows, D), "fsdp", split_axis=0, concat_axis=0, tiled=True
        ),
    )
    layer_out = (
        jnp.zeros((TOK_DEV, D), jnp.bfloat16).at[order_ids].set(back_pair[0].reshape(TOK_DEV, D))
    )
    input_grad = (
        jnp.zeros((TOK_DEV, D), jnp.bfloat16).at[order_ids].set(back_pair[1].reshape(TOK_DEV, D))
    )
    slot_count = stat_left.shape[0]
    rows_dev = flat_weights.shape[0]
    targets = (
        jnp.arange(slot_count, dtype=jnp.int32)[:, None, None]
        + slot_count * jnp.arange(peers, dtype=jnp.int32)[None, :, None]
    )
    select = (owner_slot[None, None, :] == targets).astype(jnp.float32)
    grad_pieces = mat_shard.reshape(rows_dev, NBLK, D)
    outbound = jnp.einsum("snb,rbc->snrc", select, grad_pieces, precision=PRECISE)
    inbound = lax.all_to_all(
        outbound.astype(jnp.bfloat16), "fsdp", split_axis=1, concat_axis=1, tiled=True
    ).astype(outbound.dtype)
    grad_blocks = inbound.reshape(slot_count, D, D)
    new_left = STAT_DECAY * stat_left + (1.0 - STAT_DECAY) * jnp.einsum(
        "sij,skj->sik", grad_blocks, grad_blocks, precision=PRECISE
    )
    new_right = STAT_DECAY * stat_right + (1.0 - STAT_DECAY) * jnp.einsum(
        "sji,sjk->sik", grad_blocks, grad_blocks, precision=PRECISE
    )
    left_applied = jnp.einsum("sij,sjk->sik", root_left, grad_blocks, precision=PRECISE)
    direction = jnp.einsum("sij,sjk->sik", left_applied, root_right, precision=PRECISE)
    update = direction * lax.rsqrt(
        jnp.mean(direction * direction, axis=(1, 2), keepdims=True) + RMS_EPS
    )
    returned = lax.all_to_all(
        update.reshape(slot_count, peers, rows_dev, D).astype(jnp.bfloat16),
        "fsdp",
        split_axis=1,
        concat_axis=1,
        tiled=True,
    ).astype(jnp.float32)
    step_matrix = jnp.einsum("snb,snrc->rbc", select, returned, precision=PRECISE).reshape(
        rows_dev, NBLK * D
    )
    new_weights = flat_weights - LR_MATRIX * step_matrix
    first_bias = 1.0 - BETA_ONE**STEP
    second_bias = 1.0 - BETA_TWO**STEP
    new_first = BETA_ONE * moment_first + (1.0 - BETA_ONE) * vec_shard
    new_second = BETA_TWO * moment_second + (1.0 - BETA_TWO) * vec_shard * vec_shard
    first_fixed = new_first / first_bias
    second_fixed = new_second / second_bias
    new_vectors = vectors - LR_VECTOR * first_fixed / (jnp.sqrt(second_fixed) + ADAM_EPS)
    return (
        layer_out,
        input_grad,
        mat_shard,
        new_weights,
        new_left,
        new_right,
        new_first,
        new_second,
        new_vectors,
    )


def solution(mesh):
    in_specs = (
        P(("rep", "fsdp"), None),
        P(("rep", "fsdp"), None),
        P(("rep", "fsdp")),
        P(("rep", "fsdp"), None),
        P(("rep", "fsdp"), None, None),
        P(),
        P("fsdp", None),
        P("fsdp", None),
        P("fsdp", None),
        P("fsdp", None),
        P("fsdp", None, None),
        P("fsdp", None, None),
        P("fsdp", None, None),
        P("fsdp", None, None),
    )
    out_specs = (
        P(("rep", "fsdp"), None),
        P(("rep", "fsdp"), None),
        P("fsdp", None),
        P("fsdp", None),
        P("fsdp", None, None),
        P("fsdp", None, None),
        P("fsdp", None),
        P("fsdp", None),
        P("fsdp", None),
    )
    shaped = mesh.shape["fsdp"] == 8 and mesh.shape["rep"] == 4
    body = fast_body if shaped else plain_body
    return jax.shard_map(body, mesh=mesh, in_specs=in_specs, out_specs=out_specs, check_vma=False)
```
